32 devices in a mesh: dp: 8 (over z, x), fsdp: 4 (over y, core).
Axes of the slice: x: 2, y: 2, z: 4, core: 2. Of those that a mesh axis runs over, the one named last changes fastest.
Arguments:
- inputs: bfloat16 [64, 529, 768], P(('dp', 'fsdp')), may hold values from -6 to 6
- row_kind: int32 [64], P(('dp', 'fsdp')), may hold values from 0 to 1
- ln1_gain: bfloat16 [768], P(('dp', 'fsdp')), may hold values from 0.25 to 1.75
- ln1_bias: bfloat16 [768], P(('dp', 'fsdp')), may hold values from -1.75 to 1.75
- w_qkv: bfloat16 [768, 2304], P(('dp', 'fsdp')), may hold values from -0.21875 to 0.21875
- b_query: bfloat16 [768], P(('dp', 'fsdp')), may hold values from -3 to 3
- b_value: bfloat16 [768], P(('dp', 'fsdp')), may hold values from -3 to 3
- w_out: bfloat16 [768, 768], P(('dp', 'fsdp')), may hold values from -1.75 to 1.75
- b_out: bfloat16 [768], P(('dp', 'fsdp')), may hold values from -1.75 to 1.75
- ln2_gain: bfloat16 [768], P(('dp', 'fsdp')), may hold values from 0.25 to 1.75
- ln2_bias: bfloat16 [768], P(('dp', 'fsdp')), may hold values from -1.75 to 1.75
- w_up: bfloat16 [768, 3072], P(('dp', 'fsdp')), may hold values from -0.21875 to 0.21875
- b_up: bfloat16 [3072], P(('dp', 'fsdp')), may hold values from -3 to 3
- w_down: bfloat16 [3072, 768], P(('dp', 'fsdp')), may hold values from -0.109375 to 0.109375
- b_down: bfloat16 [768], P(('dp', 'fsdp')), may hold values from -1.75 to 1.75
- out_grad: bfloat16 [64, 529, 768], P(('dp', 'fsdp')), may hold values from -6 to 6
Outputs:
- outputs: bfloat16 [64, 529, 768], P(('dp', 'fsdp'))
- input_grad: bfloat16 [64, 529, 768], P(('dp', 'fsdp'))
- grad_ln1_gain: float32 [768], P(('dp', 'fsdp'))
- grad_ln1_bias: float32 [768], P(('dp', 'fsdp'))
- grad_w_qkv: float32 [768, 2304], P(('dp', 'fsdp'))
- grad_b_query: float32 [768], P(('dp', 'fsdp'))
- grad_b_value: float32 [768], P(('dp', 'fsdp'))
- grad_w_out: float32 [768, 768], P(('dp', 'fsdp'))
- grad_b_out: float32 [768], P(('dp', 'fsdp'))
- grad_ln2_gain: float32 [768], P(('dp', 'fsdp'))
- grad_ln2_bias: float32 [768], P(('dp', 'fsdp'))
- grad_w_up: float32 [768, 3072], P(('dp', 'fsdp'))
- grad_b_up: float32 [3072], P(('dp', 'fsdp'))
- grad_w_down: float32 [3072, 768], P(('dp', 'fsdp'))
- grad_b_down: float32 [768], P(('dp', 'fsdp'))
The draws below stay inside these ranges and needn't reach their ends.
Inputs may be any that keep to these rules, and one draw needn't show every extreme that they name: `row_kind`: 0 marks a row holding one strip of 529 patches; 1 marks a row holding two half strips of 264 patches followed by one padding slot.
All inputs are finite; a program needn't handle non-finite values.
Results may differ from the reference program's by a relative error of at most 0.012.
Values may be sent and summed in bfloat16 or wider, within the bound.
A program may use at most 256 MiB of HBM per device.

```python
import math
from functools import partial
import jax
import jax.numpy as jnp
from jax import lax

D = 768
HEADS = 12
HEAD_DIM = 64
FF = 3072
SEQ = 529
HALF = 264
ROWS = 64


def with_ends(values, own_key, low, largest):
    dims = values.shape
    spot = [jax.random.randint(jax.random.fold_in(own_key, axis), (), 0, dims[axis]) for axis in range(len(dims))]
    values = values.at[tuple(spot)].set(low)
    longest = dims.index(max(dims))
    spot[longest] = (spot[longest] + 1) % dims[longest]
    return values.at[tuple(spot)].set(largest)


def spiked(drawn, stream_key, source, target, blocks, factor):
    owner, partner = [(jnp.arange(drawn.shape[dim]) // (drawn.shape[dim] // blocks)).reshape([-1 if axis == dim else 1 for axis in range(drawn.ndim)]) for dim in (source, target)]
    chosen = jax.random.permutation(stream_key, blocks)[partner]
    strong = (owner == chosen) | (owner == (partner + blocks // 2) % blocks)
    return jnp.where(strong, factor * drawn, drawn)


def steps_of(stream_key, dims, shards, least, high):
    gain = 1.0
    for dim, blocks in shards:
        heights = jax.random.uniform(jax.random.fold_in(jax.random.fold_in(stream_key, 6), dim), (blocks,), jnp.float32, least / len(shards), high / len(shards))
        gain = gain * jnp.repeat(jnp.exp(heights), dims[dim] // blocks).reshape((-1,) + (1,) * (len(dims) - 1 - dim))
    return gain


def bell_draw(rng, extent, scale, most, cuts=(), kind=jnp.bfloat16):
    level = steps_of(rng, extent, cuts, -0.22, 0.18) if cuts else 1.0
    values = jax.random.normal(rng, extent, jnp.float32) * scale * level
    return jnp.minimum(jnp.maximum(values, -most), most).astype(kind)


def bell_draw_with(own_key, dims, scale, reach, cuts, heavy, kind=jnp.bfloat16):
    array = scale * jax.random.normal(own_key, dims, jnp.float32)
    if cuts:
        array = array * steps_of(own_key, dims, cuts, -0.22, 0.18)
    return jnp.clip(spiked(array, jax.random.fold_in(own_key, 3), *heavy), -reach, reach).astype(kind)


def setup_inputs(seed: int = 0) -> dict:
    streams_of = jax.random.split(jax.random.key(seed), 17)
    inputs = bell_draw(streams_of[0], (ROWS, SEQ, D), 1.0, 6.0, ((0, 32),))
    row_kind = with_ends(jax.random.randint(streams_of[1], (ROWS,), 0, 2), jax.random.fold_in(streams_of[1], 1), 0, 1).astype(jnp.int32)
    ln1_gain = jnp.clip(1.0 + 0.15 * jax.random.normal(streams_of[2], (D,), jnp.float32), 0.25, 1.75).astype(jnp.bfloat16)
    ln1_bias = bell_draw(streams_of[3], (D,), 0.3, 1.75, ((0, 32),))
    w_qkv = bell_draw(streams_of[4], (D, 3 * D), D ** -0.5, 0.21875, ((0, 32),))
    b_query = bell_draw(streams_of[5], (D,), 0.5, 3.0, ((0, 32),))
    b_value = bell_draw(streams_of[6], (D,), 0.5, 3.0, ((0, 32),))
    w_out = bell_draw(streams_of[7], (D, D), (D // 64) ** -0.5, 1.75, ((0, 32),))
    b_out = bell_draw(streams_of[8], (D,), 0.3, 1.75, ((0, 32),))
    ln2_gain = jnp.clip(1.0 + 0.15 * jax.random.normal(streams_of[9], (D,), jnp.float32), 0.25, 1.75).astype(jnp.bfloat16)
    ln2_bias = bell_draw(streams_of[10], (D,), 0.3, 1.75, ((0, 32),))
    w_up = bell_draw(streams_of[11], (D, FF), D ** -0.5, 0.21875, ((0, 32),))
    b_up = bell_draw(streams_of[12], (FF,), 0.5, 3.0, ((0, 32),))
    w_down = bell_draw(streams_of[13], (FF, D), FF ** -0.5, 0.109375, ((0, 32),))
    b_down = bell_draw(streams_of[14], (D,), 0.3, 1.75, ((0, 32),))
    out_grad = bell_draw_with(streams_of[15], (ROWS, SEQ, D), 1.0, 6.0, ((0, 32),), (0, 2, 32, 2.75))
    return {"inputs": inputs, "row_kind": row_kind, "ln1_gain": ln1_gain, "ln1_bias": ln1_bias, "w_qkv": w_qkv, "b_query": b_query, "b_value": b_value, "w_out": w_out, "b_out": b_out, "ln2_gain": ln2_gain, "ln2_bias": ln2_bias, "w_up": w_up, "b_up": b_up, "w_down": w_down, "b_down": b_down, "out_grad": out_grad}


@jax.custom_vjp
def low(v):
    return lax.optimization_barrier(v.astype(jnp.bfloat16)).astype(jnp.float32)

@jax.custom_vjp
def low_back(v):
    return v

def low_keep(v):
    return (low(v), None)

def low_pass(kept, grad):
    return (grad,)

def back_keep(v):
    return (v, None)

def back_low(kept, grad):
    return (low(grad),)
low.defvjp(low_keep, low_pass)
low_back.defvjp(back_keep, back_low)
EPSILON = 1e-06
HIGHEST = lax.Precision.HIGHEST

def segments(row_kind):
    position = jnp.arange(SEQ, dtype=jnp.int32)
    packed = jnp.where(position < HALF, 0, jnp.where(position < 2 * HALF, 1, 2)).astype(jnp.int32)
    return jnp.where(row_kind[:, None] == 1, packed[None, :], 0).astype(jnp.int32)

def normalize(values, norm_gain, norm_shift):
    row_mean = lax.optimization_barrier(jnp.mean(values, -1, keepdims=True))
    centred = values - row_mean
    inverse = lax.rsqrt(lax.optimization_barrier(jnp.mean(centred * centred, -1, keepdims=True)) + EPSILON)
    return centred * inverse * norm_gain + norm_shift

def attend_row(packed_rows):
    query_rows, key_rows, value_rows, segment = packed_rows
    raw_scores = jnp.einsum('qhd,khd->hqk', query_rows, key_rows, precision=HIGHEST)
    scores = low_back(raw_scores * (1.0 / math.sqrt(HEAD_DIM)))
    same = segment[:, None] == segment[None, :]
    scores = jnp.where(same[None, :, :], scores, -1e+30)
    attention_probs = jax.nn.softmax(scores, axis=-1)
    return jnp.einsum('hqk,khd->qhd', low(attention_probs), value_rows, precision=HIGHEST)

def exact_gelu(values):
    return jax.nn.gelu(values, approximate=False)

def layer(activations, params, segment):
    ln1_gain, ln1_bias, w_qkv, b_query, b_value, w_out, b_out, ln2_gain, ln2_bias, w_up, b_up, w_down, b_down = params
    group, length, width = activations.shape
    normed_in = low(normalize(activations, ln1_gain, ln1_bias))
    qkv_bias = jnp.concatenate([b_query, jnp.zeros_like(b_query), b_value])
    projected = low_back(low(jnp.einsum('gsd,de->gse', normed_in, w_qkv, precision=HIGHEST) + qkv_bias))
    split = projected.reshape(group, length, 3, HEADS, HEAD_DIM)
    mixed = lax.map(jax.checkpoint(attend_row), (split[:, :, 0], split[:, :, 1], split[:, :, 2], segment))
    mixed = low_back(low(mixed.reshape(group, length, width)))
    middle = activations + low_back(jnp.einsum('gsd,de->gse', mixed, w_out, precision=HIGHEST) + b_out)
    normed_mid = low(normalize(middle, ln2_gain, ln2_bias))
    up_proj = low_back(jnp.einsum('gsd,df->gsf', normed_mid, w_up, precision=HIGHEST) + b_up)
    hidden = low(exact_gelu(up_proj))
    return middle + low_back(jnp.einsum('gsf,fd->gsd', hidden, w_down, precision=HIGHEST) + b_down)

def reference(inputs, row_kind, ln1_gain, ln1_bias, w_qkv, b_query, b_value, w_out, b_out, ln2_gain, ln2_bias, w_up, b_up, w_down, b_down, out_grad):
    params = tuple((item.astype(jnp.float32) for item in (ln1_gain, ln1_bias, w_qkv, b_query, b_value, w_out, b_out, ln2_gain, ln2_bias, w_up, b_up, w_down, b_down)))
    segment = segments(row_kind).reshape(ROWS // 4, 4, SEQ)
    activations = inputs.astype(jnp.float32).reshape(ROWS // 4, 4, SEQ, D)
    cotangent = out_grad.astype(jnp.float32).reshape(ROWS // 4, 4, SEQ, D)

    def step(totals, batch):
        act_rows, seg_rows, grad_rows = batch
        result, pull = jax.vjp(partial(layer, segment=seg_rows), act_rows, params)
        grad_input, grad_params = pull(grad_rows)
        totals = jax.tree.map(jnp.add, totals, grad_params)
        return (totals, (result.astype(jnp.bfloat16), grad_input.astype(jnp.bfloat16)))
    zeros = tuple((jnp.zeros_like(item) for item in params))
    totals, (outputs, input_grad) = lax.scan(step, zeros, (activations, segment, cotangent))
    return (outputs.reshape(ROWS, SEQ, D), input_grad.reshape(ROWS, SEQ, D), totals[0], totals[1], totals[2], totals[3], totals[4], totals[5], totals[6], totals[7], totals[8], totals[9], totals[10], totals[11], totals[12])
```

```python
import functools
import math

import jax
import jax.numpy as jnp
from jax import lax
from jax.experimental import pallas as pl
from jax.experimental.pallas import tpu as pltpu
from jax.sharding import PartitionSpec as P

D = 768
HD = 64
FF = 3072
SEQ = 529
HALF = 264
EPS = 1e-06
S = 544
T = 2 * S
MB = 272
HG = 4
QW = HG * HD
GW = 3 * QW
FC = 512
OUT_AT = 3 * D
UP_AT = 4 * D
AW = 4 * D + FF
F32 = jnp.float32
BF = jnp.bfloat16
LIMIT = 60 * 2**20
MESH = pl.DeviceIdType.MESH
NN = (((1,), (0,)), ((), ()))
NT = (((1,), (1,)), ((), ()))
TN = (((0,), (0,)), ((), ()))


def mm(a, b, dims=NN):
    return lax.dot_general(a, b, dims, preferred_element_type=F32)


def norm_parts(values):
    mean = jnp.mean(values, -1, keepdims=True)
    centred = values - mean
    inverse = lax.rsqrt(jnp.mean(centred * centred, -1, keepdims=True) + EPS)
    return centred * inverse, inverse


def norm_pull(grad, normed, inverse, gain):
    scaled = grad * gain
    return inverse * (
        scaled
        - jnp.mean(scaled, -1, keepdims=True)
        - normed * jnp.mean(scaled * normed, -1, keepdims=True)
    )


def gelu_both(u):
    a = jnp.abs(u)
    t = 1.0 / (1.0 + (0.3275911 / math.sqrt(2.0)) * a)
    e = jnp.exp(-0.5 * u * u)
    poly = t * (
        0.254829592
        + t * (-0.284496736 + t * (1.421413741 + t * (-1.453152027 + t * 1.061405429)))
    )
    tail = 0.5 * poly * e
    phi = jnp.where(u < 0, tail, 1.0 - tail)
    return u * phi, phi + u * e * (1.0 / math.sqrt(2.0 * math.pi))


def head_lanes(shape, e):
    lane = lax.broadcasted_iota(jnp.int32, shape, 1)
    return (lane // HD) == e


def whole(shape):
    return pl.BlockSpec(shape, lambda *_: (0,) * len(shape))


def rows_of(i):
    return pl.ds(pl.multiple_of(i * MB, 16), MB)


G1, B1, BQ, BV, BO, G2, B2, BD = range(8)


def attn_fwd_kernel(
    kind_ref, x_ref, wg_ref, bqkv_ref, wo_ref, vec_ref,
    h1_ref, qkv_ref, p_ref, attn_ref, rl_ref, x1_ref, fa, fb,
):
    hq, r = pl.program_id(0), pl.program_id(1)

    @pl.when((hq == 0) & (r == 0))
    def _():
        for row in range(2):
            h1_ref[pl.ds(row * S + S - 16, 16), :] = jnp.zeros((16, D), BF)
            n1, _s = norm_parts(x_ref[row].astype(F32))
            h1_ref[pl.ds(row * S, SEQ), :] = (n1 * vec_ref[G1:G1 + 1, :] + vec_ref[B1:B1 + 1, :]).astype(BF)
            slot = lax.broadcasted_iota(jnp.int32, (S, 128), 0)
            lane = lax.broadcasted_iota(jnp.int32, (S, 128), 1)
            packed = jnp.where(slot < HALF, 0, jnp.where(slot < 2 * HALF, 1, 2))
            seg = jnp.where(kind_ref[row] == 1, packed, 0)
            fa[row] = jnp.where((lane < 3) & (seg == lane), -1e30, 0.0).astype(BF)
            fb[row] = jnp.where((lane < 3) & ((seg != lane) | (slot >= SEQ)), 1.0, 0.0).astype(BF)

    @pl.when(r == 0)
    def _():
        @pl.loop(0, T // MB)
        def _(i):
            rows = rows_of(i)
            qkv_ref[rows, :] = (mm(h1_ref[rows, :], wg_ref[...]) + bqkv_ref[...]).astype(BF)

    rows = pl.ds(pl.multiple_of(r * S, 16), S)
    feat_q, feat_k = fa[r], fb[r]
    ones = jnp.ones((S, 128), BF)
    scale = math.log2(math.e) / math.sqrt(HD)
    for j in range(HG // 2):
        at = j * 384
        qp, kp, vp = (qkv_ref[rows, at + 128 * n: at + 128 * (n + 1)] for n in range(3))
        kcat = jnp.concatenate([kp, feat_k], 1)
        total = None
        inv = None
        for e in range(2):
            keep = head_lanes((S, 128), e)
            qcat = jnp.concatenate([jnp.where(keep, qp, jnp.zeros_like(qp)), feat_q], 1)
            s = mm(qcat, kcat, NT)
            m = jnp.max(s, -1, keepdims=True)
            pb = jnp.exp2((s - m) * scale).astype(BF)
            p_ref[0, 2 * j + e] = pb
            vcat = jnp.concatenate([jnp.where(keep, vp, jnp.zeros_like(vp)), ones], 1)
            o = mm(pb, vcat)
            rl = 1.0 / o[:, 128:]
            part = o[:, :128] * rl
            total = part if total is None else total + part
            inv = rl if inv is None else jnp.where(keep, rl, inv)
        out = pl.ds(pl.multiple_of(hq * QW + j * 128, 128), 128)
        attn_ref[rows, out] = total.astype(BF)
        rl_ref[rows, out] = inv

    @pl.when((hq == D // QW - 1) & (r == 1))
    def _():
        for row in range(2):
            x1_ref[pl.ds(row * S + S - 16, 16), :] = jnp.zeros((16, D), F32)
            x1_ref[pl.ds(row * S, SEQ), :] = x_ref[row].astype(F32)

        @pl.loop(0, T // MB)
        def _(i):
            rr = rows_of(i)
            x1_ref[rr, :] = x1_ref[rr, :] + mm(attn_ref[rr, :], wo_ref[...]) + vec_ref[BO:BO + 1, :]


def attn_fwd(kind, x, wide, bqkv, vec):
    return pl.pallas_call(
        attn_fwd_kernel,
        grid=(D // QW, 2),
        in_specs=[
            pl.BlockSpec(memory_space=pltpu.SMEM), whole((2, SEQ, D)),
            pl.BlockSpec((D, GW), lambda h, r: (0, h)), pl.BlockSpec((1, GW), lambda h, r: (0, h)),
            pl.BlockSpec((D, D), lambda h, r: (0, 3)), whole((8, D)),
        ],
        out_specs=[
            whole((T, D)), pl.BlockSpec((T, GW), lambda h, r: (0, h)),
            pl.BlockSpec((1, HG, S, S), lambda h, r: (r, h, 0, 0)),
            whole((T, D)), whole((T, D)), whole((T, D)),
        ],
        out_shape=[
            jax.ShapeDtypeStruct((T, D), BF), jax.ShapeDtypeStruct((T, 3 * D), BF),
            jax.ShapeDtypeStruct((2, D // HD, S, S), BF),
            jax.ShapeDtypeStruct((T, D), BF), jax.ShapeDtypeStruct((T, D), F32), jax.ShapeDtypeStruct((T, D), F32),
        ],
        scratch_shapes=[pltpu.VMEM((2, S, 128), BF), pltpu.VMEM((2, S, 128), BF)],
        compiler_params=pltpu.CompilerParams(vmem_limit_bytes=LIMIT),
        name="attention_forward",
    )(kind, x, wide, bqkv, wide, vec)


def ffn_kernel(
    x1_ref, dm_ref, wu_ref, wd_ref, bu_ref, vec_ref,
    out_ref, dx1_ref, gwu_ref, gwd_ref, gbu_ref, gg2_ref, gb2_ref, gbd_ref,
    h2, h2t, dm, yacc, dacc, gs, dus,
):
    c = pl.program_id(0)

    @pl.when(c == 0)
    def _():
        for row in range(2):
            dm[pl.ds(row * S + S - 16, 16), :] = jnp.zeros((16, D), BF)
            dm[pl.ds(row * S, SEQ), :] = dm_ref[row]

        @pl.loop(0, T // MB)
        def _(i):
            rows = rows_of(i)
            x1 = x1_ref[rows, :]
            n2, _s = norm_parts(x1)
            h2[rows, :] = (n2 * vec_ref[G2:G2 + 1, :] + vec_ref[B2:B2 + 1, :]).astype(BF)
            yacc[rows, :] = x1 + vec_ref[BD:BD + 1, :]
            dacc[rows, :] = jnp.zeros((MB, D), F32)
        h2t[...] = h2[...].T
        gbd_ref[...] = jnp.sum(dm[...].astype(F32), 0, keepdims=True)

    gbu_ref[...] = jnp.zeros_like(gbu_ref)

    @pl.loop(0, T // MB)
    def _(i):
        rows = rows_of(i)
        u = mm(h2[rows, :], wu_ref[...]) + bu_ref[...]
        g, slope = gelu_both(u)
        gb = g.astype(BF)
        gs[rows, :] = gb
        yacc[rows, :] += mm(gb, wd_ref[...])
        du = (mm(dm[rows, :], wd_ref[...], NT) * slope).astype(BF)
        dus[rows, :] = du
        gbu_ref[...] += jnp.sum(du.astype(F32), 0, keepdims=True)
        dacc[rows, :] += mm(du, wu_ref[...], NT)

    for t in range(FC // 256):
        cols = pl.ds(t * 256, 256)
        gwd_ref[cols, :] = mm(gs[:, cols], dm[...], TN).astype(BF)

    @pl.loop(0, D // 256)
    def _(t):
        rows = pl.ds(pl.multiple_of(t * 256, 256), 256)
        gwu_ref[rows, :] = mm(h2t[rows, :], dus[...]).astype(BF)

    @pl.when(c == FF // FC - 1)
    def _():
        gg2_ref[...] = jnp.zeros_like(gg2_ref)
        gb2_ref[...] = jnp.zeros_like(gb2_ref)
        for row in range(2):
            out_ref[row] = yacc[pl.ds(row * S, SEQ), :].astype(BF)

        @pl.loop(0, T // MB)
        def _(i):
            rows = rows_of(i)
            n2, s2 = norm_parts(x1_ref[rows, :])
            dh = dacc[rows, :]
            gg2_ref[...] += jnp.sum(dh * n2, 0, keepdims=True)
            gb2_ref[...] += jnp.sum(dh, 0, keepdims=True)
            dx1_ref[rows, :] = dm[rows, :].astype(F32) + norm_pull(dh, n2, s2, vec_ref[G2:G2 + 1, :])


def ffn(x1, dm, wide, down, bu, vec):
    one = jax.ShapeDtypeStruct((1, D), F32)
    return pl.pallas_call(
        ffn_kernel,
        grid=(FF // FC,),
        in_specs=[
            whole((T, D)), whole((2, SEQ, D)),
            pl.BlockSpec((D, FC), lambda c: (0, c + UP_AT // FC)), pl.BlockSpec((FC, D), lambda c: (c, 0)),
            pl.BlockSpec((1, FC), lambda c: (0, c)), whole((8, D)),
        ],
        out_specs=[
            whole((2, SEQ, D)), whole((T, D)),
            pl.BlockSpec((D, FC), lambda c: (0, c)), pl.BlockSpec((FC, D), lambda c: (c, 0)),
            pl.BlockSpec((1, FC), lambda c: (0, c)), whole((1, D)), whole((1, D)), whole((1, D)),
        ],
        out_shape=[
            jax.ShapeDtypeStruct((2, SEQ, D), BF), jax.ShapeDtypeStruct((T, D), F32),
            jax.ShapeDtypeStruct((D, FF), BF), jax.ShapeDtypeStruct((FF, D), BF),
            jax.ShapeDtypeStruct((1, FF), F32), one, one, one,
        ],
        scratch_shapes=[
            pltpu.VMEM((T, D), BF), pltpu.VMEM((D, T), BF), pltpu.VMEM((T, D), BF),
            pltpu.VMEM((T, D), F32), pltpu.VMEM((T, D), F32),
            pltpu.VMEM((T, FC), BF), pltpu.VMEM((T, FC), BF),
        ],
        compiler_params=pltpu.CompilerParams(vmem_limit_bytes=LIMIT),
        name="feed_forward",
    )(x1, dm, wide, down, bu, vec)


def attn_bwd_kernel(
    x_ref, dx1_ref, h1_ref, qkv_ref, p_ref, attn_ref, rl_ref, wo_ref, wqkv_ref, vec_ref,
    gx_ref, gwqkv_ref, gwo_ref, gbqkv_ref, gbo_ref, gg1_ref, gb1_ref,
    da, dos, h1t, dqkv,
):
    hq, r = pl.program_id(0), pl.program_id(1)

    @pl.when((hq == 0) & (r == 0))
    def _():
        gbo_ref[...] = jnp.zeros_like(gbo_ref)

        @pl.loop(0, T // MB)
        def _(i):
            rows = rows_of(i)
            d = dx1_ref[rows, :].astype(BF)
            da[rows, :] = d
            gbo_ref[...] += jnp.sum(d.astype(F32), 0, keepdims=True)
            dos[rows, :] = (mm(d, wo_ref[...], NT) * rl_ref[rows, :]).astype(BF)
        h1t[...] = h1_ref[...].T

    rows = pl.ds(pl.multiple_of(r * S, 16), S)
    scale = 1.0 / math.sqrt(HD)
    for j in range(HG // 2):
        at = j * 384
        qp, kp, vp = (qkv_ref[rows, at + 128 * n: at + 128 * (n + 1)] for n in range(3))
        do = dos[rows, pl.ds(pl.multiple_of(hq * QW + j * 128, 128), 128)]
        prod = do.astype(F32) * attn_ref[rows, j * 128:(j + 1) * 128].astype(F32)
        dq = dk = dv = None
        for e in range(2):
            keep = head_lanes((S, 128), e)
            zero = jnp.zeros_like(qp)
            doe = jnp.where(keep, do, zero)
            dot = jnp.sum(jnp.where(keep, prod, 0.0), -1, keepdims=True)
            p = p_ref[0, 2 * j + e]
            ds = (p.astype(F32) * (mm(doe, vp, NT) - dot)).astype(BF)
            a = mm(ds, jnp.where(keep, kp, zero))
            b = mm(ds, jnp.where(keep, qp, zero), TN)
            c = mm(p, doe, TN)
            dq, dk, dv = (a, b, c) if dq is None else (dq + a, dk + b, dv + c)
        for n, part in enumerate((dq * scale, dk * scale, dv)):
            col = hq * GW + j * 384 + n * 128
            dqkv[rows, pl.ds(pl.multiple_of(col, 128), 128)] = part.astype(BF)

    @pl.when(r == 1)
    def _():
        part = dqkv[:, pl.ds(pl.multiple_of(hq * GW, 128), GW)]
        gbqkv_ref[...] = jnp.sum(part.astype(F32), 0, keepdims=True)

        @pl.loop(0, D // 256)
        def _(t):
            rr = pl.ds(pl.multiple_of(t * 256, 256), 256)
            gwqkv_ref[rr, :] = mm(h1t[rr, :], part).astype(BF)
        gwo_ref[...] = mm(attn_ref[...], da[...], TN).astype(BF)

    @pl.when((hq == D // QW - 1) & (r == 1))
    def _():
        gg1_ref[...] = jnp.zeros_like(gg1_ref)
        gb1_ref[...] = jnp.zeros_like(gb1_ref)
        for row in range(2):
            rr = pl.ds(row * S, SEQ)
            dh = mm(dqkv[pl.ds(row * S, S), :], wqkv_ref[...], NT)[:SEQ]
            n1, s1 = norm_parts(x_ref[row].astype(F32))
            gg1_ref[...] += jnp.sum(dh * n1, 0, keepdims=True)
            gb1_ref[...] += jnp.sum(dh, 0, keepdims=True)
            gx_ref[row] = (dx1_ref[rr, :] + norm_pull(dh, n1, s1, vec_ref[G1:G1 + 1, :])).astype(BF)


def attn_bwd(x, dx1, h1, qkv, p, attn, rl, wide, vec):
    act = pl.BlockSpec((T, QW), lambda h, r: (0, h))
    one = jax.ShapeDtypeStruct((1, D), F32)
    return pl.pallas_call(
        attn_bwd_kernel,
        grid=(D // QW, 2),
        in_specs=[
            whole((2, SEQ, D)), whole((T, D)), whole((T, D)), pl.BlockSpec((T, GW), lambda h, r: (0, h)),
            pl.BlockSpec((1, HG, S, S), lambda h, r: (r, h, 0, 0)), act, whole((T, D)),
            pl.BlockSpec((D, D), lambda h, r: (0, 3)), whole((D, 3 * D)), whole((8, D)),
        ],
        out_specs=[
            whole((2, SEQ, D)), pl.BlockSpec((D, GW), lambda h, r: (0, h)),
            pl.BlockSpec((QW, D), lambda h, r: (h, 0)),
            pl.BlockSpec((1, GW), lambda h, r: (0, h)), whole((1, D)), whole((1, D)), whole((1, D)),
        ],
        out_shape=[
            jax.ShapeDtypeStruct((2, SEQ, D), BF), jax.ShapeDtypeStruct((D, 3 * D), BF), jax.ShapeDtypeStruct((D, D), BF),
            jax.ShapeDtypeStruct((1, 3 * D), F32), one, one, one,
        ],
        scratch_shapes=[
            pltpu.VMEM((T, D), BF), pltpu.VMEM((T, D), BF), pltpu.VMEM((D, T), BF), pltpu.VMEM((T, 3 * D), BF),
        ],
        compiler_params=pltpu.CompilerParams(vmem_limit_bytes=LIMIT),
        name="attention_backward",
    )(x, dx1, h1, qkv, p, attn, rl, wide, wide, vec)


NZ = 4
CH = 48
HW = 384
SW = 384


def where_am_i():
    dp, fs = lax.axis_index("dp"), lax.axis_index("fsdp")
    return lax.div(dp, 2), lax.rem(dp, 2), lax.div(fs, 2), lax.rem(fs, 2)


def device(z, x, y, c):
    return (z * 2 + x, y * 2 + c)


def partners(z, x, y, c):
    found = [device(lax.rem(z + k, NZ), x, y, c) for k in (1, 2, 3)]
    return found + [device(z, 1 - x, y, c), device(z, x, 1 - y, c), device(z, x, y, 1 - c)]


def greet(here):
    barrier = pltpu.get_barrier_semaphore()
    others = partners(*here)
    for other in others:
        pl.semaphore_signal(barrier, inc=1, device_id=other, device_id_type=MESH)
    pl.semaphore_wait(barrier, len(others))


def remote(src, dst, sems, n, target):
    return pltpu.make_async_remote_copy(
        src_ref=src, dst_ref=dst, send_sem=sems[0].at[n], recv_sem=sems[1].at[n],
        device_id=target, device_id_type=MESH,
    )


class Gather:
    COPIES = 7

    def __init__(self, here, sems, base, view, other_view, first):
        self.here, self.sems, self.base = here, sems, base
        z, x, y, c = here
        one = lambda i: pl.ds(i, 1)
        every = pl.ds(0, NZ)
        peers = partners(*here)
        mine = view(one(z), one(x), one(y))
        column = view(every, one(x), one(y))
        fx, fy = jnp.where(c == 0, 1 - x, x), jnp.where(c == 0, y, 1 - y)
        tx, ty = jnp.where(c == 0, x, 1 - x), jnp.where(c == 0, 1 - y, y)
        passed = view(every, one(fx), one(fy))
        all_of = view(every, pl.ds(0, 2), pl.ds(0, 2))
        make = lambda n, src, dst, to: remote(src, dst, sems, base + n, to)
        self.along_z = [make(k, first, mine, peers[k]) for k in range(3)]
        self.along_x = make(3, column, column, peers[3])
        self.along_y = make(4, column, column, peers[4])
        self.diagonal = make(5, passed, passed, device(z, tx, ty, c))
        self.sibling = make(6, all_of, all_of, peers[5])

    def start(self, phase):
        if phase == 0:
            for copy in self.along_z:
                copy.start()
        elif phase == 1:
            for copy in self.along_z:
                copy.wait_recv()
            self.along_x.start()
            self.along_y.start()
        elif phase == 2:
            self.along_x.wait_recv()
            self.along_y.wait_recv()
            self.diagonal.start()
        elif phase == 3:
            self.diagonal.wait_recv()
            self.sibling.start()
        else:
            self.sibling.wait_recv()
            for copy in (*self.along_z, self.along_x, self.along_y, self.diagonal, self.sibling):
                copy.wait_send()


N_WIDE = AW // (2 * HW)
N_DOWN = 2
DH = 2 * CH


def gather_kernel(
    wqkv_ref, wout_ref, wup_ref, wdown_ref, small_ref,
    wide_ref, down_ref, vec_ref, bu_ref, bqkv_ref,
    staged, swap, block, smalls, sems_s, sems_r, swap_s, swap_r, own_sem, small_s, small_r,
):
    here = where_am_i()
    z, x, y, c = here
    peers = partners(*here)
    for pair in range(6):
        for n in range(3):
            at = pair * 384 + n * 128
            staged[:, at:at + 128] = wqkv_ref[:, n * D + pair * 128:n * D + (pair + 1) * 128].astype(F32)
    staged[:, OUT_AT:UP_AT] = wout_ref[...].astype(F32)
    staged[:, UP_AT:] = wup_ref[...].astype(F32)
    smalls[z, x, y, c] = small_ref[...]
    greet(here)

    sems = (sems_s, sems_r)

    def half(i, core):
        return pl.ds(pl.multiple_of(i * 2 * HW + core * HW, 128), HW)

    swaps = []
    for i in range(N_WIDE):
        copy = remote(staged.at[:, half(i, 1 - c)], swap.at[:, i * HW:(i + 1) * HW], (swap_s, swap_r), i, peers[5])
        copy.start()
        swaps.append(copy)

    one = lambda i: pl.ds(i, 1)

    def small_at(zs, xs, ys, cs):
        return smalls.at[zs, xs, ys, cs]

    def small_copy(n, src, to):
        return remote(src, src, (small_s, small_r), n, to)

    mine = small_at(one(z), one(x), one(y), one(c))
    both = small_at(one(z), one(x), one(y), pl.ds(0, 2))
    column = small_at(pl.ds(0, NZ), one(x), one(y), pl.ds(0, 2))
    plane = small_at(pl.ds(0, NZ), pl.ds(0, 2), one(y), pl.ds(0, 2))
    small_c = small_copy(0, mine, peers[5])
    small_z = [small_copy(1 + k, both, peers[k]) for k in range(3)]
    small_x = small_copy(4, column, peers[3])
    small_y = small_copy(5, plane, peers[4])
    small_c.start()

    items = []
    own = []
    for i in range(N_DOWN):
        rows = lambda core, i=i: pl.ds(pl.multiple_of(core * DH + i * CH, 16), CH)
        view = lambda zs, xs, ys, rows=rows: down_ref.at[zs, xs, ys, rows(c)]
        first = wdown_ref.at[:, :, :, pl.ds(i * CH, CH)]
        items.append(Gather(here, sems, i * Gather.COPIES, view, None, first))
        own.append(pltpu.make_async_copy(first, view(one(z), one(x), one(y)), own_sem.at[i]))
    for i in range(N_WIDE):
        view = lambda zs, xs, ys, i=i: wide_ref.at[zs, xs, ys, :, half(i, c)]
        first = block.at[:, :, :, :, pl.ds(i * HW, HW)]
        n = N_DOWN + i
        items.append(Gather(here, sems, n * Gather.COPIES, view, None, first))
        own.append(pltpu.make_async_copy(first, view(one(z), one(x), one(y)), own_sem.at[n]))
    order = list(range(N_DOWN, N_DOWN + N_WIDE)) + list(range(N_DOWN))

    small_c.wait_recv()
    for copy in small_z:
        copy.start()
    for i in range(N_WIDE):
        swaps[i].wait_recv()
        mine_part = staged[:, half(i, c)]
        their_part = swap[:, i * HW:(i + 1) * HW]

        @pl.when(c == 0)
        def _(i=i, mine_part=mine_part, their_part=their_part):
            block[0, 0, 0, :, i * HW:(i + 1) * HW] = jnp.concatenate([mine_part, their_part], 0).astype(BF)

        @pl.when(c == 1)
        def _(i=i, mine_part=mine_part, their_part=their_part):
            block[0, 0, 0, :, i * HW:(i + 1) * HW] = jnp.concatenate([their_part, mine_part], 0).astype(BF)
        items[N_DOWN + i].start(0)
        own[N_DOWN + i].start()
    for i in range(N_DOWN):
        items[i].start(0)
        own[i].start()
    for copy in small_z:
        copy.wait_recv()
    small_x.start()
    for n, i in enumerate(order):
        own[i].wait()
        items[i].start(1)
        if n == 1:
            small_x.wait_recv()
            small_y.start()
    for i in order:
        items[i].start(2)
    for i in order:
        items[i].start(3)
    small_y.wait_recv()
    pieces = smalls[...].reshape(32, 8, SW)[:, 0, :].astype(BF)

    def joined(lead, size, width):
        src = lax.broadcasted_iota(jnp.int32, (SW, size), 0)
        dst = lax.broadcasted_iota(jnp.int32, (SW, size), 1)
        spread = jnp.where(src == lead + lax.rem(dst, width), 1.0, 0.0).astype(BF)
        dev = lax.broadcasted_iota(jnp.int32, (32, size), 0)
        col = lax.broadcasted_iota(jnp.int32, (32, size), 1)
        return jnp.sum(jnp.where(lax.div(col, width) == dev, mm(pieces, spread), 0.0), 0, keepdims=True)

    rows = [joined(24 * i, D, 24) for i in range(8)]
    for i in range(8):
        vec_ref[i:i + 1, :] = rows[i]
    bu_ref[...] = joined(192, FF, 96)
    for pair in range(6):
        at = pair * 384
        bqkv_ref[:, at:at + 128] = rows[BQ][:, pair * 128:(pair + 1) * 128]
        bqkv_ref[:, at + 128:at + 256] = jnp.zeros((1, 128), F32)
        bqkv_ref[:, at + 256:at + 384] = rows[BV][:, pair * 128:(pair + 1) * 128]
    for i in order:
        items[i].start(4)
    for copy in (*swaps, small_c, *small_z, small_x, small_y):
        copy.wait_send()


def gather(wqkv, wout, wup, wdown, small):
    n = N_WIDE + N_DOWN
    vm = lambda: pl.BlockSpec(memory_space=pltpu.VMEM)
    hbm = lambda: pl.BlockSpec(memory_space=pl.ANY)
    sem = lambda k: pltpu.SemaphoreType.DMA((k,))
    return pl.pallas_call(
        gather_kernel,
        in_specs=[vm()] * 5,
        out_specs=[hbm(), hbm(), vm(), vm(), vm()],
        out_shape=[
            jax.ShapeDtypeStruct((NZ, 2, 2, CH, AW), BF), jax.ShapeDtypeStruct((NZ, 2, 2, 4 * CH, D), BF),
            jax.ShapeDtypeStruct((8, D), F32), jax.ShapeDtypeStruct((1, FF), F32), jax.ShapeDtypeStruct((1, 3 * D), F32),
        ],
        scratch_shapes=[
            pltpu.VMEM((CH // 2, AW), F32), pltpu.VMEM((CH // 2, AW // 2), F32), pltpu.VMEM((1, 1, 1, CH, AW // 2), BF),
            pltpu.VMEM((NZ, 2, 2, 2, 8, SW), F32),
            sem(n * Gather.COPIES), sem(n * Gather.COPIES), sem(N_WIDE), sem(N_WIDE), sem(n), sem(6), sem(6),
        ],
        compiler_params=pltpu.CompilerParams(collective_id=0, has_side_effects=True, vmem_limit_bytes=LIMIT),
        name="gather_parameters",
    )(wqkv, wout, wup, wdown.reshape(1, 1, 1, 4 * CH // 2, D), small)


class Scatter:
    COPIES = 7

    def __init__(self, here, sems, base, theirs, mine, acc, via, last, zs):
        self.mine, self.acc, self.via, self.last, self.zs = mine, acc, via, last, zs
        z, x, y, c = here
        self.here = here
        peers = partners(*here)
        one = lambda i: pl.ds(i, 1)
        every = pl.ds(0, NZ)
        ix, iy = jnp.where(c == 0, x, 1 - x), jnp.where(c == 0, 1 - y, y)
        self.px, self.py = jnp.where(c == 0, 1 - x, x), jnp.where(c == 0, y, 1 - y)
        first, second = device(z, ix, iy, c), device(z, self.px, self.py, c)
        make = lambda n, src, dst, to: remote(src, dst, sems, base + n, to)
        at = lambda xs, ys: acc.at[every, one(xs), one(ys)]
        self.swap = make(0, theirs, acc, peers[5])
        self.far = make(1, at(1 - x, 1 - y), via.at[0], first)
        self.near = make(2, at(ix, iy), via.at[1], first)
        self.next = make(3, at(self.px, self.py), last, second)
        self.along_z = [
            make(4 + k, acc.at[one(lax.rem(z + k + 1, NZ)), one(x), one(y)], zs.at[k], peers[k]) for k in range(3)
        ]

    def start(self, phase):
        z, x, y, c = self.here
        acc = self.acc
        one = lambda i: pl.ds(i, 1)
        every = pl.ds(0, NZ)
        f = lambda v: v.astype(F32)
        if phase == 0:
            self.swap.start()
        elif phase == 1:
            self.swap.wait_recv()

            @pl.loop(0, NZ)
            def _(i):
                for xi in range(2):
                    for yi in range(2):
                        acc[i, xi, yi] = (f(acc[i, xi, yi]) + f(self.mine(i, xi, yi))).astype(BF)
            self.far.start()
            self.near.start()
        elif phase == 2:
            self.far.wait_recv()
            px, py = self.px, self.py

            @pl.loop(0, NZ)
            def _(i):
                acc[i, px, py] = (f(acc[i, px, py]) + f(self.via[0, i, 0, 0])).astype(BF)
            self.next.start()
            self.near.wait_recv()

            @pl.loop(0, NZ)
            def _(i):
                acc[i, x, y] = (f(acc[i, x, y]) + f(self.via[1, i, 0, 0])).astype(BF)
        elif phase == 3:
            self.next.wait_recv()

            @pl.loop(0, NZ)
            def _(i):
                acc[i, x, y] = (f(acc[i, x, y]) + f(self.last[i, 0, 0])).astype(BF)
            for copy in self.along_z:
                copy.start()
        else:
            for copy in self.along_z:
                copy.wait_recv()
            for copy in (self.swap, self.far, self.near, self.next, *self.along_z):
                copy.wait_send()
            return f(acc[z, x, y]) + f(self.zs[0, 0, 0, 0]) + f(self.zs[1, 0, 0, 0]) + f(self.zs[2, 0, 0, 0])


N_QKV = 3
N_UP = FF // D


def scatter_kernel(
    gqkv_ref, gout_ref, gup_ref, gdown_ref, small_ref,
    oqkv_ref, oout_ref, oup_ref, odown_ref, osmall_ref, obu_ref,
    acc_w, via_w, last_w, zs_w, acc_d, via_d, last_d, zs_d, done, small_in,
    sems_s, sems_r, fin_s, fin_r, small_s, small_r,
):
    here = where_am_i()
    z, x, y, c = here
    peers = partners(*here)
    greet(here)
    sems = (sems_s, sems_r)

    def half(i, core):
        return pl.ds(pl.multiple_of(i * 2 * HW + core * HW, 128), HW)

    items = []
    every = pl.ds(0, NZ)
    two = pl.ds(0, 2)
    for i in range(N_DOWN):
        rows = lambda core, i=i: pl.ds(pl.multiple_of(core * DH + i * CH, 16), CH)
        theirs = gdown_ref.at[every, two, two, rows(1 - c)]
        mine = lambda a, b, d, rows=rows: gdown_ref[a, b, d, rows(c)]
        items.append(Scatter(here, sems, i * 7, theirs, mine, acc_d.at[i], via_d.at[i], last_d.at[i], zs_d.at[i]))
    wide = [(gup_ref, i) for i in range(N_UP)] + [(gout_ref, 0)] + [(gqkv_ref, i) for i in range(N_QKV)]
    for n, (ref, i) in enumerate(wide):
        theirs = ref.at[every, two, two, :, half(i, 1 - c)]
        mine = lambda a, b, d, ref=ref, i=i: ref[a, b, d, :, half(i, c)]
        items.append(
            Scatter(here, sems, (N_DOWN + n) * 7, theirs, mine, acc_w.at[n], via_w.at[n], last_w.at[n], zs_w.at[n])
        )
    small_in[0] = small_ref[...]
    small_copies = []

    def small_step(n, src, dst, to):
        copy = remote(small_in.at[src], small_in.at[dst], (small_s, small_r), n, to)
        copy.start()
        small_copies.append(copy)
        return copy

    small_step(0, 0, 1, peers[5])
    for item in items:
        item.start(0)
    small_copies[0].wait_recv()
    small_in[2] = small_in[0] + small_in[1]
    small_step(1, 2, 3, peers[3])
    for item in items:
        item.start(1)
    small_copies[1].wait_recv()
    small_in[4] = small_in[2] + small_in[3]
    small_step(2, 4, 5, peers[4])
    for item in items:
        item.start(2)
    small_copies[2].wait_recv()
    small_in[6] = small_in[4] + small_in[5]
    for k in range(3):
        small_step(3 + k, 6, 7 + k, peers[k])
    for item in items:
        item.start(3)
    for k in range(3):
        small_copies[3 + k].wait_recv()
    total = small_in[6] + small_in[7] + small_in[8] + small_in[9]
    me = lax.axis_index("dp") * lax.axis_size("fsdp") + lax.axis_index("fsdp")
    src = lax.broadcasted_iota(jnp.int32, (D, 128), 0)
    dst = lax.broadcasted_iota(jnp.int32, (D, 128), 1)

    def pick(rows, width, at):
        chosen = jnp.where((src == at + dst) & (dst < width), 1.0, 0.0)
        return lax.dot_general(rows, chosen, NN, precision=lax.Precision.HIGHEST, preferred_element_type=F32)

    osmall_ref[...] = pick(total[:8], 24, me * 24)
    row = lax.broadcasted_iota(jnp.int32, (8, D), 0)
    longest = jnp.sum(jnp.where(row == lax.div(me, 8), total[8:16], 0.0), 0, keepdims=True)
    obu_ref[...] = pick(jnp.broadcast_to(longest, (8, D)), 96, lax.rem(me, 8) * 96)
    for i in range(N_DOWN):
        odown_ref[pl.ds(i * CH, CH), :] = items[i].start(4)
    finals = []
    for n, (ref, i) in enumerate(wide):
        done[n] = items[N_DOWN + n].start(4)
        mine = done.at[n, pl.ds(pl.multiple_of(c * 24, 8), 24)]
        other = done.at[n, pl.ds(pl.multiple_of((1 - c) * 24, 8), 24)]
        if ref is gqkv_ref:
            for b in range(3):
                cols = pl.ds(pl.multiple_of(b * D + i * QW + c * 128, 128), 128)
                k = N_UP + 1 + i * 3 + b
                part = pl.ds(b * 128, 128)
                copy = remote(
                    done.at[n, pl.ds(pl.multiple_of((1 - c) * 24, 8), 24), part], oqkv_ref.at[:, cols],
                    (fin_s, fin_r), k, peers[5],
                )
                copy.start()
                finals.append(copy)
                oqkv_ref[:, cols] = done[n, pl.ds(pl.multiple_of(c * 24, 8), 24), part]
        else:
            target = oout_ref if ref is gout_ref else oup_ref
            copy = remote(other, target.at[:, half(i, c)], (fin_s, fin_r), n, peers[5])
            copy.start()
            finals.append(copy)
            target[:, half(i, c)] = mine[...]
    for copy in finals:
        copy.wait()
    for copy in small_copies:
        copy.wait_send()


def scatter(gqkv, gout, gup, gdown, small):
    nw = N_QKV + 1 + N_UP
    vm = lambda: pl.BlockSpec(memory_space=pltpu.VMEM)
    sem = lambda k: pltpu.SemaphoreType.DMA((k,))
    chips = lambda v: v.reshape(NZ, 2, 2, v.shape[0] // 16, v.shape[1])
    n = (nw + N_DOWN) * 7
    return pl.pallas_call(
        scatter_kernel,
        in_specs=[vm()] * 5,
        out_specs=[vm()] * 6,
        out_shape=[
            jax.ShapeDtypeStruct((24, 3 * D), F32), jax.ShapeDtypeStruct((24, D), F32),
            jax.ShapeDtypeStruct((24, FF), F32), jax.ShapeDtypeStruct((96, D), F32),
            jax.ShapeDtypeStruct((8, 128), F32), jax.ShapeDtypeStruct((8, 128), F32),
        ],
        scratch_shapes=[
            pltpu.VMEM((nw, NZ, 2, 2, CH, HW), BF), pltpu.VMEM((nw, 2, NZ, 1, 1, CH, HW), BF),
            pltpu.VMEM((nw, NZ, 1, 1, CH, HW), BF), pltpu.VMEM((nw, 3, 1, 1, 1, CH, HW), BF),
            pltpu.VMEM((N_DOWN, NZ, 2, 2, CH, D), BF), pltpu.VMEM((N_DOWN, 2, NZ, 1, 1, CH, D), BF),
            pltpu.VMEM((N_DOWN, NZ, 1, 1, CH, D), BF), pltpu.VMEM((N_DOWN, 3, 1, 1, 1, CH, D), BF),
            pltpu.VMEM((nw, CH, HW), F32), pltpu.VMEM((10, 16, D), F32),
            sem(n), sem(n), sem(N_UP + 1 + 9), sem(N_UP + 1 + 9), sem(6), sem(6),
        ],
        compiler_params=pltpu.CompilerParams(collective_id=1, has_side_effects=True, vmem_limit_bytes=LIMIT),
        name="sum_gradients",
    )(chips(gqkv), chips(gout), chips(gup), chips(gdown), small)


def by_pair(v):
    return v.reshape(v.shape[0], 3, 6, 128).transpose(0, 2, 1, 3).reshape(v.shape[0], 3 * D)


def by_kind(v):
    return v.reshape(v.shape[0], 6, 3, 128).transpose(0, 2, 1, 3).reshape(v.shape[0], 3 * D)


def on_device(copies, inputs, row_kind, ln1_gain, ln1_bias, w_qkv, b_query, b_value, w_out, b_out, ln2_gain, ln2_bias, w_up, b_up, w_down, b_down, out_grad):
    axes = ("dp", "fsdp")
    vectors = (ln1_gain, ln1_bias, b_query, b_value, b_out, ln2_gain, ln2_bias, b_down)
    if copies:
        small = jnp.concatenate([*vectors, b_up]).astype(F32)
        small = jnp.broadcast_to(jnp.pad(small, (0, SW - small.shape[0]))[None], (8, SW))
        wide, down, vec, bu, bqkv = gather(w_qkv, w_out, w_up, w_down, small)
        wide, down = wide.reshape(D, AW), down.reshape(FF, D)
    else:
        get = lambda v: lax.all_gather(v, axes, axis=0, tiled=True)
        wide = jnp.concatenate([by_pair(get(w_qkv)), get(w_out), get(w_up)], 1)
        down = get(w_down)
        full = [get(v).astype(F32) for v in vectors]
        vec = jnp.stack(full)
        bu = get(b_up).astype(F32)[None]
        bqkv = by_pair(jnp.concatenate([full[BQ], jnp.zeros_like(full[BQ]), full[BV]])[None])
    h1, qkv, p, attn, rl, x1 = attn_fwd(row_kind, inputs, wide, bqkv, vec)
    outputs, dx1, gup, gdown, gbu, gg2, gb2, gbd = ffn(x1, out_grad, wide, down, bu, vec)
    input_grad, gqkv, gout, gbqkv, gbo, gg1, gb1 = attn_bwd(inputs, dx1, h1, qkv, p, attn, rl, wide, vec)
    gbqkv = by_kind(gbqkv)
    small = [gg1, gb1, gbqkv[:, :D], gbqkv[:, 2 * D:], gbo, gg2, gb2, gbd]
    if copies:
        small = jnp.concatenate([*small, gbu.reshape(4, D), jnp.zeros((4, D), F32)], 0)
        gqkv, gout, gup, gdown, small, gbu = scatter(gqkv, gout, gup, gdown, small)
        small = [small[i, :24] for i in range(8)]
        gbu = gbu[0, :96]
    else:
        give = lambda v: lax.psum_scatter(v.astype(F32), axes, scatter_dimension=0, tiled=True)
        gqkv, gout, gup, gdown = give(by_kind(gqkv)), give(gout), give(gup), give(gdown)
        small = [give(v[0]) for v in small]
        gbu = give(gbu[0])
    gg1, gb1, gbq, gbv, gbo, gg2, gb2, gbd = small
    return outputs, input_grad, gg1, gb1, gqkv, gbq, gbv, gout, gbo, gg2, gb2, gup, gbu, gdown, gbd


def solution(mesh):
    both = ("dp", "fsdp")
    row = P(both)
    mat = P(both, None)
    act = P(both, None, None)
    in_specs = (act, row, row, row, mat, row, row, mat, row, row, row, mat, row, mat, row, act)
    out_specs = (act, act, row, row, mat, row, row, mat, row, row, row, mat, row, mat, row)
    copies = mesh.shape["dp"] == 2 * NZ and mesh.shape["fsdp"] == 4
    return jax.shard_map(
        functools.partial(on_device, copies), mesh=mesh, in_specs=in_specs, out_specs=out_specs, check_vma=False
    )
```

```python
import functools
import math

import jax
import jax.numpy as jnp
from jax import lax
from jax.experimental import pallas as pl
from jax.experimental.pallas import tpu as pltpu
from jax.sharding import PartitionSpec as P

D = 768
HD = 64
FF = 3072
SEQ = 529
HALF = 264
EPS = 1e-06
S = 544
T = 2 * S
MB = 272
HG = 4
QW = HG * HD
GW = 3 * QW
FC = 512
OUT_AT = 3 * D
UP_AT = 4 * D
AW = 4 * D + FF
F32 = jnp.float32
BF = jnp.bfloat16
LIMIT = 62 * 2**20
MESH = pl.DeviceIdType.MESH
NN = (((1,), (0,)), ((), ()))
NT = (((1,), (1,)), ((), ()))
TN = (((0,), (0,)), ((), ()))


def mm(a, b, dims=NN):
    return lax.dot_general(a, b, dims, preferred_element_type=F32)


def norm_parts(values):
    mean = jnp.mean(values, -1, keepdims=True)
    centred = values - mean
    inverse = lax.rsqrt(jnp.mean(centred * centred, -1, keepdims=True) + EPS)
    return centred * inverse, inverse


def norm_pull(grad, normed, inverse, gain):
    scaled = grad * gain
    return inverse * (
        scaled
        - jnp.mean(scaled, -1, keepdims=True)
        - normed * jnp.mean(scaled * normed, -1, keepdims=True)
    )


def gelu_both(u):
    a = jnp.abs(u)
    t = 1.0 / (1.0 + (0.3275911 / math.sqrt(2.0)) * a)
    e = jnp.exp(-0.5 * u * u)
    poly = t * (
        0.254829592
        + t * (-0.284496736 + t * (1.421413741 + t * (-1.453152027 + t * 1.061405429)))
    )
    tail = 0.5 * poly * e
    phi = jnp.where(u < 0, tail, 1.0 - tail)
    return u * phi, phi + u * e * (1.0 / math.sqrt(2.0 * math.pi))


def head_lanes(shape, e):
    lane = lax.broadcasted_iota(jnp.int32, shape, 1)
    return (lane // HD) == e


def whole(shape):
    return pl.BlockSpec(shape, lambda *_: (0,) * len(shape))


def rows_of(i):
    return pl.ds(pl.multiple_of(i * MB, 16), MB)


G1, B1, BQ, BV, BO, G2, B2, BD = range(8)


def attn_fwd_kernel(
    kind_ref, x_ref, wg_ref, bqkv_ref, wo_ref, vec_ref,
    h1_ref, qkv_ref, p_ref, attn_ref, rl_ref, x1_ref, fa, fb,
):
    hq, r = pl.program_id(0), pl.program_id(1)

    @pl.when((hq == 0) & (r == 0))
    def _():
        for row in range(2):
            h1_ref[pl.ds(row * S + S - 16, 16), :] = jnp.zeros((16, D), BF)
            n1, _s = norm_parts(x_ref[row].astype(F32))
            h1_ref[pl.ds(row * S, SEQ), :] = (n1 * vec_ref[G1:G1 + 1, :] + vec_ref[B1:B1 + 1, :]).astype(BF)
            slot = lax.broadcasted_iota(jnp.int32, (S, 128), 0)
            lane = lax.broadcasted_iota(jnp.int32, (S, 128), 1)
            packed = jnp.where(slot < HALF, 0, jnp.where(slot < 2 * HALF, 1, 2))
            seg = jnp.where(kind_ref[row] == 1, packed, 0)
            fa[row] = jnp.where((lane < 3) & (seg == lane), -1e30, 0.0).astype(BF)
            fb[row] = jnp.where((lane < 3) & ((seg != lane) | (slot >= SEQ)), 1.0, 0.0).astype(BF)

    @pl.when(r == 0)
    def _():
        @pl.loop(0, T // MB)
        def _(i):
            rows = rows_of(i)
            qkv_ref[rows, :] = (mm(h1_ref[rows, :], wg_ref[...]) + bqkv_ref[...]).astype(BF)

    rows = pl.ds(pl.multiple_of(r * S, 16), S)
    feat_q, feat_k = fa[r], fb[r]
    ones = jnp.ones((S, 128), BF)
    scale = math.log2(math.e) / math.sqrt(HD)
    for j in range(HG // 2):
        at = j * 384
        qp, kp, vp = (qkv_ref[rows, at + 128 * n: at + 128 * (n + 1)] for n in range(3))
        kcat = jnp.concatenate([kp, feat_k], 1)
        total = None
        inv = None
        for e in range(2):
            keep = head_lanes((S, 128), e)
            qcat = jnp.concatenate([jnp.where(keep, qp, jnp.zeros_like(qp)), feat_q], 1)
            s = mm(qcat, kcat, NT)
            m = jnp.max(s, -1, keepdims=True)
            pb = jnp.exp2((s - m) * scale).astype(BF)
            p_ref[0, 2 * j + e] = pb
            vcat = jnp.concatenate([jnp.where(keep, vp, jnp.zeros_like(vp)), ones], 1)
            o = mm(pb, vcat)
            rl = 1.0 / o[:, 128:]
            part = o[:, :128] * rl
            total = part if total is None else total + part
            inv = rl if inv is None else jnp.where(keep, rl, inv)
        out = pl.ds(pl.multiple_of(hq * QW + j * 128, 128), 128)
        attn_ref[rows, out] = total.astype(BF)
        rl_ref[rows, out] = inv

    @pl.when((hq == D // QW - 1) & (r == 1))
    def _():
        for row in range(2):
            x1_ref[pl.ds(row * S + S - 16, 16), :] = jnp.zeros((16, D), F32)
            x1_ref[pl.ds(row * S, SEQ), :] = x_ref[row].astype(F32)

        @pl.loop(0, T // MB)
        def _(i):
            rr = rows_of(i)
            x1_ref[rr, :] = x1_ref[rr, :] + mm(attn_ref[rr, :], wo_ref[...]) + vec_ref[BO:BO + 1, :]


def attn_fwd(kind, x, wide, bqkv, vec):
    return pl.pallas_call(
        attn_fwd_kernel,
        grid=(D // QW, 2),
        in_specs=[
            pl.BlockSpec(memory_space=pltpu.SMEM), whole((2, SEQ, D)),
            pl.BlockSpec((D, GW), lambda h, r: (0, h)), pl.BlockSpec((1, GW), lambda h, r: (0, h)),
            pl.BlockSpec((D, D), lambda h, r: (0, 3)), whole((8, D)),
        ],
        out_specs=[
            whole((T, D)), pl.BlockSpec((T, GW), lambda h, r: (0, h)),
            pl.BlockSpec((1, HG, S, S), lambda h, r: (r, h, 0, 0)),
            whole((T, D)), whole((T, D)), whole((T, D)),
        ],
        out_shape=[
            jax.ShapeDtypeStruct((T, D), BF), jax.ShapeDtypeStruct((T, 3 * D), BF),
            jax.ShapeDtypeStruct((2, D // HD, S, S), BF),
            jax.ShapeDtypeStruct((T, D), BF), jax.ShapeDtypeStruct((T, D), F32), jax.ShapeDtypeStruct((T, D), F32),
        ],
        scratch_shapes=[pltpu.VMEM((2, S, 128), BF), pltpu.VMEM((2, S, 128), BF)],
        compiler_params=pltpu.CompilerParams(vmem_limit_bytes=LIMIT),
        name="attention_forward",
    )(kind, x, wide, bqkv, wide, vec)


def ffn_kernel(
    x1_ref, dm_ref, wu_ref, wd_ref, bu_ref, vec_ref,
    out_ref, dx1_ref, gwu_ref, gwd_ref, gbu_ref, gg2_ref, gb2_ref, gbd_ref,
    h2, h2t, dm, yacc, dacc, gs, dus,
):
    c = pl.program_id(0)

    @pl.when(c == 0)
    def _():
        for row in range(2):
            dm[pl.ds(row * S + S - 16, 16), :] = jnp.zeros((16, D), BF)
            dm[pl.ds(row * S, SEQ), :] = dm_ref[row]

        @pl.loop(0, T // MB)
        def _(i):
            rows = rows_of(i)
            x1 = x1_ref[rows, :]
            n2, _s = norm_parts(x1)
            h2[rows, :] = (n2 * vec_ref[G2:G2 + 1, :] + vec_ref[B2:B2 + 1, :]).astype(BF)
            yacc[rows, :] = x1 + vec_ref[BD:BD + 1, :]
            dacc[rows, :] = jnp.zeros((MB, D), F32)
        h2t[...] = h2[...].T
        gbd_ref[...] = jnp.sum(dm[...].astype(F32), 0, keepdims=True)

    gbu_ref[...] = jnp.zeros_like(gbu_ref)

    @pl.loop(0, T // MB)
    def _(i):
        rows = rows_of(i)
        u = mm(h2[rows, :], wu_ref[...]) + bu_ref[...]
        g, slope = gelu_both(u)
        gb = g.astype(BF)
        gs[rows, :] = gb
        yacc[rows, :] += mm(gb, wd_ref[...])
        du = (mm(dm[rows, :], wd_ref[...], NT) * slope).astype(BF)
        dus[rows, :] = du
        gbu_ref[...] += jnp.sum(du.astype(F32), 0, keepdims=True)
        dacc[rows, :] += mm(du, wu_ref[...], NT)

    for t in range(FC // 256):
        cols = pl.ds(t * 256, 256)
        gwd_ref[cols, :] = mm(gs[:, cols], dm[...], TN).astype(BF)

    @pl.loop(0, D // 256)
    def _(t):
        rows = pl.ds(pl.multiple_of(t * 256, 256), 256)
        gwu_ref[rows, :] = mm(h2t[rows, :], dus[...]).astype(BF)

    @pl.when(c == FF // FC - 1)
    def _():
        gg2_ref[...] = jnp.zeros_like(gg2_ref)
        gb2_ref[...] = jnp.zeros_like(gb2_ref)
        for row in range(2):
            out_ref[row] = yacc[pl.ds(row * S, SEQ), :].astype(BF)

        @pl.loop(0, T // MB)
        def _(i):
            rows = rows_of(i)
            n2, s2 = norm_parts(x1_ref[rows, :])
            dh = dacc[rows, :]
            gg2_ref[...] += jnp.sum(dh * n2, 0, keepdims=True)
            gb2_ref[...] += jnp.sum(dh, 0, keepdims=True)
            dx1_ref[rows, :] = dm[rows, :].astype(F32) + norm_pull(dh, n2, s2, vec_ref[G2:G2 + 1, :])


def ffn(x1, dm, wide, down, bu, vec):
    one = jax.ShapeDtypeStruct((1, D), F32)
    return pl.pallas_call(
        ffn_kernel,
        grid=(FF // FC,),
        in_specs=[
            whole((T, D)), whole((2, SEQ, D)),
            pl.BlockSpec((D, FC), lambda c: (0, c + UP_AT // FC)), pl.BlockSpec((FC, D), lambda c: (c, 0)),
            pl.BlockSpec((1, FC), lambda c: (0, c)), whole((8, D)),
        ],
        out_specs=[
            whole((2, SEQ, D)), whole((T, D)),
            pl.BlockSpec((D, FC), lambda c: (0, c)), pl.BlockSpec((FC, D), lambda c: (c, 0)),
            pl.BlockSpec((1, FC), lambda c: (0, c)), whole((1, D)), whole((1, D)), whole((1, D)),
        ],
        out_shape=[
            jax.ShapeDtypeStruct((2, SEQ, D), BF), jax.ShapeDtypeStruct((T, D), F32),
            jax.ShapeDtypeStruct((D, FF), BF), jax.ShapeDtypeStruct((FF, D), BF),
            jax.ShapeDtypeStruct((1, FF), F32), one, one, one,
        ],
        scratch_shapes=[
            pltpu.VMEM((T, D), BF), pltpu.VMEM((D, T), BF), pltpu.VMEM((T, D), BF),
            pltpu.VMEM((T, D), F32), pltpu.VMEM((T, D), F32),
            pltpu.VMEM((T, FC), BF), pltpu.VMEM((T, FC), BF),
        ],
        compiler_params=pltpu.CompilerParams(vmem_limit_bytes=LIMIT),
        name="feed_forward",
    )(x1, dm, wide, down, bu, vec)


def attn_bwd_kernel(
    x_ref, dx1_ref, h1_ref, qkv_ref, p_ref, attn_ref, rl_ref, wo_ref, wqkv_ref, vec_ref,
    gx_ref, gwqkv_ref, gwo_ref, gbqkv_ref, gbo_ref, gg1_ref, gb1_ref,
    da, dos, h1t, dqkv,
):
    hq, r = pl.program_id(0), pl.program_id(1)

    @pl.when((hq == 0) & (r == 0))
    def _():
        gbo_ref[...] = jnp.zeros_like(gbo_ref)

        @pl.loop(0, T // MB)
        def _(i):
            rows = rows_of(i)
            d = dx1_ref[rows, :].astype(BF)
            da[rows, :] = d
            gbo_ref[...] += jnp.sum(d.astype(F32), 0, keepdims=True)
            dos[rows, :] = (mm(d, wo_ref[...], NT) * rl_ref[rows, :]).astype(BF)
        h1t[...] = h1_ref[...].T

    rows = pl.ds(pl.multiple_of(r * S, 16), S)
    scale = 1.0 / math.sqrt(HD)
    for j in range(HG // 2):
        at = j * 384
        qp, kp, vp = (qkv_ref[rows, at + 128 * n: at + 128 * (n + 1)] for n in range(3))
        do = dos[rows, pl.ds(pl.multiple_of(hq * QW + j * 128, 128), 128)]
        prod = do.astype(F32) * attn_ref[rows, j * 128:(j + 1) * 128].astype(F32)
        dq = dk = dv = None
        for e in range(2):
            keep = head_lanes((S, 128), e)
            zero = jnp.zeros_like(qp)
            doe = jnp.where(keep, do, zero)
            dot = jnp.sum(jnp.where(keep, prod, 0.0), -1, keepdims=True)
            p = p_ref[0, 2 * j + e]
            ds = (p.astype(F32) * (mm(doe, vp, NT) - dot)).astype(BF)
            a = mm(ds, jnp.where(keep, kp, zero))
            b = mm(ds, jnp.where(keep, qp, zero), TN)
            c = mm(p, doe, TN)
            dq, dk, dv = (a, b, c) if dq is None else (dq + a, dk + b, dv + c)
        for n, part in enumerate((dq * scale, dk * scale, dv)):
            col = hq * GW + j * 384 + n * 128
            dqkv[rows, pl.ds(pl.multiple_of(col, 128), 128)] = part.astype(BF)

    @pl.when(r == 1)
    def _():
        part = dqkv[:, pl.ds(pl.multiple_of(hq * GW, 128), GW)]
        gbqkv_ref[...] = jnp.sum(part.astype(F32), 0, keepdims=True)

        @pl.loop(0, D // 256)
        def _(t):
            rr = pl.ds(pl.multiple_of(t * 256, 256), 256)
            gwqkv_ref[rr, :] = mm(h1t[rr, :], part).astype(BF)
        gwo_ref[...] = mm(attn_ref[...], da[...], TN).astype(BF)

    @pl.when((hq == D // QW - 1) & (r == 1))
    def _():
        gg1_ref[...] = jnp.zeros_like(gg1_ref)
        gb1_ref[...] = jnp.zeros_like(gb1_ref)
        for row in range(2):
            rr = pl.ds(row * S, SEQ)
            dh = mm(dqkv[pl.ds(row * S, S), :], wqkv_ref[...], NT)[:SEQ]
            n1, s1 = norm_parts(x_ref[row].astype(F32))
            gg1_ref[...] += jnp.sum(dh * n1, 0, keepdims=True)
            gb1_ref[...] += jnp.sum(dh, 0, keepdims=True)
            gx_ref[row] = (dx1_ref[rr, :] + norm_pull(dh, n1, s1, vec_ref[G1:G1 + 1, :])).astype(BF)


def attn_bwd(x, dx1, h1, qkv, p, attn, rl, wide, vec):
    act = pl.BlockSpec((T, QW), lambda h, r: (0, h))
    one = jax.ShapeDtypeStruct((1, D), F32)
    return pl.pallas_call(
        attn_bwd_kernel,
        grid=(D // QW, 2),
        in_specs=[
            whole((2, SEQ, D)), whole((T, D)), whole((T, D)), pl.BlockSpec((T, GW), lambda h, r: (0, h)),
            pl.BlockSpec((1, HG, S, S), lambda h, r: (r, h, 0, 0)), act, whole((T, D)),
            pl.BlockSpec((D, D), lambda h, r: (0, 3)), whole((D, 3 * D)), whole((8, D)),
        ],
        out_specs=[
            whole((2, SEQ, D)), pl.BlockSpec((D, GW), lambda h, r: (0, h)),
            pl.BlockSpec((QW, D), lambda h, r: (h, 0)),
            pl.BlockSpec((1, GW), lambda h, r: (0, h)), whole((1, D)), whole((1, D)), whole((1, D)),
        ],
        out_shape=[
            jax.ShapeDtypeStruct((2, SEQ, D), BF), jax.ShapeDtypeStruct((D, 3 * D), BF), jax.ShapeDtypeStruct((D, D), BF),
            jax.ShapeDtypeStruct((1, 3 * D), F32), one, one, one,
        ],
        scratch_shapes=[
            pltpu.VMEM((T, D), BF), pltpu.VMEM((T, D), BF), pltpu.VMEM((D, T), BF), pltpu.VMEM((T, 3 * D), BF),
        ],
        compiler_params=pltpu.CompilerParams(vmem_limit_bytes=LIMIT),
        name="attention_backward",
    )(x, dx1, h1, qkv, p, attn, rl, wide, wide, vec)


NZ = 4
CH = 48
HW = 384
SW = 384
N_WIDE = AW // (2 * HW)
N_DOWN = 2
N_UP = FF // D
DH = 2 * CH
NV = 8
VW = (24,) * NV + (96,)


def one(i):
    return pl.ds(i, 1)


EVERY = pl.ds(0, NZ)
TWO = pl.ds(0, 2)


def where_am_i():
    dp, fs = lax.axis_index("dp"), lax.axis_index("fsdp")
    return lax.div(dp, 2), lax.rem(dp, 2), lax.div(fs, 2), lax.rem(fs, 2)


def device(z, x, y, c):
    return (z * 2 + x, y * 2 + c)


def partners(z, x, y, c):
    found = [device(lax.rem(z + k, NZ), x, y, c) for k in (1, 2, 3)]
    return found + [device(z, 1 - x, y, c), device(z, x, 1 - y, c), device(z, x, y, 1 - c)]


def say_hello(here):
    barrier = pltpu.get_barrier_semaphore()
    for other in partners(*here):
        pl.semaphore_signal(barrier, inc=1, device_id=other, device_id_type=MESH)


def await_all():
    pl.semaphore_wait(pltpu.get_barrier_semaphore(), 6)


def remote(src, dst, sems, n, target):
    return pltpu.make_async_remote_copy(
        src_ref=src, dst_ref=dst, send_sem=sems[0].at[n], recv_sem=sems[1].at[n],
        device_id=target, device_id_type=MESH,
    )


def half(i, core):
    return pl.ds(pl.multiple_of(i * 2 * HW + core * HW, 128), HW)


def add(a, b):
    return (a.astype(F32) + b.astype(F32)).astype(BF)


def plan(entries, ticks):
    table = {n: [] for n in range(len(ticks))}
    for due, action in sorted(entries, key=lambda e: e[0]):
        table[min((n for n, t in enumerate(ticks) if t >= due), default=len(ticks) - 1)].append(action)
    return table


class Gather:
    COPIES = 7

    def __init__(self, here, sems, base, view, first):
        z, x, y, c = here
        peers = partners(*here)
        mine = view(one(z), one(x), one(y))
        column = view(EVERY, one(x), one(y))
        fx, fy = jnp.where(c == 0, 1 - x, x), jnp.where(c == 0, y, 1 - y)
        tx, ty = jnp.where(c == 0, x, 1 - x), jnp.where(c == 0, 1 - y, y)
        passed = view(EVERY, one(fx), one(fy))
        all_of = view(EVERY, TWO, TWO)
        make = lambda n, src, dst, to: remote(src, dst, sems, base + n, to)
        self.along_z = [make(k, mine if first is None else first, mine, peers[k]) for k in range(3)]
        self.along_x = make(3, column, column, peers[3])
        self.along_y = make(4, column, column, peers[4])
        self.diagonal = make(5, passed, passed, device(z, tx, ty, c))
        self.sibling = make(6, all_of, all_of, peers[5])

    def start(self, phase):
        if phase == 0:
            for copy in self.along_z:
                copy.start()
        elif phase == 1:
            for copy in self.along_z:
                copy.wait_recv()
            self.along_x.start()
            self.along_y.start()
        elif phase == 2:
            self.along_x.wait_recv()
            self.along_y.wait_recv()
            self.diagonal.start()
        elif phase == 3:
            self.diagonal.wait_recv()
            self.sibling.start()
        else:
            self.sibling.wait_recv()

    def drain(self):
        for copy in (*self.along_z, self.along_x, self.along_y, self.diagonal, self.sibling):
            copy.wait_send()


class Scatter:
    COPIES = 7

    def __init__(self, here, sems, base, theirs, mine, acc, via, last, zs):
        self.mine, self.acc, self.via, self.last, self.zs = mine, acc, via, last, zs
        z, x, y, c = self.here = here
        peers = partners(*here)
        ix, iy = jnp.where(c == 0, x, 1 - x), jnp.where(c == 0, 1 - y, y)
        self.px, self.py = jnp.where(c == 0, 1 - x, x), jnp.where(c == 0, y, 1 - y)
        first, second = device(z, ix, iy, c), device(z, self.px, self.py, c)
        make = lambda n, src, dst, to: remote(src, dst, sems, base + n, to)
        at = lambda xs, ys: acc.at[EVERY, one(xs), one(ys)]
        self.swap = make(0, theirs, acc, peers[5])
        self.far = make(1, at(1 - x, 1 - y), via.at[0], first)
        self.near = make(2, at(ix, iy), via.at[1], first)
        self.next = make(3, at(self.px, self.py), last, second)
        self.along_z = [
            make(4 + k, acc.at[one(lax.rem(z + k + 1, NZ)), one(x), one(y)], zs.at[k], peers[k]) for k in range(3)
        ]

    def start(self, phase):
        z, x, y, c = self.here
        acc = self.acc
        if phase == 0:
            self.swap.start()
        elif phase == 1:
            self.swap.wait_recv()

            @pl.loop(0, NZ)
            def _(i):
                for xi in range(2):
                    for yi in range(2):
                        acc[i, xi, yi] = add(acc[i, xi, yi], self.mine(i, xi, yi))
            self.far.start()
            self.near.start()
        elif phase == 2:
            self.far.wait_recv()
            px, py = self.px, self.py

            @pl.loop(0, NZ)
            def _(i):
                acc[i, px, py] = add(acc[i, px, py], self.via[0, i, 0, 0])
            self.next.start()
            self.near.wait_recv()

            @pl.loop(0, NZ)
            def _(i):
                acc[i, x, y] = add(acc[i, x, y], self.via[1, i, 0, 0])
        elif phase == 3:
            self.next.wait_recv()

            @pl.loop(0, NZ)
            def _(i):
                acc[i, x, y] = add(acc[i, x, y], self.last[i, 0, 0])
            for copy in self.along_z:
                copy.start()

    def total(self):
        z, x, y, c = self.here
        for copy in self.along_z:
            copy.wait_recv()
        parts = [self.acc[z, x, y]] + [self.zs[k, 0, 0, 0] for k in range(3)]
        return sum(part.astype(F32) for part in parts)

    def drain(self):
        for copy in (self.swap, self.far, self.near, self.next, *self.along_z):
            copy.wait_send()


def scatter_bufs(n, width):
    return [
        pltpu.VMEM((n, NZ, 2, 2, CH, width), BF), pltpu.VMEM((n, 2, NZ, 1, 1, CH, width), BF),
        pltpu.VMEM((n, NZ, 1, 1, CH, width), BF), pltpu.VMEM((n, 3, 1, 1, 1, CH, width), BF),
    ]


def dma_sems(*counts):
    return [pltpu.SemaphoreType.DMA((k,)) for k in counts]


def fixed(shape):
    return pl.BlockSpec(shape, lambda s: (0,) * len(shape), pipeline_mode=pl.Buffered(1))


def vmem():
    return pl.BlockSpec(memory_space=pltpu.VMEM)


def hbm():
    return pl.BlockSpec(memory_space=pl.ANY)


N_ATT = 2 * (D // QW)
FORWARD_TICKS = [2.9 * n for n in range(20)]


def forward_kernel(
    kind_ref, x_ref, dm_ref, wqkv_ref, wout_ref, wup_ref, wdown_ref, *refs,
):
    small_refs = refs[:NV + 1]
    (
        h1t_ref, qkv_ref, p_ref, attn_ref, rl_ref, x1_ref, dmp_ref, h2t_ref, g_ref, slope_ref, gdown_ref,
        vec_ref, watt_out, wup_out, down_out,
        fa, fb, h1, h2, staged, swap, watt, wup, bqkv, bu, smalls,
        sems_s, sems_r, swap_s, swap_r, small_s, small_r, copy_sem,
    ) = refs[NV + 1:]
    step = pl.program_id(0)
    here = where_am_i()
    z, x, y, c = here
    peers = partners(*here)
    sems = (sems_s, sems_r)

    swaps = [
        remote(staged.at[:, half(i, 1 - c)], swap.at[:, i * HW:(i + 1) * HW], (swap_s, swap_r), i, peers[5])
        for i in range(N_WIDE)
    ]
    items, own = [], []
    for i in range(N_WIDE):
        buf, at = (watt, i) if i < 4 else (wup, i - 4)
        view = lambda zs, xs, ys, buf=buf, at=at: buf.at[zs, xs, ys, :, half(at, c)]
        items.append(Gather(here, sems, i * Gather.COPIES, view, None))
    for i in range(N_DOWN):
        rows = pl.ds(pl.multiple_of(c * DH + i * CH, 16), CH)
        view = lambda zs, xs, ys, rows=rows: down_out.at[zs, xs, ys, rows]
        first = wdown_ref.at[:, :, :, pl.ds(i * CH, CH)]
        items.append(Gather(here, sems, (N_WIDE + i) * Gather.COPIES, view, first))
        own.append(pltpu.make_async_copy(first, view(one(z), one(x), one(y)), copy_sem.at[N_WIDE + i]))
    keeps = []
    for i in range(N_WIDE):
        src, dst, at = (watt, watt_out, i) if i < 4 else (wup, wup_out, i - 4)
        cols = pl.ds(at * D, D)
        keeps.append(pltpu.make_async_copy(
            src.at[:, :, :, :, cols], dst.at[:, :, :, :, cols], copy_sem.at[i]))

    def act(action):
        i, phase = action
        if i >= N_WIDE and phase == 1:
            own[i - N_WIDE].wait()
        items[i].start(phase)
        if phase == 4 and i < N_WIDE:
            keeps[i].start()

    LAG = (0.0, 0.0, 6.0, 10.0, 14.0)
    entries = []
    begin = -10.0
    for i in range(1, N_WIDE + N_DOWN):
        length = 4.9 if i < N_WIDE else 9.8
        for phase in range(1, 5):
            due = begin + LAG[phase] * (length / 4.9 if i >= N_WIDE else 1.0)
            if phase == 4 and i < N_WIDE:
                due = min(due, FORWARD_TICKS[(4, 8, 11, 12, 14, 16, 18)[i - 1]])
            entries.append((due, (i, phase)))
        begin += length
    early = [a for t, a in sorted(entries, key=lambda e: e[0]) if t < 0.0]
    table = plan([e for e in entries if e[0] >= 0.0], FORWARD_TICKS)

    def tick(part):
        for s in range(10):
            todo = table[2 * s + part]
            if todo:
                @pl.when(step == s)
                def _(todo=todo):
                    for action in todo:
                        act(action)

    @pl.when(step == 0)
    def _():
        say_hello(here)
        for pair in range(6):
            for n in range(3):
                at = pair * 384 + n * 128
                staged[:, at:at + 128] = wqkv_ref[:, n * D + pair * 128:n * D + (pair + 1) * 128].astype(F32)
        staged[:, OUT_AT:UP_AT] = wout_ref[...].astype(F32)
        staged[:, UP_AT:] = wup_ref[...].astype(F32)
        at = 0
        line = smalls.at[z, x, y, c]
        line[...] = jnp.zeros((8, SW), F32)
        for ref, width in zip(small_refs, VW):
            line[0:1, at:at + width] = ref[...].astype(F32).reshape(1, width)
            at += width
        await_all()
        swaps[0].start()

        def small_copy(n, src, to):
            return remote(src, src, (small_s, small_r), n, to)

        small_c = small_copy(0, smalls.at[one(z), one(x), one(y), one(c)], peers[5])
        both = smalls.at[one(z), one(x), one(y), TWO]
        small_z = [small_copy(1 + k, both, peers[k]) for k in range(3)]
        small_x = small_copy(4, smalls.at[EVERY, one(x), one(y), TWO], peers[3])
        small_y = small_copy(5, smalls.at[EVERY, TWO, one(y), TWO], peers[4])
        small_c.start()
        for i in range(1, N_WIDE):
            swaps[i].start()
        for i in range(N_WIDE):
            swaps[i].wait_recv()
            mine_part = staged[:, half(i, c)]
            their_part = swap[:, i * HW:(i + 1) * HW]
            buf, at = (watt, i) if i < 4 else (wup, i - 4)
            lower = jnp.where(c == 0, mine_part, their_part)
            upper = jnp.where(c == 0, their_part, mine_part)
            buf[z, x, y, :, half(at, c)] = jnp.concatenate([lower, upper], 0).astype(BF)
            items[i].start(0)
            if i == 0:
                small_c.wait_recv()
                for copy in small_z:
                    copy.start()
        for i in range(N_DOWN):
            items[N_WIDE + i].start(0)
            own[i].start()

        def take_row(row):
            for ref in (x1_ref, dmp_ref):
                ref[pl.ds(row * S + S - 16, 16), :] = jnp.zeros((16, D), ref.dtype)
            x1_ref[pl.ds(row * S, SEQ), :] = x_ref[:, row, :].astype(F32)

        items[0].start(1)
        for copy in small_z:
            copy.wait_recv()
        small_x.start()
        take_row(0)
        items[0].start(2)
        small_x.wait_recv()
        small_y.start()
        take_row(1)
        for row in range(2):
            dmp_ref[pl.ds(row * S, SEQ), :] = dm_ref[:, row, :]
        items[0].start(3)
        for action in early:
            act(action)
        small_y.wait_recv()
        pieces = smalls[...].reshape(32, 8, SW)[:, 0, :].astype(BF)

        def joined(lead, size, width):
            src = lax.broadcasted_iota(jnp.int32, (SW, size), 0)
            dst = lax.broadcasted_iota(jnp.int32, (SW, size), 1)
            spread = jnp.where(src == lead + lax.rem(dst, width), 1.0, 0.0).astype(BF)
            dev = lax.broadcasted_iota(jnp.int32, (32, size), 0)
            col = lax.broadcasted_iota(jnp.int32, (32, size), 1)
            return jnp.sum(jnp.where(lax.div(col, width) == dev, mm(pieces, spread), 0.0), 0, keepdims=True)

        vectors = [joined(24 * i, D, 24) for i in range(NV)]
        for i in range(NV):
            vec_ref[i:i + 1, :] = vectors[i]
        for part in range(N_UP):
            src = lax.broadcasted_iota(jnp.int32, (SW, D), 0)
            dst = lax.broadcasted_iota(jnp.int32, (SW, D), 1)
            spread = jnp.where(src == 24 * NV + lax.rem(dst, 96), 1.0, 0.0).astype(BF)
            dev = lax.broadcasted_iota(jnp.int32, (32, D), 0)
            col = lax.broadcasted_iota(jnp.int32, (32, D), 1)
            found = jnp.where(lax.div(col, 96) + 8 * part == dev, mm(pieces, spread), 0.0)
            bu[part] = jnp.sum(found, 0, keepdims=True)
        for pair in range(6):
            n, at = pair // 2, (pair % 2) * 384
            bqkv[n, :, at:at + 128] = vectors[BQ][:, pair * 128:(pair + 1) * 128]
            bqkv[n, :, at + 128:at + 256] = jnp.zeros((1, 128), F32)
            bqkv[n, :, at + 256:at + 384] = vectors[BV][:, pair * 128:(pair + 1) * 128]

        @pl.loop(0, T // MB)
        def _(i):
            rows = rows_of(i)
            n1, _s = norm_parts(x1_ref[rows, :])
            h1[rows, :] = (n1 * vec_ref[G1:G1 + 1, :] + vec_ref[B1:B1 + 1, :]).astype(BF)
        for row in range(2):
            slot = lax.broadcasted_iota(jnp.int32, (S, 128), 0)
            lane = lax.broadcasted_iota(jnp.int32, (S, 128), 1)
            packed = jnp.where(slot < HALF, 0, jnp.where(slot < 2 * HALF, 1, 2))
            seg = jnp.where(kind_ref[row] == 1, packed, 0)
            fa[row] = jnp.where((lane < 3) & (seg == lane), -1e30, 0.0).astype(BF)
            fb[row] = jnp.where((lane < 3) & ((seg != lane) | (slot >= SEQ)), 1.0, 0.0).astype(BF)
        h1t_ref[...] = h1[...].T
        rl_ref[...] = jnp.zeros_like(rl_ref)
        act((0, 4))
        for copy in (small_c, *small_z, small_x, small_y, *swaps):
            copy.wait_send()

    tick(0)

    @pl.when(step < N_ATT)
    def _():
        hq, r = lax.div(step, 2), lax.rem(step, 2)

        @pl.when(r == 0)
        def _():
            @pl.loop(0, T // MB)
            def _(i):
                rows = rows_of(i)
                w = watt[:, :, :, :, pl.ds(pl.multiple_of(hq * GW, 128), GW)].reshape(D, GW)
                qkv_ref[rows, :] = (mm(h1[rows, :], w) + bqkv[hq]).astype(BF)

        rows = pl.ds(pl.multiple_of(r * S, 16), S)
        feat_q, feat_k = fa[r], fb[r]
        ones = jnp.ones((S, 128), BF)
        scale = math.log2(math.e) / math.sqrt(HD)
        for j in range(HG // 2):
            if j:
                tick(1)
            at = j * 384
            qp, kp, vp = (qkv_ref[rows, at + 128 * n: at + 128 * (n + 1)] for n in range(3))
            kcat = jnp.concatenate([kp, feat_k], 1)
            total = None
            for e in range(2):
                keep = head_lanes((S, 128), e)
                qcat = jnp.concatenate([jnp.where(keep, qp, jnp.zeros_like(qp)), feat_q], 1)
                s = mm(qcat, kcat, NT)
                m = jnp.max(s, -1, keepdims=True)
                pb = jnp.exp2((s - m) * scale).astype(BF)
                p_ref[0, 2 * j + e] = pb
                vcat = jnp.concatenate([jnp.where(keep, vp, jnp.zeros_like(vp)), ones], 1)
                o = mm(pb, vcat)
                rl = 1.0 / o[:, 128:]
                part = o[:, :128] * rl
                total = part if total is None else total + part
                spot = lax.broadcasted_iota(jnp.int32, (S, 128), 1) == hq * HG + 2 * j + e
                rl_ref[rows, :] = jnp.where(spot, rl, rl_ref[rows, :])
            out = pl.ds(pl.multiple_of(hq * QW + j * 128, 128), 128)
            attn_ref[rows, out] = total.astype(BF)

    @pl.when(step == N_ATT - 1)
    def _():
        @pl.loop(0, T // MB)
        def _(i):
            rows = rows_of(i)
            wo = watt[:, :, :, :, OUT_AT:UP_AT].reshape(D, D)
            x1 = x1_ref[rows, :] + mm(attn_ref[rows, :], wo) + vec_ref[BO:BO + 1, :]
            x1_ref[rows, :] = x1
            n2, _s = norm_parts(x1)
            h2[rows, :] = (n2 * vec_ref[G2:G2 + 1, :] + vec_ref[B2:B2 + 1, :]).astype(BF)
        h2t_ref[...] = h2[...].T

    @pl.when(step >= N_ATT)
    def _():
        part = step - N_ATT

        def hidden(i):
            rows = rows_of(i)
            w = wup[:, :, :, :, pl.ds(pl.multiple_of(part * D, 128), D)].reshape(D, D)
            g, slope = gelu_both(mm(h2[rows, :], w) + bu[part])
            g_ref[rows, :] = g.astype(BF)
            slope_ref[rows, :] = slope.astype(BF)

        pl.loop(0, T // MB // 2)(hidden)
        tick(1)
        pl.loop(T // MB // 2, T // MB)(hidden)
        for t in range(D // 256):
            cols = pl.ds(t * 256, 256)
            gdown_ref[cols, :] = mm(g_ref[:, cols], dmp_ref[...], TN).astype(BF)

    @pl.when(step == 9)
    def _():
        for item in items:
            item.drain()
        for copy in keeps:
            copy.wait()


def forward(kind, x, dm, wqkv, wout, wup, wdown, smalls):
    n = N_WIDE + N_DOWN
    att = lambda s: jnp.minimum(s, N_ATT - 1)
    ff = lambda s: jnp.maximum(s - N_ATT, 0)
    shape = jax.ShapeDtypeStruct
    return pl.pallas_call(
        forward_kernel,
        grid=(N_ATT + N_UP,),
        in_specs=[
            pl.BlockSpec(memory_space=pltpu.SMEM), fixed((SEQ, 2, D)), fixed((SEQ, 2, D)),
            fixed((24, 3 * D)), fixed((24, D)), fixed((24, FF)), fixed((1, 1, 1, 96, D)),
            *[pl.BlockSpec((w,), lambda s: (0,), pipeline_mode=pl.Buffered(1)) for w in VW],
        ],
        out_specs=[
            fixed((D, T)), pl.BlockSpec((T, GW), lambda s: (0, att(s) // 2)),
            pl.BlockSpec((1, HG, S, S), lambda s: (att(s) % 2, att(s) // 2, 0, 0)),
            fixed((T, D)), fixed((T, 128)), fixed((T, D)), fixed((T, D)), fixed((D, T)),
            pl.BlockSpec((T, D), lambda s: (0, ff(s))), pl.BlockSpec((T, D), lambda s: (0, ff(s))),
            pl.BlockSpec((D, D), lambda s: (ff(s), 0)),
            fixed((NV, D)), hbm(), hbm(), hbm(),
        ],
        out_shape=[
            shape((D, T), BF), shape((T, 3 * D), BF), shape((2, D // HD, S, S), BF),
            shape((T, D), BF), shape((T, 128), F32), shape((T, D), F32), shape((T, D), BF), shape((D, T), BF),
            shape((T, FF), BF), shape((T, FF), BF), shape((FF, D), BF), shape((NV, D), F32),
            shape((NZ, 2, 2, CH, UP_AT), BF), shape((NZ, 2, 2, CH, FF), BF), shape((NZ, 2, 2, 4 * CH, D), BF),
        ],
        scratch_shapes=[
            pltpu.VMEM((2, S, 128), BF), pltpu.VMEM((2, S, 128), BF), pltpu.VMEM((T, D), BF), pltpu.VMEM((T, D), BF),
            pltpu.VMEM((24, AW), F32), pltpu.VMEM((24, AW // 2), F32),
            pltpu.VMEM((NZ, 2, 2, CH, UP_AT), BF), pltpu.VMEM((NZ, 2, 2, CH, FF), BF),
            pltpu.VMEM((3, 1, GW), F32), pltpu.VMEM((N_UP, 1, D), F32), pltpu.VMEM((NZ, 2, 2, 2, 8, SW), F32),
            *dma_sems(n * Gather.COPIES, n * Gather.COPIES, N_WIDE, N_WIDE, 6, 6, n),
        ],
        compiler_params=pltpu.CompilerParams(collective_id=0, has_side_effects=True, vmem_limit_bytes=LIMIT),
        name="forward",
    )(kind, x, dm, wqkv, wout, wup, wdown.reshape(1, 1, 1, 96, D), *smalls)


def ffn_back_kernel(
    x1_ref, dm_ref, g_ref, slope_ref, wu_ref, wd_ref, h2t_ref, vec_ref, gdown_ref,
    y_ref, dx1_ref, gup_ref, sums_ref, odown_ref,
    yacc, dacc, dus, mine, acc, via, last, zs, sems_s, sems_r, own_sem,
):
    step = pl.program_id(0)
    here = where_am_i()
    z, x, y, c = here
    items, own = [], []
    for i in range(N_DOWN):
        rows = lambda core, i=i: pl.ds(pl.multiple_of(core * DH + i * CH, 16), CH)
        own.append(pltpu.make_async_copy(gdown_ref.at[:, :, :, rows(c)], mine.at[i], own_sem.at[i]))
        items.append(Scatter(
            here, (sems_s, sems_r), i * Scatter.COPIES, gdown_ref.at[EVERY, TWO, TWO, rows(1 - c)],
            lambda a, b, d, i=i: mine[i, a, b, d], acc.at[i], via.at[i], last.at[i], zs.at[i],
        ))

    @pl.when(step == 0)
    def _():
        say_hello(here)
        for copy in own:
            copy.start()

        @pl.loop(0, T // MB)
        def _(i):
            rows = rows_of(i)
            yacc[rows, :] = x1_ref[rows, :] + vec_ref[BD:BD + 1, :]
            dacc[rows, :] = jnp.zeros((MB, D), F32)
        sums_ref[...] = jnp.zeros_like(sums_ref)
        sums_ref[2:3, :] = jnp.sum(dm_ref[...].astype(F32), 0, keepdims=True)
        await_all()
        for item in items:
            item.start(0)

    for s in range(1, N_UP):
        @pl.when(step == s)
        def _(s=s):
            for i, item in enumerate(items):
                if s == 1:
                    own[i].wait()
                item.start(s)

    def block(i):
        rows = rows_of(i)
        g = g_ref[rows, :]
        yacc[rows, :] += mm(g, wd_ref[...])
        du = (mm(dm_ref[rows, :], wd_ref[...], NT) * slope_ref[rows, :].astype(F32)).astype(BF)
        dus[rows, :] = du
        sums_ref[pl.ds(3 + step, 1), :] += jnp.sum(du.astype(F32), 0, keepdims=True)
        dacc[rows, :] += mm(du, wu_ref[...], NT)

    pl.loop(0, T // MB)(block)

    @pl.loop(0, D // 256)
    def _(t):
        rows = pl.ds(pl.multiple_of(t * 256, 256), 256)
        gup_ref[rows, :] = mm(h2t_ref[rows, :], dus[...]).astype(BF)

    @pl.when(step == N_UP - 1)
    def _():
        @pl.loop(0, T // MB)
        def _(i):
            rows = rows_of(i)
            n2, s2 = norm_parts(x1_ref[rows, :])
            dh = dacc[rows, :]
            sums_ref[0:1, :] += jnp.sum(dh * n2, 0, keepdims=True)
            sums_ref[1:2, :] += jnp.sum(dh, 0, keepdims=True)
            dx1_ref[rows, :] = dm_ref[rows, :].astype(F32) + norm_pull(dh, n2, s2, vec_ref[G2:G2 + 1, :])
            y_ref[rows, :] = yacc[rows, :].astype(BF)
        for i, item in enumerate(items):
            odown_ref[pl.ds(i * CH, CH), :] = item.total()
            item.drain()


def ffn_back(x1, dm, g, slope, wup, down, h2t, vec, gdown):
    shape = jax.ShapeDtypeStruct
    col = pl.BlockSpec((T, D), lambda s: (0, s))
    return pl.pallas_call(
        ffn_back_kernel,
        grid=(N_UP,),
        in_specs=[
            fixed((T, D)), fixed((T, D)), col, col,
            pl.BlockSpec((D, D), lambda s: (0, s)), pl.BlockSpec((D, D), lambda s: (s, 0)),
            fixed((D, T)), fixed((NV, D)), hbm(),
        ],
        out_specs=[
            fixed((T, D)), fixed((T, D)), pl.BlockSpec((D, D), lambda s: (0, s)), fixed((8, D)), fixed((96, D)),
        ],
        out_shape=[
            shape((T, D), BF), shape((T, D), F32), shape((D, FF), BF), shape((8, D), F32), shape((96, D), F32),
        ],
        scratch_shapes=[
            pltpu.VMEM((T, D), F32), pltpu.VMEM((T, D), F32), pltpu.VMEM((T, D), BF),
            pltpu.VMEM((N_DOWN, NZ, 2, 2, CH, D), BF), *scatter_bufs(N_DOWN, D),
            *dma_sems(N_DOWN * 7, N_DOWN * 7, N_DOWN),
        ],
        compiler_params=pltpu.CompilerParams(collective_id=1, has_side_effects=True, vmem_limit_bytes=LIMIT),
        name="feed_forward_back",
    )(x1, dm, g, slope, wup, down, h2t, vec, gdown.reshape(NZ, 2, 2, 4 * CH, D))


BACK_TICKS = [4.0 * n for n in range(12)]
N_BACK = N_UP + 4


def attn_back_kernel(
    x_ref, yb_ref, dx1_ref, h1t_ref, qkv_ref, p_ref, attn_ref, rl_ref, wo_ref, wqkv_ref, vec_ref, sums_ref, gup_ref,
    out_ref, gx_ref, oqkv_ref, oout_ref, oup_ref, *refs,
):
    small_outs = refs[:NV + 1]
    (
        da, dos, dqkv, dh1, gqkv, gout, mine, acc, via, last, zs, done, landed, small,
        sems_s, sems_r, fin_s, fin_r, small_s, small_r, own_sem,
    ) = refs[NV + 1:]
    step = pl.program_id(0)
    hq, r = lax.div(step, 2), lax.rem(step, 2)
    here = where_am_i()
    z, x, y, c = here
    peers = partners(*here)
    items, own = [], []
    for n in range(N_BACK):
        if n < N_UP:
            theirs = gup_ref.at[EVERY, TWO, TWO, :, half(n, 1 - c)]
            own.append(pltpu.make_async_copy(gup_ref.at[:, :, :, :, half(n, c)], mine.at[n], own_sem.at[n]))
            get = lambda a, b, d, n=n: mine[n, a, b, d]
        elif n == N_UP:
            theirs = gout.at[EVERY, TWO, TWO, :, half(0, 1 - c)]
            get = lambda a, b, d: gout[a, b, d, :, half(0, c)]
        else:
            i = n - N_UP - 1
            theirs = gqkv.at[i, EVERY, TWO, TWO, :, half(0, 1 - c)]
            get = lambda a, b, d, i=i: gqkv[i, a, b, d, :, half(0, c)]
        items.append(Scatter(
            here, (sems_s, sems_r), n * Scatter.COPIES, theirs, get, acc.at[n], via.at[n], last.at[n], zs.at[n]))

    def final(n):
        theirs = pl.ds(pl.multiple_of((1 - c) * 24, 8), 24)
        return remote(done.at[n, theirs], landed.at[n], (fin_s, fin_r), n, peers[5])

    def put(n, core, value):
        if n > N_UP:
            for b in range(3):
                cols = pl.ds(pl.multiple_of(b * D + (n - N_UP - 1) * QW + core * 128, 128), 128)
                oqkv_ref[:, cols] = value[:, b * 128:(b + 1) * 128]
        elif n == N_UP:
            oout_ref[:, half(0, core)] = value
        else:
            oup_ref[:, half(n, core)] = value

    def finish(n):
        done[n] = items[n].total()
        final(n).start()
        put(n, c, done[n, pl.ds(pl.multiple_of(c * 24, 8), 24)])

    def act(action):
        n, phase = action
        if n < N_UP and phase == 1:
            own[n].wait()
        if phase == 4:
            finish(n)
        else:
            items[n].start(phase)

    LAG = (0.0, 3.0, 8.0, 11.0, 17.0)
    entries = []
    begin = 0.0
    for n in range(N_BACK):
        if n == N_UP + 1:
            begin = max(begin, BACK_TICKS[4])
        if n == N_UP + 2:
            begin = max(begin, BACK_TICKS[8])
        if n == N_UP + 3:
            begin = max(begin, BACK_TICKS[-1] + 4.0)
        for phase in range(1, 5):
            entries.append((begin + LAG[phase], (n, phase)))
        begin += 4.9
    tail = [a for t, a in sorted(entries, key=lambda e: e[0]) if t > BACK_TICKS[-1] or a[0] == N_BACK - 1]
    table = plan([e for e in entries if e[0] <= BACK_TICKS[-1] and e[1][0] != N_BACK - 1], BACK_TICKS)

    def tick(part):
        for s in range(N_ATT):
            todo = table[2 * s + part]
            if todo:
                @pl.when(step == s)
                def _(todo=todo):
                    for action in todo:
                        act(action)

    @pl.when(step == 0)
    def _():
        say_hello(here)
        for copy in own:
            copy.start()
        small[0] = jnp.zeros((16, D), F32)
        await_all()
        for n in range(N_UP):
            items[n].start(0)

        src = lax.broadcasted_iota(jnp.int32, (128, D), 0)
        dst = lax.broadcasted_iota(jnp.int32, (128, D), 1)
        spread = jnp.where(lax.div(dst, HD) == src, 1.0, 0.0)

        @pl.loop(0, T // MB)
        def _(i):
            rows = rows_of(i)
            d = dx1_ref[rows, :].astype(BF)
            da[rows, :] = d
            rl = lax.dot_general(
                rl_ref[rows, :], spread, NN, precision=lax.Precision.HIGHEST, preferred_element_type=F32)
            small[0, 4:5, :] += jnp.sum(d.astype(F32), 0, keepdims=True)
            dos[rows, :] = (mm(d, wo_ref[...], NT) * rl).astype(BF)
            dh1[rows, :] = jnp.zeros((MB, D), F32)
        for t in range(D // 192):
            cols = pl.ds(t * 192, 192)
            part = mm(attn_ref[:, t * 192:(t + 1) * 192], da[...], TN)
            gout[t] = part.astype(BF).reshape(2, 2, CH, D)
        items[N_UP].start(0)

    tick(0)
    rows = pl.ds(pl.multiple_of(r * S, 16), S)
    scale = 1.0 / math.sqrt(HD)
    for j in range(HG // 2):
        if j:
            tick(1)
        at = j * 384
        qp, kp, vp = (qkv_ref[rows, at + 128 * n: at + 128 * (n + 1)] for n in range(3))
        lanes = pl.ds(pl.multiple_of(hq * QW + j * 128, 128), 128)
        do = dos[rows, lanes]
        prod = do.astype(F32) * attn_ref[rows, lanes].astype(F32)
        dq = dk = dv = None
        for e in range(2):
            keep = head_lanes((S, 128), e)
            zero = jnp.zeros_like(qp)
            doe = jnp.where(keep, do, zero)
            dot = jnp.sum(jnp.where(keep, prod, 0.0), -1, keepdims=True)
            p = p_ref[0, 2 * j + e]
            ds = (p.astype(F32) * (mm(doe, vp, NT) - dot)).astype(BF)
            a_, b_, c_ = mm(ds, jnp.where(keep, kp, zero)), mm(ds, jnp.where(keep, qp, zero), TN), mm(p, doe, TN)
            dq, dk, dv = (a_, b_, c_) if dq is None else (dq + a_, dk + b_, dv + c_)
        for n, part in enumerate((dq * scale, dk * scale, dv)):
            dqkv[rows, at + 128 * n:at + 128 * (n + 1)] = part.astype(BF)

    @pl.when(r == 1)
    def _():
        sums = jnp.sum(dqkv[...].astype(F32), 0, keepdims=True)
        for j in range(2):
            cols = pl.ds(pl.multiple_of(hq * QW + j * 128, 128), 128)
            small[0, 2:3, cols] = sums[:, j * 384:j * 384 + 128]
            small[0, 3:4, cols] = sums[:, j * 384 + 256:j * 384 + 384]
        for t in range(D // 192):
            part = mm(h1t_ref[t * 192:(t + 1) * 192, :], dqkv[...])
            gqkv[hq, t] = part.astype(BF).reshape(2, 2, CH, GW)
        for i in range(3):
            @pl.when(hq == i)
            def _(i=i):
                items[N_UP + 1 + i].start(0)

        @pl.loop(0, T // MB)
        def _(i):
            rr = rows_of(i)
            dh1[rr, :] += mm(dqkv[rr, :], wqkv_ref[...], NT)

    @pl.when(step == N_ATT - 1)
    def _():
        rest = list(tail)
        act(rest.pop(0))

        def norm_row(row):
            rr = pl.ds(row * S, SEQ)
            dh = dh1[rr, :]
            n1, s1 = norm_parts(x_ref[:, row, :].astype(F32))
            small[0, 0:1, :] += jnp.sum(dh * n1, 0, keepdims=True)
            small[0, 1:2, :] += jnp.sum(dh, 0, keepdims=True)
            gx_ref[:, row, :] = (dx1_ref[rr, :] + norm_pull(dh, n1, s1, vec_ref[G1:G1 + 1, :])).astype(BF)

        norm_row(0)
        norm_row(1)
        small[0, 5:12, :] = sums_ref[0:7, :]
        copies = []

        def send_small(n, src, dst, to):
            copy = remote(small.at[src], small.at[dst], (small_s, small_r), n, to)
            copy.start()
            copies.append(copy)

        send_small(0, 0, 1, peers[5])
        hops = [(1, 2, 3, peers[3]), (2, 4, 5, peers[4])]
        level = 0
        while rest or level < 4:
            if rest:
                act(rest.pop(0))
            if level == 0:
                for row in range(2):
                    out_ref[:, row, :] = yb_ref[pl.ds(row * S, SEQ), :]
            if level < 2:
                copies[level].wait_recv()
                small[2 * level + 2] = small[2 * level] + small[2 * level + 1]
                send_small(*hops[level])
            elif level == 2:
                copies[2].wait_recv()
                small[6] = small[4] + small[5]
                for k in range(3):
                    send_small(3 + k, 6, 7 + k, peers[k])
            elif level == 3:
                for k in range(3):
                    copies[3 + k].wait_recv()
                total = small[6] + small[7] + small[8] + small[9]
                me = lax.axis_index("dp") * lax.axis_size("fsdp") + lax.axis_index("fsdp")
                src = lax.broadcasted_iota(jnp.int32, (D, 128), 0)
                dst = lax.broadcasted_iota(jnp.int32, (D, 128), 1)

                def pick(lines, width, at):
                    chosen = jnp.where((src == at + dst) & (dst < width), 1.0, 0.0)
                    return lax.dot_general(
                        lines, chosen, NN, precision=lax.Precision.HIGHEST, preferred_element_type=F32)

                mine_of = pick(total[:8], 24, me * 24)
                for n in range(NV):
                    small_outs[n][...] = mine_of[n, :24]
                row = lax.broadcasted_iota(jnp.int32, (8, D), 0)
                longest = jnp.sum(jnp.where(row == lax.div(me, 8), total[8:16], 0.0), 0, keepdims=True)
                small_outs[NV][...] = pick(jnp.broadcast_to(longest, (8, D)), 96, lax.rem(me, 8) * 96)[0, :96]
            level += 1
        for n in range(N_BACK):
            copy = final(n)
            copy.wait_recv()
            put(n, 1 - c, landed[n])
            copy.wait_send()
            items[n].drain()
        for copy in copies:
            copy.wait_send()


def attn_back(x, yb, dx1, h1t, qkv, p, attn, rl, watt, vec, sums, gup):
    shape = jax.ShapeDtypeStruct
    n_fin = N_BACK
    return pl.pallas_call(
        attn_back_kernel,
        grid=(N_ATT,),
        in_specs=[
            fixed((SEQ, 2, D)), fixed((T, D)), fixed((T, D)), fixed((D, T)), pl.BlockSpec((T, GW), lambda s: (0, s // 2)),
            pl.BlockSpec((1, HG, S, S), lambda s: (s % 2, s // 2, 0, 0)), fixed((T, D)), fixed((T, 128)),
            pl.BlockSpec((D, D), lambda s: (0, 3), pipeline_mode=pl.Buffered(1)),
            pl.BlockSpec((D, GW), lambda s: (0, s // 2)), fixed((NV, D)), fixed((8, D)), hbm(),
        ],
        out_specs=[
            fixed((SEQ, 2, D)), fixed((SEQ, 2, D)), fixed((24, 3 * D)), fixed((24, D)), fixed((24, FF)),
            *[pl.BlockSpec((w,), lambda s: (0,), pipeline_mode=pl.Buffered(1)) for w in VW],
        ],
        out_shape=[
            shape((SEQ, 2, D), BF), shape((SEQ, 2, D), BF), shape((24, 3 * D), F32), shape((24, D), F32),
            shape((24, FF), F32), *[shape((w,), F32) for w in VW],
        ],
        scratch_shapes=[
            pltpu.VMEM((T, D), BF), pltpu.VMEM((T, D), BF), pltpu.VMEM((T, GW), BF), pltpu.VMEM((T, D), F32),
            pltpu.VMEM((3, NZ, 2, 2, CH, GW), BF), pltpu.VMEM((NZ, 2, 2, CH, D), BF),
            pltpu.VMEM((N_UP, NZ, 2, 2, CH, HW), BF), *scatter_bufs(N_BACK, HW),
            pltpu.VMEM((N_BACK, CH, HW), F32), pltpu.VMEM((N_BACK, 24, HW), F32), pltpu.VMEM((10, 16, D), F32),
            *dma_sems(N_BACK * 7, N_BACK * 7, n_fin, n_fin, 6, 6, N_UP),
        ],
        compiler_params=pltpu.CompilerParams(collective_id=2, has_side_effects=True, vmem_limit_bytes=LIMIT),
        name="attention_back",
    )(x, yb, dx1, h1t, qkv, p, attn, rl, watt, watt, vec, sums, gup.reshape(NZ, 2, 2, CH, FF))


def by_pair(v):
    return v.reshape(v.shape[0], 3, 6, 128).transpose(0, 2, 1, 3).reshape(v.shape[0], 3 * D)


def by_kind(v):
    return v.reshape(v.shape[0], 6, 3, 128).transpose(0, 2, 1, 3).reshape(v.shape[0], 3 * D)


def with_own_copies(inputs, row_kind, w_qkv, w_out, w_up, w_down, vectors, b_up, out_grad):
    x, dm = inputs.transpose(1, 0, 2), out_grad.transpose(1, 0, 2)
    h1t, qkv, p, attn, rl, x1, dmp, h2t, g, slope, gdown, vec, watt, wup, down = forward(
        row_kind, x, dm, w_qkv, w_out, w_up, w_down, (*vectors, b_up))
    yb, dx1, gup, sums, gdown = ffn_back(
        x1, dmp, g, slope, wup.reshape(D, FF), down.reshape(FF, D), h2t, vec, gdown)
    out, gx, gqkv, gout, gup, *small = attn_back(
        x, yb, dx1, h1t, qkv, p, attn, rl, watt.reshape(D, UP_AT), vec, sums, gup)
    return out.transpose(1, 0, 2), gx.transpose(1, 0, 2), gqkv, gout, gup, gdown, small[:NV], small[NV]


def with_collectives(inputs, row_kind, w_qkv, w_out, w_up, w_down, vectors, b_up, out_grad):
    axes = ("dp", "fsdp")
    get = lambda v: lax.all_gather(v, axes, axis=0, tiled=True)
    wide = jnp.concatenate([by_pair(get(w_qkv)), get(w_out), get(w_up)], 1)
    down = get(w_down)
    full = [get(v).astype(F32) for v in vectors]
    vec = jnp.stack(full)
    bu = get(b_up).astype(F32)[None]
    bqkv = by_pair(jnp.concatenate([full[BQ], jnp.zeros_like(full[BQ]), full[BV]])[None])
    h1, qkv, p, attn, rl, x1 = attn_fwd(row_kind, inputs, wide, bqkv, vec)
    outputs, dx1, gup, gdown, gbu, gg2, gb2, gbd = ffn(x1, out_grad, wide, down, bu, vec)
    input_grad, gqkv, gout, gbqkv, gbo, gg1, gb1 = attn_bwd(inputs, dx1, h1, qkv, p, attn, rl, wide, vec)
    gbqkv = by_kind(gbqkv)
    small = [gg1, gb1, gbqkv[:, :D], gbqkv[:, 2 * D:], gbo, gg2, gb2, gbd]
    give = lambda v: lax.psum_scatter(v.astype(F32), axes, scatter_dimension=0, tiled=True)
    return (
        outputs, input_grad, give(by_kind(gqkv)), give(gout), give(gup), give(gdown),
        [give(v[0]) for v in small], give(gbu[0]),
    )


def on_device(
    copies, inputs, row_kind, ln1_gain, ln1_bias, w_qkv, b_query, b_value, w_out, b_out, ln2_gain, ln2_bias,
    w_up, b_up, w_down, b_down, out_grad,
):
    vectors = (ln1_gain, ln1_bias, b_query, b_value, b_out, ln2_gain, ln2_bias, b_down)
    run = with_own_copies if copies else with_collectives
    outputs, input_grad, gqkv, gout, gup, gdown, small, gbu = run(
        inputs, row_kind, w_qkv, w_out, w_up, w_down, vectors, b_up, out_grad)
    gg1, gb1, gbq, gbv, gbo, gg2, gb2, gbd = small
    return outputs, input_grad, gg1, gb1, gqkv, gbq, gbv, gout, gbo, gg2, gb2, gup, gbu, gdown, gbd


def solution(mesh):
    both = ("dp", "fsdp")
    row = P(both)
    mat = P(both, None)
    act = P(both, None, None)
    in_specs = (act, row, row, row, mat, row, row, mat, row, row, row, mat, row, mat, row, act)
    out_specs = (act, act, row, row, mat, row, row, mat, row, row, row, mat, row, mat, row)
    copies = mesh.shape["dp"] == 2 * NZ and mesh.shape["fsdp"] == 4
    return jax.shard_map(
        functools.partial(on_device, copies), mesh=mesh, in_specs=in_specs, out_specs=out_specs, check_vma=False
    )
```

```python
import functools
import math

import jax
import jax.numpy as jnp
from jax import lax
from jax.experimental import pallas as pl
from jax.experimental.pallas import tpu as pltpu
from jax.sharding import PartitionSpec as P

D = 768
HD = 64
FF = 3072
SEQ = 529
HALF = 264
EPS = 1e-06
S = 544
T = 2 * S
MB = 272
HG = 4
QW = HG * HD
GW = 3 * QW
FC = 512
OUT_AT = 3 * D
UP_AT = 4 * D
AW = 4 * D + FF
F32 = jnp.float32
BF = jnp.bfloat16
LIMIT = 62 * 2**20
MESH = pl.DeviceIdType.MESH
NN = (((1,), (0,)), ((), ()))
NT = (((1,), (1,)), ((), ()))
TN = (((0,), (0,)), ((), ()))


def mm(a, b, dims=NN):
    return lax.dot_general(a, b, dims, preferred_element_type=F32)


def norm_parts(values):
    mean = jnp.mean(values, -1, keepdims=True)
    centred = values - mean
    inverse = lax.rsqrt(jnp.mean(centred * centred, -1, keepdims=True) + EPS)
    return centred * inverse, inverse


def norm_pull(grad, normed, inverse, gain):
    scaled = grad * gain
    return inverse * (
        scaled
        - jnp.mean(scaled, -1, keepdims=True)
        - normed * jnp.mean(scaled * normed, -1, keepdims=True)
    )


def gelu_both(u):
    a = jnp.abs(u)
    t = 1.0 / (1.0 + (0.3275911 / math.sqrt(2.0)) * a)
    e = jnp.exp(-0.5 * u * u)
    poly = t * (
        0.254829592
        + t * (-0.284496736 + t * (1.421413741 + t * (-1.453152027 + t * 1.061405429)))
    )
    tail = 0.5 * poly * e
    phi = jnp.where(u < 0, tail, 1.0 - tail)
    return u * phi, phi + u * e * (1.0 / math.sqrt(2.0 * math.pi))


def head_lanes(shape, e):
    lane = lax.broadcasted_iota(jnp.int32, shape, 1)
    return (lane // HD) == e


def whole(shape):
    return pl.BlockSpec(shape, lambda *_: (0,) * len(shape))


def rows_of(i):
    return pl.ds(pl.multiple_of(i * MB, 16), MB)


G1, B1, BQ, BV, BO, G2, B2, BD = range(8)


def attn_fwd_kernel(
    kind_ref, x_ref, wg_ref, bqkv_ref, wo_ref, vec_ref,
    h1_ref, qkv_ref, p_ref, attn_ref, rl_ref, x1_ref, fa, fb,
):
    hq, r = pl.program_id(0), pl.program_id(1)

    @pl.when((hq == 0) & (r == 0))
    def _():
        for row in range(2):
            h1_ref[pl.ds(row * S + S - 16, 16), :] = jnp.zeros((16, D), BF)
            n1, _s = norm_parts(x_ref[row].astype(F32))
            h1_ref[pl.ds(row * S, SEQ), :] = (n1 * vec_ref[G1:G1 + 1, :] + vec_ref[B1:B1 + 1, :]).astype(BF)
            slot = lax.broadcasted_iota(jnp.int32, (S, 128), 0)
            lane = lax.broadcasted_iota(jnp.int32, (S, 128), 1)
            packed = jnp.where(slot < HALF, 0, jnp.where(slot < 2 * HALF, 1, 2))
            seg = jnp.where(kind_ref[row] == 1, packed, 0)
            fa[row] = jnp.where((lane < 3) & (seg == lane), -1e30, 0.0).astype(BF)
            fb[row] = jnp.where((lane < 3) & ((seg != lane) | (slot >= SEQ)), 1.0, 0.0).astype(BF)

    @pl.when(r == 0)
    def _():
        @pl.loop(0, T // MB)
        def _(i):
            rows = rows_of(i)
            qkv_ref[rows, :] = (mm(h1_ref[rows, :], wg_ref[...]) + bqkv_ref[...]).astype(BF)

    rows = pl.ds(pl.multiple_of(r * S, 16), S)
    feat_q, feat_k = fa[r], fb[r]
    ones = jnp.ones((S, 128), BF)
    scale = math.log2(math.e) / math.sqrt(HD)
    for j in range(HG // 2):
        at = j * 384
        qp, kp, vp = (qkv_ref[rows, at + 128 * n: at + 128 * (n + 1)] for n in range(3))
        kcat = jnp.concatenate([kp, feat_k], 1)
        total = None
        inv = None
        for e in range(2):
            keep = head_lanes((S, 128), e)
            qcat = jnp.concatenate([jnp.where(keep, qp, jnp.zeros_like(qp)), feat_q], 1)
            s = mm(qcat, kcat, NT)
            m = jnp.max(s, -1, keepdims=True)
            pb = jnp.exp2((s - m) * scale).astype(BF)
            p_ref[0, 2 * j + e] = pb
            vcat = jnp.concatenate([jnp.where(keep, vp, jnp.zeros_like(vp)), ones], 1)
            o = mm(pb, vcat)
            rl = 1.0 / o[:, 128:]
            part = o[:, :128] * rl
            total = part if total is None else total + part
            inv = rl if inv is None else jnp.where(keep, rl, inv)
        out = pl.ds(pl.multiple_of(hq * QW + j * 128, 128), 128)
        attn_ref[rows, out] = total.astype(BF)
        rl_ref[rows, out] = inv

    @pl.when((hq == D // QW - 1) & (r == 1))
    def _():
        for row in range(2):
            x1_ref[pl.ds(row * S + S - 16, 16), :] = jnp.zeros((16, D), F32)
            x1_ref[pl.ds(row * S, SEQ), :] = x_ref[row].astype(F32)

        @pl.loop(0, T // MB)
        def _(i):
            rr = rows_of(i)
            x1_ref[rr, :] = x1_ref[rr, :] + mm(attn_ref[rr, :], wo_ref[...]) + vec_ref[BO:BO + 1, :]


def attn_fwd(kind, x, wide, bqkv, vec):
    return pl.pallas_call(
        attn_fwd_kernel,
        grid=(D // QW, 2),
        in_specs=[
            pl.BlockSpec(memory_space=pltpu.SMEM), whole((2, SEQ, D)),
            pl.BlockSpec((D, GW), lambda h, r: (0, h)), pl.BlockSpec((1, GW), lambda h, r: (0, h)),
            pl.BlockSpec((D, D), lambda h, r: (0, 3)), whole((8, D)),
        ],
        out_specs=[
            whole((T, D)), pl.BlockSpec((T, GW), lambda h, r: (0, h)),
            pl.BlockSpec((1, HG, S, S), lambda h, r: (r, h, 0, 0)),
            whole((T, D)), whole((T, D)), whole((T, D)),
        ],
        out_shape=[
            jax.ShapeDtypeStruct((T, D), BF), jax.ShapeDtypeStruct((T, 3 * D), BF),
            jax.ShapeDtypeStruct((2, D // HD, S, S), BF),
            jax.ShapeDtypeStruct((T, D), BF), jax.ShapeDtypeStruct((T, D), F32), jax.ShapeDtypeStruct((T, D), F32),
        ],
        scratch_shapes=[pltpu.VMEM((2, S, 128), BF), pltpu.VMEM((2, S, 128), BF)],
        compiler_params=pltpu.CompilerParams(vmem_limit_bytes=LIMIT),
        name="attention_forward",
    )(kind, x, wide, bqkv, wide, vec)


def ffn_kernel(
    x1_ref, dm_ref, wu_ref, wd_ref, bu_ref, vec_ref,
    out_ref, dx1_ref, gwu_ref, gwd_ref, gbu_ref, gg2_ref, gb2_ref, gbd_ref,
    h2, h2t, dm, yacc, dacc, gs, dus,
):
    c = pl.program_id(0)

    @pl.when(c == 0)
    def _():
        for row in range(2):
            dm[pl.ds(row * S + S - 16, 16), :] = jnp.zeros((16, D), BF)
            dm[pl.ds(row * S, SEQ), :] = dm_ref[row]

        @pl.loop(0, T // MB)
        def _(i):
            rows = rows_of(i)
            x1 = x1_ref[rows, :]
            n2, _s = norm_parts(x1)
            h2[rows, :] = (n2 * vec_ref[G2:G2 + 1, :] + vec_ref[B2:B2 + 1, :]).astype(BF)
            yacc[rows, :] = x1 + vec_ref[BD:BD + 1, :]
            dacc[rows, :] = jnp.zeros((MB, D), F32)
        h2t[...] = h2[...].T
        gbd_ref[...] = jnp.sum(dm[...].astype(F32), 0, keepdims=True)

    gbu_ref[...] = jnp.zeros_like(gbu_ref)

    @pl.loop(0, T // MB)
    def _(i):
        rows = rows_of(i)
        u = mm(h2[rows, :], wu_ref[...]) + bu_ref[...]
        g, slope = gelu_both(u)
        gb = g.astype(BF)
        gs[rows, :] = gb
        yacc[rows, :] += mm(gb, wd_ref[...])
        du = (mm(dm[rows, :], wd_ref[...], NT) * slope).astype(BF)
        dus[rows, :] = du
        gbu_ref[...] += jnp.sum(du.astype(F32), 0, keepdims=True)
        dacc[rows, :] += mm(du, wu_ref[...], NT)

    for t in range(FC // 256):
        cols = pl.ds(t * 256, 256)
        gwd_ref[cols, :] = mm(gs[:, cols], dm[...], TN).astype(BF)

    @pl.loop(0, D // 256)
    def _(t):
        rows = pl.ds(pl.multiple_of(t * 256, 256), 256)
        gwu_ref[rows, :] = mm(h2t[rows, :], dus[...]).astype(BF)

    @pl.when(c == FF // FC - 1)
    def _():
        gg2_ref[...] = jnp.zeros_like(gg2_ref)
        gb2_ref[...] = jnp.zeros_like(gb2_ref)
        for row in range(2):
            out_ref[row] = yacc[pl.ds(row * S, SEQ), :].astype(BF)

        @pl.loop(0, T // MB)
        def _(i):
            rows = rows_of(i)
            n2, s2 = norm_parts(x1_ref[rows, :])
            dh = dacc[rows, :]
            gg2_ref[...] += jnp.sum(dh * n2, 0, keepdims=True)
            gb2_ref[...] += jnp.sum(dh, 0, keepdims=True)
            dx1_ref[rows, :] = dm[rows, :].astype(F32) + norm_pull(dh, n2, s2, vec_ref[G2:G2 + 1, :])


def ffn(x1, dm, wide, down, bu, vec):
    one = jax.ShapeDtypeStruct((1, D), F32)
    return pl.pallas_call(
        ffn_kernel,
        grid=(FF // FC,),
        in_specs=[
            whole((T, D)), whole((2, SEQ, D)),
            pl.BlockSpec((D, FC), lambda c: (0, c + UP_AT // FC)), pl.BlockSpec((FC, D), lambda c: (c, 0)),
            pl.BlockSpec((1, FC), lambda c: (0, c)), whole((8, D)),
        ],
        out_specs=[
            whole((2, SEQ, D)), whole((T, D)),
            pl.BlockSpec((D, FC), lambda c: (0, c)), pl.BlockSpec((FC, D), lambda c: (c, 0)),
            pl.BlockSpec((1, FC), lambda c: (0, c)), whole((1, D)), whole((1, D)), whole((1, D)),
        ],
        out_shape=[
            jax.ShapeDtypeStruct((2, SEQ, D), BF), jax.ShapeDtypeStruct((T, D), F32),
            jax.ShapeDtypeStruct((D, FF), BF), jax.ShapeDtypeStruct((FF, D), BF),
            jax.ShapeDtypeStruct((1, FF), F32), one, one, one,
        ],
        scratch_shapes=[
            pltpu.VMEM((T, D), BF), pltpu.VMEM((D, T), BF), pltpu.VMEM((T, D), BF),
            pltpu.VMEM((T, D), F32), pltpu.VMEM((T, D), F32),
            pltpu.VMEM((T, FC), BF), pltpu.VMEM((T, FC), BF),
        ],
        compiler_params=pltpu.CompilerParams(vmem_limit_bytes=LIMIT),
        name="feed_forward",
    )(x1, dm, wide, down, bu, vec)


def attn_bwd_kernel(
    x_ref, dx1_ref, h1_ref, qkv_ref, p_ref, attn_ref, rl_ref, wo_ref, wqkv_ref, vec_ref,
    gx_ref, gwqkv_ref, gwo_ref, gbqkv_ref, gbo_ref, gg1_ref, gb1_ref,
    da, dos, h1t, dqkv,
):
    hq, r = pl.program_id(0), pl.program_id(1)

    @pl.when((hq == 0) & (r == 0))
    def _():
        gbo_ref[...] = jnp.zeros_like(gbo_ref)

        @pl.loop(0, T // MB)
        def _(i):
            rows = rows_of(i)
            d = dx1_ref[rows, :].astype(BF)
            da[rows, :] = d
            gbo_ref[...] += jnp.sum(d.astype(F32), 0, keepdims=True)
            dos[rows, :] = (mm(d, wo_ref[...], NT) * rl_ref[rows, :]).astype(BF)
        h1t[...] = h1_ref[...].T

    rows = pl.ds(pl.multiple_of(r * S, 16), S)
    scale = 1.0 / math.sqrt(HD)
    for j in range(HG // 2):
        at = j * 384
        qp, kp, vp = (qkv_ref[rows, at + 128 * n: at + 128 * (n + 1)] for n in range(3))
        do = dos[rows, pl.ds(pl.multiple_of(hq * QW + j * 128, 128), 128)]
        prod = do.astype(F32) * attn_ref[rows, j * 128:(j + 1) * 128].astype(F32)
        dq = dk = dv = None
        for e in range(2):
            keep = head_lanes((S, 128), e)
            zero = jnp.zeros_like(qp)
            doe = jnp.where(keep, do, zero)
            dot = jnp.sum(jnp.where(keep, prod, 0.0), -1, keepdims=True)
            p = p_ref[0, 2 * j + e]
            ds = (p.astype(F32) * (mm(doe, vp, NT) - dot)).astype(BF)
            a = mm(ds, jnp.where(keep, kp, zero))
            b = mm(ds, jnp.where(keep, qp, zero), TN)
            c = mm(p, doe, TN)
            dq, dk, dv = (a, b, c) if dq is None else (dq + a, dk + b, dv + c)
        for n, part in enumerate((dq * scale, dk * scale, dv)):
            col = hq * GW + j * 384 + n * 128
            dqkv[rows, pl.ds(pl.multiple_of(col, 128), 128)] = part.astype(BF)

    @pl.when(r == 1)
    def _():
        part = dqkv[:, pl.ds(pl.multiple_of(hq * GW, 128), GW)]
        gbqkv_ref[...] = jnp.sum(part.astype(F32), 0, keepdims=True)

        @pl.loop(0, D // 256)
        def _(t):
            rr = pl.ds(pl.multiple_of(t * 256, 256), 256)
            gwqkv_ref[rr, :] = mm(h1t[rr, :], part).astype(BF)
        gwo_ref[...] = mm(attn_ref[...], da[...], TN).astype(BF)

    @pl.when((hq == D // QW - 1) & (r == 1))
    def _():
        gg1_ref[...] = jnp.zeros_like(gg1_ref)
        gb1_ref[...] = jnp.zeros_like(gb1_ref)
        for row in range(2):
            rr = pl.ds(row * S, SEQ)
            dh = mm(dqkv[pl.ds(row * S, S), :], wqkv_ref[...], NT)[:SEQ]
            n1, s1 = norm_parts(x_ref[row].astype(F32))
            gg1_ref[...] += jnp.sum(dh * n1, 0, keepdims=True)
            gb1_ref[...] += jnp.sum(dh, 0, keepdims=True)
            gx_ref[row] = (dx1_ref[rr, :] + norm_pull(dh, n1, s1, vec_ref[G1:G1 + 1, :])).astype(BF)


def attn_bwd(x, dx1, h1, qkv, p, attn, rl, wide, vec):
    act = pl.BlockSpec((T, QW), lambda h, r: (0, h))
    one = jax.ShapeDtypeStruct((1, D), F32)
    return pl.pallas_call(
        attn_bwd_kernel,
        grid=(D // QW, 2),
        in_specs=[
            whole((2, SEQ, D)), whole((T, D)), whole((T, D)), pl.BlockSpec((T, GW), lambda h, r: (0, h)),
            pl.BlockSpec((1, HG, S, S), lambda h, r: (r, h, 0, 0)), act, whole((T, D)),
            pl.BlockSpec((D, D), lambda h, r: (0, 3)), whole((D, 3 * D)), whole((8, D)),
        ],
        out_specs=[
            whole((2, SEQ, D)), pl.BlockSpec((D, GW), lambda h, r: (0, h)),
            pl.BlockSpec((QW, D), lambda h, r: (h, 0)),
            pl.BlockSpec((1, GW), lambda h, r: (0, h)), whole((1, D)), whole((1, D)), whole((1, D)),
        ],
        out_shape=[
            jax.ShapeDtypeStruct((2, SEQ, D), BF), jax.ShapeDtypeStruct((D, 3 * D), BF), jax.ShapeDtypeStruct((D, D), BF),
            jax.ShapeDtypeStruct((1, 3 * D), F32), one, one, one,
        ],
        scratch_shapes=[
            pltpu.VMEM((T, D), BF), pltpu.VMEM((T, D), BF), pltpu.VMEM((D, T), BF), pltpu.VMEM((T, 3 * D), BF),
        ],
        compiler_params=pltpu.CompilerParams(vmem_limit_bytes=LIMIT),
        name="attention_backward",
    )(x, dx1, h1, qkv, p, attn, rl, wide, wide, vec)


NZ = 4
CH = 48
HW = 384
SW = 384
N_WIDE = AW // (2 * HW)
N_DOWN = 4
N_UP = FF // D
DH = 2 * CH
NV = 8
VW = (24,) * NV + (96,)


def one(i):
    return pl.ds(i, 1)


EVERY = pl.ds(0, NZ)
TWO = pl.ds(0, 2)


def where_am_i():
    dp, fs = lax.axis_index("dp"), lax.axis_index("fsdp")
    return lax.div(dp, 2), lax.rem(dp, 2), lax.div(fs, 2), lax.rem(fs, 2)


def device(z, x, y, c):
    return (z * 2 + x, y * 2 + c)


def partners(z, x, y, c):
    found = [device(lax.rem(z + k, NZ), x, y, c) for k in (1, 2, 3)]
    return found + [device(z, 1 - x, y, c), device(z, x, 1 - y, c), device(z, x, y, 1 - c)]


def say_hello(here):
    barrier = pltpu.get_barrier_semaphore()
    for other in partners(*here):
        pl.semaphore_signal(barrier, inc=1, device_id=other, device_id_type=MESH)


def await_all():
    pl.semaphore_wait(pltpu.get_barrier_semaphore(), 6)


def remote(src, dst, sems, n, target):
    return pltpu.make_async_remote_copy(
        src_ref=src, dst_ref=dst, send_sem=sems[0].at[n], recv_sem=sems[1].at[n],
        device_id=target, device_id_type=MESH,
    )


def half(i, core):
    return pl.ds(pl.multiple_of(i * 2 * HW + core * HW, 128), HW)


def down_rows(i, core):
    return pl.ds(pl.multiple_of(core * DH + (i // 2) * CH, 16), CH)


def down_cols(i):
    return pl.ds((i % 2) * HW, HW)


def add(a, b):
    return (a.astype(F32) + b.astype(F32)).astype(BF)


def plan(entries, ticks):
    table = {n: [] for n in range(len(ticks))}
    rest = []
    for due, action in sorted(entries, key=lambda e: e[0]):
        slot = min((n for n, t in enumerate(ticks) if t >= due), default=None)
        (rest if slot is None else table[slot]).append(action)
    return table, rest


class Gather:
    COPIES = 7

    def __init__(self, here, sems, base, view, first):
        z, x, y, c = here
        peers = partners(*here)
        mine = view(one(z), one(x), one(y))
        column = view(EVERY, one(x), one(y))
        fx, fy = jnp.where(c == 0, 1 - x, x), jnp.where(c == 0, y, 1 - y)
        tx, ty = jnp.where(c == 0, x, 1 - x), jnp.where(c == 0, 1 - y, y)
        passed = view(EVERY, one(fx), one(fy))
        all_of = view(EVERY, TWO, TWO)
        make = lambda n, src, dst, to: remote(src, dst, sems, base + n, to)
        self.along_z = [make(k, mine if first is None else first, mine, peers[k]) for k in range(3)]
        self.along_x = make(3, column, column, peers[3])
        self.along_y = make(4, column, column, peers[4])
        self.diagonal = make(5, passed, passed, device(z, tx, ty, c))
        self.sibling = make(6, all_of, all_of, peers[5])

    def start(self, phase):
        if phase == 0:
            for copy in self.along_z:
                copy.start()
        elif phase == 1:
            for copy in self.along_z:
                copy.wait_recv()
            self.along_x.start()
            self.along_y.start()
        elif phase == 2:
            self.along_x.wait_recv()
            self.along_y.wait_recv()
            self.diagonal.start()
        elif phase == 3:
            self.diagonal.wait_recv()
            self.sibling.start()
        else:
            self.sibling.wait_recv()

    def drain(self):
        for copy in (*self.along_z, self.along_x, self.along_y, self.diagonal, self.sibling):
            copy.wait_send()


class Scatter:
    COPIES = 7

    def __init__(self, here, sems, base, theirs, mine, acc, via, last, zs):
        self.mine, self.acc, self.via, self.last, self.zs = mine, acc, via, last, zs
        z, x, y, c = self.here = here
        peers = partners(*here)
        ix, iy = jnp.where(c == 0, x, 1 - x), jnp.where(c == 0, 1 - y, y)
        self.px, self.py = jnp.where(c == 0, 1 - x, x), jnp.where(c == 0, y, 1 - y)
        first, second = device(z, ix, iy, c), device(z, self.px, self.py, c)
        make = lambda n, src, dst, to: remote(src, dst, sems, base + n, to)
        at = lambda xs, ys: acc.at[EVERY, one(xs), one(ys)]
        self.swap = make(0, theirs, acc, peers[5])
        self.far = make(1, at(1 - x, 1 - y), via.at[0], first)
        self.near = make(2, at(ix, iy), via.at[1], first)
        self.next = make(3, at(self.px, self.py), last, second)
        self.along_z = [
            make(4 + k, acc.at[one(lax.rem(z + k + 1, NZ)), one(x), one(y)], zs.at[k], peers[k]) for k in range(3)
        ]

    def start(self, phase):
        z, x, y, c = self.here
        acc = self.acc
        if phase == 0:
            self.swap.start()
        elif phase == 1:
            self.swap.wait_recv()

            @pl.loop(0, NZ)
            def _(i):
                for xi in range(2):
                    for yi in range(2):
                        acc[i, xi, yi] = add(acc[i, xi, yi], self.mine(i, xi, yi))
            self.far.start()
            self.near.start()
        elif phase == 2:
            self.far.wait_recv()
            px, py = self.px, self.py

            @pl.loop(0, NZ)
            def _(i):
                acc[i, px, py] = add(acc[i, px, py], self.via[0, i, 0, 0])
            self.next.start()
            self.near.wait_recv()

            @pl.loop(0, NZ)
            def _(i):
                acc[i, x, y] = add(acc[i, x, y], self.via[1, i, 0, 0])
        elif phase == 3:
            self.next.wait_recv()

            @pl.loop(0, NZ)
            def _(i):
                acc[i, x, y] = add(acc[i, x, y], self.last[i, 0, 0])
            for copy in self.along_z:
                copy.start()

    def total(self):
        z, x, y, c = self.here
        for copy in self.along_z:
            copy.wait_recv()
        parts = [self.acc[z, x, y]] + [self.zs[k, 0, 0, 0] for k in range(3)]
        return sum(part.astype(F32) for part in parts)

    def drain(self):
        for copy in (self.swap, self.far, self.near, self.next, *self.along_z):
            copy.wait_send()


def scatter_bufs(n, width):
    return [
        pltpu.VMEM((n, NZ, 2, 2, CH, width), BF), pltpu.VMEM((n, 2, NZ, 1, 1, CH, width), BF),
        pltpu.VMEM((n, NZ, 1, 1, CH, width), BF), pltpu.VMEM((n, 3, 1, 1, 1, CH, width), BF),
    ]


def dma_sems(*counts):
    return [pltpu.SemaphoreType.DMA((k,)) for k in counts]


def fixed(shape):
    return pl.BlockSpec(shape, lambda s: (0,) * len(shape), pipeline_mode=pl.Buffered(1))


def vmem():
    return pl.BlockSpec(memory_space=pltpu.VMEM)


def hbm():
    return pl.BlockSpec(memory_space=pl.ANY)


N_ATT = 2 * (D // QW)
PACE = 5.4
FORWARD_LAG = (0.0, 10.0, 20.0, 27.0, 33.0)
FORWARD_FROM = 19.0
FORWARD_TICKS = [FORWARD_FROM + 2.9 * n for n in range(12)] + [FORWARD_FROM + 35.0 + 2.1 * n for n in range(16)]


def forward_kernel(
    kind_ref, x_ref, dm_ref, wqkv_ref, wout_ref, wup_ref, wdown_ref, *refs,
):
    small_refs = refs[:NV + 1]
    (
        h1t_ref, qkv_ref, p_ref, attn_ref, rl_ref, x1_ref, dmp_ref, h2t_ref, g_ref, slope_ref, gdown_ref,
        vec_ref, watt_out, wup_out, down_out,
        fa, fb, h1, h2, staged, swap, watt, wup, bqkv, bu, smalls,
        sems_s, sems_r, swap_s, swap_r, small_s, small_r, copy_sem,
    ) = refs[NV + 1:]
    step = pl.program_id(0)
    here = where_am_i()
    z, x, y, c = here
    peers = partners(*here)
    sems = (sems_s, sems_r)

    swaps = [
        remote(staged.at[:, half(i, 1 - c)], swap.at[:, i * HW:(i + 1) * HW], (swap_s, swap_r), i, peers[5])
        for i in range(N_WIDE)
    ]
    items, own = [], []
    for i in range(N_WIDE):
        buf, at = (watt, i) if i < 4 else (wup, i - 4)
        view = lambda zs, xs, ys, buf=buf, at=at: buf.at[zs, xs, ys, :, half(at, c)]
        items.append(Gather(here, sems, i * Gather.COPIES, view, None))
    for i in range(N_DOWN):
        rows, cols = down_rows(i, c), down_cols(i)
        view = lambda zs, xs, ys, rows=rows, cols=cols: down_out.at[zs, xs, ys, rows, cols]
        first = wdown_ref.at[:, :, :, pl.ds((i // 2) * CH, CH), cols]
        items.append(Gather(here, sems, (N_WIDE + i) * Gather.COPIES, view, first))
        own.append(pltpu.make_async_copy(first, view(one(z), one(x), one(y)), copy_sem.at[N_WIDE + i]))
    keeps = []
    for i in range(N_WIDE):
        src, dst, at = (watt, watt_out, i) if i < 4 else (wup, wup_out, i - 4)
        cols = pl.ds(at * D, D)
        keeps.append(pltpu.make_async_copy(
            src.at[:, :, :, :, cols], dst.at[:, :, :, :, cols], copy_sem.at[i]))

    def act(action):
        i, phase = action
        if i >= N_WIDE and phase == 0:
            own[i - N_WIDE].start()
        if i >= N_WIDE and phase == 1:
            own[i - N_WIDE].wait()
        items[i].start(phase)
        if phase == 4 and i < N_WIDE:
            keeps[i].start()

    needed = {1: 4, 2: 8, 3: 11, 4: 12, 5: 16, 6: 20, 7: 24}
    entries = []
    for i in range(1, N_WIDE + N_DOWN):
        for phase in range(5):
            due = PACE * i + FORWARD_LAG[phase]
            if i in needed:
                due = min(due, FORWARD_TICKS[needed[i]])
            entries.append((due, (i, phase)))
    early = [a for t, a in sorted(entries, key=lambda e: e[0]) if t < FORWARD_FROM]
    table, late = plan([e for e in entries if e[0] >= FORWARD_FROM], FORWARD_TICKS)

    def tick(slot, could_be):
        for n in could_be:
            if table[n]:
                @pl.when(slot == n)
                def _(n=n):
                    for action in table[n]:
                        act(action)

    @pl.when(step == 0)
    def _():
        say_hello(here)
        for pair in range(6):
            for n in range(3):
                at = pair * 384 + n * 128
                staged[:, at:at + 128] = wqkv_ref[:, n * D + pair * 128:n * D + (pair + 1) * 128].astype(F32)
        staged[:, OUT_AT:UP_AT] = wout_ref[...].astype(F32)
        staged[:, UP_AT:] = wup_ref[...].astype(F32)
        at = 0
        line = smalls.at[z, x, y, c]
        line[...] = jnp.zeros((8, SW), F32)
        for ref, width in zip(small_refs, VW):
            line[0:1, at:at + width] = ref[...].astype(F32).reshape(1, width)
            at += width
        await_all()
        swaps[0].start()

        def small_copy(n, src, to):
            return remote(src, src, (small_s, small_r), n, to)

        small_c = small_copy(0, smalls.at[one(z), one(x), one(y), one(c)], peers[5])
        both = smalls.at[one(z), one(x), one(y), TWO]
        small_z = [small_copy(1 + k, both, peers[k]) for k in range(3)]
        small_x = small_copy(4, smalls.at[EVERY, one(x), one(y), TWO], peers[3])
        small_y = small_copy(5, smalls.at[EVERY, TWO, one(y), TWO], peers[4])
        small_c.start()
        for i in range(1, N_WIDE):
            swaps[i].start()

        def take_block(i):
            swaps[i].wait_recv()
            mine_part = staged[:, half(i, c)]
            their_part = swap[:, i * HW:(i + 1) * HW]
            buf, at = (watt, i) if i < 4 else (wup, i - 4)
            lower = jnp.where(c == 0, mine_part, their_part)
            upper = jnp.where(c == 0, their_part, mine_part)
            buf[z, x, y, :, half(at, c)] = jnp.concatenate([lower, upper], 0).astype(BF)

        def take_row(row):
            for ref in (x1_ref, dmp_ref):
                ref[pl.ds(row * S + S - 16, 16), :] = jnp.zeros((16, D), ref.dtype)
            x1_ref[pl.ds(row * S, SEQ), :] = x_ref[:, row, :].astype(F32)

        waiting = list(early)

        def act_some(count):
            for _n in range(min(count, len(waiting))):
                act(waiting.pop(0))

        take_block(0)
        items[0].start(0)
        small_c.wait_recv()
        for copy in small_z:
            copy.start()
        for i in range(1, N_WIDE):
            take_block(i)
        take_row(0)
        for copy in small_z:
            copy.wait_recv()
        small_x.start()
        act_some(1)
        items[0].start(1)
        take_row(1)
        small_x.wait_recv()
        small_y.start()
        act_some(1)
        items[0].start(2)
        act_some(1)
        for row in range(2):
            dmp_ref[pl.ds(row * S, SEQ), :] = dm_ref[:, row, :]
        items[0].start(3)
        small_y.wait_recv()
        pieces = smalls[...].reshape(32, 8, SW)[:, 0, :].astype(BF)

        def joined(lead, size, width):
            src = lax.broadcasted_iota(jnp.int32, (SW, size), 0)
            dst = lax.broadcasted_iota(jnp.int32, (SW, size), 1)
            spread = jnp.where(src == lead + lax.rem(dst, width), 1.0, 0.0).astype(BF)
            dev = lax.broadcasted_iota(jnp.int32, (32, size), 0)
            col = lax.broadcasted_iota(jnp.int32, (32, size), 1)
            return jnp.sum(jnp.where(lax.div(col, width) == dev, mm(pieces, spread), 0.0), 0, keepdims=True)

        vectors = [joined(24 * i, D, 24) for i in range(NV)]
        for i in range(NV):
            vec_ref[i:i + 1, :] = vectors[i]
        for part in range(N_UP):
            src = lax.broadcasted_iota(jnp.int32, (SW, D), 0)
            dst = lax.broadcasted_iota(jnp.int32, (SW, D), 1)
            spread = jnp.where(src == 24 * NV + lax.rem(dst, 96), 1.0, 0.0).astype(BF)
            dev = lax.broadcasted_iota(jnp.int32, (32, D), 0)
            col = lax.broadcasted_iota(jnp.int32, (32, D), 1)
            found = jnp.where(lax.div(col, 96) + 8 * part == dev, mm(pieces, spread), 0.0)
            bu[part] = jnp.sum(found, 0, keepdims=True)
        for pair in range(6):
            n, at = pair // 2, (pair % 2) * 384
            bqkv[n, :, at:at + 128] = vectors[BQ][:, pair * 128:(pair + 1) * 128]
            bqkv[n, :, at + 128:at + 256] = jnp.zeros((1, 128), F32)
            bqkv[n, :, at + 256:at + 384] = vectors[BV][:, pair * 128:(pair + 1) * 128]
        act_some(2)

        @pl.loop(0, T // MB)
        def _(i):
            rows = rows_of(i)
            n1, _s = norm_parts(x1_ref[rows, :])
            h1[rows, :] = (n1 * vec_ref[G1:G1 + 1, :] + vec_ref[B1:B1 + 1, :]).astype(BF)
        for row in range(2):
            slot = lax.broadcasted_iota(jnp.int32, (S, 128), 0)
            lane = lax.broadcasted_iota(jnp.int32, (S, 128), 1)
            packed = jnp.where(slot < HALF, 0, jnp.where(slot < 2 * HALF, 1, 2))
            seg = jnp.where(kind_ref[row] == 1, packed, 0)
            fa[row] = jnp.where((lane < 3) & (seg == lane), -1e30, 0.0).astype(BF)
            fb[row] = jnp.where((lane < 3) & ((seg != lane) | (slot >= SEQ)), 1.0, 0.0).astype(BF)
        act_some(len(waiting))
        h1t_ref[...] = h1[...].T
        rl_ref[...] = jnp.zeros_like(rl_ref)
        act((0, 4))
        for copy in (small_c, *small_z, small_x, small_y, *swaps):
            copy.wait_send()

    @pl.when(step < N_ATT)
    def _():
        hq, r = lax.div(step, 2), lax.rem(step, 2)
        tick(2 * step, range(0, 12, 2))

        @pl.when(r == 0)
        def _():
            @pl.loop(0, T // MB)
            def _(i):
                rows = rows_of(i)
                w = watt[:, :, :, :, pl.ds(pl.multiple_of(hq * GW, 128), GW)].reshape(D, GW)
                qkv_ref[rows, :] = (mm(h1[rows, :], w) + bqkv[hq]).astype(BF)

        rows = pl.ds(pl.multiple_of(r * S, 16), S)
        feat_q, feat_k = fa[r], fb[r]
        ones = jnp.ones((S, 128), BF)
        scale = math.log2(math.e) / math.sqrt(HD)
        for j in range(HG // 2):
            if j:
                tick(2 * step + 1, range(1, 12, 2))
            at = j * 384
            qp, kp, vp = (qkv_ref[rows, at + 128 * n: at + 128 * (n + 1)] for n in range(3))
            kcat = jnp.concatenate([kp, feat_k], 1)
            total = None
            for e in range(2):
                keep = head_lanes((S, 128), e)
                qcat = jnp.concatenate([jnp.where(keep, qp, jnp.zeros_like(qp)), feat_q], 1)
                s = mm(qcat, kcat, NT)
                m = jnp.max(s, -1, keepdims=True)
                pb = jnp.exp2((s - m) * scale).astype(BF)
                p_ref[0, 2 * j + e] = pb
                vcat = jnp.concatenate([jnp.where(keep, vp, jnp.zeros_like(vp)), ones], 1)
                o = mm(pb, vcat)
                rl = 1.0 / o[:, 128:]
                part = o[:, :128] * rl
                total = part if total is None else total + part
                spot = lax.broadcasted_iota(jnp.int32, (S, 128), 1) == hq * HG + 2 * j + e
                rl_ref[rows, :] = jnp.where(spot, rl, rl_ref[rows, :])
            out = pl.ds(pl.multiple_of(hq * QW + j * 128, 128), 128)
            attn_ref[rows, out] = total.astype(BF)

    @pl.when(step == N_ATT - 1)
    def _():
        @pl.loop(0, T // MB)
        def _(i):
            rows = rows_of(i)
            wo = watt[:, :, :, :, OUT_AT:UP_AT].reshape(D, D)
            x1 = x1_ref[rows, :] + mm(attn_ref[rows, :], wo) + vec_ref[BO:BO + 1, :]
            x1_ref[rows, :] = x1
            n2, _s = norm_parts(x1)
            h2[rows, :] = (n2 * vec_ref[G2:G2 + 1, :] + vec_ref[B2:B2 + 1, :]).astype(BF)
        h2t_ref[...] = h2[...].T

    @pl.when(step >= N_ATT)
    def _():
        part = step - N_ATT

        @pl.loop(0, T // MB)
        def _(i):
            tick(12 + 4 * part + i, range(12, len(FORWARD_TICKS)))
            rows = rows_of(i)
            w = wup[:, :, :, :, pl.ds(pl.multiple_of(part * D, 128), D)].reshape(D, D)
            g, slope = gelu_both(mm(h2[rows, :], w) + bu[part])
            g_ref[rows, :] = g.astype(BF)
            slope_ref[rows, :] = slope.astype(BF)

        for t in range(D // 256):
            cols = pl.ds(t * 256, 256)
            gdown_ref[cols, :] = mm(g_ref[:, cols], dmp_ref[...], TN).astype(BF)

    @pl.when(step == N_ATT + N_UP - 1)
    def _():
        for action in late:
            act(action)
        for item in items:
            item.drain()
        for copy in keeps:
            copy.wait()


def forward(kind, x, dm, wqkv, wout, wup, wdown, smalls):
    n = N_WIDE + N_DOWN
    att = lambda s: jnp.minimum(s, N_ATT - 1)
    ff = lambda s: jnp.maximum(s - N_ATT, 0)
    shape = jax.ShapeDtypeStruct
    return pl.pallas_call(
        forward_kernel,
        grid=(N_ATT + N_UP,),
        in_specs=[
            pl.BlockSpec(memory_space=pltpu.SMEM), fixed((SEQ, 2, D)), fixed((SEQ, 2, D)),
            fixed((24, 3 * D)), fixed((24, D)), fixed((24, FF)), fixed((1, 1, 1, 96, D)),
            *[pl.BlockSpec((w,), lambda s: (0,), pipeline_mode=pl.Buffered(1)) for w in VW],
        ],
        out_specs=[
            fixed((D, T)), pl.BlockSpec((T, GW), lambda s: (0, att(s) // 2)),
            pl.BlockSpec((1, HG, S, S), lambda s: (att(s) % 2, att(s) // 2, 0, 0)),
            fixed((T, D)), fixed((T, 128)), fixed((T, D)), fixed((T, D)), fixed((D, T)),
            pl.BlockSpec((T, D), lambda s: (0, ff(s))), pl.BlockSpec((T, D), lambda s: (0, ff(s))),
            pl.BlockSpec((D, D), lambda s: (ff(s), 0)),
            fixed((NV, D)), hbm(), hbm(), hbm(),
        ],
        out_shape=[
            shape((D, T), BF), shape((T, 3 * D), BF), shape((2, D // HD, S, S), BF),
            shape((T, D), BF), shape((T, 128), F32), shape((T, D), F32), shape((T, D), BF), shape((D, T), BF),
            shape((T, FF), BF), shape((T, FF), BF), shape((FF, D), BF), shape((NV, D), F32),
            shape((NZ, 2, 2, CH, UP_AT), BF), shape((NZ, 2, 2, CH, FF), BF), shape((NZ, 2, 2, 4 * CH, D), BF),
        ],
        scratch_shapes=[
            pltpu.VMEM((2, S, 128), BF), pltpu.VMEM((2, S, 128), BF), pltpu.VMEM((T, D), BF), pltpu.VMEM((T, D), BF),
            pltpu.VMEM((24, AW), F32), pltpu.VMEM((24, AW // 2), F32),
            pltpu.VMEM((NZ, 2, 2, CH, UP_AT), BF), pltpu.VMEM((NZ, 2, 2, CH, FF), BF),
            pltpu.VMEM((3, 1, GW), F32), pltpu.VMEM((N_UP, 1, D), F32), pltpu.VMEM((NZ, 2, 2, 2, 8, SW), F32),
            *dma_sems(n * Gather.COPIES, n * Gather.COPIES, N_WIDE, N_WIDE, 6, 6, n),
        ],
        compiler_params=pltpu.CompilerParams(collective_id=0, has_side_effects=True, vmem_limit_bytes=LIMIT),
        name="forward",
    )(kind, x, dm, wqkv, wout, wup, wdown.reshape(1, 1, 1, 96, D), *smalls)


BACK_LAG = (0.0, 5.0, 15.0, 23.0, 32.0)
FFN_TICKS = [1.0 + 1.45 * n for n in range(28)]


def ffn_back_kernel(
    x1_ref, dm_ref, g_ref, slope_ref, wu_ref, wd_ref, h2t_ref, vec_ref, gdown_ref,
    y_ref, dx1_ref, gup_ref, sums_ref, odown_ref,
    yacc, dacc, dus, mine, acc, via, last, zs, sems_s, sems_r, own_sem,
):
    step = pl.program_id(0)
    here = where_am_i()
    z, x, y, c = here
    items, own = [], []
    for i in range(N_DOWN):
        rows, cols = down_rows(i, c), down_cols(i)
        own.append(pltpu.make_async_copy(gdown_ref.at[:, :, :, rows, cols], mine.at[i], own_sem.at[i]))
        items.append(Scatter(
            here, (sems_s, sems_r), i * Scatter.COPIES, gdown_ref.at[EVERY, TWO, TWO, down_rows(i, 1 - c), cols],
            lambda a, b, d, i=i: mine[i, a, b, d], acc.at[i], via.at[i], last.at[i], zs.at[i],
        ))
    entries = [
        (PACE * i + lag, (i, phase)) for i in range(N_DOWN) for phase, lag in enumerate(BACK_LAG) if (i, phase) != (0, 0)
    ]
    table, late = plan(entries, FFN_TICKS)

    def act(action):
        i, phase = action
        if phase == 1:
            own[i].wait()
        if phase == 4:
            odown_ref[pl.ds((i // 2) * CH, CH), down_cols(i)] = items[i].total()
        else:
            items[i].start(phase)

    def tick(slot):
        for n, todo in table.items():
            if todo:
                @pl.when(slot == n)
                def _(todo=todo):
                    for action in todo:
                        act(action)

    @pl.when(step == 0)
    def _():
        say_hello(here)
        for copy in own:
            copy.start()

        @pl.loop(0, T // MB)
        def _(i):
            rows = rows_of(i)
            yacc[rows, :] = x1_ref[rows, :] + vec_ref[BD:BD + 1, :]
            dacc[rows, :] = jnp.zeros((MB, D), F32)
        sums_ref[...] = jnp.zeros_like(sums_ref)
        sums_ref[2:3, :] = jnp.sum(dm_ref[...].astype(F32), 0, keepdims=True)
        await_all()
        act((0, 0))

    @pl.loop(0, T // MB)
    def _(i):
        tick(7 * step + i)
        rows = rows_of(i)
        g = g_ref[rows, :]
        yacc[rows, :] += mm(g, wd_ref[...])
        du = (mm(dm_ref[rows, :], wd_ref[...], NT) * slope_ref[rows, :].astype(F32)).astype(BF)
        dus[rows, :] = du
        sums_ref[pl.ds(3 + step, 1), :] += jnp.sum(du.astype(F32), 0, keepdims=True)
        dacc[rows, :] += mm(du, wu_ref[...], NT)

    @pl.loop(0, D // 256)
    def _(t):
        tick(7 * step + 4 + t)
        rows = pl.ds(pl.multiple_of(t * 256, 256), 256)
        gup_ref[rows, :] = mm(h2t_ref[rows, :], dus[...]).astype(BF)

    @pl.when(step == N_UP - 1)
    def _():
        @pl.loop(0, T // MB)
        def _(i):
            rows = rows_of(i)
            n2, s2 = norm_parts(x1_ref[rows, :])
            dh = dacc[rows, :]
            sums_ref[0:1, :] += jnp.sum(dh * n2, 0, keepdims=True)
            sums_ref[1:2, :] += jnp.sum(dh, 0, keepdims=True)
            dx1_ref[rows, :] = dm_ref[rows, :].astype(F32) + norm_pull(dh, n2, s2, vec_ref[G2:G2 + 1, :])
            y_ref[rows, :] = yacc[rows, :].astype(BF)
        for action in late:
            act(action)
        for item in items:
            item.drain()


def ffn_back(x1, dm, g, slope, wup, down, h2t, vec, gdown):
    shape = jax.ShapeDtypeStruct
    col = pl.BlockSpec((T, D), lambda s: (0, s))
    return pl.pallas_call(
        ffn_back_kernel,
        grid=(N_UP,),
        in_specs=[
            fixed((T, D)), fixed((T, D)), col, col,
            pl.BlockSpec((D, D), lambda s: (0, s)), pl.BlockSpec((D, D), lambda s: (s, 0)),
            fixed((D, T)), fixed((NV, D)), hbm(),
        ],
        out_specs=[
            fixed((T, D)), fixed((T, D)), pl.BlockSpec((D, D), lambda s: (0, s)), fixed((8, D)), fixed((96, D)),
        ],
        out_shape=[
            shape((T, D), BF), shape((T, D), F32), shape((D, FF), BF), shape((8, D), F32), shape((96, D), F32),
        ],
        scratch_shapes=[
            pltpu.VMEM((T, D), F32), pltpu.VMEM((T, D), F32), pltpu.VMEM((T, D), BF),
            pltpu.VMEM((N_DOWN, NZ, 2, 2, CH, HW), BF), *scatter_bufs(N_DOWN, HW),
            *dma_sems(N_DOWN * 7, N_DOWN * 7, N_DOWN),
        ],
        compiler_params=pltpu.CompilerParams(collective_id=1, has_side_effects=True, vmem_limit_bytes=LIMIT),
        name="feed_forward_back",
    )(x1, dm, g, slope, wup, down, h2t, vec, gdown.reshape(NZ, 2, 2, 4 * CH, D))


BACK_TICKS = [2.0 + 4.8 * n for n in range(12)]
N_BACK = N_UP + 4


def attn_back_kernel(
    x_ref, yb_ref, dx1_ref, h1t_ref, qkv_ref, p_ref, attn_ref, rl_ref, wo_ref, wqkv_ref, vec_ref, sums_ref, gup_ref,
    out_ref, gx_ref, oqkv_ref, oout_ref, oup_ref, *refs,
):
    small_outs = refs[:NV + 1]
    (
        da, dos, dqkv, dh1, gqkv, gout, mine, acc, via, last, zs, done, landed, small,
        sems_s, sems_r, fin_s, fin_r, small_s, small_r, own_sem,
    ) = refs[NV + 1:]
    step = pl.program_id(0)
    hq, r = lax.div(step, 2), lax.rem(step, 2)
    here = where_am_i()
    z, x, y, c = here
    peers = partners(*here)
    items, own = [], []
    for n in range(N_BACK):
        if n < N_UP:
            theirs = gup_ref.at[EVERY, TWO, TWO, :, half(n, 1 - c)]
            own.append(pltpu.make_async_copy(gup_ref.at[:, :, :, :, half(n, c)], mine.at[n], own_sem.at[n]))
            get = lambda a, b, d, n=n: mine[n, a, b, d]
        elif n == N_UP:
            theirs = gout.at[EVERY, TWO, TWO, :, half(0, 1 - c)]
            get = lambda a, b, d: gout[a, b, d, :, half(0, c)]
        else:
            i = n - N_UP - 1
            theirs = gqkv.at[i, EVERY, TWO, TWO, :, half(0, 1 - c)]
            get = lambda a, b, d, i=i: gqkv[i, a, b, d, :, half(0, c)]
        items.append(Scatter(
            here, (sems_s, sems_r), n * Scatter.COPIES, theirs, get, acc.at[n], via.at[n], last.at[n], zs.at[n]))

    def final(n):
        theirs = pl.ds(pl.multiple_of((1 - c) * 24, 8), 24)
        return remote(done.at[n, theirs], landed.at[n], (fin_s, fin_r), n, peers[5])

    def put(n, core, value):
        if n > N_UP:
            for b in range(3):
                cols = pl.ds(pl.multiple_of(b * D + (n - N_UP - 1) * QW + core * 128, 128), 128)
                oqkv_ref[:, cols] = value[:, b * 128:(b + 1) * 128]
        elif n == N_UP:
            oout_ref[:, half(0, core)] = value
        else:
            oup_ref[:, half(n, core)] = value

    def finish(n):
        done[n] = items[n].total()
        final(n).start()
        put(n, c, done[n, pl.ds(pl.multiple_of(c * 24, 8), 24)])

    def act(action):
        n, phase = action
        if n < N_UP and phase == 1:
            own[n].wait()
        if phase == 4:
            finish(n)
        else:
            items[n].start(phase)

    entries = []
    begin = 0.0
    for n in range(N_BACK):
        if n > N_UP:
            begin = max(begin, BACK_TICKS[0] + 19.2 * (n - N_UP))
        for phase in range(5):
            if n < N_UP or phase > 0:
                entries.append((begin + BACK_LAG[phase], (n, phase)))
        begin += PACE
    entries.remove((0.0, (0, 0)))
    table, tail = plan(entries, BACK_TICKS)

    def tick(slot, could_be):
        for n in could_be:
            if table[n]:
                @pl.when(slot == n)
                def _(n=n):
                    for action in table[n]:
                        act(action)

    @pl.when(step == 0)
    def _():
        say_hello(here)
        for copy in own:
            copy.start()
        small[0] = jnp.zeros((16, D), F32)
        await_all()
        act((0, 0))
        src = lax.broadcasted_iota(jnp.int32, (128, D), 0)
        dst = lax.broadcasted_iota(jnp.int32, (128, D), 1)
        spread = jnp.where(lax.div(dst, HD) == src, 1.0, 0.0)

        @pl.loop(0, T // MB)
        def _(i):
            rows = rows_of(i)
            d = dx1_ref[rows, :].astype(BF)
            da[rows, :] = d
            rl = lax.dot_general(
                rl_ref[rows, :], spread, NN, precision=lax.Precision.HIGHEST, preferred_element_type=F32)
            small[0, 4:5, :] += jnp.sum(d.astype(F32), 0, keepdims=True)
            dos[rows, :] = (mm(d, wo_ref[...], NT) * rl).astype(BF)
            dh1[rows, :] = jnp.zeros((MB, D), F32)
        for t in range(D // 192):
            cols = pl.ds(t * 192, 192)
            part = mm(attn_ref[:, t * 192:(t + 1) * 192], da[...], TN)
            gout[t] = part.astype(BF).reshape(2, 2, CH, D)
        items[N_UP].start(0)

    tick(2 * step, range(0, 12, 2))
    rows = pl.ds(pl.multiple_of(r * S, 16), S)
    scale = 1.0 / math.sqrt(HD)
    for j in range(HG // 2):
        if j:
            tick(2 * step + 1, range(1, 12, 2))
        at = j * 384
        qp, kp, vp = (qkv_ref[rows, at + 128 * n: at + 128 * (n + 1)] for n in range(3))
        lanes = pl.ds(pl.multiple_of(hq * QW + j * 128, 128), 128)
        do = dos[rows, lanes]
        prod = do.astype(F32) * attn_ref[rows, lanes].astype(F32)
        dq = dk = dv = None
        for e in range(2):
            keep = head_lanes((S, 128), e)
            zero = jnp.zeros_like(qp)
            doe = jnp.where(keep, do, zero)
            dot = jnp.sum(jnp.where(keep, prod, 0.0), -1, keepdims=True)
            p = p_ref[0, 2 * j + e]
            ds = (p.astype(F32) * (mm(doe, vp, NT) - dot)).astype(BF)
            a_, b_, c_ = mm(ds, jnp.where(keep, kp, zero)), mm(ds, jnp.where(keep, qp, zero), TN), mm(p, doe, TN)
            dq, dk, dv = (a_, b_, c_) if dq is None else (dq + a_, dk + b_, dv + c_)
        for n, part in enumerate((dq * scale, dk * scale, dv)):
            dqkv[rows, at + 128 * n:at + 128 * (n + 1)] = part.astype(BF)

    @pl.when(r == 1)
    def _():
        sums = jnp.sum(dqkv[...].astype(F32), 0, keepdims=True)
        for j in range(2):
            cols = pl.ds(pl.multiple_of(hq * QW + j * 128, 128), 128)
            small[0, 2:3, cols] = sums[:, j * 384:j * 384 + 128]
            small[0, 3:4, cols] = sums[:, j * 384 + 256:j * 384 + 384]
        for t in range(D // 192):
            part = mm(h1t_ref[t * 192:(t + 1) * 192, :], dqkv[...])
            gqkv[hq, t] = part.astype(BF).reshape(2, 2, CH, GW)
        for i in range(3):
            @pl.when(hq == i)
            def _(i=i):
                items[N_UP + 1 + i].start(0)

        @pl.loop(0, T // MB)
        def _(i):
            rr = rows_of(i)
            dh1[rr, :] += mm(dqkv[rr, :], wqkv_ref[...], NT)

    @pl.when(step == N_ATT - 1)
    def _():
        rest = list(tail)
        act(rest.pop(0))

        def norm_row(row):
            rr = pl.ds(row * S, SEQ)
            dh = dh1[rr, :]
            n1, s1 = norm_parts(x_ref[:, row, :].astype(F32))
            small[0, 0:1, :] += jnp.sum(dh * n1, 0, keepdims=True)
            small[0, 1:2, :] += jnp.sum(dh, 0, keepdims=True)
            gx_ref[:, row, :] = (dx1_ref[rr, :] + norm_pull(dh, n1, s1, vec_ref[G1:G1 + 1, :])).astype(BF)

        norm_row(0)
        norm_row(1)
        small[0, 5:12, :] = sums_ref[0:7, :]
        copies = []

        def send_small(n, src, dst, to):
            copy = remote(small.at[src], small.at[dst], (small_s, small_r), n, to)
            copy.start()
            copies.append(copy)

        send_small(0, 0, 1, peers[5])
        hops = [(1, 2, 3, peers[3]), (2, 4, 5, peers[4])]
        level = 0
        while rest or level < 4:
            if rest:
                act(rest.pop(0))
            if level == 0:
                for row in range(2):
                    out_ref[:, row, :] = yb_ref[pl.ds(row * S, SEQ), :]
            if level < 2:
                copies[level].wait_recv()
                small[2 * level + 2] = small[2 * level] + small[2 * level + 1]
                send_small(*hops[level])
            elif level == 2:
                copies[2].wait_recv()
                small[6] = small[4] + small[5]
                for k in range(3):
                    send_small(3 + k, 6, 7 + k, peers[k])
            elif level == 3:
                for k in range(3):
                    copies[3 + k].wait_recv()
                total = small[6] + small[7] + small[8] + small[9]
                me = lax.axis_index("dp") * lax.axis_size("fsdp") + lax.axis_index("fsdp")
                src = lax.broadcasted_iota(jnp.int32, (D, 128), 0)
                dst = lax.broadcasted_iota(jnp.int32, (D, 128), 1)

                def pick(lines, width, at):
                    chosen = jnp.where((src == at + dst) & (dst < width), 1.0, 0.0)
                    return lax.dot_general(
                        lines, chosen, NN, precision=lax.Precision.HIGHEST, preferred_element_type=F32)

                mine_of = pick(total[:8], 24, me * 24)
                for n in range(NV):
                    small_outs[n][...] = mine_of[n, :24]
                row = lax.broadcasted_iota(jnp.int32, (8, D), 0)
                longest = jnp.sum(jnp.where(row == lax.div(me, 8), total[8:16], 0.0), 0, keepdims=True)
                small_outs[NV][...] = pick(jnp.broadcast_to(longest, (8, D)), 96, lax.rem(me, 8) * 96)[0, :96]
            level += 1
        for n in range(N_BACK):
            copy = final(n)
            copy.wait_recv()
            put(n, 1 - c, landed[n])
            copy.wait_send()
            items[n].drain()
        for copy in copies:
            copy.wait_send()


def attn_back(x, yb, dx1, h1t, qkv, p, attn, rl, watt, vec, sums, gup):
    shape = jax.ShapeDtypeStruct
    n_fin = N_BACK
    return pl.pallas_call(
        attn_back_kernel,
        grid=(N_ATT,),
        in_specs=[
            fixed((SEQ, 2, D)), fixed((T, D)), fixed((T, D)), fixed((D, T)), pl.BlockSpec((T, GW), lambda s: (0, s // 2)),
            pl.BlockSpec((1, HG, S, S), lambda s: (s % 2, s // 2, 0, 0)), fixed((T, D)), fixed((T, 128)),
            pl.BlockSpec((D, D), lambda s: (0, 3), pipeline_mode=pl.Buffered(1)),
            pl.BlockSpec((D, GW), lambda s: (0, s // 2)), fixed((NV, D)), fixed((8, D)), hbm(),
        ],
        out_specs=[
            fixed((SEQ, 2, D)), fixed((SEQ, 2, D)), fixed((24, 3 * D)), fixed((24, D)), fixed((24, FF)),
            *[pl.BlockSpec((w,), lambda s: (0,), pipeline_mode=pl.Buffered(1)) for w in VW],
        ],
        out_shape=[
            shape((SEQ, 2, D), BF), shape((SEQ, 2, D), BF), shape((24, 3 * D), F32), shape((24, D), F32),
            shape((24, FF), F32), *[shape((w,), F32) for w in VW],
        ],
        scratch_shapes=[
            pltpu.VMEM((T, D), BF), pltpu.VMEM((T, D), BF), pltpu.VMEM((T, GW), BF), pltpu.VMEM((T, D), F32),
            pltpu.VMEM((3, NZ, 2, 2, CH, GW), BF), pltpu.VMEM((NZ, 2, 2, CH, D), BF),
            pltpu.VMEM((N_UP, NZ, 2, 2, CH, HW), BF), *scatter_bufs(N_BACK, HW),
            pltpu.VMEM((N_BACK, CH, HW), F32), pltpu.VMEM((N_BACK, 24, HW), F32), pltpu.VMEM((10, 16, D), F32),
            *dma_sems(N_BACK * 7, N_BACK * 7, n_fin, n_fin, 6, 6, N_UP),
        ],
        compiler_params=pltpu.CompilerParams(collective_id=2, has_side_effects=True, vmem_limit_bytes=LIMIT),
        name="attention_back",
    )(x, yb, dx1, h1t, qkv, p, attn, rl, watt, watt, vec, sums, gup.reshape(NZ, 2, 2, CH, FF))


def hand_over_kernel(*refs):
    n = len(refs) // 2
    for i in range(n):
        refs[n + i][...] = refs[i][...]


def hand_over(values):
    return pl.pallas_call(
        hand_over_kernel,
        in_specs=[vmem()] * len(values),
        out_specs=[vmem()] * len(values),
        out_shape=[jax.ShapeDtypeStruct(v.shape, v.dtype) for v in values],
        compiler_params=pltpu.CompilerParams(vmem_limit_bytes=LIMIT),
        name="results",
    )(*values)


def by_pair(v):
    return v.reshape(v.shape[0], 3, 6, 128).transpose(0, 2, 1, 3).reshape(v.shape[0], 3 * D)


def by_kind(v):
    return v.reshape(v.shape[0], 6, 3, 128).transpose(0, 2, 1, 3).reshape(v.shape[0], 3 * D)


def with_own_copies(inputs, row_kind, w_qkv, w_out, w_up, w_down, vectors, b_up, out_grad):
    x, dm = inputs.transpose(1, 0, 2), out_grad.transpose(1, 0, 2)
    h1t, qkv, p, attn, rl, x1, dmp, h2t, g, slope, gdown, vec, watt, wup, down = forward(
        row_kind, x, dm, w_qkv, w_out, w_up, w_down, (*vectors, b_up))
    yb, dx1, gup, sums, gdown = ffn_back(
        x1, dmp, g, slope, wup.reshape(D, FF), down.reshape(FF, D), h2t, vec, gdown)
    results = attn_back(x, yb, dx1, h1t, qkv, p, attn, rl, watt.reshape(D, UP_AT), vec, sums, gup)
    out, gx, gqkv, gout, gup, gdown, *small = hand_over((*results[:5], gdown, *results[5:]))
    return out.transpose(1, 0, 2), gx.transpose(1, 0, 2), gqkv, gout, gup, gdown, small[:NV], small[NV]


def with_collectives(inputs, row_kind, w_qkv, w_out, w_up, w_down, vectors, b_up, out_grad):
    axes = ("dp", "fsdp")
    get = lambda v: lax.all_gather(v, axes, axis=0, tiled=True)
    wide = jnp.concatenate([by_pair(get(w_qkv)), get(w_out), get(w_up)], 1)
    down = get(w_down)
    full = [get(v).astype(F32) for v in vectors]
    vec = jnp.stack(full)
    bu = get(b_up).astype(F32)[None]
    bqkv = by_pair(jnp.concatenate([full[BQ], jnp.zeros_like(full[BQ]), full[BV]])[None])
    h1, qkv, p, attn, rl, x1 = attn_fwd(row_kind, inputs, wide, bqkv, vec)
    outputs, dx1, gup, gdown, gbu, gg2, gb2, gbd = ffn(x1, out_grad, wide, down, bu, vec)
    input_grad, gqkv, gout, gbqkv, gbo, gg1, gb1 = attn_bwd(inputs, dx1, h1, qkv, p, attn, rl, wide, vec)
    gbqkv = by_kind(gbqkv)
    small = [gg1, gb1, gbqkv[:, :D], gbqkv[:, 2 * D:], gbo, gg2, gb2, gbd]
    give = lambda v: lax.psum_scatter(v.astype(F32), axes, scatter_dimension=0, tiled=True)
    return (
        outputs, input_grad, give(by_kind(gqkv)), give(gout), give(gup), give(gdown),
        [give(v[0]) for v in small], give(gbu[0]),
    )


def on_device(
    copies, inputs, row_kind, ln1_gain, ln1_bias, w_qkv, b_query, b_value, w_out, b_out, ln2_gain, ln2_bias,
    w_up, b_up, w_down, b_down, out_grad,
):
    vectors = (ln1_gain, ln1_bias, b_query, b_value, b_out, ln2_gain, ln2_bias, b_down)
    run = with_own_copies if copies else with_collectives
    outputs, input_grad, gqkv, gout, gup, gdown, small, gbu = run(
        inputs, row_kind, w_qkv, w_out, w_up, w_down, vectors, b_up, out_grad)
    gg1, gb1, gbq, gbv, gbo, gg2, gb2, gbd = small
    return outputs, input_grad, gg1, gb1, gqkv, gbq, gbv, gout, gbo, gg2, gb2, gup, gbu, gdown, gbd


def solution(mesh):
    both = ("dp", "fsdp")
    row = P(both)
    mat = P(both, None)
    act = P(both, None, None)
    in_specs = (act, row, row, row, mat, row, row, mat, row, row, row, mat, row, mat, row, act)
    out_specs = (act, act, row, row, mat, row, row, mat, row, row, row, mat, row, mat, row)
    copies = mesh.shape["dp"] == 2 * NZ and mesh.shape["fsdp"] == 4
    return jax.shard_map(
        functools.partial(on_device, copies), mesh=mesh, in_specs=in_specs, out_specs=out_specs, check_vma=False
    )
```

```python
import functools
import math

import jax
import jax.numpy as jnp
from jax import lax
from jax.experimental import pallas as pl
from jax.experimental.pallas import tpu as pltpu
from jax.sharding import PartitionSpec as P

D = 768
HD = 64
FF = 3072
SEQ = 529
HALF = 264
EPS = 1e-06
S = 544
T = 2 * S
MB = 272
HG = 4
QW = HG * HD
GW = 3 * QW
FC = 512
OUT_AT = 3 * D
UP_AT = 4 * D
AW = 4 * D + FF
F32 = jnp.float32
BF = jnp.bfloat16
LIMIT = 62 * 2**20
MESH = pl.DeviceIdType.MESH
NN = (((1,), (0,)), ((), ()))
NT = (((1,), (1,)), ((), ()))
TN = (((0,), (0,)), ((), ()))


def mm(a, b, dims=NN):
    return lax.dot_general(a, b, dims, preferred_element_type=F32)


def norm_parts(values):
    mean = jnp.mean(values, -1, keepdims=True)
    centred = values - mean
    inverse = lax.rsqrt(jnp.mean(centred * centred, -1, keepdims=True) + EPS)
    return centred * inverse, inverse


def norm_pull(grad, normed, inverse, gain):
    scaled = grad * gain
    return inverse * (
        scaled
        - jnp.mean(scaled, -1, keepdims=True)
        - normed * jnp.mean(scaled * normed, -1, keepdims=True)
    )


def gelu_both(u):
    a = jnp.abs(u)
    t = 1.0 / (1.0 + (0.3275911 / math.sqrt(2.0)) * a)
    e = jnp.exp(-0.5 * u * u)
    poly = t * (
        0.254829592
        + t * (-0.284496736 + t * (1.421413741 + t * (-1.453152027 + t * 1.061405429)))
    )
    tail = 0.5 * poly * e
    phi = jnp.where(u < 0, tail, 1.0 - tail)
    return u * phi, phi + u * e * (1.0 / math.sqrt(2.0 * math.pi))


def head_lanes(shape, e):
    lane = lax.broadcasted_iota(jnp.int32, shape, 1)
    return (lane // HD) == e


def whole(shape):
    return pl.BlockSpec(shape, lambda *_: (0,) * len(shape))


def rows_of(i):
    return pl.ds(pl.multiple_of(i * MB, 16), MB)


def row_of(i):
    return pl.ds(pl.multiple_of(i * S, 16), S)


G1, B1, BQ, BV, BO, G2, B2, BD = range(8)


def attn_fwd_kernel(
    kind_ref, x_ref, wg_ref, bqkv_ref, wo_ref, vec_ref,
    h1_ref, qkv_ref, p_ref, attn_ref, rl_ref, x1_ref, fa, fb,
):
    hq, r = pl.program_id(0), pl.program_id(1)

    @pl.when((hq == 0) & (r == 0))
    def _():
        for row in range(2):
            h1_ref[pl.ds(row * S + S - 16, 16), :] = jnp.zeros((16, D), BF)
            n1, _s = norm_parts(x_ref[row].astype(F32))
            h1_ref[pl.ds(row * S, SEQ), :] = (n1 * vec_ref[G1:G1 + 1, :] + vec_ref[B1:B1 + 1, :]).astype(BF)
            slot = lax.broadcasted_iota(jnp.int32, (S, 128), 0)
            lane = lax.broadcasted_iota(jnp.int32, (S, 128), 1)
            packed = jnp.where(slot < HALF, 0, jnp.where(slot < 2 * HALF, 1, 2))
            seg = jnp.where(kind_ref[row] == 1, packed, 0)
            fa[row] = jnp.where((lane < 3) & (seg == lane), -1e30, 0.0).astype(BF)
            fb[row] = jnp.where((lane < 3) & ((seg != lane) | (slot >= SEQ)), 1.0, 0.0).astype(BF)

    @pl.when(r == 0)
    def _():
        @pl.loop(0, T // MB)
        def _(i):
            rows = rows_of(i)
            qkv_ref[rows, :] = (mm(h1_ref[rows, :], wg_ref[...]) + bqkv_ref[...]).astype(BF)

    rows = pl.ds(pl.multiple_of(r * S, 16), S)
    feat_q, feat_k = fa[r], fb[r]
    ones = jnp.ones((S, 128), BF)
    scale = math.log2(math.e) / math.sqrt(HD)
    for j in range(HG // 2):
        at = j * 384
        qp, kp, vp = (qkv_ref[rows, at + 128 * n: at + 128 * (n + 1)] for n in range(3))
        kcat = jnp.concatenate([kp, feat_k], 1)
        total = None
        inv = None
        for e in range(2):
            keep = head_lanes((S, 128), e)
            qcat = jnp.concatenate([jnp.where(keep, qp, jnp.zeros_like(qp)), feat_q], 1)
            s = mm(qcat, kcat, NT)
            m = jnp.max(s, -1, keepdims=True)
            pb = jnp.exp2((s - m) * scale).astype(BF)
            p_ref[0, 2 * j + e] = pb
            vcat = jnp.concatenate([jnp.where(keep, vp, jnp.zeros_like(vp)), ones], 1)
            o = mm(pb, vcat)
            rl = 1.0 / o[:, 128:]
            part = o[:, :128] * rl
            total = part if total is None else total + part
            inv = rl if inv is None else jnp.where(keep, rl, inv)
        out = pl.ds(pl.multiple_of(hq * QW + j * 128, 128), 128)
        attn_ref[rows, out] = total.astype(BF)
        rl_ref[rows, out] = inv

    @pl.when((hq == D // QW - 1) & (r == 1))
    def _():
        for row in range(2):
            x1_ref[pl.ds(row * S + S - 16, 16), :] = jnp.zeros((16, D), F32)
            x1_ref[pl.ds(row * S, SEQ), :] = x_ref[row].astype(F32)

        @pl.loop(0, T // MB)
        def _(i):
            rr = rows_of(i)
            x1_ref[rr, :] = x1_ref[rr, :] + mm(attn_ref[rr, :], wo_ref[...]) + vec_ref[BO:BO + 1, :]


def attn_fwd(kind, x, wide, bqkv, vec):
    return pl.pallas_call(
        attn_fwd_kernel,
        grid=(D // QW, 2),
        in_specs=[
            pl.BlockSpec(memory_space=pltpu.SMEM), whole((2, SEQ, D)),
            pl.BlockSpec((D, GW), lambda h, r: (0, h)), pl.BlockSpec((1, GW), lambda h, r: (0, h)),
            pl.BlockSpec((D, D), lambda h, r: (0, 3)), whole((8, D)),
        ],
        out_specs=[
            whole((T, D)), pl.BlockSpec((T, GW), lambda h, r: (0, h)),
            pl.BlockSpec((1, HG, S, S), lambda h, r: (r, h, 0, 0)),
            whole((T, D)), whole((T, D)), whole((T, D)),
        ],
        out_shape=[
            jax.ShapeDtypeStruct((T, D), BF), jax.ShapeDtypeStruct((T, 3 * D), BF),
            jax.ShapeDtypeStruct((2, D // HD, S, S), BF),
            jax.ShapeDtypeStruct((T, D), BF), jax.ShapeDtypeStruct((T, D), F32), jax.ShapeDtypeStruct((T, D), F32),
        ],
        scratch_shapes=[pltpu.VMEM((2, S, 128), BF), pltpu.VMEM((2, S, 128), BF)],
        compiler_params=pltpu.CompilerParams(vmem_limit_bytes=LIMIT),
        name="attention_forward",
    )(kind, x, wide, bqkv, wide, vec)


def ffn_kernel(
    x1_ref, dm_ref, wu_ref, wd_ref, bu_ref, vec_ref,
    out_ref, dx1_ref, gwu_ref, gwd_ref, gbu_ref, gg2_ref, gb2_ref, gbd_ref,
    h2, h2t, dm, yacc, dacc, gs, dus,
):
    c = pl.program_id(0)

    @pl.when(c == 0)
    def _():
        for row in range(2):
            dm[pl.ds(row * S + S - 16, 16), :] = jnp.zeros((16, D), BF)
            dm[pl.ds(row * S, SEQ), :] = dm_ref[row]

        @pl.loop(0, T // MB)
        def _(i):
            rows = rows_of(i)
            x1 = x1_ref[rows, :]
            n2, _s = norm_parts(x1)
            h2[rows, :] = (n2 * vec_ref[G2:G2 + 1, :] + vec_ref[B2:B2 + 1, :]).astype(BF)
            yacc[rows, :] = x1 + vec_ref[BD:BD + 1, :]
            dacc[rows, :] = jnp.zeros((MB, D), F32)
        h2t[...] = h2[...].T
        gbd_ref[...] = jnp.sum(dm[...].astype(F32), 0, keepdims=True)

    gbu_ref[...] = jnp.zeros_like(gbu_ref)

    @pl.loop(0, T // MB)
    def _(i):
        rows = rows_of(i)
        u = mm(h2[rows, :], wu_ref[...]) + bu_ref[...]
        g, slope = gelu_both(u)
        gb = g.astype(BF)
        gs[rows, :] = gb
        yacc[rows, :] += mm(gb, wd_ref[...])
        du = (mm(dm[rows, :], wd_ref[...], NT) * slope).astype(BF)
        dus[rows, :] = du
        gbu_ref[...] += jnp.sum(du.astype(F32), 0, keepdims=True)
        dacc[rows, :] += mm(du, wu_ref[...], NT)

    for t in range(FC // 256):
        cols = pl.ds(t * 256, 256)
        gwd_ref[cols, :] = mm(gs[:, cols], dm[...], TN).astype(BF)

    @pl.loop(0, D // 256)
    def _(t):
        rows = pl.ds(pl.multiple_of(t * 256, 256), 256)
        gwu_ref[rows, :] = mm(h2t[rows, :], dus[...]).astype(BF)

    @pl.when(c == FF // FC - 1)
    def _():
        gg2_ref[...] = jnp.zeros_like(gg2_ref)
        gb2_ref[...] = jnp.zeros_like(gb2_ref)
        for row in range(2):
            out_ref[row] = yacc[pl.ds(row * S, SEQ), :].astype(BF)

        @pl.loop(0, T // MB)
        def _(i):
            rows = rows_of(i)
            n2, s2 = norm_parts(x1_ref[rows, :])
            dh = dacc[rows, :]
            gg2_ref[...] += jnp.sum(dh * n2, 0, keepdims=True)
            gb2_ref[...] += jnp.sum(dh, 0, keepdims=True)
            dx1_ref[rows, :] = dm[rows, :].astype(F32) + norm_pull(dh, n2, s2, vec_ref[G2:G2 + 1, :])


def ffn(x1, dm, wide, down, bu, vec):
    one = jax.ShapeDtypeStruct((1, D), F32)
    return pl.pallas_call(
        ffn_kernel,
        grid=(FF // FC,),
        in_specs=[
            whole((T, D)), whole((2, SEQ, D)),
            pl.BlockSpec((D, FC), lambda c: (0, c + UP_AT // FC)), pl.BlockSpec((FC, D), lambda c: (c, 0)),
            pl.BlockSpec((1, FC), lambda c: (0, c)), whole((8, D)),
        ],
        out_specs=[
            whole((2, SEQ, D)), whole((T, D)),
            pl.BlockSpec((D, FC), lambda c: (0, c)), pl.BlockSpec((FC, D), lambda c: (c, 0)),
            pl.BlockSpec((1, FC), lambda c: (0, c)), whole((1, D)), whole((1, D)), whole((1, D)),
        ],
        out_shape=[
            jax.ShapeDtypeStruct((2, SEQ, D), BF), jax.ShapeDtypeStruct((T, D), F32),
            jax.ShapeDtypeStruct((D, FF), BF), jax.ShapeDtypeStruct((FF, D), BF),
            jax.ShapeDtypeStruct((1, FF), F32), one, one, one,
        ],
        scratch_shapes=[
            pltpu.VMEM((T, D), BF), pltpu.VMEM((D, T), BF), pltpu.VMEM((T, D), BF),
            pltpu.VMEM((T, D), F32), pltpu.VMEM((T, D), F32),
            pltpu.VMEM((T, FC), BF), pltpu.VMEM((T, FC), BF),
        ],
        compiler_params=pltpu.CompilerParams(vmem_limit_bytes=LIMIT),
        name="feed_forward",
    )(x1, dm, wide, down, bu, vec)


def attn_bwd_kernel(
    x_ref, dx1_ref, h1_ref, qkv_ref, p_ref, attn_ref, rl_ref, wo_ref, wqkv_ref, vec_ref,
    gx_ref, gwqkv_ref, gwo_ref, gbqkv_ref, gbo_ref, gg1_ref, gb1_ref,
    da, dos, h1t, dqkv,
):
    hq, r = pl.program_id(0), pl.program_id(1)

    @pl.when((hq == 0) & (r == 0))
    def _():
        gbo_ref[...] = jnp.zeros_like(gbo_ref)

        @pl.loop(0, T // MB)
        def _(i):
            rows = rows_of(i)
            d = dx1_ref[rows, :].astype(BF)
            da[rows, :] = d
            gbo_ref[...] += jnp.sum(d.astype(F32), 0, keepdims=True)
            dos[rows, :] = (mm(d, wo_ref[...], NT) * rl_ref[rows, :]).astype(BF)
        h1t[...] = h1_ref[...].T

    rows = pl.ds(pl.multiple_of(r * S, 16), S)
    scale = 1.0 / math.sqrt(HD)
    for j in range(HG // 2):
        at = j * 384
        qp, kp, vp = (qkv_ref[rows, at + 128 * n: at + 128 * (n + 1)] for n in range(3))
        do = dos[rows, pl.ds(pl.multiple_of(hq * QW + j * 128, 128), 128)]
        prod = do.astype(F32) * attn_ref[rows, j * 128:(j + 1) * 128].astype(F32)
        dq = dk = dv = None
        for e in range(2):
            keep = head_lanes((S, 128), e)
            zero = jnp.zeros_like(qp)
            doe = jnp.where(keep, do, zero)
            dot = jnp.sum(jnp.where(keep, prod, 0.0), -1, keepdims=True)
            p = p_ref[0, 2 * j + e]
            ds = (p.astype(F32) * (mm(doe, vp, NT) - dot)).astype(BF)
            a = mm(ds, jnp.where(keep, kp, zero))
            b = mm(ds, jnp.where(keep, qp, zero), TN)
            c = mm(p, doe, TN)
            dq, dk, dv = (a, b, c) if dq is None else (dq + a, dk + b, dv + c)
        for n, part in enumerate((dq * scale, dk * scale, dv)):
            col = hq * GW + j * 384 + n * 128
            dqkv[rows, pl.ds(pl.multiple_of(col, 128), 128)] = part.astype(BF)

    @pl.when(r == 1)
    def _():
        part = dqkv[:, pl.ds(pl.multiple_of(hq * GW, 128), GW)]
        gbqkv_ref[...] = jnp.sum(part.astype(F32), 0, keepdims=True)

        @pl.loop(0, D // 256)
        def _(t):
            rr = pl.ds(pl.multiple_of(t * 256, 256), 256)
            gwqkv_ref[rr, :] = mm(h1t[rr, :], part).astype(BF)
        gwo_ref[...] = mm(attn_ref[...], da[...], TN).astype(BF)

    @pl.when((hq == D // QW - 1) & (r == 1))
    def _():
        gg1_ref[...] = jnp.zeros_like(gg1_ref)
        gb1_ref[...] = jnp.zeros_like(gb1_ref)
        for row in range(2):
            rr = pl.ds(row * S, SEQ)
            dh = mm(dqkv[pl.ds(row * S, S), :], wqkv_ref[...], NT)[:SEQ]
            n1, s1 = norm_parts(x_ref[row].astype(F32))
            gg1_ref[...] += jnp.sum(dh * n1, 0, keepdims=True)
            gb1_ref[...] += jnp.sum(dh, 0, keepdims=True)
            gx_ref[row] = (dx1_ref[rr, :] + norm_pull(dh, n1, s1, vec_ref[G1:G1 + 1, :])).astype(BF)


def attn_bwd(x, dx1, h1, qkv, p, attn, rl, wide, vec):
    act = pl.BlockSpec((T, QW), lambda h, r: (0, h))
    one = jax.ShapeDtypeStruct((1, D), F32)
    return pl.pallas_call(
        attn_bwd_kernel,
        grid=(D // QW, 2),
        in_specs=[
            whole((2, SEQ, D)), whole((T, D)), whole((T, D)), pl.BlockSpec((T, GW), lambda h, r: (0, h)),
            pl.BlockSpec((1, HG, S, S), lambda h, r: (r, h, 0, 0)), act, whole((T, D)),
            pl.BlockSpec((D, D), lambda h, r: (0, 3)), whole((D, 3 * D)), whole((8, D)),
        ],
        out_specs=[
            whole((2, SEQ, D)), pl.BlockSpec((D, GW), lambda h, r: (0, h)),
            pl.BlockSpec((QW, D), lambda h, r: (h, 0)),
            pl.BlockSpec((1, GW), lambda h, r: (0, h)), whole((1, D)), whole((1, D)), whole((1, D)),
        ],
        out_shape=[
            jax.ShapeDtypeStruct((2, SEQ, D), BF), jax.ShapeDtypeStruct((D, 3 * D), BF), jax.ShapeDtypeStruct((D, D), BF),
            jax.ShapeDtypeStruct((1, 3 * D), F32), one, one, one,
        ],
        scratch_shapes=[
            pltpu.VMEM((T, D), BF), pltpu.VMEM((T, D), BF), pltpu.VMEM((D, T), BF), pltpu.VMEM((T, 3 * D), BF),
        ],
        compiler_params=pltpu.CompilerParams(vmem_limit_bytes=LIMIT),
        name="attention_backward",
    )(x, dx1, h1, qkv, p, attn, rl, wide, wide, vec)


NZ = 4
CH = 48
HW = 384
SR = 16
N_WIDE = AW // (2 * HW)
N_DOWN = 4
N_UP = FF // D
DH = 2 * CH
NV = 8
VW = (24,) * NV + (96,)


def one(i):
    return pl.ds(i, 1)


EVERY = pl.ds(0, NZ)
TWO = pl.ds(0, 2)


def where_am_i():
    dp, fs = lax.axis_index("dp"), lax.axis_index("fsdp")
    return lax.div(dp, 2), lax.rem(dp, 2), lax.div(fs, 2), lax.rem(fs, 2)


def device(z, x, y, c):
    return (z * 2 + x, y * 2 + c)


def partners(z, x, y, c):
    found = [device(lax.rem(z + k, NZ), x, y, c) for k in (1, 2, 3)]
    return found + [device(z, 1 - x, y, c), device(z, x, 1 - y, c), device(z, x, y, 1 - c)]


def say_hello(here):
    barrier = pltpu.get_barrier_semaphore()
    for other in partners(*here):
        pl.semaphore_signal(barrier, inc=1, device_id=other, device_id_type=MESH)


def await_all():
    pl.semaphore_wait(pltpu.get_barrier_semaphore(), 6)


def remote(src, dst, sems, n, target):
    return pltpu.make_async_remote_copy(
        src_ref=src, dst_ref=dst, send_sem=sems[0].at[n], recv_sem=sems[1].at[n],
        device_id=target, device_id_type=MESH,
    )


def half(i, core):
    return pl.ds(pl.multiple_of(i * 2 * HW + core * HW, 128), HW)


def down_rows(i, core):
    return pl.ds(pl.multiple_of(core * DH + (i // 2) * CH, 16), CH)


def down_cols(i):
    return pl.ds((i % 2) * HW, HW)


TOK = 48


def rows_in(src, row, *targets):
    for ref in targets:
        ref[pl.ds(row * S + S - 16, 16), :] = jnp.zeros((16, D), ref.dtype)

    @pl.loop(0, SEQ // TOK)
    def _(i):
        part = src[pl.ds(i * TOK, TOK), row, :]
        for ref in targets:
            ref[pl.ds(pl.multiple_of(row * S + i * TOK, 16), TOK), :] = part.astype(ref.dtype)
    last = src[SEQ - 1:SEQ, row, :]
    for ref in targets:
        ref[pl.ds(row * S + SEQ - 1, 1), :] = last.astype(ref.dtype)


def rows_out(src, target, row):
    @pl.loop(0, SEQ // TOK)
    def _(i):
        target[pl.ds(i * TOK, TOK), row, :] = src[pl.ds(pl.multiple_of(row * S + i * TOK, 16), TOK), :]
    target[SEQ - 1:SEQ, row, :] = src[pl.ds(row * S + SEQ - 1, 1), :]


def transpose_into(target, src):
    @pl.loop(0, D // 128)
    def _(i):
        cols = pl.ds(pl.multiple_of(i * 128, 128), 128)
        target[cols, :] = src[:, cols].T


def add(a, b):
    return (a.astype(F32) + b.astype(F32)).astype(BF)


def plan(entries, ticks):
    table = {n: [] for n in range(len(ticks))}
    rest = []
    for due, action in sorted(entries, key=lambda e: e[0]):
        slot = min((n for n, t in enumerate(ticks) if t >= due), default=None)
        (rest if slot is None else table[slot]).append(action)
    return table, rest


class Gather:
    COPIES = 7

    def __init__(self, here, sems, base, view, first):
        z, x, y, c = here
        peers = partners(*here)
        mine = view(one(z), one(x), one(y))
        column = view(EVERY, one(x), one(y))
        fx, fy = jnp.where(c == 0, 1 - x, x), jnp.where(c == 0, y, 1 - y)
        tx, ty = jnp.where(c == 0, x, 1 - x), jnp.where(c == 0, 1 - y, y)
        passed = view(EVERY, one(fx), one(fy))
        all_of = view(EVERY, TWO, TWO)
        make = lambda n, src, dst, to: remote(src, dst, sems, base + n, to)
        self.along_z = [make(k, mine if first is None else first, mine, peers[k]) for k in range(3)]
        self.along_x = make(3, column, column, peers[3])
        self.along_y = make(4, column, column, peers[4])
        self.diagonal = make(5, passed, passed, device(z, tx, ty, c))
        self.sibling = make(6, all_of, all_of, peers[5])

    def start(self, phase):
        if phase == 0:
            for copy in self.along_z:
                copy.start()
        elif phase == 1:
            for copy in self.along_z:
                copy.wait_recv()
            self.along_x.start()
            self.along_y.start()
        elif phase == 2:
            self.along_x.wait_recv()
            self.along_y.wait_recv()
            self.diagonal.start()
        elif phase == 3:
            self.diagonal.wait_recv()
            self.sibling.start()
        else:
            self.sibling.wait_recv()

    def drain(self):
        for copy in (*self.along_z, self.along_x, self.along_y, self.diagonal, self.sibling):
            copy.wait_send()


class Scatter:
    COPIES = 7

    def __init__(self, here, sems, base, theirs, mine, acc, via, last, zs):
        self.mine, self.acc, self.via, self.last, self.zs = mine, acc, via, last, zs
        z, x, y, c = self.here = here
        peers = partners(*here)
        ix, iy = jnp.where(c == 0, x, 1 - x), jnp.where(c == 0, 1 - y, y)
        self.px, self.py = jnp.where(c == 0, 1 - x, x), jnp.where(c == 0, y, 1 - y)
        first, second = device(z, ix, iy, c), device(z, self.px, self.py, c)
        make = lambda n, src, dst, to: remote(src, dst, sems, base + n, to)
        at = lambda xs, ys: acc.at[EVERY, one(xs), one(ys)]
        self.swap = make(0, theirs, acc, peers[5])
        self.far = make(1, at(1 - x, 1 - y), via.at[0], first)
        self.near = make(2, at(ix, iy), via.at[1], first)
        self.next = make(3, at(self.px, self.py), last, second)
        self.along_z = [
            make(4 + k, acc.at[one(lax.rem(z + k + 1, NZ)), one(x), one(y)], zs.at[k], peers[k]) for k in range(3)
        ]

    def start(self, phase):
        z, x, y, c = self.here
        acc = self.acc
        if phase == 0:
            self.swap.start()
        elif phase == 1:
            self.swap.wait_recv()

            @pl.loop(0, NZ)
            def _(i):
                for xi in range(2):
                    for yi in range(2):
                        acc[i, xi, yi] = add(acc[i, xi, yi], self.mine(i, xi, yi))
            self.far.start()
            self.near.start()
        elif phase == 2:
            self.far.wait_recv()
            px, py = self.px, self.py

            @pl.loop(0, NZ)
            def _(i):
                acc[i, px, py] = add(acc[i, px, py], self.via[0, i, 0, 0])
            self.next.start()
            self.near.wait_recv()

            @pl.loop(0, NZ)
            def _(i):
                acc[i, x, y] = add(acc[i, x, y], self.via[1, i, 0, 0])
        elif phase == 3:
            self.next.wait_recv()

            @pl.loop(0, NZ)
            def _(i):
                acc[i, x, y] = add(acc[i, x, y], self.last[i, 0, 0])
            for copy in self.along_z:
                copy.start()

    def total(self):
        z, x, y, c = self.here
        for copy in self.along_z:
            copy.wait_recv()
        parts = [self.acc[z, x, y]] + [self.zs[k, 0, 0, 0] for k in range(3)]
        return sum(part.astype(F32) for part in parts)

    def drain(self):
        for copy in (self.swap, self.far, self.near, self.next, *self.along_z):
            copy.wait_send()


def scatter_bufs(n, width):
    return [
        pltpu.VMEM((n, NZ, 2, 2, CH, width), BF), pltpu.VMEM((n, 2, NZ, 1, 1, CH, width), BF),
        pltpu.VMEM((n, NZ, 1, 1, CH, width), BF), pltpu.VMEM((n, 3, 1, 1, 1, CH, width), BF),
    ]


def dma_sems(*counts):
    return [pltpu.SemaphoreType.DMA((k,)) for k in counts]


def fixed(shape):
    return pl.BlockSpec(shape, lambda s: (0,) * len(shape), pipeline_mode=pl.Buffered(1))


def vmem():
    return pl.BlockSpec(memory_space=pltpu.VMEM)


def hbm():
    return pl.BlockSpec(memory_space=pl.ANY)


N_ATT = 2 * (D // QW)
PACE = 5.4
FORWARD_LAG = (0.0, 8.0, 20.0, 28.0, 34.0)
FORWARD_FROM = 26.0
FIRST_PACE = 3.6
FORWARD_PACE = 5.4
FORWARD_TICKS = [FORWARD_FROM + 2.9 * n for n in range(12)] + [FORWARD_FROM + 35.0 + 2.1 * n for n in range(16)]


def forward_kernel(
    kind_ref, x_ref, dm_ref, wqkv_ref, wout_ref, wup_ref, wdown_ref, *refs,
):
    small_refs = refs[:NV + 1]
    (
        h1t_ref, qkv_ref, p_ref, attn_ref, rl_ref, x1_ref, dmp_ref, h2t_ref, g_ref, slope_ref, gdown_ref,
        vec_ref, xb_ref, watt_out, wup_out, down_out,
        fa, fb, h1, h2, staged, swap, watt, wup, bqkv, bu, smalls,
        sems_s, sems_r, swap_s, swap_r, small_s, small_r, copy_sem,
    ) = refs[NV + 1:]
    step = pl.program_id(0)
    here = where_am_i()
    z, x, y, c = here
    peers = partners(*here)
    sems = (sems_s, sems_r)

    swaps = [
        remote(staged.at[:, half(i, 1 - c)], swap.at[:, i * HW:(i + 1) * HW], (swap_s, swap_r), i, peers[5])
        for i in range(N_WIDE)
    ]
    items, own = [], []
    for i in range(N_WIDE):
        buf, at = (watt, i) if i < 4 else (wup, i - 4)
        view = lambda zs, xs, ys, buf=buf, at=at: buf.at[zs, xs, ys, :, half(at, c)]
        items.append(Gather(here, sems, i * Gather.COPIES, view, None))
    for i in range(N_DOWN):
        rows, cols = down_rows(i, c), down_cols(i)
        view = lambda zs, xs, ys, rows=rows, cols=cols: down_out.at[zs, xs, ys, rows, cols]
        first = wdown_ref.at[:, :, :, pl.ds((i // 2) * CH, CH), cols]
        items.append(Gather(here, sems, (N_WIDE + i) * Gather.COPIES, view, first))
        own.append(pltpu.make_async_copy(first, view(one(z), one(x), one(y)), copy_sem.at[N_WIDE + i]))
    keeps = []
    for i in range(N_WIDE):
        src, dst, at = (watt, watt_out, i) if i < 4 else (wup, wup_out, i - 4)
        cols = pl.ds(at * D, D)
        keeps.append(pltpu.make_async_copy(
            src.at[:, :, :, :, cols], dst.at[:, :, :, :, cols], copy_sem.at[i]))

    def act(action):
        i, phase = action
        if i >= N_WIDE and phase == 0:
            own[i - N_WIDE].start()
        if i >= N_WIDE and phase == 1:
            own[i - N_WIDE].wait()
        items[i].start(phase)
        if phase == 4 and i < N_WIDE:
            keeps[i].start()

    needed = {1: 4, 2: 8, 3: 11, 4: 12, 5: 16, 6: 20, 7: 24}
    entries = []
    for i in range(1, N_WIDE + N_DOWN):
        for phase in range(5):
            due = FORWARD_PACE * i + FORWARD_LAG[phase] if phase else FIRST_PACE * i
            if i in needed:
                due = min(due, FORWARD_TICKS[needed[i]])
            entries.append((due, (i, phase)))
    early = [a for t, a in sorted(entries, key=lambda e: e[0]) if t < FORWARD_FROM]
    table, late = plan([e for e in entries if e[0] >= FORWARD_FROM], FORWARD_TICKS)

    def tick(slot, could_be):
        for n in could_be:
            if table[n]:
                @pl.when(slot == n)
                def _(n=n):
                    for action in table[n]:
                        act(action)

    @pl.when(step == 0)
    def _():
        say_hello(here)
        for pair in range(6):
            for n in range(3):
                at = pair * 384 + n * 128
                staged[:, at:at + 128] = wqkv_ref[:, n * D + pair * 128:n * D + (pair + 1) * 128].astype(F32)
        staged[:, OUT_AT:UP_AT] = wout_ref[...].astype(F32)
        staged[:, UP_AT:] = wup_ref[...].astype(F32)
        line = smalls.at[z, x, y, c]
        line[...] = jnp.zeros((SR, 128), F32)
        for n, (ref, width) in enumerate(zip(small_refs, VW)):
            line[n:n + 1, 0:width] = ref[...].astype(F32).reshape(1, width)
        await_all()
        swaps[0].start()

        def small_copy(n, src, to):
            return remote(src, src, (small_s, small_r), n, to)

        small_c = small_copy(0, smalls.at[one(z), one(x), one(y), one(c)], peers[5])
        both = smalls.at[one(z), one(x), one(y), TWO]
        small_z = [small_copy(1 + k, both, peers[k]) for k in range(3)]
        small_x = small_copy(4, smalls.at[EVERY, one(x), one(y), TWO], peers[3])
        small_y = small_copy(5, smalls.at[EVERY, TWO, one(y), TWO], peers[4])
        small_c.start()
        for i in range(1, N_WIDE):
            swaps[i].start()

        def take_block(i):
            swaps[i].wait_recv()
            mine_part = staged[:, half(i, c)]
            their_part = swap[:, i * HW:(i + 1) * HW]
            buf, at = (watt, i) if i < 4 else (wup, i - 4)
            lower = jnp.where(c == 0, mine_part, their_part)
            upper = jnp.where(c == 0, their_part, mine_part)
            buf[z, x, y, :, half(at, c)] = jnp.concatenate([lower, upper], 0).astype(BF)

        waiting = list(early)

        def act_some(count):
            for _n in range(min(count, len(waiting))):
                act(waiting.pop(0))

        take_block(0)
        items[0].start(0)
        small_c.wait_recv()
        for copy in small_z:
            copy.start()
        for i in range(1, N_WIDE):
            take_block(i)
        rows_in(x_ref, 0, x1_ref, xb_ref)
        for copy in small_z:
            copy.wait_recv()
        small_x.start()
        act_some(1)
        items[0].start(1)
        rows_in(x_ref, 1, x1_ref, xb_ref)
        small_x.wait_recv()
        small_y.start()
        act_some(1)
        items[0].start(2)
        act_some(1)
        for row in range(2):
            rows_in(dm_ref, row, dmp_ref)
        items[0].start(3)
        small_y.wait_recv()
        src = lax.broadcasted_iota(jnp.int32, (128, D), 0)
        dst = lax.broadcasted_iota(jnp.int32, (128, D), 1)
        spread_short = jnp.where(lax.rem(dst, 24) == src, 1.0, 0.0).astype(BF)
        spread_long = jnp.where(lax.rem(dst, 96) == src, 1.0, 0.0).astype(BF)
        col = lax.broadcasted_iota(jnp.int32, (8, D), 1)
        vec_ref[...] = jnp.zeros_like(vec_ref)

        @pl.loop(0, NZ)
        def _(zi):
            pieces = smalls[zi].reshape(8 * SR, 128).astype(BF)
            short, long = mm(pieces, spread_short), mm(pieces, spread_long)
            for k in range(8):
                at = SR * k
                part = jnp.where(lax.div(col, 24) == zi * 8 + k, short[at:at + NV], 0.0)
                more = jnp.where(lax.div(col, 96) == k, long[at + NV:at + SR], 0.0)
                vectors, hidden_bias = (part, more) if k == 0 else (vectors + part, hidden_bias + more)
            vec_ref[...] += vectors
            bu[zi] = hidden_bias
        for pair in range(6):
            n, at = pair // 2, (pair % 2) * 384
            bqkv[n, :, at:at + 128] = vec_ref[BQ:BQ + 1, pair * 128:(pair + 1) * 128]
            bqkv[n, :, at + 128:at + 256] = jnp.zeros((1, 128), F32)
            bqkv[n, :, at + 256:at + 384] = vec_ref[BV:BV + 1, pair * 128:(pair + 1) * 128]
        act_some(2)

        @pl.loop(0, T // MB)
        def _(i):
            rows = rows_of(i)
            n1, _s = norm_parts(x1_ref[rows, :])
            h1[rows, :] = (n1 * vec_ref[G1:G1 + 1, :] + vec_ref[B1:B1 + 1, :]).astype(BF)
        for row in range(2):
            slot = lax.broadcasted_iota(jnp.int32, (S, 128), 0)
            lane = lax.broadcasted_iota(jnp.int32, (S, 128), 1)
            packed = jnp.where(slot < HALF, 0, jnp.where(slot < 2 * HALF, 1, 2))
            seg = jnp.where(kind_ref[row] == 1, packed, 0)
            fa[row] = jnp.where((lane < 3) & (seg == lane), -1e30, 0.0).astype(BF)
            fb[row] = jnp.where((lane < 3) & ((seg != lane) | (slot >= SEQ)), 1.0, 0.0).astype(BF)
        act_some(len(waiting))
        transpose_into(h1t_ref, h1)
        rl_ref[...] = jnp.zeros_like(rl_ref)
        act((0, 4))
        for copy in (small_c, *small_z, small_x, small_y, *swaps):
            copy.wait_send()

    @pl.when(step < N_ATT)
    def _():
        hq, r = lax.div(step, 2), lax.rem(step, 2)
        tick(2 * step, range(0, 12, 2))

        @pl.when(r == 0)
        def _():
            @pl.loop(0, 2)
            def _(i):
                rows = row_of(i)
                w = watt[:, :, :, :, pl.ds(pl.multiple_of(hq * GW, 128), GW)].reshape(D, GW)
                qkv_ref[rows, :] = (mm(h1[rows, :], w) + bqkv[hq]).astype(BF)

        rows = pl.ds(pl.multiple_of(r * S, 16), S)
        feat_q, feat_k = fa[r], fb[r]
        ones = jnp.ones((S, 128), BF)
        scale = math.log2(math.e) / math.sqrt(HD)
        for j in range(HG // 2):
            if j:
                tick(2 * step + 1, range(1, 12, 2))
            at = j * 384
            qp, kp, vp = (qkv_ref[rows, at + 128 * n: at + 128 * (n + 1)] for n in range(3))
            kcat = jnp.concatenate([kp, feat_k], 1)
            total = None
            for e in range(2):
                keep = head_lanes((S, 128), e)
                qcat = jnp.concatenate([jnp.where(keep, qp, jnp.zeros_like(qp)), feat_q], 1)
                s = mm(qcat, kcat, NT)
                m = jnp.max(s, -1, keepdims=True)
                pb = jnp.exp2((s - m) * scale).astype(BF)
                p_ref[0, 2 * j + e] = pb
                vcat = jnp.concatenate([jnp.where(keep, vp, jnp.zeros_like(vp)), ones], 1)
                o = mm(pb, vcat)
                rl = 1.0 / o[:, 128:]
                part = o[:, :128] * rl
                total = part if total is None else total + part
                spot = lax.broadcasted_iota(jnp.int32, (S, 128), 1) == hq * HG + 2 * j + e
                rl_ref[rows, :] = jnp.where(spot, rl, rl_ref[rows, :])
            out = pl.ds(pl.multiple_of(hq * QW + j * 128, 128), 128)
            attn_ref[rows, out] = total.astype(BF)

    @pl.when(step == N_ATT - 1)
    def _():
        @pl.loop(0, T // MB)
        def _(i):
            rows = rows_of(i)
            wo = watt[:, :, :, :, OUT_AT:UP_AT].reshape(D, D)
            x1 = x1_ref[rows, :] + mm(attn_ref[rows, :], wo) + vec_ref[BO:BO + 1, :]
            x1_ref[rows, :] = x1
            n2, _s = norm_parts(x1)
            h2[rows, :] = (n2 * vec_ref[G2:G2 + 1, :] + vec_ref[B2:B2 + 1, :]).astype(BF)
        transpose_into(h2t_ref, h2)

    @pl.when(step >= N_ATT)
    def _():
        part = step - N_ATT

        @pl.loop(0, 2)
        def _(i):
            tick(12 + 4 * part + 2 * i, range(12, len(FORWARD_TICKS), 2))
            tick(12 + 4 * part + 2 * i + 1, range(13, len(FORWARD_TICKS), 2))
            rows = row_of(i)
            w = wup[:, :, :, :, pl.ds(pl.multiple_of(part * D, 128), D)].reshape(D, D)
            g, slope = gelu_both(mm(h2[rows, :], w) + bu[part, 0:1, :])
            g_ref[rows, :] = g.astype(BF)
            slope_ref[rows, :] = slope.astype(BF)

        @pl.loop(0, 2)
        def _(t):
            cols = pl.ds(pl.multiple_of(t * 384, 128), 384)
            gdown_ref[cols, :] = mm(g_ref[:, cols], dmp_ref[...], TN).astype(BF)

    @pl.when(step == N_ATT + N_UP - 1)
    def _():
        for action in late:
            act(action)
        for item in items:
            item.drain()
        for copy in keeps:
            copy.wait()


def forward(kind, x, dm, wqkv, wout, wup, wdown, smalls):
    n = N_WIDE + N_DOWN
    att = lambda s: jnp.minimum(s, N_ATT - 1)
    ff = lambda s: jnp.maximum(s - N_ATT, 0)
    shape = jax.ShapeDtypeStruct
    return pl.pallas_call(
        forward_kernel,
        grid=(N_ATT + N_UP,),
        in_specs=[
            pl.BlockSpec(memory_space=pltpu.SMEM), fixed((SEQ, 2, D)), fixed((SEQ, 2, D)),
            fixed((24, 3 * D)), fixed((24, D)), fixed((24, FF)), fixed((1, 1, 1, 96, D)),
            *[pl.BlockSpec((w,), lambda s: (0,), pipeline_mode=pl.Buffered(1)) for w in VW],
        ],
        out_specs=[
            fixed((D, T)), pl.BlockSpec((T, GW), lambda s: (0, att(s) // 2)),
            pl.BlockSpec((1, HG, S, S), lambda s: (att(s) % 2, att(s) // 2, 0, 0)),
            fixed((T, D)), fixed((T, 128)), fixed((T, D)), fixed((T, D)), fixed((D, T)),
            pl.BlockSpec((T, D), lambda s: (0, ff(s))), pl.BlockSpec((T, D), lambda s: (0, ff(s))),
            pl.BlockSpec((D, D), lambda s: (ff(s), 0)),
            fixed((NV, D)), fixed((T, D)), hbm(), hbm(), hbm(),
        ],
        out_shape=[
            shape((D, T), BF), shape((T, 3 * D), BF), shape((2, D // HD, S, S), BF),
            shape((T, D), BF), shape((T, 128), F32), shape((T, D), F32), shape((T, D), BF), shape((D, T), BF),
            shape((T, FF), BF), shape((T, FF), BF), shape((FF, D), BF), shape((NV, D), F32), shape((T, D), BF),
            shape((NZ, 2, 2, CH, UP_AT), BF), shape((NZ, 2, 2, CH, FF), BF), shape((NZ, 2, 2, 4 * CH, D), BF),
        ],
        scratch_shapes=[
            pltpu.VMEM((2, S, 128), BF), pltpu.VMEM((2, S, 128), BF), pltpu.VMEM((T, D), BF), pltpu.VMEM((T, D), BF),
            pltpu.VMEM((24, AW), F32), pltpu.VMEM((24, AW // 2), F32),
            pltpu.VMEM((NZ, 2, 2, CH, UP_AT), BF), pltpu.VMEM((NZ, 2, 2, CH, FF), BF),
            pltpu.VMEM((3, 1, GW), F32), pltpu.VMEM((N_UP, 8, D), F32), pltpu.VMEM((NZ, 2, 2, 2, SR, 128), F32),
            *dma_sems(n * Gather.COPIES, n * Gather.COPIES, N_WIDE, N_WIDE, 6, 6, n),
        ],
        compiler_params=pltpu.CompilerParams(collective_id=0, has_side_effects=True, vmem_limit_bytes=LIMIT),
        name="forward",
    )(kind, x, dm, wqkv, wout, wup, wdown.reshape(1, 1, 1, 96, D), *smalls)


BACK_LAG = (0.0, 5.0, 15.0, 23.0, 32.0)
FFN_TICKS = [4.0 + 9.0 * s + t for s in range(4) for t in (0.0, 0.1, 2.8, 2.9, 5.7, 7.3)]


def ffn_back_kernel(
    x1_ref, dm_ref, g_ref, slope_ref, wu_ref, wd_ref, h2t_ref, vec_ref, gdown_ref,
    y_ref, dx1_ref, gup_ref, sums_ref, odown_ref,
    yacc, dacc, dus, mine, acc, via, last, zs, sems_s, sems_r, own_sem,
):
    step = pl.program_id(0)
    here = where_am_i()
    z, x, y, c = here
    items, own = [], []
    for i in range(N_DOWN):
        rows, cols = down_rows(i, c), down_cols(i)
        own.append(pltpu.make_async_copy(gdown_ref.at[:, :, :, rows, cols], mine.at[i], own_sem.at[i]))
        items.append(Scatter(
            here, (sems_s, sems_r), i * Scatter.COPIES, gdown_ref.at[EVERY, TWO, TWO, down_rows(i, 1 - c), cols],
            lambda a, b, d, i=i: mine[i, a, b, d], acc.at[i], via.at[i], last.at[i], zs.at[i],
        ))
    entries = [
        (5.0 + PACE * i + lag, (i, phase)) for i in range(N_DOWN) for phase, lag in enumerate(BACK_LAG) if (i, phase) != (0, 0)
    ]
    table, late = plan(entries, FFN_TICKS)

    def act(action):
        i, phase = action
        if phase == 1:
            own[i].wait()
        if phase == 4:
            odown_ref[pl.ds((i // 2) * CH, CH), down_cols(i)] = items[i].total()
        else:
            items[i].start(phase)

    def tick(slot):
        for n, todo in table.items():
            if todo:
                @pl.when(slot == n)
                def _(todo=todo):
                    for action in todo:
                        act(action)

    @pl.when(step == 0)
    def _():
        say_hello(here)
        for copy in own:
            copy.start()

        @pl.loop(0, T // MB)
        def _(i):
            rows = rows_of(i)
            yacc[rows, :] = x1_ref[rows, :] + vec_ref[BD:BD + 1, :]
            dacc[rows, :] = jnp.zeros((MB, D), F32)
        sums_ref[...] = jnp.zeros_like(sums_ref)
        sums_ref[2:3, :] = jnp.sum(dm_ref[...].astype(F32), 0, keepdims=True)

    @pl.loop(0, 2)
    def _(i):
        @pl.when((step == 0) & (i == 1))
        def _():
            await_all()
            act((0, 0))

        tick(6 * step + 2 * i)
        tick(6 * step + 2 * i + 1)
        rows = row_of(i)
        g = g_ref[rows, :]
        yacc[rows, :] += mm(g, wd_ref[...])
        du = (mm(dm_ref[rows, :], wd_ref[...], NT) * slope_ref[rows, :].astype(F32)).astype(BF)
        dus[rows, :] = du
        sums_ref[pl.ds(3 + step, 1), :] += jnp.sum(du.astype(F32), 0, keepdims=True)
        dacc[rows, :] += mm(du, wu_ref[...], NT)

    @pl.loop(0, 2)
    def _(t):
        tick(6 * step + 4 + t)
        rows = pl.ds(pl.multiple_of(t * 384, 128), 384)
        gup_ref[rows, :] = mm(h2t_ref[rows, :], dus[...]).astype(BF)

    @pl.when(step == N_UP - 1)
    def _():
        @pl.loop(0, T // MB)
        def _(i):
            rows = rows_of(i)
            n2, s2 = norm_parts(x1_ref[rows, :])
            dh = dacc[rows, :]
            sums_ref[0:1, :] += jnp.sum(dh * n2, 0, keepdims=True)
            sums_ref[1:2, :] += jnp.sum(dh, 0, keepdims=True)
            dx1_ref[rows, :] = dm_ref[rows, :].astype(F32) + norm_pull(dh, n2, s2, vec_ref[G2:G2 + 1, :])
            y_ref[rows, :] = yacc[rows, :].astype(BF)
        for action in late:
            act(action)
        for item in items:
            item.drain()


def ffn_back(x1, dm, g, slope, wup, down, h2t, vec, gdown):
    shape = jax.ShapeDtypeStruct
    col = pl.BlockSpec((T, D), lambda s: (0, s))
    return pl.pallas_call(
        ffn_back_kernel,
        grid=(N_UP,),
        in_specs=[
            fixed((T, D)), fixed((T, D)), col, col,
            pl.BlockSpec((D, D), lambda s: (0, s)), pl.BlockSpec((D, D), lambda s: (s, 0)),
            fixed((D, T)), fixed((NV, D)), hbm(),
        ],
        out_specs=[
            fixed((T, D)), fixed((T, D)), pl.BlockSpec((D, D), lambda s: (0, s)), fixed((8, D)), fixed((96, D)),
        ],
        out_shape=[
            shape((T, D), BF), shape((T, D), F32), shape((D, FF), BF), shape((8, D), F32), shape((96, D), F32),
        ],
        scratch_shapes=[
            pltpu.VMEM((T, D), F32), pltpu.VMEM((T, D), F32), pltpu.VMEM((T, D), BF),
            pltpu.VMEM((N_DOWN, NZ, 2, 2, CH, HW), BF), *scatter_bufs(N_DOWN, HW),
            *dma_sems(N_DOWN * 7, N_DOWN * 7, N_DOWN),
        ],
        compiler_params=pltpu.CompilerParams(collective_id=1, has_side_effects=True, vmem_limit_bytes=LIMIT),
        name="feed_forward_back",
    )(x1, dm, g, slope, wup, down, h2t, vec, gdown.reshape(NZ, 2, 2, 4 * CH, D))


BACK_TICKS = [2.0 + 4.8 * n for n in range(12)]
N_BACK = N_UP + 4
END_LAG = (0.0, 4.0, 9.0, 14.0, 19.0)


def attn_back_kernel(
    xb_ref, yb_ref, dx1_ref, h1t_ref, qkv_ref, p_ref, attn_ref, rl_ref, wo_ref, wqkv_ref, vec_ref, sums_ref, gup_ref,
    out_ref, gx_ref, oqkv_ref, oout_ref, oup_ref, *refs,
):
    small_outs = refs[:NV + 1]
    (
        da, dos, dqkv, dh1, gqkv, gout, mine, acc, via, last, zs, done, landed, small,
        sems_s, sems_r, fin_s, fin_r, small_s, small_r, own_sem,
    ) = refs[NV + 1:]
    step = pl.program_id(0)
    hq, r = lax.div(step, 2), lax.rem(step, 2)
    here = where_am_i()
    z, x, y, c = here
    peers = partners(*here)
    items, own = [], []
    for n in range(N_BACK):
        if n < N_UP:
            theirs = gup_ref.at[EVERY, TWO, TWO, :, half(n, 1 - c)]
            own.append(pltpu.make_async_copy(gup_ref.at[:, :, :, :, half(n, c)], mine.at[n], own_sem.at[n]))
            get = lambda a, b, d, n=n: mine[n, a, b, d]
        elif n == N_UP:
            theirs = gout.at[EVERY, TWO, TWO, :, half(0, 1 - c)]
            get = lambda a, b, d: gout[a, b, d, :, half(0, c)]
        else:
            i = n - N_UP - 1
            theirs = gqkv.at[i, EVERY, TWO, TWO, :, half(0, 1 - c)]
            get = lambda a, b, d, i=i: gqkv[i, a, b, d, :, half(0, c)]
        items.append(Scatter(
            here, (sems_s, sems_r), n * Scatter.COPIES, theirs, get, acc.at[n], via.at[n], last.at[n], zs.at[n]))

    def final(n):
        theirs = pl.ds(pl.multiple_of((1 - c) * 24, 8), 24)
        return remote(done.at[n, theirs], landed.at[n], (fin_s, fin_r), n, peers[5])

    def put(n, core, value):
        if n > N_UP:
            for b in range(3):
                cols = pl.ds(pl.multiple_of(b * D + (n - N_UP - 1) * QW + core * 128, 128), 128)
                oqkv_ref[:, cols] = value[:, b * 128:(b + 1) * 128]
        elif n == N_UP:
            oout_ref[:, half(0, core)] = value
        else:
            oup_ref[:, half(n, core)] = value

    def finish(n):
        done[n] = items[n].total()
        final(n).start()
        put(n, c, done[n, pl.ds(pl.multiple_of(c * 24, 8), 24)])

    def act(action):
        n, phase = action
        if n < N_UP and phase == 1:
            own[n].wait()
        if phase == 4:
            finish(n)
        else:
            items[n].start(phase)

    entries = []
    begin = 0.0
    for n in range(N_BACK):
        if n > N_UP:
            begin = max(begin, BACK_TICKS[0] + 19.2 * (n - N_UP))
        for phase in range(5):
            if n < N_UP or phase > 0:
                lag = BACK_LAG if n < N_BACK - 2 else END_LAG
                entries.append((begin + lag[phase], (n, phase)))
        begin += PACE
    entries.remove((0.0, (0, 0)))
    table, tail = plan(entries, BACK_TICKS)
    final_steps = [a for a in tail if a[0] == N_BACK - 1]
    earlier = [a for a in tail if a[0] != N_BACK - 1]

    def tick(slot, could_be):
        for n in could_be:
            if table[n]:
                @pl.when(slot == n)
                def _(n=n):
                    for action in table[n]:
                        act(action)

    @pl.when(step == 0)
    def _():
        say_hello(here)
        for copy in own:
            copy.start()
        small[0] = jnp.zeros((16, D), F32)
        src = lax.broadcasted_iota(jnp.int32, (128, D), 0)
        dst = lax.broadcasted_iota(jnp.int32, (128, D), 1)
        spread = jnp.where(lax.div(dst, HD) == src, 1.0, 0.0)

        @pl.loop(0, T // MB)
        def _(i):
            rows = rows_of(i)
            d = dx1_ref[rows, :].astype(BF)
            da[rows, :] = d
            rl = lax.dot_general(
                rl_ref[rows, :], spread, NN, precision=lax.Precision.HIGHEST, preferred_element_type=F32)
            small[0, 4:5, :] += jnp.sum(d.astype(F32), 0, keepdims=True)
            dos[rows, :] = (mm(d, wo_ref[...], NT) * rl).astype(BF)
            dh1[rows, :] = jnp.zeros((MB, D), F32)
        @pl.loop(0, 2)
        def _(t):
            part = mm(attn_ref[:, pl.ds(pl.multiple_of(t * 384, 128), 384)], da[...], TN)
            gout[pl.ds(2 * t, 2)] = part.astype(BF).reshape(2, 2, 2, CH, D)

        await_all()
        act((0, 0))
        items[N_UP].start(0)

    tick(2 * step, range(0, 12, 2))
    rows = pl.ds(pl.multiple_of(r * S, 16), S)
    scale = 1.0 / math.sqrt(HD)
    for j in range(HG // 2):
        if j:
            tick(2 * step + 1, range(1, 12, 2))
        at = j * 384
        qp, kp, vp = (qkv_ref[rows, at + 128 * n: at + 128 * (n + 1)] for n in range(3))
        lanes = pl.ds(pl.multiple_of(hq * QW + j * 128, 128), 128)
        do = dos[rows, lanes]
        prod = do.astype(F32) * attn_ref[rows, lanes].astype(F32)
        dq = dk = dv = None
        for e in range(2):
            keep = head_lanes((S, 128), e)
            zero = jnp.zeros_like(qp)
            doe = jnp.where(keep, do, zero)
            dot = jnp.sum(jnp.where(keep, prod, 0.0), -1, keepdims=True)
            p = p_ref[0, 2 * j + e]
            ds = (p.astype(F32) * (mm(doe, vp, NT) - dot)).astype(BF)
            a_, b_, c_ = mm(ds, jnp.where(keep, kp, zero)), mm(ds, jnp.where(keep, qp, zero), TN), mm(p, doe, TN)
            dq, dk, dv = (a_, b_, c_) if dq is None else (dq + a_, dk + b_, dv + c_)
        for n, part in enumerate((dq * scale, dk * scale, dv)):
            dqkv[rows, at + 128 * n:at + 128 * (n + 1)] = part.astype(BF)

    @pl.when(r == 1)
    def _():
        sums = jnp.sum(dqkv[...].astype(F32), 0, keepdims=True)
        for j in range(2):
            cols = pl.ds(pl.multiple_of(hq * QW + j * 128, 128), 128)
            small[0, 2:3, cols] = sums[:, j * 384:j * 384 + 128]
            small[0, 3:4, cols] = sums[:, j * 384 + 256:j * 384 + 384]
        @pl.loop(0, 2)
        def _(t):
            part = mm(h1t_ref[pl.ds(pl.multiple_of(t * 384, 16), 384), :], dqkv[...])
            gqkv[hq, pl.ds(2 * t, 2)] = part.astype(BF).reshape(2, 2, 2, CH, GW)

        for i in range(3):
            @pl.when(hq == i)
            def _(i=i):
                items[N_UP + 1 + i].start(0)

        @pl.loop(0, 2)
        def _(i):
            rr = row_of(i)
            dh1[rr, :] += mm(dqkv[rr, :], wqkv_ref[...], NT)

    @pl.when(step == N_ATT - 1)
    def _():
        rest = final_steps[1:]

        @pl.loop(0, T // MB)
        def _(i):
            @pl.when(i == 0)
            def _():
                for action in earlier[:-1]:
                    act(action)

            @pl.when(i == 1)
            def _():
                act(final_steps[0])

            @pl.when(i == 3)
            def _():
                for action in earlier[-1:]:
                    act(action)
            rr = rows_of(i)
            dh = dh1[rr, :]
            n1, s1 = norm_parts(xb_ref[rr, :].astype(F32))
            small[0, 0:1, :] += jnp.sum(dh * n1, 0, keepdims=True)
            small[0, 1:2, :] += jnp.sum(dh, 0, keepdims=True)
            da[rr, :] = (dx1_ref[rr, :] + norm_pull(dh, n1, s1, vec_ref[G1:G1 + 1, :])).astype(BF)
        small[0, 5:12, :] = sums_ref[0:7, :]
        copies = []

        def send_small(n, src, dst, to):
            copy = remote(small.at[src], small.at[dst], (small_s, small_r), n, to)
            copy.start()
            copies.append(copy)

        send_small(0, 0, 1, peers[5])
        hops = [(1, 2, 3, peers[3]), (2, 4, 5, peers[4])]
        level = 0
        while rest or level < 4:
            if rest:
                act(rest.pop(0))
            if level == 0:
                for row in range(2):
                    rows_out(da, gx_ref, row)
            if level == 1:
                for row in range(2):
                    rows_out(yb_ref, out_ref, row)
            if level < 2:
                copies[level].wait_recv()
                small[2 * level + 2] = small[2 * level] + small[2 * level + 1]
                send_small(*hops[level])
            elif level == 2:
                copies[2].wait_recv()
                small[6] = small[4] + small[5]
                for k in range(3):
                    send_small(3 + k, 6, 7 + k, peers[k])
            elif level == 3:
                for k in range(3):
                    copies[3 + k].wait_recv()
                total = small[6] + small[7] + small[8] + small[9]
                me = lax.axis_index("dp") * lax.axis_size("fsdp") + lax.axis_index("fsdp")
                src = lax.broadcasted_iota(jnp.int32, (D, 128), 0)
                dst = lax.broadcasted_iota(jnp.int32, (D, 128), 1)

                def pick(lines, width, at):
                    chosen = jnp.where((src == at + dst) & (dst < width), 1.0, 0.0)
                    return lax.dot_general(
                        lines, chosen, NN, precision=lax.Precision.HIGHEST, preferred_element_type=F32)

                mine_of = pick(total[:8], 24, me * 24)
                for n in range(NV):
                    small_outs[n][...] = mine_of[n, :24]
                row = lax.broadcasted_iota(jnp.int32, (8, D), 0)
                longest = jnp.sum(jnp.where(row == lax.div(me, 8), total[8:16], 0.0), 0, keepdims=True)
                small_outs[NV][...] = pick(jnp.broadcast_to(longest, (8, D)), 96, lax.rem(me, 8) * 96)[0, :96]
            level += 1
        for n in range(N_BACK):
            copy = final(n)
            copy.wait_recv()
            put(n, 1 - c, landed[n])
            copy.wait_send()
            items[n].drain()
        for copy in copies:
            copy.wait_send()


def attn_back(x, yb, dx1, h1t, qkv, p, attn, rl, watt, vec, sums, gup):
    shape = jax.ShapeDtypeStruct
    n_fin = N_BACK
    return pl.pallas_call(
        attn_back_kernel,
        grid=(N_ATT,),
        in_specs=[
            fixed((T, D)), fixed((T, D)), fixed((T, D)), fixed((D, T)), pl.BlockSpec((T, GW), lambda s: (0, s // 2)),
            pl.BlockSpec((1, HG, S, S), lambda s: (s % 2, s // 2, 0, 0)), fixed((T, D)), fixed((T, 128)),
            pl.BlockSpec((D, D), lambda s: (0, 3), pipeline_mode=pl.Buffered(1)),
            pl.BlockSpec((D, GW), lambda s: (0, s // 2)), fixed((NV, D)), fixed((8, D)), hbm(),
        ],
        out_specs=[
            fixed((SEQ, 2, D)), fixed((SEQ, 2, D)), fixed((24, 3 * D)), fixed((24, D)), fixed((24, FF)),
            *[pl.BlockSpec((w,), lambda s: (0,), pipeline_mode=pl.Buffered(1)) for w in VW],
        ],
        out_shape=[
            shape((SEQ, 2, D), BF), shape((SEQ, 2, D), BF), shape((24, 3 * D), F32), shape((24, D), F32),
            shape((24, FF), F32), *[shape((w,), F32) for w in VW],
        ],
        scratch_shapes=[
            pltpu.VMEM((T, D), BF), pltpu.VMEM((T, D), BF), pltpu.VMEM((T, GW), BF), pltpu.VMEM((T, D), F32),
            pltpu.VMEM((3, NZ, 2, 2, CH, GW), BF), pltpu.VMEM((NZ, 2, 2, CH, D), BF),
            pltpu.VMEM((N_UP, NZ, 2, 2, CH, HW), BF), *scatter_bufs(N_BACK, HW),
            pltpu.VMEM((N_BACK, CH, HW), F32), pltpu.VMEM((N_BACK, 24, HW), F32), pltpu.VMEM((10, 16, D), F32),
            *dma_sems(N_BACK * 7, N_BACK * 7, n_fin, n_fin, 6, 6, N_UP),
        ],
        compiler_params=pltpu.CompilerParams(collective_id=2, has_side_effects=True, vmem_limit_bytes=LIMIT),
        name="attention_back",
    )(x, yb, dx1, h1t, qkv, p, attn, rl, watt, watt, vec, sums, gup.reshape(NZ, 2, 2, CH, FF))


def hand_over_kernel(*refs):
    n = len(refs) // 2
    for i in range(n):
        refs[n + i][...] = refs[i][...]


def hand_over(values):
    return pl.pallas_call(
        hand_over_kernel,
        in_specs=[vmem()] * len(values),
        out_specs=[vmem()] * len(values),
        out_shape=[jax.ShapeDtypeStruct(v.shape, v.dtype) for v in values],
        compiler_params=pltpu.CompilerParams(vmem_limit_bytes=LIMIT),
        name="results",
    )(*values)


def by_pair(v):
    return v.reshape(v.shape[0], 3, 6, 128).transpose(0, 2, 1, 3).reshape(v.shape[0], 3 * D)


def by_kind(v):
    return v.reshape(v.shape[0], 6, 3, 128).transpose(0, 2, 1, 3).reshape(v.shape[0], 3 * D)


def with_own_copies(inputs, row_kind, w_qkv, w_out, w_up, w_down, vectors, b_up, out_grad):
    x, dm = inputs.transpose(1, 0, 2), out_grad.transpose(1, 0, 2)
    h1t, qkv, p, attn, rl, x1, dmp, h2t, g, slope, gdown, vec, xb, watt, wup, down = forward(
        row_kind, x, dm, w_qkv, w_out, w_up, w_down, (*vectors, b_up))
    yb, dx1, gup, sums, gdown = ffn_back(
        x1, dmp, g, slope, wup.reshape(D, FF), down.reshape(FF, D), h2t, vec, gdown)
    results = attn_back(xb, yb, dx1, h1t, qkv, p, attn, rl, watt.reshape(D, UP_AT), vec, sums, gup)
    out, gx, gqkv, gout, gup, gdown, *small = hand_over((*results[:5], gdown, *results[5:]))
    return out.transpose(1, 0, 2), gx.transpose(1, 0, 2), gqkv, gout, gup, gdown, small[:NV], small[NV]


def with_collectives(inputs, row_kind, w_qkv, w_out, w_up, w_down, vectors, b_up, out_grad):
    axes = ("dp", "fsdp")
    get = lambda v: lax.all_gather(v, axes, axis=0, tiled=True)
    wide = jnp.concatenate([by_pair(get(w_qkv)), get(w_out), get(w_up)], 1)
    down = get(w_down)
    full = [get(v).astype(F32) for v in vectors]
    vec = jnp.stack(full)
    bu = get(b_up).astype(F32)[None]
    bqkv = by_pair(jnp.concatenate([full[BQ], jnp.zeros_like(full[BQ]), full[BV]])[None])
    h1, qkv, p, attn, rl, x1 = attn_fwd(row_kind, inputs, wide, bqkv, vec)
    outputs, dx1, gup, gdown, gbu, gg2, gb2, gbd = ffn(x1, out_grad, wide, down, bu, vec)
    input_grad, gqkv, gout, gbqkv, gbo, gg1, gb1 = attn_bwd(inputs, dx1, h1, qkv, p, attn, rl, wide, vec)
    gbqkv = by_kind(gbqkv)
    small = [gg1, gb1, gbqkv[:, :D], gbqkv[:, 2 * D:], gbo, gg2, gb2, gbd]
    give = lambda v: lax.psum_scatter(v.astype(F32), axes, scatter_dimension=0, tiled=True)
    return (
        outputs, input_grad, give(by_kind(gqkv)), give(gout), give(gup), give(gdown),
        [give(v[0]) for v in small], give(gbu[0]),
    )


def on_device(
    copies, inputs, row_kind, ln1_gain, ln1_bias, w_qkv, b_query, b_value, w_out, b_out, ln2_gain, ln2_bias,
    w_up, b_up, w_down, b_down, out_grad,
):
    vectors = (ln1_gain, ln1_bias, b_query, b_value, b_out, ln2_gain, ln2_bias, b_down)
    run = with_own_copies if copies else with_collectives
    outputs, input_grad, gqkv, gout, gup, gdown, small, gbu = run(
        inputs, row_kind, w_qkv, w_out, w_up, w_down, vectors, b_up, out_grad)
    gg1, gb1, gbq, gbv, gbo, gg2, gb2, gbd = small
    return outputs, input_grad, gg1, gb1, gqkv, gbq, gbv, gout, gbo, gg2, gb2, gup, gbu, gdown, gbd


def solution(mesh):
    both = ("dp", "fsdp")
    row = P(both)
    mat = P(both, None)
    act = P(both, None, None)
    in_specs = (act, row, row, row, mat, row, row, mat, row, row, row, mat, row, mat, row, act)
    out_specs = (act, act, row, row, mat, row, row, mat, row, row, row, mat, row, mat, row)
    copies = mesh.shape["dp"] == 2 * NZ and mesh.shape["fsdp"] == 4
    return jax.shard_map(
        functools.partial(on_device, copies), mesh=mesh, in_specs=in_specs, out_specs=out_specs, check_vma=False
    )
```

```python
import functools
import math

import jax
import jax.numpy as jnp
from jax import lax
from jax.experimental import pallas as pl
from jax.experimental.pallas import tpu as pltpu
from jax.sharding import PartitionSpec as P

D = 768
HD = 64
FF = 3072
SEQ = 529
HALF = 264
EPS = 1e-06
S = 544
T = 2 * S
MB = 272
HG = 4
QW = HG * HD
GW = 3 * QW
FC = 512
OUT_AT = 3 * D
UP_AT = 4 * D
AW = 4 * D + FF
F32 = jnp.float32
BF = jnp.bfloat16
LIMIT = 62 * 2**20
MESH = pl.DeviceIdType.MESH
NN = (((1,), (0,)), ((), ()))
NT = (((1,), (1,)), ((), ()))
TN = (((0,), (0,)), ((), ()))


def mm(a, b, dims=NN):
    return lax.dot_general(a, b, dims, preferred_element_type=F32)


def norm_parts(values):
    mean = jnp.mean(values, -1, keepdims=True)
    centred = values - mean
    inverse = lax.rsqrt(jnp.mean(centred * centred, -1, keepdims=True) + EPS)
    return centred * inverse, inverse


def norm_pull(grad, normed, inverse, gain):
    scaled = grad * gain
    return inverse * (
        scaled
        - jnp.mean(scaled, -1, keepdims=True)
        - normed * jnp.mean(scaled * normed, -1, keepdims=True)
    )


def gelu_both(u):
    a = jnp.abs(u)
    t = 1.0 / (1.0 + (0.3275911 / math.sqrt(2.0)) * a)
    e = jnp.exp(-0.5 * u * u)
    poly = t * (
        0.254829592
        + t * (-0.284496736 + t * (1.421413741 + t * (-1.453152027 + t * 1.061405429)))
    )
    tail = 0.5 * poly * e
    phi = jnp.where(u < 0, tail, 1.0 - tail)
    return u * phi, phi + u * e * (1.0 / math.sqrt(2.0 * math.pi))


def head_lanes(shape, e):
    lane = lax.broadcasted_iota(jnp.int32, shape, 1)
    return (lane // HD) == e


def whole(shape):
    return pl.BlockSpec(shape, lambda *_: (0,) * len(shape))


def rows_of(i):
    return pl.ds(pl.multiple_of(i * MB, 16), MB)


def row_of(i):
    return pl.ds(pl.multiple_of(i * S, 16), S)


G1, B1, BQ, BV, BO, G2, B2, BD = range(8)


def attn_fwd_kernel(
    kind_ref, x_ref, wg_ref, bqkv_ref, wo_ref, vec_ref,
    h1_ref, qkv_ref, p_ref, attn_ref, rl_ref, x1_ref, fa, fb,
):
    hq, r = pl.program_id(0), pl.program_id(1)

    @pl.when((hq == 0) & (r == 0))
    def _():
        for row in range(2):
            h1_ref[pl.ds(row * S + S - 16, 16), :] = jnp.zeros((16, D), BF)
            n1, _s = norm_parts(x_ref[row].astype(F32))
            h1_ref[pl.ds(row * S, SEQ), :] = (n1 * vec_ref[G1:G1 + 1, :] + vec_ref[B1:B1 + 1, :]).astype(BF)
            slot = lax.broadcasted_iota(jnp.int32, (S, 128), 0)
            lane = lax.broadcasted_iota(jnp.int32, (S, 128), 1)
            packed = jnp.where(slot < HALF, 0, jnp.where(slot < 2 * HALF, 1, 2))
            seg = jnp.where(kind_ref[row] == 1, packed, 0)
            fa[row] = jnp.where((lane < 3) & (seg == lane), -1e30, 0.0).astype(BF)
            fb[row] = jnp.where((lane < 3) & ((seg != lane) | (slot >= SEQ)), 1.0, 0.0).astype(BF)

    @pl.when(r == 0)
    def _():
        @pl.loop(0, T // MB)
        def _(i):
            rows = rows_of(i)
            qkv_ref[rows, :] = (mm(h1_ref[rows, :], wg_ref[...]) + bqkv_ref[...]).astype(BF)

    rows = pl.ds(pl.multiple_of(r * S, 16), S)
    feat_q, feat_k = fa[r], fb[r]
    ones = jnp.ones((S, 128), BF)
    scale = math.log2(math.e) / math.sqrt(HD)
    for j in range(HG // 2):
        at = j * 384
        qp, kp, vp = (qkv_ref[rows, at + 128 * n: at + 128 * (n + 1)] for n in range(3))
        kcat = jnp.concatenate([kp, feat_k], 1)
        total = None
        inv = None
        for e in range(2):
            keep = head_lanes((S, 128), e)
            qcat = jnp.concatenate([jnp.where(keep, qp, jnp.zeros_like(qp)), feat_q], 1)
            s = mm(qcat, kcat, NT)
            m = jnp.max(s, -1, keepdims=True)
            pb = jnp.exp2((s - m) * scale).astype(BF)
            p_ref[0, 2 * j + e] = pb
            vcat = jnp.concatenate([jnp.where(keep, vp, jnp.zeros_like(vp)), ones], 1)
            o = mm(pb, vcat)
            rl = 1.0 / o[:, 128:]
            part = o[:, :128] * rl
            total = part if total is None else total + part
            inv = rl if inv is None else jnp.where(keep, rl, inv)
        out = pl.ds(pl.multiple_of(hq * QW + j * 128, 128), 128)
        attn_ref[rows, out] = total.astype(BF)
        rl_ref[rows, out] = inv

    @pl.when((hq == D // QW - 1) & (r == 1))
    def _():
        for row in range(2):
            x1_ref[pl.ds(row * S + S - 16, 16), :] = jnp.zeros((16, D), F32)
            x1_ref[pl.ds(row * S, SEQ), :] = x_ref[row].astype(F32)

        @pl.loop(0, T // MB)
        def _(i):
            rr = rows_of(i)
            x1_ref[rr, :] = x1_ref[rr, :] + mm(attn_ref[rr, :], wo_ref[...]) + vec_ref[BO:BO + 1, :]


def attn_fwd(kind, x, wide, bqkv, vec):
    return pl.pallas_call(
        attn_fwd_kernel,
        grid=(D // QW, 2),
        in_specs=[
            pl.BlockSpec(memory_space=pltpu.SMEM), whole((2, SEQ, D)),
            pl.BlockSpec((D, GW), lambda h, r: (0, h)), pl.BlockSpec((1, GW), lambda h, r: (0, h)),
            pl.BlockSpec((D, D), lambda h, r: (0, 3)), whole((8, D)),
        ],
        out_specs=[
            whole((T, D)), pl.BlockSpec((T, GW), lambda h, r: (0, h)),
            pl.BlockSpec((1, HG, S, S), lambda h, r: (r, h, 0, 0)),
            whole((T, D)), whole((T, D)), whole((T, D)),
        ],
        out_shape=[
            jax.ShapeDtypeStruct((T, D), BF), jax.ShapeDtypeStruct((T, 3 * D), BF),
            jax.ShapeDtypeStruct((2, D // HD, S, S), BF),
            jax.ShapeDtypeStruct((T, D), BF), jax.ShapeDtypeStruct((T, D), F32), jax.ShapeDtypeStruct((T, D), F32),
        ],
        scratch_shapes=[pltpu.VMEM((2, S, 128), BF), pltpu.VMEM((2, S, 128), BF)],
        compiler_params=pltpu.CompilerParams(vmem_limit_bytes=LIMIT),
        name="attention_forward",
    )(kind, x, wide, bqkv, wide, vec)


def ffn_kernel(
    x1_ref, dm_ref, wu_ref, wd_ref, bu_ref, vec_ref,
    out_ref, dx1_ref, gwu_ref, gwd_ref, gbu_ref, gg2_ref, gb2_ref, gbd_ref,
    h2, h2t, dm, yacc, dacc, gs, dus,
):
    c = pl.program_id(0)

    @pl.when(c == 0)
    def _():
        for row in range(2):
            dm[pl.ds(row * S + S - 16, 16), :] = jnp.zeros((16, D), BF)
            dm[pl.ds(row * S, SEQ), :] = dm_ref[row]

        @pl.loop(0, T // MB)
        def _(i):
            rows = rows_of(i)
            x1 = x1_ref[rows, :]
            n2, _s = norm_parts(x1)
            h2[rows, :] = (n2 * vec_ref[G2:G2 + 1, :] + vec_ref[B2:B2 + 1, :]).astype(BF)
            yacc[rows, :] = x1 + vec_ref[BD:BD + 1, :]
            dacc[rows, :] = jnp.zeros((MB, D), F32)
        h2t[...] = h2[...].T
        gbd_ref[...] = jnp.sum(dm[...].astype(F32), 0, keepdims=True)

    gbu_ref[...] = jnp.zeros_like(gbu_ref)

    @pl.loop(0, T // MB)
    def _(i):
        rows = rows_of(i)
        u = mm(h2[rows, :], wu_ref[...]) + bu_ref[...]
        g, slope = gelu_both(u)
        gb = g.astype(BF)
        gs[rows, :] = gb
        yacc[rows, :] += mm(gb, wd_ref[...])
        du = (mm(dm[rows, :], wd_ref[...], NT) * slope).astype(BF)
        dus[rows, :] = du
        gbu_ref[...] += jnp.sum(du.astype(F32), 0, keepdims=True)
        dacc[rows, :] += mm(du, wu_ref[...], NT)

    for t in range(FC // 256):
        cols = pl.ds(t * 256, 256)
        gwd_ref[cols, :] = mm(gs[:, cols], dm[...], TN).astype(BF)

    @pl.loop(0, D // 256)
    def _(t):
        rows = pl.ds(pl.multiple_of(t * 256, 256), 256)
        gwu_ref[rows, :] = mm(h2t[rows, :], dus[...]).astype(BF)

    @pl.when(c == FF // FC - 1)
    def _():
        gg2_ref[...] = jnp.zeros_like(gg2_ref)
        gb2_ref[...] = jnp.zeros_like(gb2_ref)
        for row in range(2):
            out_ref[row] = yacc[pl.ds(row * S, SEQ), :].astype(BF)

        @pl.loop(0, T // MB)
        def _(i):
            rows = rows_of(i)
            n2, s2 = norm_parts(x1_ref[rows, :])
            dh = dacc[rows, :]
            gg2_ref[...] += jnp.sum(dh * n2, 0, keepdims=True)
            gb2_ref[...] += jnp.sum(dh, 0, keepdims=True)
            dx1_ref[rows, :] = dm[rows, :].astype(F32) + norm_pull(dh, n2, s2, vec_ref[G2:G2 + 1, :])


def ffn(x1, dm, wide, down, bu, vec):
    one = jax.ShapeDtypeStruct((1, D), F32)
    return pl.pallas_call(
        ffn_kernel,
        grid=(FF // FC,),
        in_specs=[
            whole((T, D)), whole((2, SEQ, D)),
            pl.BlockSpec((D, FC), lambda c: (0, c + UP_AT // FC)), pl.BlockSpec((FC, D), lambda c: (c, 0)),
            pl.BlockSpec((1, FC), lambda c: (0, c)), whole((8, D)),
        ],
        out_specs=[
            whole((2, SEQ, D)), whole((T, D)),
            pl.BlockSpec((D, FC), lambda c: (0, c)), pl.BlockSpec((FC, D), lambda c: (c, 0)),
            pl.BlockSpec((1, FC), lambda c: (0, c)), whole((1, D)), whole((1, D)), whole((1, D)),
        ],
        out_shape=[
            jax.ShapeDtypeStruct((2, SEQ, D), BF), jax.ShapeDtypeStruct((T, D), F32),
            jax.ShapeDtypeStruct((D, FF), BF), jax.ShapeDtypeStruct((FF, D), BF),
            jax.ShapeDtypeStruct((1, FF), F32), one, one, one,
        ],
        scratch_shapes=[
            pltpu.VMEM((T, D), BF), pltpu.VMEM((D, T), BF), pltpu.VMEM((T, D), BF),
            pltpu.VMEM((T, D), F32), pltpu.VMEM((T, D), F32),
            pltpu.VMEM((T, FC), BF), pltpu.VMEM((T, FC), BF),
        ],
        compiler_params=pltpu.CompilerParams(vmem_limit_bytes=LIMIT),
        name="feed_forward",
    )(x1, dm, wide, down, bu, vec)


def attn_bwd_kernel(
    x_ref, dx1_ref, h1_ref, qkv_ref, p_ref, attn_ref, rl_ref, wo_ref, wqkv_ref, vec_ref,
    gx_ref, gwqkv_ref, gwo_ref, gbqkv_ref, gbo_ref, gg1_ref, gb1_ref,
    da, dos, h1t, dqkv,
):
    hq, r = pl.program_id(0), pl.program_id(1)

    @pl.when((hq == 0) & (r == 0))
    def _():
        gbo_ref[...] = jnp.zeros_like(gbo_ref)

        @pl.loop(0, T // MB)
        def _(i):
            rows = rows_of(i)
            d = dx1_ref[rows, :].astype(BF)
            da[rows, :] = d
            gbo_ref[...] += jnp.sum(d.astype(F32), 0, keepdims=True)
            dos[rows, :] = (mm(d, wo_ref[...], NT) * rl_ref[rows, :]).astype(BF)
        h1t[...] = h1_ref[...].T

    rows = pl.ds(pl.multiple_of(r * S, 16), S)
    scale = 1.0 / math.sqrt(HD)
    for j in range(HG // 2):
        at = j * 384
        qp, kp, vp = (qkv_ref[rows, at + 128 * n: at + 128 * (n + 1)] for n in range(3))
        do = dos[rows, pl.ds(pl.multiple_of(hq * QW + j * 128, 128), 128)]
        prod = do.astype(F32) * attn_ref[rows, j * 128:(j + 1) * 128].astype(F32)
        dq = dk = dv = None
        for e in range(2):
            keep = head_lanes((S, 128), e)
            zero = jnp.zeros_like(qp)
            doe = jnp.where(keep, do, zero)
            dot = jnp.sum(jnp.where(keep, prod, 0.0), -1, keepdims=True)
            p = p_ref[0, 2 * j + e]
            ds = (p.astype(F32) * (mm(doe, vp, NT) - dot)).astype(BF)
            a = mm(ds, jnp.where(keep, kp, zero))
            b = mm(ds, jnp.where(keep, qp, zero), TN)
            c = mm(p, doe, TN)
            dq, dk, dv = (a, b, c) if dq is None else (dq + a, dk + b, dv + c)
        for n, part in enumerate((dq * scale, dk * scale, dv)):
            col = hq * GW + j * 384 + n * 128
            dqkv[rows, pl.ds(pl.multiple_of(col, 128), 128)] = part.astype(BF)

    @pl.when(r == 1)
    def _():
        part = dqkv[:, pl.ds(pl.multiple_of(hq * GW, 128), GW)]
        gbqkv_ref[...] = jnp.sum(part.astype(F32), 0, keepdims=True)

        @pl.loop(0, D // 256)
        def _(t):
            rr = pl.ds(pl.multiple_of(t * 256, 256), 256)
            gwqkv_ref[rr, :] = mm(h1t[rr, :], part).astype(BF)
        gwo_ref[...] = mm(attn_ref[...], da[...], TN).astype(BF)

    @pl.when((hq == D // QW - 1) & (r == 1))
    def _():
        gg1_ref[...] = jnp.zeros_like(gg1_ref)
        gb1_ref[...] = jnp.zeros_like(gb1_ref)
        for row in range(2):
            rr = pl.ds(row * S, SEQ)
            dh = mm(dqkv[pl.ds(row * S, S), :], wqkv_ref[...], NT)[:SEQ]
            n1, s1 = norm_parts(x_ref[row].astype(F32))
            gg1_ref[...] += jnp.sum(dh * n1, 0, keepdims=True)
            gb1_ref[...] += jnp.sum(dh, 0, keepdims=True)
            gx_ref[row] = (dx1_ref[rr, :] + norm_pull(dh, n1, s1, vec_ref[G1:G1 + 1, :])).astype(BF)


def attn_bwd(x, dx1, h1, qkv, p, attn, rl, wide, vec):
    act = pl.BlockSpec((T, QW), lambda h, r: (0, h))
    one = jax.ShapeDtypeStruct((1, D), F32)
    return pl.pallas_call(
        attn_bwd_kernel,
        grid=(D // QW, 2),
        in_specs=[
            whole((2, SEQ, D)), whole((T, D)), whole((T, D)), pl.BlockSpec((T, GW), lambda h, r: (0, h)),
            pl.BlockSpec((1, HG, S, S), lambda h, r: (r, h, 0, 0)), act, whole((T, D)),
            pl.BlockSpec((D, D), lambda h, r: (0, 3)), whole((D, 3 * D)), whole((8, D)),
        ],
        out_specs=[
            whole((2, SEQ, D)), pl.BlockSpec((D, GW), lambda h, r: (0, h)),
            pl.BlockSpec((QW, D), lambda h, r: (h, 0)),
            pl.BlockSpec((1, GW), lambda h, r: (0, h)), whole((1, D)), whole((1, D)), whole((1, D)),
        ],
        out_shape=[
            jax.ShapeDtypeStruct((2, SEQ, D), BF), jax.ShapeDtypeStruct((D, 3 * D), BF), jax.ShapeDtypeStruct((D, D), BF),
            jax.ShapeDtypeStruct((1, 3 * D), F32), one, one, one,
        ],
        scratch_shapes=[
            pltpu.VMEM((T, D), BF), pltpu.VMEM((T, D), BF), pltpu.VMEM((D, T), BF), pltpu.VMEM((T, 3 * D), BF),
        ],
        compiler_params=pltpu.CompilerParams(vmem_limit_bytes=LIMIT),
        name="attention_backward",
    )(x, dx1, h1, qkv, p, attn, rl, wide, wide, vec)


NZ = 4
CH = 48
HW = 384
SR = 16
N_WIDE = AW // (2 * HW)
N_DOWN = 4
N_UP = FF // D
DH = 2 * CH
NV = 8
VW = (24,) * NV + (96,)


def one(i):
    return pl.ds(i, 1)


EVERY = pl.ds(0, NZ)
TWO = pl.ds(0, 2)


def where_am_i():
    dp, fs = lax.axis_index("dp"), lax.axis_index("fsdp")
    return lax.div(dp, 2), lax.rem(dp, 2), lax.div(fs, 2), lax.rem(fs, 2)


def device(z, x, y, c):
    return (z * 2 + x, y * 2 + c)


def partners(z, x, y, c):
    found = [device(lax.rem(z + k, NZ), x, y, c) for k in (1, 2, 3)]
    return found + [device(z, 1 - x, y, c), device(z, x, 1 - y, c), device(z, x, y, 1 - c)]


def say_hello(here):
    barrier = pltpu.get_barrier_semaphore()
    for other in partners(*here):
        pl.semaphore_signal(barrier, inc=1, device_id=other, device_id_type=MESH)


def await_all():
    pl.semaphore_wait(pltpu.get_barrier_semaphore(), 6)


def remote(src, dst, sems, n, target):
    return pltpu.make_async_remote_copy(
        src_ref=src, dst_ref=dst, send_sem=sems[0].at[n], recv_sem=sems[1].at[n],
        device_id=target, device_id_type=MESH,
    )


def half(i, core):
    return pl.ds(pl.multiple_of(i * 2 * HW + core * HW, 128), HW)


def down_rows(i, core):
    return pl.ds(pl.multiple_of(core * DH + (i // 2) * CH, 16), CH)


def down_cols(i):
    return pl.ds((i % 2) * HW, HW)


TOK = 48


def rows_in(src, row, *targets):
    for ref in targets:
        ref[pl.ds(row * S + S - 16, 16), :] = jnp.zeros((16, D), ref.dtype)

    @pl.loop(0, SEQ // TOK)
    def _(i):
        part = src[pl.ds(i * TOK, TOK), row, :]
        for ref in targets:
            ref[pl.ds(pl.multiple_of(row * S + i * TOK, 16), TOK), :] = part.astype(ref.dtype)
    last = src[SEQ - 1:SEQ, row, :]
    for ref in targets:
        ref[pl.ds(row * S + SEQ - 1, 1), :] = last.astype(ref.dtype)


def rows_out(src, target, row):
    @pl.loop(0, SEQ // TOK)
    def _(i):
        target[pl.ds(i * TOK, TOK), row, :] = src[pl.ds(pl.multiple_of(row * S + i * TOK, 16), TOK), :]
    target[SEQ - 1:SEQ, row, :] = src[pl.ds(row * S + SEQ - 1, 1), :]


def transpose_into(target, src):
    @pl.loop(0, D // 128)
    def _(i):
        cols = pl.ds(pl.multiple_of(i * 128, 128), 128)
        target[cols, :] = src[:, cols].T


def add(a, b):
    return (a.astype(F32) + b.astype(F32)).astype(BF)


def plan(entries, ticks):
    table = {n: [] for n in range(len(ticks))}
    rest = []
    for due, action in sorted(entries, key=lambda e: e[0]):
        slot = min((n for n, t in enumerate(ticks) if t >= due), default=None)
        (rest if slot is None else table[slot]).append(action)
    return table, rest


class Gather:
    COPIES = 7

    def __init__(self, here, sems, base, view, first):
        z, x, y, c = here
        peers = partners(*here)
        mine = view(one(z), one(x), one(y))
        column = view(EVERY, one(x), one(y))
        fx, fy = jnp.where(c == 0, 1 - x, x), jnp.where(c == 0, y, 1 - y)
        tx, ty = jnp.where(c == 0, x, 1 - x), jnp.where(c == 0, 1 - y, y)
        passed = view(EVERY, one(fx), one(fy))
        all_of = view(EVERY, TWO, TWO)
        make = lambda n, src, dst, to: remote(src, dst, sems, base + n, to)
        self.along_z = [make(k, mine if first is None else first, mine, peers[k]) for k in range(3)]
        self.along_x = make(3, column, column, peers[3])
        self.along_y = make(4, column, column, peers[4])
        self.diagonal = make(5, passed, passed, device(z, tx, ty, c))
        self.sibling = make(6, all_of, all_of, peers[5])

    def start(self, phase):
        if phase == 0:
            for copy in self.along_z:
                copy.start()
        elif phase == 1:
            for copy in self.along_z:
                copy.wait_recv()
            self.along_x.start()
            self.along_y.start()
        elif phase == 2:
            self.along_x.wait_recv()
            self.along_y.wait_recv()
            self.diagonal.start()
        elif phase == 3:
            self.diagonal.wait_recv()
            self.sibling.start()
        else:
            self.sibling.wait_recv()

    def drain(self):
        for copy in (*self.along_z, self.along_x, self.along_y, self.diagonal, self.sibling):
            copy.wait_send()


class Scatter:
    COPIES = 7

    def __init__(self, here, sems, base, theirs, mine, acc, via, last, zs):
        self.mine, self.acc, self.via, self.last, self.zs = mine, acc, via, last, zs
        z, x, y, c = self.here = here
        peers = partners(*here)
        ix, iy = jnp.where(c == 0, x, 1 - x), jnp.where(c == 0, 1 - y, y)
        self.px, self.py = jnp.where(c == 0, 1 - x, x), jnp.where(c == 0, y, 1 - y)
        first, second = device(z, ix, iy, c), device(z, self.px, self.py, c)
        make = lambda n, src, dst, to: remote(src, dst, sems, base + n, to)
        at = lambda xs, ys: acc.at[EVERY, one(xs), one(ys)]
        self.swap = make(0, theirs, acc, peers[5])
        self.far = make(1, at(1 - x, 1 - y), via.at[0], first)
        self.near = make(2, at(ix, iy), via.at[1], first)
        self.next = make(3, at(self.px, self.py), last, second)
        self.along_z = [
            make(4 + k, acc.at[one(lax.rem(z + k + 1, NZ)), one(x), one(y)], zs.at[k], peers[k]) for k in range(3)
        ]

    def start(self, phase):
        z, x, y, c = self.here
        acc = self.acc
        if phase == 0:
            self.swap.start()
        elif phase == 1:
            self.swap.wait_recv()

            @pl.loop(0, NZ)
            def _(i):
                for xi in range(2):
                    for yi in range(2):
                        acc[i, xi, yi] = add(acc[i, xi, yi], self.mine(i, xi, yi))
            self.far.start()
            self.near.start()
        elif phase == 2:
            self.far.wait_recv()
            px, py = self.px, self.py

            @pl.loop(0, NZ)
            def _(i):
                acc[i, px, py] = add(acc[i, px, py], self.via[0, i, 0, 0])
            self.next.start()
            self.near.wait_recv()

            @pl.loop(0, NZ)
            def _(i):
                acc[i, x, y] = add(acc[i, x, y], self.via[1, i, 0, 0])
        elif phase == 3:
            self.next.wait_recv()

            @pl.loop(0, NZ)
            def _(i):
                acc[i, x, y] = add(acc[i, x, y], self.last[i, 0, 0])
            for copy in self.along_z:
                copy.start()

    def total(self):
        z, x, y, c = self.here
        for copy in self.along_z:
            copy.wait_recv()
        parts = [self.acc[z, x, y]] + [self.zs[k, 0, 0, 0] for k in range(3)]
        return sum(part.astype(F32) for part in parts)

    def drain(self):
        for copy in (self.swap, self.far, self.near, self.next, *self.along_z):
            copy.wait_send()


def scatter_bufs(n, width):
    return [
        pltpu.VMEM((n, NZ, 2, 2, CH, width), BF), pltpu.VMEM((n, 2, NZ, 1, 1, CH, width), BF),
        pltpu.VMEM((n, NZ, 1, 1, CH, width), BF), pltpu.VMEM((n, 3, 1, 1, 1, CH, width), BF),
    ]


def dma_sems(*counts):
    return [pltpu.SemaphoreType.DMA((k,)) for k in counts]


def fixed(shape):
    return pl.BlockSpec(shape, lambda s: (0,) * len(shape), pipeline_mode=pl.Buffered(1))


def vmem():
    return pl.BlockSpec(memory_space=pltpu.VMEM)


def hbm():
    return pl.BlockSpec(memory_space=pl.ANY)


N_ATT = 2 * (D // QW)
PACE = 5.4
FORWARD_LAG = (0.0, 8.0, 20.0, 28.0, 34.0)
FORWARD_FROM = 26.0
FIRST_PACE = 3.6
FORWARD_PACE = 5.4
FORWARD_TICKS = [FORWARD_FROM + 2.9 * n for n in range(12)] + [FORWARD_FROM + 35.0 + 2.1 * n for n in range(16)]


def forward_kernel(
    kind_ref, x_ref, dm_ref, wqkv_ref, wout_ref, wup_ref, wdown_ref, *refs,
):
    small_refs = refs[:NV + 1]
    (
        h1t_out, qkv_ref, p_ref, attn_out, rl_out, x1_out, dmp_out, h2t_out, g_ref, slope_ref, gdown_ref,
        vec_ref, xb_out, watt_out, wup_out, down_out,
        h1t_ref, attn_ref, rl_ref, x1_ref, dmp_ref, h2t_ref, xb_ref, out_sem,
        fa, fb, h1, h2, staged, swap, watt, wup, bqkv, bu, smalls,
        sems_s, sems_r, swap_s, swap_r, small_s, small_r, copy_sem,
    ) = refs[NV + 1:]
    step = pl.program_id(0)
    here = where_am_i()
    z, x, y, c = here
    peers = partners(*here)
    sems = (sems_s, sems_r)

    swaps = [
        remote(staged.at[:, half(i, 1 - c)], swap.at[:, i * HW:(i + 1) * HW], (swap_s, swap_r), i, peers[5])
        for i in range(N_WIDE)
    ]
    items, own = [], []
    for i in range(N_WIDE):
        buf, at = (watt, i) if i < 4 else (wup, i - 4)
        view = lambda zs, xs, ys, buf=buf, at=at: buf.at[zs, xs, ys, :, half(at, c)]
        items.append(Gather(here, sems, i * Gather.COPIES, view, None))
    for i in range(N_DOWN):
        rows, cols = down_rows(i, c), down_cols(i)
        view = lambda zs, xs, ys, rows=rows, cols=cols: down_out.at[zs, xs, ys, rows, cols]
        first = wdown_ref.at[:, :, :, pl.ds((i // 2) * CH, CH), cols]
        items.append(Gather(here, sems, (N_WIDE + i) * Gather.COPIES, view, first))
        own.append(pltpu.make_async_copy(first, view(one(z), one(x), one(y)), copy_sem.at[N_WIDE + i]))
    keeps = []
    for i in range(N_WIDE):
        src, dst, at = (watt, watt_out, i) if i < 4 else (wup, wup_out, i - 4)
        cols = pl.ds(at * D, D)
        keeps.append(pltpu.make_async_copy(
            src.at[:, :, :, :, cols], dst.at[:, :, :, :, cols], copy_sem.at[i]))

    first_out = [
        pltpu.make_async_copy(a, b, out_sem.at[n])
        for n, (a, b) in enumerate(((h1t_ref, h1t_out), (dmp_ref, dmp_out), (xb_ref, xb_out)))
    ]
    next_out = [
        pltpu.make_async_copy(a, b, out_sem.at[3 + n])
        for n, (a, b) in enumerate(((attn_ref, attn_out), (rl_ref, rl_out), (x1_ref, x1_out), (h2t_ref, h2t_out)))
    ]

    def act(action):
        i, phase = action
        if i >= N_WIDE and phase == 0:
            own[i - N_WIDE].start()
        if i >= N_WIDE and phase == 1:
            own[i - N_WIDE].wait()
        items[i].start(phase)
        if phase == 4 and i < N_WIDE:
            keeps[i].start()

    needed = {1: 4, 2: 8, 3: 11, 4: 12, 5: 16, 6: 20, 7: 24}
    entries = []
    for i in range(1, N_WIDE + N_DOWN):
        for phase in range(5):
            due = FORWARD_PACE * i + FORWARD_LAG[phase] if phase else FIRST_PACE * i
            if i in needed:
                due = min(due, FORWARD_TICKS[needed[i]])
            entries.append((due, (i, phase)))
    early = [a for t, a in sorted(entries, key=lambda e: e[0]) if t < FORWARD_FROM]
    table, late = plan([e for e in entries if e[0] >= FORWARD_FROM], FORWARD_TICKS)

    def tick(slot, could_be):
        for n in could_be:
            if table[n]:
                @pl.when(slot == n)
                def _(n=n):
                    for action in table[n]:
                        act(action)

    @pl.when(step == 0)
    def _():
        say_hello(here)
        for pair in range(6):
            for n in range(3):
                at = pair * 384 + n * 128
                staged[:, at:at + 128] = wqkv_ref[:, n * D + pair * 128:n * D + (pair + 1) * 128].astype(F32)
        staged[:, OUT_AT:UP_AT] = wout_ref[...].astype(F32)
        staged[:, UP_AT:] = wup_ref[...].astype(F32)
        line = smalls.at[z, x, y, c]
        line[...] = jnp.zeros((SR, 128), F32)
        for n, (ref, width) in enumerate(zip(small_refs, VW)):
            line[n:n + 1, 0:width] = ref[...].astype(F32).reshape(1, width)
        await_all()
        swaps[0].start()

        def small_copy(n, src, to):
            return remote(src, src, (small_s, small_r), n, to)

        small_c = small_copy(0, smalls.at[one(z), one(x), one(y), one(c)], peers[5])
        both = smalls.at[one(z), one(x), one(y), TWO]
        small_z = [small_copy(1 + k, both, peers[k]) for k in range(3)]
        small_x = small_copy(4, smalls.at[EVERY, one(x), one(y), TWO], peers[3])
        small_y = small_copy(5, smalls.at[EVERY, TWO, one(y), TWO], peers[4])
        small_c.start()
        for i in range(1, N_WIDE):
            swaps[i].start()

        def take_block(i):
            swaps[i].wait_recv()
            mine_part = staged[:, half(i, c)]
            their_part = swap[:, i * HW:(i + 1) * HW]
            buf, at = (watt, i) if i < 4 else (wup, i - 4)
            lower = jnp.where(c == 0, mine_part, their_part)
            upper = jnp.where(c == 0, their_part, mine_part)
            buf[z, x, y, :, half(at, c)] = jnp.concatenate([lower, upper], 0).astype(BF)

        waiting = list(early)

        def act_some(count):
            for _n in range(min(count, len(waiting))):
                act(waiting.pop(0))

        take_block(0)
        items[0].start(0)
        small_c.wait_recv()
        for copy in small_z:
            copy.start()
        for i in range(1, N_WIDE):
            take_block(i)
        rows_in(x_ref, 0, x1_ref, xb_ref)
        for copy in small_z:
            copy.wait_recv()
        small_x.start()
        act_some(1)
        items[0].start(1)
        rows_in(x_ref, 1, x1_ref, xb_ref)
        small_x.wait_recv()
        small_y.start()
        act_some(1)
        items[0].start(2)
        act_some(1)
        for row in range(2):
            rows_in(dm_ref, row, dmp_ref)
        items[0].start(3)
        small_y.wait_recv()
        src = lax.broadcasted_iota(jnp.int32, (128, D), 0)
        dst = lax.broadcasted_iota(jnp.int32, (128, D), 1)
        spread_short = jnp.where(lax.rem(dst, 24) == src, 1.0, 0.0).astype(BF)
        spread_long = jnp.where(lax.rem(dst, 96) == src, 1.0, 0.0).astype(BF)
        col = lax.broadcasted_iota(jnp.int32, (8, D), 1)
        vec_ref[...] = jnp.zeros_like(vec_ref)

        @pl.loop(0, NZ)
        def _(zi):
            pieces = smalls[zi].reshape(8 * SR, 128).astype(BF)
            short, long = mm(pieces, spread_short), mm(pieces, spread_long)
            for k in range(8):
                at = SR * k
                part = jnp.where(lax.div(col, 24) == zi * 8 + k, short[at:at + NV], 0.0)
                more = jnp.where(lax.div(col, 96) == k, long[at + NV:at + SR], 0.0)
                vectors, hidden_bias = (part, more) if k == 0 else (vectors + part, hidden_bias + more)
            vec_ref[...] += vectors
            bu[zi] = hidden_bias
        for pair in range(6):
            n, at = pair // 2, (pair % 2) * 384
            bqkv[n, :, at:at + 128] = vec_ref[BQ:BQ + 1, pair * 128:(pair + 1) * 128]
            bqkv[n, :, at + 128:at + 256] = jnp.zeros((1, 128), F32)
            bqkv[n, :, at + 256:at + 384] = vec_ref[BV:BV + 1, pair * 128:(pair + 1) * 128]
        act_some(2)

        @pl.loop(0, T // MB)
        def _(i):
            rows = rows_of(i)
            n1, _s = norm_parts(x1_ref[rows, :])
            h1[rows, :] = (n1 * vec_ref[G1:G1 + 1, :] + vec_ref[B1:B1 + 1, :]).astype(BF)
        for row in range(2):
            slot = lax.broadcasted_iota(jnp.int32, (S, 128), 0)
            lane = lax.broadcasted_iota(jnp.int32, (S, 128), 1)
            packed = jnp.where(slot < HALF, 0, jnp.where(slot < 2 * HALF, 1, 2))
            seg = jnp.where(kind_ref[row] == 1, packed, 0)
            fa[row] = jnp.where((lane < 3) & (seg == lane), -1e30, 0.0).astype(BF)
            fb[row] = jnp.where((lane < 3) & ((seg != lane) | (slot >= SEQ)), 1.0, 0.0).astype(BF)
        act_some(len(waiting))
        transpose_into(h1t_ref, h1)
        for copy in first_out:
            copy.start()
        rl_ref[...] = jnp.zeros_like(rl_ref)
        act((0, 4))
        for copy in (small_c, *small_z, small_x, small_y, *swaps):
            copy.wait_send()

    @pl.when(step < N_ATT)
    def _():
        hq, r = lax.div(step, 2), lax.rem(step, 2)
        tick(2 * step, range(0, 12, 2))

        @pl.when(r == 0)
        def _():
            @pl.loop(0, 2)
            def _(i):
                rows = row_of(i)
                w = watt[:, :, :, :, pl.ds(pl.multiple_of(hq * GW, 128), GW)].reshape(D, GW)
                qkv_ref[rows, :] = (mm(h1[rows, :], w) + bqkv[hq]).astype(BF)

        rows = pl.ds(pl.multiple_of(r * S, 16), S)
        feat_q, feat_k = fa[r], fb[r]
        ones = jnp.ones((S, 128), BF)
        scale = math.log2(math.e) / math.sqrt(HD)
        for j in range(HG // 2):
            if j:
                tick(2 * step + 1, range(1, 12, 2))
            at = j * 384
            qp, kp, vp = (qkv_ref[rows, at + 128 * n: at + 128 * (n + 1)] for n in range(3))
            kcat = jnp.concatenate([kp, feat_k], 1)
            total = None
            for e in range(2):
                keep = head_lanes((S, 128), e)
                qcat = jnp.concatenate([jnp.where(keep, qp, jnp.zeros_like(qp)), feat_q], 1)
                s = mm(qcat, kcat, NT)
                m = jnp.max(s, -1, keepdims=True)
                pb = jnp.exp2((s - m) * scale).astype(BF)
                p_ref[0, 2 * j + e] = pb
                vcat = jnp.concatenate([jnp.where(keep, vp, jnp.zeros_like(vp)), ones], 1)
                o = mm(pb, vcat)
                rl = 1.0 / o[:, 128:]
                part = o[:, :128] * rl
                total = part if total is None else total + part
                spot = lax.broadcasted_iota(jnp.int32, (S, 128), 1) == hq * HG + 2 * j + e
                rl_ref[rows, :] = jnp.where(spot, rl, rl_ref[rows, :])
            out = pl.ds(pl.multiple_of(hq * QW + j * 128, 128), 128)
            attn_ref[rows, out] = total.astype(BF)

    @pl.when(step == N_ATT - 1)
    def _():
        @pl.loop(0, T // MB)
        def _(i):
            rows = rows_of(i)
            wo = watt[:, :, :, :, OUT_AT:UP_AT].reshape(D, D)
            x1 = x1_ref[rows, :] + mm(attn_ref[rows, :], wo) + vec_ref[BO:BO + 1, :]
            x1_ref[rows, :] = x1
            n2, _s = norm_parts(x1)
            h2[rows, :] = (n2 * vec_ref[G2:G2 + 1, :] + vec_ref[B2:B2 + 1, :]).astype(BF)
        transpose_into(h2t_ref, h2)
        for copy in next_out:
            copy.start()

    @pl.when(step >= N_ATT)
    def _():
        part = step - N_ATT

        @pl.loop(0, 2)
        def _(i):
            tick(12 + 4 * part + 2 * i, range(12, len(FORWARD_TICKS), 2))
            tick(12 + 4 * part + 2 * i + 1, range(13, len(FORWARD_TICKS), 2))
            rows = row_of(i)
            w = wup[:, :, :, :, pl.ds(pl.multiple_of(part * D, 128), D)].reshape(D, D)
            g, slope = gelu_both(mm(h2[rows, :], w) + bu[part, 0:1, :])
            g_ref[rows, :] = g.astype(BF)
            slope_ref[rows, :] = slope.astype(BF)

        @pl.loop(0, 2)
        def _(t):
            cols = pl.ds(pl.multiple_of(t * 384, 128), 384)
            gdown_ref[cols, :] = mm(g_ref[:, cols], dmp_ref[...], TN).astype(BF)

    @pl.when(step == N_ATT + N_UP - 1)
    def _():
        for action in late:
            act(action)
        for item in items:
            item.drain()
        for copy in (*keeps, *first_out, *next_out):
            copy.wait()


def forward(kind, x, dm, wqkv, wout, wup, wdown, smalls):
    n = N_WIDE + N_DOWN
    att = lambda s: jnp.minimum(s, N_ATT - 1)
    ff = lambda s: jnp.maximum(s - N_ATT, 0)
    shape = jax.ShapeDtypeStruct
    return pl.pallas_call(
        forward_kernel,
        grid=(N_ATT + N_UP,),
        in_specs=[
            pl.BlockSpec(memory_space=pltpu.SMEM), fixed((SEQ, 2, D)), fixed((SEQ, 2, D)),
            fixed((24, 3 * D)), fixed((24, D)), fixed((24, FF)), fixed((1, 1, 1, 96, D)),
            *[pl.BlockSpec((w,), lambda s: (0,), pipeline_mode=pl.Buffered(1)) for w in VW],
        ],
        out_specs=[
            hbm(), pl.BlockSpec((T, GW), lambda s: (0, att(s) // 2)),
            pl.BlockSpec((1, HG, S, S), lambda s: (att(s) % 2, att(s) // 2, 0, 0)),
            hbm(), hbm(), hbm(), hbm(), hbm(),
            pl.BlockSpec((T, D), lambda s: (0, ff(s))), pl.BlockSpec((T, D), lambda s: (0, ff(s))),
            pl.BlockSpec((D, D), lambda s: (ff(s), 0)),
            fixed((NV, D)), hbm(), hbm(), hbm(), hbm(),
        ],
        out_shape=[
            shape((D, T), BF), shape((T, 3 * D), BF), shape((2, D // HD, S, S), BF),
            shape((T, D), BF), shape((T, 128), F32), shape((T, D), F32), shape((T, D), BF), shape((D, T), BF),
            shape((T, FF), BF), shape((T, FF), BF), shape((FF, D), BF), shape((NV, D), F32), shape((T, D), BF),
            shape((NZ, 2, 2, CH, UP_AT), BF), shape((NZ, 2, 2, CH, FF), BF), shape((NZ, 2, 2, 4 * CH, D), BF),
        ],
        scratch_shapes=[
            pltpu.VMEM((D, T), BF), pltpu.VMEM((T, D), BF), pltpu.VMEM((T, 128), F32), pltpu.VMEM((T, D), F32),
            pltpu.VMEM((T, D), BF), pltpu.VMEM((D, T), BF), pltpu.VMEM((T, D), BF), *dma_sems(7),
            pltpu.VMEM((2, S, 128), BF), pltpu.VMEM((2, S, 128), BF), pltpu.VMEM((T, D), BF), pltpu.VMEM((T, D), BF),
            pltpu.VMEM((24, AW), F32), pltpu.VMEM((24, AW // 2), F32),
            pltpu.VMEM((NZ, 2, 2, CH, UP_AT), BF), pltpu.VMEM((NZ, 2, 2, CH, FF), BF),
            pltpu.VMEM((3, 1, GW), F32), pltpu.VMEM((N_UP, 8, D), F32), pltpu.VMEM((NZ, 2, 2, 2, SR, 128), F32),
            *dma_sems(n * Gather.COPIES, n * Gather.COPIES, N_WIDE, N_WIDE, 6, 6, n),
        ],
        compiler_params=pltpu.CompilerParams(collective_id=0, has_side_effects=True, vmem_limit_bytes=LIMIT),
        name="forward",
    )(kind, x, dm, wqkv, wout, wup, wdown.reshape(1, 1, 1, 96, D), *smalls)


BACK_LAG = (0.0, 5.0, 15.0, 23.0, 32.0)
FFN_LAG = (0.0, 4.0, 13.0, 20.0, 27.0)
FFN_PACE = 4.0
FFN_TICKS = [4.0 + 9.0 * s + t for s in range(4) for t in (0.0, 0.1, 2.8, 2.9, 5.7, 7.3)]


def ffn_back_kernel(
    x1_in, dm_ref, g_ref, slope_ref, wu_ref, wd_ref, h2t_in, vec_ref, gdown_ref,
    y_ref, dx1_ref, da_ref, gup_ref, sums_ref, odown_ref,
    x1_ref, h2t_ref, in_sem, yacc, dacc, dus, mine, acc, via, last, zs, sems_s, sems_r, own_sem,
):
    step = pl.program_id(0)
    here = where_am_i()
    z, x, y, c = here
    items, own = [], []
    for i in range(N_DOWN):
        rows, cols = down_rows(i, c), down_cols(i)
        own.append(pltpu.make_async_copy(gdown_ref.at[:, :, :, rows, cols], mine.at[i], own_sem.at[i]))
        items.append(Scatter(
            here, (sems_s, sems_r), i * Scatter.COPIES, gdown_ref.at[EVERY, TWO, TWO, down_rows(i, 1 - c), cols],
            lambda a, b, d, i=i: mine[i, a, b, d], acc.at[i], via.at[i], last.at[i], zs.at[i],
        ))
    later = [
        pltpu.make_async_copy(a, b, in_sem.at[n])
        for n, (a, b) in enumerate(((h2t_in, h2t_ref), (x1_in, x1_ref)))
    ]
    entries = [
        (5.0 + FFN_PACE * i + lag, (i, phase)) for i in range(N_DOWN) for phase, lag in enumerate(FFN_LAG) if (i, phase) != (0, 0)
    ]
    table, late = plan(entries, FFN_TICKS)

    def act(action):
        i, phase = action
        if phase == 1:
            own[i].wait()
        if phase == 4:
            odown_ref[pl.ds((i // 2) * CH, CH), down_cols(i)] = items[i].total()
        else:
            items[i].start(phase)

    def tick(slot):
        for n, todo in table.items():
            if todo:
                @pl.when(slot == n)
                def _(todo=todo):
                    for action in todo:
                        act(action)

    @pl.when(step == 0)
    def _():
        say_hello(here)
        for copy in (*later, *own):
            copy.start()

        @pl.loop(0, T // MB)
        def _(i):
            rows = rows_of(i)
            yacc[rows, :] = jnp.broadcast_to(vec_ref[BD:BD + 1, :], (MB, D))
            dacc[rows, :] = jnp.zeros((MB, D), F32)
        sums_ref[...] = jnp.zeros_like(sums_ref)
        sums_ref[2:3, :] = jnp.sum(dm_ref[...].astype(F32), 0, keepdims=True)

    @pl.loop(0, 2)
    def _(i):
        @pl.when((step == 0) & (i == 1))
        def _():
            await_all()
            act((0, 0))

        tick(6 * step + 2 * i)
        tick(6 * step + 2 * i + 1)
        rows = row_of(i)
        g = g_ref[rows, :]
        yacc[rows, :] += mm(g, wd_ref[...])
        du = (mm(dm_ref[rows, :], wd_ref[...], NT) * slope_ref[rows, :].astype(F32)).astype(BF)
        dus[rows, :] = du
        sums_ref[pl.ds(3 + step, 1), :] += jnp.sum(du.astype(F32), 0, keepdims=True)
        dacc[rows, :] += mm(du, wu_ref[...], NT)

    @pl.when(step == 0)
    def _():
        later[0].wait()

    @pl.loop(0, 2)
    def _(t):
        tick(6 * step + 4 + t)
        rows = pl.ds(pl.multiple_of(t * 384, 128), 384)
        gup_ref[rows, :] = mm(h2t_ref[rows, :], dus[...]).astype(BF)

    @pl.when(step == N_UP - 1)
    def _():
        later[1].wait()

        @pl.loop(0, T // MB)
        def _(i):
            rows = rows_of(i)
            x1 = x1_ref[rows, :]
            n2, s2 = norm_parts(x1)
            dh = dacc[rows, :]
            sums_ref[0:1, :] += jnp.sum(dh * n2, 0, keepdims=True)
            sums_ref[1:2, :] += jnp.sum(dh, 0, keepdims=True)
            dx1 = dm_ref[rows, :].astype(F32) + norm_pull(dh, n2, s2, vec_ref[G2:G2 + 1, :])
            dx1_ref[rows, :] = dx1
            da_ref[rows, :] = dx1.astype(BF)
            y_ref[rows, :] = (x1 + yacc[rows, :]).astype(BF)
        for action in late:
            act(action)
        for item in items:
            item.drain()


def ffn_back(x1, dm, g, slope, wup, down, h2t, vec, gdown):
    shape = jax.ShapeDtypeStruct
    col = pl.BlockSpec((T, D), lambda s: (0, s))
    return pl.pallas_call(
        ffn_back_kernel,
        grid=(N_UP,),
        in_specs=[
            hbm(), fixed((T, D)), col, col,
            pl.BlockSpec((D, D), lambda s: (0, s)), pl.BlockSpec((D, D), lambda s: (s, 0)),
            hbm(), fixed((NV, D)), hbm(),
        ],
        out_specs=[
            fixed((T, D)), fixed((T, D)), fixed((T, D)), pl.BlockSpec((D, D), lambda s: (0, s)), fixed((8, D)),
            fixed((96, D)),
        ],
        out_shape=[
            shape((T, D), BF), shape((T, D), F32), shape((T, D), BF), shape((D, FF), BF), shape((8, D), F32),
            shape((96, D), F32),
        ],
        scratch_shapes=[
            pltpu.VMEM((T, D), F32), pltpu.VMEM((D, T), BF), *dma_sems(2),
            pltpu.VMEM((T, D), F32), pltpu.VMEM((T, D), F32), pltpu.VMEM((T, D), BF),
            pltpu.VMEM((N_DOWN, NZ, 2, 2, CH, HW), BF), *scatter_bufs(N_DOWN, HW),
            *dma_sems(N_DOWN * 7, N_DOWN * 7, N_DOWN),
        ],
        compiler_params=pltpu.CompilerParams(collective_id=1, has_side_effects=True, vmem_limit_bytes=LIMIT),
        name="feed_forward_back",
    )(x1, dm, g, slope, wup, down, h2t, vec, gdown.reshape(NZ, 2, 2, 4 * CH, D))


BACK_TICKS = [2.0 + 4.8 * n for n in range(12)]
N_BACK = N_UP + 4
END_LAG = (0.0, 4.0, 9.0, 14.0, 19.0)


def attn_back_kernel(
    xb_in, yb_in, dx1_in, da_ref, h1t_in, qkv_ref, p_ref, attn_ref, rl_ref, wo_ref, wqkv_ref, vec_ref, sums_ref, gup_ref,
    out_ref, gx_ref, oqkv_ref, oout_ref, oup_ref, *refs,
):
    small_outs = refs[:NV + 1]
    (
        xb_ref, yb_ref, dx1_ref, h1t_ref, in_sem, dos, dqkv, dh1, gqkv, gout, mine, acc, via, last, zs, done, landed, small,
        sems_s, sems_r, fin_s, fin_r, small_s, small_r, own_sem,
    ) = refs[NV + 1:]
    step = pl.program_id(0)
    hq, r = lax.div(step, 2), lax.rem(step, 2)
    here = where_am_i()
    z, x, y, c = here
    peers = partners(*here)
    items, own = [], []
    for n in range(N_BACK):
        if n < N_UP:
            theirs = gup_ref.at[EVERY, TWO, TWO, :, half(n, 1 - c)]
            own.append(pltpu.make_async_copy(gup_ref.at[:, :, :, :, half(n, c)], mine.at[n], own_sem.at[n]))
            get = lambda a, b, d, n=n: mine[n, a, b, d]
        elif n == N_UP:
            theirs = gout.at[EVERY, TWO, TWO, :, half(0, 1 - c)]
            get = lambda a, b, d: gout[a, b, d, :, half(0, c)]
        else:
            i = n - N_UP - 1
            theirs = gqkv.at[i, EVERY, TWO, TWO, :, half(0, 1 - c)]
            get = lambda a, b, d, i=i: gqkv[i, a, b, d, :, half(0, c)]
        items.append(Scatter(
            here, (sems_s, sems_r), n * Scatter.COPIES, theirs, get, acc.at[n], via.at[n], last.at[n], zs.at[n]))

    later = [
        pltpu.make_async_copy(a, b, in_sem.at[n])
        for n, (a, b) in enumerate(((h1t_in, h1t_ref), (xb_in, xb_ref), (dx1_in, dx1_ref), (yb_in, yb_ref)))
    ]

    def final(n):
        theirs = pl.ds(pl.multiple_of((1 - c) * 24, 8), 24)
        return remote(done.at[n, theirs], landed.at[n], (fin_s, fin_r), n, peers[5])

    def put(n, core, value):
        if n > N_UP:
            for b in range(3):
                cols = pl.ds(pl.multiple_of(b * D + (n - N_UP - 1) * QW + core * 128, 128), 128)
                oqkv_ref[:, cols] = value[:, b * 128:(b + 1) * 128]
        elif n == N_UP:
            oout_ref[:, half(0, core)] = value
        else:
            oup_ref[:, half(n, core)] = value

    def finish(n):
        done[n] = items[n].total()
        final(n).start()
        put(n, c, done[n, pl.ds(pl.multiple_of(c * 24, 8), 24)])

    def act(action):
        n, phase = action
        if n < N_UP and phase == 1:
            own[n].wait()
        if phase == 4:
            finish(n)
        else:
            items[n].start(phase)

    entries = []
    begin = 0.0
    for n in range(N_BACK):
        if n > N_UP:
            begin = max(begin, BACK_TICKS[0] + 19.2 * (n - N_UP))
        for phase in range(5):
            if n < N_UP or phase > 0:
                lag = BACK_LAG if n < N_BACK - 2 else END_LAG
                entries.append((begin + lag[phase], (n, phase)))
        begin += PACE
    entries.remove((0.0, (0, 0)))
    table, tail = plan(entries, BACK_TICKS)
    final_steps = [a for a in tail if a[0] == N_BACK - 1]
    earlier = [a for a in tail if a[0] != N_BACK - 1]

    def tick(slot, could_be):
        for n in could_be:
            if table[n]:
                @pl.when(slot == n)
                def _(n=n):
                    for action in table[n]:
                        act(action)

    @pl.when(step == 0)
    def _():
        say_hello(here)
        for copy in (*own, *later):
            copy.start()
        small[0] = jnp.zeros((16, D), F32)
        src = lax.broadcasted_iota(jnp.int32, (128, D), 0)
        dst = lax.broadcasted_iota(jnp.int32, (128, D), 1)
        spread = jnp.where(lax.div(dst, HD) == src, 1.0, 0.0)

        @pl.loop(0, T // MB)
        def _(i):
            rows = rows_of(i)
            d = da_ref[rows, :]
            rl = lax.dot_general(
                rl_ref[rows, :], spread, NN, precision=lax.Precision.HIGHEST, preferred_element_type=F32)
            small[0, 4:5, :] += jnp.sum(d.astype(F32), 0, keepdims=True)
            dos[rows, :] = (mm(d, wo_ref[...], NT) * rl).astype(BF)
            dh1[rows, :] = jnp.zeros((MB, D), F32)
        @pl.loop(0, 2)
        def _(t):
            part = mm(attn_ref[:, pl.ds(pl.multiple_of(t * 384, 128), 384)], da_ref[...], TN)
            gout[pl.ds(2 * t, 2)] = part.astype(BF).reshape(2, 2, 2, CH, D)

        await_all()
        act((0, 0))
        items[N_UP].start(0)

    tick(2 * step, range(0, 12, 2))
    rows = pl.ds(pl.multiple_of(r * S, 16), S)
    scale = 1.0 / math.sqrt(HD)
    for j in range(HG // 2):
        if j:
            tick(2 * step + 1, range(1, 12, 2))
        at = j * 384
        qp, kp, vp = (qkv_ref[rows, at + 128 * n: at + 128 * (n + 1)] for n in range(3))
        lanes = pl.ds(pl.multiple_of(hq * QW + j * 128, 128), 128)
        do = dos[rows, lanes]
        prod = do.astype(F32) * attn_ref[rows, lanes].astype(F32)
        dq = dk = dv = None
        for e in range(2):
            keep = head_lanes((S, 128), e)
            zero = jnp.zeros_like(qp)
            doe = jnp.where(keep, do, zero)
            dot = jnp.sum(jnp.where(keep, prod, 0.0), -1, keepdims=True)
            p = p_ref[0, 2 * j + e]
            ds = (p.astype(F32) * (mm(doe, vp, NT) - dot)).astype(BF)
            a_, b_, c_ = mm(ds, jnp.where(keep, kp, zero)), mm(ds, jnp.where(keep, qp, zero), TN), mm(p, doe, TN)
            dq, dk, dv = (a_, b_, c_) if dq is None else (dq + a_, dk + b_, dv + c_)
        for n, part in enumerate((dq * scale, dk * scale, dv)):
            dqkv[rows, at + 128 * n:at + 128 * (n + 1)] = part.astype(BF)

    @pl.when(step == 1)
    def _():
        later[0].wait()

    @pl.when(r == 1)
    def _():
        sums = jnp.sum(dqkv[...].astype(F32), 0, keepdims=True)
        for j in range(2):
            cols = pl.ds(pl.multiple_of(hq * QW + j * 128, 128), 128)
            small[0, 2:3, cols] = sums[:, j * 384:j * 384 + 128]
            small[0, 3:4, cols] = sums[:, j * 384 + 256:j * 384 + 384]
        @pl.loop(0, 2)
        def _(t):
            part = mm(h1t_ref[pl.ds(pl.multiple_of(t * 384, 16), 384), :], dqkv[...])
            gqkv[hq, pl.ds(2 * t, 2)] = part.astype(BF).reshape(2, 2, 2, CH, GW)

        for i in range(3):
            @pl.when(hq == i)
            def _(i=i):
                items[N_UP + 1 + i].start(0)

        @pl.loop(0, 2)
        def _(i):
            rr = row_of(i)
            dh1[rr, :] += mm(dqkv[rr, :], wqkv_ref[...], NT)

    @pl.when(step == N_ATT - 1)
    def _():
        rest = final_steps[1:]
        for copy in later[1:]:
            copy.wait()

        @pl.loop(0, T // MB)
        def _(i):
            @pl.when(i == 0)
            def _():
                for action in earlier[:-1]:
                    act(action)

            @pl.when(i == 1)
            def _():
                act(final_steps[0])

            @pl.when(i == 3)
            def _():
                for action in earlier[-1:]:
                    act(action)
            rr = rows_of(i)
            dh = dh1[rr, :]
            n1, s1 = norm_parts(xb_ref[rr, :].astype(F32))
            small[0, 0:1, :] += jnp.sum(dh * n1, 0, keepdims=True)
            small[0, 1:2, :] += jnp.sum(dh, 0, keepdims=True)
            xb_ref[rr, :] = (dx1_ref[rr, :] + norm_pull(dh, n1, s1, vec_ref[G1:G1 + 1, :])).astype(BF)
        small[0, 5:12, :] = sums_ref[0:7, :]
        copies = []

        def send_small(n, src, dst, to):
            copy = remote(small.at[src], small.at[dst], (small_s, small_r), n, to)
            copy.start()
            copies.append(copy)

        send_small(0, 0, 1, peers[5])
        hops = [(1, 2, 3, peers[3]), (2, 4, 5, peers[4])]
        level = 0
        while rest or level < 4:
            if rest:
                act(rest.pop(0))
            if level == 0:
                for row in range(2):
                    rows_out(xb_ref, gx_ref, row)
            if level == 1:
                for row in range(2):
                    rows_out(yb_ref, out_ref, row)
            if level < 2:
                copies[level].wait_recv()
                small[2 * level + 2] = small[2 * level] + small[2 * level + 1]
                send_small(*hops[level])
            elif level == 2:
                copies[2].wait_recv()
                small[6] = small[4] + small[5]
                for k in range(3):
                    send_small(3 + k, 6, 7 + k, peers[k])
            elif level == 3:
                for k in range(3):
                    copies[3 + k].wait_recv()
                total = small[6] + small[7] + small[8] + small[9]
                me = lax.axis_index("dp") * lax.axis_size("fsdp") + lax.axis_index("fsdp")
                src = lax.broadcasted_iota(jnp.int32, (D, 128), 0)
                dst = lax.broadcasted_iota(jnp.int32, (D, 128), 1)

                def pick(lines, width, at):
                    chosen = jnp.where((src == at + dst) & (dst < width), 1.0, 0.0)
                    return lax.dot_general(
                        lines, chosen, NN, precision=lax.Precision.HIGHEST, preferred_element_type=F32)

                mine_of = pick(total[:8], 24, me * 24)
                for n in range(NV):
                    small_outs[n][...] = mine_of[n, :24]
                row = lax.broadcasted_iota(jnp.int32, (8, D), 0)
                longest = jnp.sum(jnp.where(row == lax.div(me, 8), total[8:16], 0.0), 0, keepdims=True)
                small_outs[NV][...] = pick(jnp.broadcast_to(longest, (8, D)), 96, lax.rem(me, 8) * 96)[0, :96]
            level += 1
        for n in range(N_BACK):
            copy = final(n)
            copy.wait_recv()
            put(n, 1 - c, landed[n])
            copy.wait_send()
            items[n].drain()
        for copy in copies:
            copy.wait_send()


def attn_back(x, yb, dx1, da, h1t, qkv, p, attn, rl, watt, vec, sums, gup):
    shape = jax.ShapeDtypeStruct
    n_fin = N_BACK
    return pl.pallas_call(
        attn_back_kernel,
        grid=(N_ATT,),
        in_specs=[
            hbm(), hbm(), hbm(), fixed((T, D)), hbm(), pl.BlockSpec((T, GW), lambda s: (0, s // 2)),
            pl.BlockSpec((1, HG, S, S), lambda s: (s % 2, s // 2, 0, 0)), fixed((T, D)), fixed((T, 128)),
            pl.BlockSpec((D, D), lambda s: (0, 3), pipeline_mode=pl.Buffered(1)),
            pl.BlockSpec((D, GW), lambda s: (0, s // 2)), fixed((NV, D)), fixed((8, D)), hbm(),
        ],
        out_specs=[
            fixed((SEQ, 2, D)), fixed((SEQ, 2, D)), fixed((24, 3 * D)), fixed((24, D)), fixed((24, FF)),
            *[pl.BlockSpec((w,), lambda s: (0,), pipeline_mode=pl.Buffered(1)) for w in VW],
        ],
        out_shape=[
            shape((SEQ, 2, D), BF), shape((SEQ, 2, D), BF), shape((24, 3 * D), F32), shape((24, D), F32),
            shape((24, FF), F32), *[shape((w,), F32) for w in VW],
        ],
        scratch_shapes=[
            pltpu.VMEM((T, D), BF), pltpu.VMEM((T, D), BF), pltpu.VMEM((T, D), F32), pltpu.VMEM((D, T), BF), *dma_sems(4),
            pltpu.VMEM((T, D), BF), pltpu.VMEM((T, GW), BF), pltpu.VMEM((T, D), F32),
            pltpu.VMEM((3, NZ, 2, 2, CH, GW), BF), pltpu.VMEM((NZ, 2, 2, CH, D), BF),
            pltpu.VMEM((N_UP, NZ, 2, 2, CH, HW), BF), *scatter_bufs(N_BACK, HW),
            pltpu.VMEM((N_BACK, CH, HW), F32), pltpu.VMEM((N_BACK, 24, HW), F32), pltpu.VMEM((10, 16, D), F32),
            *dma_sems(N_BACK * 7, N_BACK * 7, n_fin, n_fin, 6, 6, N_UP),
        ],
        compiler_params=pltpu.CompilerParams(collective_id=2, has_side_effects=True, vmem_limit_bytes=LIMIT),
        name="attention_back",
    )(x, yb, dx1, da, h1t, qkv, p, attn, rl, watt, watt, vec, sums, gup.reshape(NZ, 2, 2, CH, FF))


def hand_over_kernel(*refs):
    n = (len(refs) - 2) // 3
    sems_in, sems_out = refs[-2:]
    held = refs[2 * n:3 * n]
    arrive = [pltpu.make_async_copy(refs[i], held[i], sems_in.at[i]) for i in range(n)]
    leave = [pltpu.make_async_copy(held[i], refs[n + i], sems_out.at[i]) for i in range(n)]
    for copy in arrive:
        copy.start()
    for i in range(n):
        arrive[i].wait()
        leave[i].start()
    for copy in leave:
        copy.wait()


def hand_over(values):
    return pl.pallas_call(
        hand_over_kernel,
        in_specs=[hbm()] * len(values),
        out_specs=[hbm()] * len(values),
        out_shape=[jax.ShapeDtypeStruct(v.shape, v.dtype) for v in values],
        scratch_shapes=[*[pltpu.VMEM(v.shape, v.dtype) for v in values], *dma_sems(len(values), len(values))],
        compiler_params=pltpu.CompilerParams(vmem_limit_bytes=LIMIT),
        name="results",
    )(*values)


def by_pair(v):
    return v.reshape(v.shape[0], 3, 6, 128).transpose(0, 2, 1, 3).reshape(v.shape[0], 3 * D)


def by_kind(v):
    return v.reshape(v.shape[0], 6, 3, 128).transpose(0, 2, 1, 3).reshape(v.shape[0], 3 * D)


def with_own_copies(inputs, row_kind, w_qkv, w_out, w_up, w_down, vectors, b_up, out_grad):
    x, dm = inputs.transpose(1, 0, 2), out_grad.transpose(1, 0, 2)
    h1t, qkv, p, attn, rl, x1, dmp, h2t, g, slope, gdown, vec, xb, watt, wup, down = forward(
        row_kind, x, dm, w_qkv, w_out, w_up, w_down, (*vectors, b_up))
    yb, dx1, da, gup, sums, gdown = ffn_back(
        x1, dmp, g, slope, wup.reshape(D, FF), down.reshape(FF, D), h2t, vec, gdown)
    results = attn_back(xb, yb, dx1, da, h1t, qkv, p, attn, rl, watt.reshape(D, UP_AT), vec, sums, gup)
    out, gx, gqkv, gout, gup, gdown, *small = hand_over((*results[:5], gdown, *results[5:]))
    return out.transpose(1, 0, 2), gx.transpose(1, 0, 2), gqkv, gout, gup, gdown, small[:NV], small[NV]


def with_collectives(inputs, row_kind, w_qkv, w_out, w_up, w_down, vectors, b_up, out_grad):
    axes = ("dp", "fsdp")
    get = lambda v: lax.all_gather(v, axes, axis=0, tiled=True)
    wide = jnp.concatenate([by_pair(get(w_qkv)), get(w_out), get(w_up)], 1)
    down = get(w_down)
    full = [get(v).astype(F32) for v in vectors]
    vec = jnp.stack(full)
    bu = get(b_up).astype(F32)[None]
    bqkv = by_pair(jnp.concatenate([full[BQ], jnp.zeros_like(full[BQ]), full[BV]])[None])
    h1, qkv, p, attn, rl, x1 = attn_fwd(row_kind, inputs, wide, bqkv, vec)
    outputs, dx1, gup, gdown, gbu, gg2, gb2, gbd = ffn(x1, out_grad, wide, down, bu, vec)
    input_grad, gqkv, gout, gbqkv, gbo, gg1, gb1 = attn_bwd(inputs, dx1, h1, qkv, p, attn, rl, wide, vec)
    gbqkv = by_kind(gbqkv)
    small = [gg1, gb1, gbqkv[:, :D], gbqkv[:, 2 * D:], gbo, gg2, gb2, gbd]
    give = lambda v: lax.psum_scatter(v.astype(F32), axes, scatter_dimension=0, tiled=True)
    return (
        outputs, input_grad, give(by_kind(gqkv)), give(gout), give(gup), give(gdown),
        [give(v[0]) for v in small], give(gbu[0]),
    )


def on_device(
    copies, inputs, row_kind, ln1_gain, ln1_bias, w_qkv, b_query, b_value, w_out, b_out, ln2_gain, ln2_bias,
    w_up, b_up, w_down, b_down, out_grad,
):
    vectors = (ln1_gain, ln1_bias, b_query, b_value, b_out, ln2_gain, ln2_bias, b_down)
    run = with_own_copies if copies else with_collectives
    outputs, input_grad, gqkv, gout, gup, gdown, small, gbu = run(
        inputs, row_kind, w_qkv, w_out, w_up, w_down, vectors, b_up, out_grad)
    gg1, gb1, gbq, gbv, gbo, gg2, gb2, gbd = small
    return outputs, input_grad, gg1, gb1, gqkv, gbq, gbv, gout, gbo, gg2, gb2, gup, gbu, gdown, gbd


def solution(mesh):
    both = ("dp", "fsdp")
    row = P(both)
    mat = P(both, None)
    act = P(both, None, None)
    in_specs = (act, row, row, row, mat, row, row, mat, row, row, row, mat, row, mat, row, act)
    out_specs = (act, act, row, row, mat, row, row, mat, row, row, row, mat, row, mat, row)
    copies = mesh.shape["dp"] == 2 * NZ and mesh.shape["fsdp"] == 4
    return jax.shard_map(
        functools.partial(on_device, copies), mesh=mesh, in_specs=in_specs, out_specs=out_specs, check_vma=False
    )
```

```python
import functools
import math

import jax
import jax.numpy as jnp
from jax import lax
from jax.experimental import pallas as pl
from jax.experimental.pallas import tpu as pltpu
from jax.sharding import PartitionSpec as P

D = 768
HD = 64
FF = 3072
SEQ = 529
HALF = 264
EPS = 1e-06
S = 544
T = 2 * S
MB = 272
HG = 4
QW = HG * HD
GW = 3 * QW
FC = 512
OUT_AT = 3 * D
UP_AT = 4 * D
AW = 4 * D + FF
F32 = jnp.float32
BF = jnp.bfloat16
LIMIT = 62 * 2**20
MESH = pl.DeviceIdType.MESH
NN = (((1,), (0,)), ((), ()))
NT = (((1,), (1,)), ((), ()))
TN = (((0,), (0,)), ((), ()))


def mm(a, b, dims=NN):
    return lax.dot_general(a, b, dims, preferred_element_type=F32)


def norm_parts(values):
    mean = jnp.mean(values, -1, keepdims=True)
    centred = values - mean
    inverse = lax.rsqrt(jnp.mean(centred * centred, -1, keepdims=True) + EPS)
    return centred * inverse, inverse


def norm_pull(grad, normed, inverse, gain):
    scaled = grad * gain
    return inverse * (
        scaled
        - jnp.mean(scaled, -1, keepdims=True)
        - normed * jnp.mean(scaled * normed, -1, keepdims=True)
    )


def gelu_both(u):
    a = jnp.abs(u)
    t = 1.0 / (1.0 + (0.3275911 / math.sqrt(2.0)) * a)
    e = jnp.exp(-0.5 * u * u)
    poly = t * (
        0.254829592
        + t * (-0.284496736 + t * (1.421413741 + t * (-1.453152027 + t * 1.061405429)))
    )
    tail = 0.5 * poly * e
    phi = jnp.where(u < 0, tail, 1.0 - tail)
    return u * phi, phi + u * e * (1.0 / math.sqrt(2.0 * math.pi))


def head_lanes(shape, e):
    lane = lax.broadcasted_iota(jnp.int32, shape, 1)
    return (lane // HD) == e


def whole(shape):
    return pl.BlockSpec(shape, lambda *_: (0,) * len(shape))


def rows_of(i):
    return pl.ds(pl.multiple_of(i * MB, 16), MB)


def row_of(i):
    return pl.ds(pl.multiple_of(i * S, 16), S)


G1, B1, BQ, BV, BO, G2, B2, BD = range(8)


def attn_fwd_kernel(
    kind_ref, x_ref, wg_ref, bqkv_ref, wo_ref, vec_ref,
    h1_ref, qkv_ref, p_ref, attn_ref, rl_ref, x1_ref, fa, fb,
):
    hq, r = pl.program_id(0), pl.program_id(1)

    @pl.when((hq == 0) & (r == 0))
    def _():
        for row in range(2):
            h1_ref[pl.ds(row * S + S - 16, 16), :] = jnp.zeros((16, D), BF)
            n1, _s = norm_parts(x_ref[row].astype(F32))
            h1_ref[pl.ds(row * S, SEQ), :] = (n1 * vec_ref[G1:G1 + 1, :] + vec_ref[B1:B1 + 1, :]).astype(BF)
            slot = lax.broadcasted_iota(jnp.int32, (S, 128), 0)
            lane = lax.broadcasted_iota(jnp.int32, (S, 128), 1)
            packed = jnp.where(slot < HALF, 0, jnp.where(slot < 2 * HALF, 1, 2))
            seg = jnp.where(kind_ref[row] == 1, packed, 0)
            fa[row] = jnp.where((lane < 3) & (seg == lane), -1e30, 0.0).astype(BF)
            fb[row] = jnp.where((lane < 3) & ((seg != lane) | (slot >= SEQ)), 1.0, 0.0).astype(BF)

    @pl.when(r == 0)
    def _():
        @pl.loop(0, T // MB)
        def _(i):
            rows = rows_of(i)
            qkv_ref[rows, :] = (mm(h1_ref[rows, :], wg_ref[...]) + bqkv_ref[...]).astype(BF)

    rows = pl.ds(pl.multiple_of(r * S, 16), S)
    feat_q, feat_k = fa[r], fb[r]
    ones = jnp.ones((S, 128), BF)
    scale = math.log2(math.e) / math.sqrt(HD)
    for j in range(HG // 2):
        at = j * 384
        qp, kp, vp = (qkv_ref[rows, at + 128 * n: at + 128 * (n + 1)] for n in range(3))
        kcat = jnp.concatenate([kp, feat_k], 1)
        total = None
        inv = None
        for e in range(2):
            keep = head_lanes((S, 128), e)
            qcat = jnp.concatenate([jnp.where(keep, qp, jnp.zeros_like(qp)), feat_q], 1)
            s = mm(qcat, kcat, NT)
            m = jnp.max(s, -1, keepdims=True)
            pb = jnp.exp2((s - m) * scale).astype(BF)
            p_ref[0, 2 * j + e] = pb
            vcat = jnp.concatenate([jnp.where(keep, vp, jnp.zeros_like(vp)), ones], 1)
            o = mm(pb, vcat)
            rl = 1.0 / o[:, 128:]
            part = o[:, :128] * rl
            total = part if total is None else total + part
            inv = rl if inv is None else jnp.where(keep, rl, inv)
        out = pl.ds(pl.multiple_of(hq * QW + j * 128, 128), 128)
        attn_ref[rows, out] = total.astype(BF)
        rl_ref[rows, out] = inv

    @pl.when((hq == D // QW - 1) & (r == 1))
    def _():
        for row in range(2):
            x1_ref[pl.ds(row * S + S - 16, 16), :] = jnp.zeros((16, D), F32)
            x1_ref[pl.ds(row * S, SEQ), :] = x_ref[row].astype(F32)

        @pl.loop(0, T // MB)
        def _(i):
            rr = rows_of(i)
            x1_ref[rr, :] = x1_ref[rr, :] + mm(attn_ref[rr, :], wo_ref[...]) + vec_ref[BO:BO + 1, :]


def attn_fwd(kind, x, wide, bqkv, vec):
    return pl.pallas_call(
        attn_fwd_kernel,
        grid=(D // QW, 2),
        in_specs=[
            pl.BlockSpec(memory_space=pltpu.SMEM), whole((2, SEQ, D)),
            pl.BlockSpec((D, GW), lambda h, r: (0, h)), pl.BlockSpec((1, GW), lambda h, r: (0, h)),
            pl.BlockSpec((D, D), lambda h, r: (0, 3)), whole((8, D)),
        ],
        out_specs=[
            whole((T, D)), pl.BlockSpec((T, GW), lambda h, r: (0, h)),
            pl.BlockSpec((1, HG, S, S), lambda h, r: (r, h, 0, 0)),
            whole((T, D)), whole((T, D)), whole((T, D)),
        ],
        out_shape=[
            jax.ShapeDtypeStruct((T, D), BF), jax.ShapeDtypeStruct((T, 3 * D), BF),
            jax.ShapeDtypeStruct((2, D // HD, S, S), BF),
            jax.ShapeDtypeStruct((T, D), BF), jax.ShapeDtypeStruct((T, D), F32), jax.ShapeDtypeStruct((T, D), F32),
        ],
        scratch_shapes=[pltpu.VMEM((2, S, 128), BF), pltpu.VMEM((2, S, 128), BF)],
        compiler_params=pltpu.CompilerParams(vmem_limit_bytes=LIMIT),
        name="attention_forward",
    )(kind, x, wide, bqkv, wide, vec)


def ffn_kernel(
    x1_ref, dm_ref, wu_ref, wd_ref, bu_ref, vec_ref,
    out_ref, dx1_ref, gwu_ref, gwd_ref, gbu_ref, gg2_ref, gb2_ref, gbd_ref,
    h2, h2t, dm, yacc, dacc, gs, dus,
):
    c = pl.program_id(0)

    @pl.when(c == 0)
    def _():
        for row in range(2):
            dm[pl.ds(row * S + S - 16, 16), :] = jnp.zeros((16, D), BF)
            dm[pl.ds(row * S, SEQ), :] = dm_ref[row]

        @pl.loop(0, T // MB)
        def _(i):
            rows = rows_of(i)
            x1 = x1_ref[rows, :]
            n2, _s = norm_parts(x1)
            h2[rows, :] = (n2 * vec_ref[G2:G2 + 1, :] + vec_ref[B2:B2 + 1, :]).astype(BF)
            yacc[rows, :] = x1 + vec_ref[BD:BD + 1, :]
            dacc[rows, :] = jnp.zeros((MB, D), F32)
        h2t[...] = h2[...].T
        gbd_ref[...] = jnp.sum(dm[...].astype(F32), 0, keepdims=True)

    gbu_ref[...] = jnp.zeros_like(gbu_ref)

    @pl.loop(0, T // MB)
    def _(i):
        rows = rows_of(i)
        u = mm(h2[rows, :], wu_ref[...]) + bu_ref[...]
        g, slope = gelu_both(u)
        gb = g.astype(BF)
        gs[rows, :] = gb
        yacc[rows, :] += mm(gb, wd_ref[...])
        du = (mm(dm[rows, :], wd_ref[...], NT) * slope).astype(BF)
        dus[rows, :] = du
        gbu_ref[...] += jnp.sum(du.astype(F32), 0, keepdims=True)
        dacc[rows, :] += mm(du, wu_ref[...], NT)

    for t in range(FC // 256):
        cols = pl.ds(t * 256, 256)
        gwd_ref[cols, :] = mm(gs[:, cols], dm[...], TN).astype(BF)

    @pl.loop(0, D // 256)
    def _(t):
        rows = pl.ds(pl.multiple_of(t * 256, 256), 256)
        gwu_ref[rows, :] = mm(h2t[rows, :], dus[...]).astype(BF)

    @pl.when(c == FF // FC - 1)
    def _():
        gg2_ref[...] = jnp.zeros_like(gg2_ref)
        gb2_ref[...] = jnp.zeros_like(gb2_ref)
        for row in range(2):
            out_ref[row] = yacc[pl.ds(row * S, SEQ), :].astype(BF)

        @pl.loop(0, T // MB)
        def _(i):
            rows = rows_of(i)
            n2, s2 = norm_parts(x1_ref[rows, :])
            dh = dacc[rows, :]
            gg2_ref[...] += jnp.sum(dh * n2, 0, keepdims=True)
            gb2_ref[...] += jnp.sum(dh, 0, keepdims=True)
            dx1_ref[rows, :] = dm[rows, :].astype(F32) + norm_pull(dh, n2, s2, vec_ref[G2:G2 + 1, :])


def ffn(x1, dm, wide, down, bu, vec):
    one = jax.ShapeDtypeStruct((1, D), F32)
    return pl.pallas_call(
        ffn_kernel,
        grid=(FF // FC,),
        in_specs=[
            whole((T, D)), whole((2, SEQ, D)),
            pl.BlockSpec((D, FC), lambda c: (0, c + UP_AT // FC)), pl.BlockSpec((FC, D), lambda c: (c, 0)),
            pl.BlockSpec((1, FC), lambda c: (0, c)), whole((8, D)),
        ],
        out_specs=[
            whole((2, SEQ, D)), whole((T, D)),
            pl.BlockSpec((D, FC), lambda c: (0, c)), pl.BlockSpec((FC, D), lambda c: (c, 0)),
            pl.BlockSpec((1, FC), lambda c: (0, c)), whole((1, D)), whole((1, D)), whole((1, D)),
        ],
        out_shape=[
            jax.ShapeDtypeStruct((2, SEQ, D), BF), jax.ShapeDtypeStruct((T, D), F32),
            jax.ShapeDtypeStruct((D, FF), BF), jax.ShapeDtypeStruct((FF, D), BF),
            jax.ShapeDtypeStruct((1, FF), F32), one, one, one,
        ],
        scratch_shapes=[
            pltpu.VMEM((T, D), BF), pltpu.VMEM((D, T), BF), pltpu.VMEM((T, D), BF),
            pltpu.VMEM((T, D), F32), pltpu.VMEM((T, D), F32),
            pltpu.VMEM((T, FC), BF), pltpu.VMEM((T, FC), BF),
        ],
        compiler_params=pltpu.CompilerParams(vmem_limit_bytes=LIMIT),
        name="feed_forward",
    )(x1, dm, wide, down, bu, vec)


def attn_bwd_kernel(
    x_ref, dx1_ref, h1_ref, qkv_ref, p_ref, attn_ref, rl_ref, wo_ref, wqkv_ref, vec_ref,
    gx_ref, gwqkv_ref, gwo_ref, gbqkv_ref, gbo_ref, gg1_ref, gb1_ref,
    da, dos, h1t, dqkv,
):
    hq, r = pl.program_id(0), pl.program_id(1)

    @pl.when((hq == 0) & (r == 0))
    def _():
        gbo_ref[...] = jnp.zeros_like(gbo_ref)

        @pl.loop(0, T // MB)
        def _(i):
            rows = rows_of(i)
            d = dx1_ref[rows, :].astype(BF)
            da[rows, :] = d
            gbo_ref[...] += jnp.sum(d.astype(F32), 0, keepdims=True)
            dos[rows, :] = (mm(d, wo_ref[...], NT) * rl_ref[rows, :]).astype(BF)
        h1t[...] = h1_ref[...].T

    rows = pl.ds(pl.multiple_of(r * S, 16), S)
    scale = 1.0 / math.sqrt(HD)
    for j in range(HG // 2):
        at = j * 384
        qp, kp, vp = (qkv_ref[rows, at + 128 * n: at + 128 * (n + 1)] for n in range(3))
        do = dos[rows, pl.ds(pl.multiple_of(hq * QW + j * 128, 128), 128)]
        prod = do.astype(F32) * attn_ref[rows, j * 128:(j + 1) * 128].astype(F32)
        dq = dk = dv = None
        for e in range(2):
            keep = head_lanes((S, 128), e)
            zero = jnp.zeros_like(qp)
            doe = jnp.where(keep, do, zero)
            dot = jnp.sum(jnp.where(keep, prod, 0.0), -1, keepdims=True)
            p = p_ref[0, 2 * j + e]
            ds = (p.astype(F32) * (mm(doe, vp, NT) - dot)).astype(BF)
            a = mm(ds, jnp.where(keep, kp, zero))
            b = mm(ds, jnp.where(keep, qp, zero), TN)
            c = mm(p, doe, TN)
            dq, dk, dv = (a, b, c) if dq is None else (dq + a, dk + b, dv + c)
        for n, part in enumerate((dq * scale, dk * scale, dv)):
            col = hq * GW + j * 384 + n * 128
            dqkv[rows, pl.ds(pl.multiple_of(col, 128), 128)] = part.astype(BF)

    @pl.when(r == 1)
    def _():
        part = dqkv[:, pl.ds(pl.multiple_of(hq * GW, 128), GW)]
        gbqkv_ref[...] = jnp.sum(part.astype(F32), 0, keepdims=True)

        @pl.loop(0, D // 256)
        def _(t):
            rr = pl.ds(pl.multiple_of(t * 256, 256), 256)
            gwqkv_ref[rr, :] = mm(h1t[rr, :], part).astype(BF)
        gwo_ref[...] = mm(attn_ref[...], da[...], TN).astype(BF)

    @pl.when((hq == D // QW - 1) & (r == 1))
    def _():
        gg1_ref[...] = jnp.zeros_like(gg1_ref)
        gb1_ref[...] = jnp.zeros_like(gb1_ref)
        for row in range(2):
            rr = pl.ds(row * S, SEQ)
            dh = mm(dqkv[pl.ds(row * S, S), :], wqkv_ref[...], NT)[:SEQ]
            n1, s1 = norm_parts(x_ref[row].astype(F32))
            gg1_ref[...] += jnp.sum(dh * n1, 0, keepdims=True)
            gb1_ref[...] += jnp.sum(dh, 0, keepdims=True)
            gx_ref[row] = (dx1_ref[rr, :] + norm_pull(dh, n1, s1, vec_ref[G1:G1 + 1, :])).astype(BF)


def attn_bwd(x, dx1, h1, qkv, p, attn, rl, wide, vec):
    act = pl.BlockSpec((T, QW), lambda h, r: (0, h))
    one = jax.ShapeDtypeStruct((1, D), F32)
    return pl.pallas_call(
        attn_bwd_kernel,
        grid=(D // QW, 2),
        in_specs=[
            whole((2, SEQ, D)), whole((T, D)), whole((T, D)), pl.BlockSpec((T, GW), lambda h, r: (0, h)),
            pl.BlockSpec((1, HG, S, S), lambda h, r: (r, h, 0, 0)), act, whole((T, D)),
            pl.BlockSpec((D, D), lambda h, r: (0, 3)), whole((D, 3 * D)), whole((8, D)),
        ],
        out_specs=[
            whole((2, SEQ, D)), pl.BlockSpec((D, GW), lambda h, r: (0, h)),
            pl.BlockSpec((QW, D), lambda h, r: (h, 0)),
            pl.BlockSpec((1, GW), lambda h, r: (0, h)), whole((1, D)), whole((1, D)), whole((1, D)),
        ],
        out_shape=[
            jax.ShapeDtypeStruct((2, SEQ, D), BF), jax.ShapeDtypeStruct((D, 3 * D), BF), jax.ShapeDtypeStruct((D, D), BF),
            jax.ShapeDtypeStruct((1, 3 * D), F32), one, one, one,
        ],
        scratch_shapes=[
            pltpu.VMEM((T, D), BF), pltpu.VMEM((T, D), BF), pltpu.VMEM((D, T), BF), pltpu.VMEM((T, 3 * D), BF),
        ],
        compiler_params=pltpu.CompilerParams(vmem_limit_bytes=LIMIT),
        name="attention_backward",
    )(x, dx1, h1, qkv, p, attn, rl, wide, wide, vec)


NZ = 4
CH = 48
HW = 384
SR = 16
N_WIDE = AW // (2 * HW)
N_DOWN = 4
N_UP = FF // D
DH = 2 * CH
NV = 8
VW = (24,) * NV + (96,)


def one(i):
    return pl.ds(i, 1)


EVERY = pl.ds(0, NZ)
TWO = pl.ds(0, 2)


def where_am_i():
    dp, fs = lax.axis_index("dp"), lax.axis_index("fsdp")
    return lax.div(dp, 2), lax.rem(dp, 2), lax.div(fs, 2), lax.rem(fs, 2)


def device(z, x, y, c):
    return (z * 2 + x, y * 2 + c)


def partners(z, x, y, c):
    found = [device(lax.rem(z + k, NZ), x, y, c) for k in (1, 2, 3)]
    return found + [device(z, 1 - x, y, c), device(z, x, 1 - y, c), device(z, x, y, 1 - c)]


def say_hello(here):
    barrier = pltpu.get_barrier_semaphore()
    for other in partners(*here):
        pl.semaphore_signal(barrier, inc=1, device_id=other, device_id_type=MESH)


def await_all():
    pl.semaphore_wait(pltpu.get_barrier_semaphore(), 6)


def remote(src, dst, sems, n, target):
    return pltpu.make_async_remote_copy(
        src_ref=src, dst_ref=dst, send_sem=sems[0].at[n], recv_sem=sems[1].at[n],
        device_id=target, device_id_type=MESH,
    )


def half(i, core):
    return pl.ds(pl.multiple_of(i * 2 * HW + core * HW, 128), HW)


def down_rows(i, core):
    return pl.ds(pl.multiple_of(core * DH + (i // 2) * CH, 16), CH)


def down_cols(i):
    return pl.ds((i % 2) * HW, HW)


TOK = 48


def rows_in(src, row, *targets):
    for ref in targets:
        ref[pl.ds(row * S + S - 16, 16), :] = jnp.zeros((16, D), ref.dtype)

    @pl.loop(0, SEQ // TOK)
    def _(i):
        part = src[pl.ds(i * TOK, TOK), row, :]
        for ref in targets:
            ref[pl.ds(pl.multiple_of(row * S + i * TOK, 16), TOK), :] = part.astype(ref.dtype)
    last = src[SEQ - 1:SEQ, row, :]
    for ref in targets:
        ref[pl.ds(row * S + SEQ - 1, 1), :] = last.astype(ref.dtype)


def rows_out(src, target, row):
    @pl.loop(0, SEQ // TOK)
    def _(i):
        target[pl.ds(i * TOK, TOK), row, :] = src[pl.ds(pl.multiple_of(row * S + i * TOK, 16), TOK), :]
    target[SEQ - 1:SEQ, row, :] = src[pl.ds(row * S + SEQ - 1, 1), :]


def transpose_into(target, src):
    @pl.loop(0, D // 128)
    def _(i):
        cols = pl.ds(pl.multiple_of(i * 128, 128), 128)
        target[cols, :] = src[:, cols].T


def add(a, b):
    return (a.astype(F32) + b.astype(F32)).astype(BF)


def plan(entries, ticks):
    table = {n: [] for n in range(len(ticks))}
    rest = []
    for due, action in sorted(entries, key=lambda e: e[0]):
        slot = min((n for n, t in enumerate(ticks) if t >= due), default=None)
        (rest if slot is None else table[slot]).append(action)
    return table, rest


class Gather:
    COPIES = 7

    def __init__(self, here, sems, base, view, first):
        z, x, y, c = here
        peers = partners(*here)
        mine = view(one(z), one(x), one(y))
        column = view(EVERY, one(x), one(y))
        fx, fy = jnp.where(c == 0, 1 - x, x), jnp.where(c == 0, y, 1 - y)
        tx, ty = jnp.where(c == 0, x, 1 - x), jnp.where(c == 0, 1 - y, y)
        passed = view(EVERY, one(fx), one(fy))
        all_of = view(EVERY, TWO, TWO)
        make = lambda n, src, dst, to: remote(src, dst, sems, base + n, to)
        self.along_z = [make(k, mine if first is None else first, mine, peers[k]) for k in range(3)]
        self.along_x = make(3, column, column, peers[3])
        self.along_y = make(4, column, column, peers[4])
        self.diagonal = make(5, passed, passed, device(z, tx, ty, c))
        self.sibling = make(6, all_of, all_of, peers[5])

    def start(self, phase):
        if phase == 0:
            for copy in self.along_z:
                copy.start()
        elif phase == 1:
            for copy in self.along_z:
                copy.wait_recv()
            self.along_x.start()
            self.along_y.start()
        elif phase == 2:
            self.along_x.wait_recv()
            self.along_y.wait_recv()
            self.diagonal.start()
        elif phase == 3:
            self.diagonal.wait_recv()
            self.sibling.start()
        else:
            self.sibling.wait_recv()

    def drain(self):
        for copy in (*self.along_z, self.along_x, self.along_y, self.diagonal, self.sibling):
            copy.wait_send()


class Scatter:
    COPIES = 7

    def __init__(self, here, sems, base, theirs, mine, acc, via, last, zs):
        self.mine, self.acc, self.via, self.last, self.zs = mine, acc, via, last, zs
        z, x, y, c = self.here = here
        peers = partners(*here)
        ix, iy = jnp.where(c == 0, x, 1 - x), jnp.where(c == 0, 1 - y, y)
        self.px, self.py = jnp.where(c == 0, 1 - x, x), jnp.where(c == 0, y, 1 - y)
        first, second = device(z, ix, iy, c), device(z, self.px, self.py, c)
        make = lambda n, src, dst, to: remote(src, dst, sems, base + n, to)
        at = lambda xs, ys: acc.at[EVERY, one(xs), one(ys)]
        self.swap = make(0, theirs, acc, peers[5])
        self.far = make(1, at(1 - x, 1 - y), via.at[0], first)
        self.near = make(2, at(ix, iy), via.at[1], first)
        self.next = make(3, at(self.px, self.py), last, second)
        self.along_z = [
            make(4 + k, acc.at[one(lax.rem(z + k + 1, NZ)), one(x), one(y)], zs.at[k], peers[k]) for k in range(3)
        ]

    def start(self, phase):
        z, x, y, c = self.here
        acc = self.acc
        if phase == 0:
            self.swap.start()
        elif phase == 1:
            self.swap.wait_recv()

            @pl.loop(0, NZ)
            def _(i):
                for xi in range(2):
                    for yi in range(2):
                        acc[i, xi, yi] = add(acc[i, xi, yi], self.mine(i, xi, yi))
            self.far.start()
            self.near.start()
        elif phase == 2:
            self.far.wait_recv()
            px, py = self.px, self.py

            @pl.loop(0, NZ)
            def _(i):
                acc[i, px, py] = add(acc[i, px, py], self.via[0, i, 0, 0])
            self.next.start()
            self.near.wait_recv()

            @pl.loop(0, NZ)
            def _(i):
                acc[i, x, y] = add(acc[i, x, y], self.via[1, i, 0, 0])
        elif phase == 3:
            self.next.wait_recv()

            @pl.loop(0, NZ)
            def _(i):
                acc[i, x, y] = add(acc[i, x, y], self.last[i, 0, 0])
            for copy in self.along_z:
                copy.start()

    def total(self):
        z, x, y, c = self.here
        for copy in self.along_z:
            copy.wait_recv()
        parts = [self.acc[z, x, y]] + [self.zs[k, 0, 0, 0] for k in range(3)]
        return sum(part.astype(F32) for part in parts)

    def drain(self):
        for copy in (self.swap, self.far, self.near, self.next, *self.along_z):
            copy.wait_send()


def scatter_bufs(n, width):
    return [
        pltpu.VMEM((n, NZ, 2, 2, CH, width), BF), pltpu.VMEM((n, 2, NZ, 1, 1, CH, width), BF),
        pltpu.VMEM((n, NZ, 1, 1, CH, width), BF), pltpu.VMEM((n, 3, 1, 1, 1, CH, width), BF),
    ]


def dma_sems(*counts):
    return [pltpu.SemaphoreType.DMA((k,)) for k in counts]


def fixed(shape):
    return pl.BlockSpec(shape, lambda s: (0,) * len(shape), pipeline_mode=pl.Buffered(1))


def vmem():
    return pl.BlockSpec(memory_space=pltpu.VMEM)


def hbm():
    return pl.BlockSpec(memory_space=pl.ANY)


N_ATT = 2 * (D // QW)
PACE = 5.4
FORWARD_LAG = (0.0, 10.0, 24.0, 33.0, 40.0)
FORWARD_FROM = 28.0
FIRST_PACE = 3.2
FORWARD_PACE = 5.4
FORWARD_TICKS = [FORWARD_FROM + 2.9 * n for n in range(12)] + [FORWARD_FROM + 35.0 + 2.1 * n for n in range(16)]


def forward_kernel(
    kind_ref, x_in, dm_in, wqkv_ref, wout_ref, wup_ref, wdown_ref, *refs,
):
    small_refs = refs[:NV + 1]
    (
        h1t_out, qkv_ref, p_ref, attn_out, rl_out, x1_out, dmp_out, h2t_out, g_ref, slope_ref, gdown_ref,
        vec_ref, xb_out, watt_out, wup_out, down_out,
        h1t_ref, attn_ref, rl_ref, x1_ref, dmp_ref, h2t_ref, xb_ref, out_sem, x_ref, dm_ref, in_sem,
        fa, fb, h1, h2, staged, swap, watt, wup, bqkv, bu, smalls,
        sems_s, sems_r, swap_s, swap_r, small_s, small_r, copy_sem,
    ) = refs[NV + 1:]
    step = pl.program_id(0)
    here = where_am_i()
    z, x, y, c = here
    peers = partners(*here)
    sems = (sems_s, sems_r)

    swaps = [
        remote(staged.at[:, half(i, 1 - c)], swap.at[:, i * HW:(i + 1) * HW], (swap_s, swap_r), i, peers[5])
        for i in range(N_WIDE)
    ]
    items, own = [], []
    for i in range(N_WIDE):
        buf, at = (watt, i) if i < 4 else (wup, i - 4)
        view = lambda zs, xs, ys, buf=buf, at=at: buf.at[zs, xs, ys, :, half(at, c)]
        items.append(Gather(here, sems, i * Gather.COPIES, view, None))
    for i in range(N_DOWN):
        rows, cols = down_rows(i, c), down_cols(i)
        view = lambda zs, xs, ys, rows=rows, cols=cols: down_out.at[zs, xs, ys, rows, cols]
        first = wdown_ref.at[:, :, :, pl.ds((i // 2) * CH, CH), cols]
        items.append(Gather(here, sems, (N_WIDE + i) * Gather.COPIES, view, first))
        own.append(pltpu.make_async_copy(first, view(one(z), one(x), one(y)), copy_sem.at[N_WIDE + i]))
    keeps = []
    for i in range(N_WIDE):
        src, dst, at = (watt, watt_out, i) if i < 4 else (wup, wup_out, i - 4)
        cols = pl.ds(at * D, D)
        keeps.append(pltpu.make_async_copy(
            src.at[:, :, :, :, cols], dst.at[:, :, :, :, cols], copy_sem.at[i]))

    x_load = pltpu.make_async_copy(x_in, x_ref, in_sem.at[0])
    dm_load = pltpu.make_async_copy(dm_in, dm_ref, in_sem.at[1])
    first_out = [
        pltpu.make_async_copy(a, b, out_sem.at[n])
        for n, (a, b) in enumerate(((h1t_ref, h1t_out), (dmp_ref, dmp_out), (xb_ref, xb_out)))
    ]
    next_out = [
        pltpu.make_async_copy(a, b, out_sem.at[3 + n])
        for n, (a, b) in enumerate(((attn_ref, attn_out), (rl_ref, rl_out), (x1_ref, x1_out), (h2t_ref, h2t_out)))
    ]

    def act(action):
        i, phase = action
        if i >= N_WIDE and phase == 0:
            own[i - N_WIDE].start()
        if i >= N_WIDE and phase == 1:
            own[i - N_WIDE].wait()
        items[i].start(phase)
        if phase == 4 and i < N_WIDE:
            keeps[i].start()

    needed = {1: 4, 2: 8, 3: 11, 4: 12, 5: 16, 6: 20, 7: 24}
    entries = []
    for i in range(1, N_WIDE + N_DOWN):
        for phase in range(5):
            due = FORWARD_PACE * i + FORWARD_LAG[phase] if phase else FIRST_PACE * i
            if i in needed:
                due = min(due, FORWARD_TICKS[needed[i]])
            entries.append((due, (i, phase)))
    early = [a for t, a in sorted(entries, key=lambda e: e[0]) if t < FORWARD_FROM]
    table, late = plan([e for e in entries if e[0] >= FORWARD_FROM], FORWARD_TICKS)

    def tick(slot, could_be):
        for n in could_be:
            if table[n]:
                @pl.when(slot == n)
                def _(n=n):
                    for action in table[n]:
                        act(action)

    @pl.when(step == 0)
    def _():
        say_hello(here)
        x_load.start()
        dm_load.start()
        for pair in range(6):
            for n in range(3):
                at = pair * 384 + n * 128
                staged[:, at:at + 128] = wqkv_ref[:, n * D + pair * 128:n * D + (pair + 1) * 128].astype(F32)
        staged[:, OUT_AT:UP_AT] = wout_ref[...].astype(F32)
        staged[:, UP_AT:] = wup_ref[...].astype(F32)
        line = smalls.at[z, x, y, c]
        line[...] = jnp.zeros((SR, 128), F32)
        for n, (ref, width) in enumerate(zip(small_refs, VW)):
            line[n:n + 1, 0:width] = ref[...].astype(F32).reshape(1, width)
        await_all()
        swaps[0].start()

        def small_copy(n, src, to):
            return remote(src, src, (small_s, small_r), n, to)

        small_c = small_copy(0, smalls.at[one(z), one(x), one(y), one(c)], peers[5])
        both = smalls.at[one(z), one(x), one(y), TWO]
        small_z = [small_copy(1 + k, both, peers[k]) for k in range(3)]
        small_x = small_copy(4, smalls.at[EVERY, one(x), one(y), TWO], peers[3])
        small_y = small_copy(5, smalls.at[EVERY, TWO, one(y), TWO], peers[4])
        small_c.start()
        for i in range(1, N_WIDE):
            swaps[i].start()

        def take_block(i):
            swaps[i].wait_recv()
            mine_part = staged[:, half(i, c)]
            their_part = swap[:, i * HW:(i + 1) * HW]
            buf, at = (watt, i) if i < 4 else (wup, i - 4)
            lower = jnp.where(c == 0, mine_part, their_part)
            upper = jnp.where(c == 0, their_part, mine_part)
            buf[z, x, y, :, half(at, c)] = jnp.concatenate([lower, upper], 0).astype(BF)

        waiting = list(early)

        def act_some(count):
            for _n in range(min(count, len(waiting))):
                act(waiting.pop(0))

        take_block(0)
        items[0].start(0)
        small_c.wait_recv()
        for copy in small_z:
            copy.start()
        for i in range(1, N_WIDE):
            take_block(i)
        x_load.wait()
        rows_in(x_ref, 0, x1_ref, xb_ref)
        for copy in small_z:
            copy.wait_recv()
        small_x.start()
        act_some(1)
        items[0].start(1)
        rows_in(x_ref, 1, x1_ref, xb_ref)
        small_x.wait_recv()
        small_y.start()
        act_some(1)
        items[0].start(2)
        act_some(1)
        dm_load.wait()
        for row in range(2):
            rows_in(dm_ref, row, dmp_ref)
        items[0].start(3)
        small_y.wait_recv()
        src = lax.broadcasted_iota(jnp.int32, (128, D), 0)
        dst = lax.broadcasted_iota(jnp.int32, (128, D), 1)
        spread_short = jnp.where(lax.rem(dst, 24) == src, 1.0, 0.0).astype(BF)
        spread_long = jnp.where(lax.rem(dst, 96) == src, 1.0, 0.0).astype(BF)
        col = lax.broadcasted_iota(jnp.int32, (8, D), 1)
        vec_ref[...] = jnp.zeros_like(vec_ref)

        @pl.loop(0, NZ)
        def _(zi):
            pieces = smalls[zi].reshape(8 * SR, 128).astype(BF)
            short, long = mm(pieces, spread_short), mm(pieces, spread_long)
            for k in range(8):
                at = SR * k
                part = jnp.where(lax.div(col, 24) == zi * 8 + k, short[at:at + NV], 0.0)
                more = jnp.where(lax.div(col, 96) == k, long[at + NV:at + SR], 0.0)
                vectors, hidden_bias = (part, more) if k == 0 else (vectors + part, hidden_bias + more)
            vec_ref[...] += vectors
            bu[zi] = hidden_bias
        for pair in range(6):
            n, at = pair // 2, (pair % 2) * 384
            bqkv[n, :, at:at + 128] = vec_ref[BQ:BQ + 1, pair * 128:(pair + 1) * 128]
            bqkv[n, :, at + 128:at + 256] = jnp.zeros((1, 128), F32)
            bqkv[n, :, at + 256:at + 384] = vec_ref[BV:BV + 1, pair * 128:(pair + 1) * 128]
        act_some(2)

        @pl.loop(0, T // MB)
        def _(i):
            rows = rows_of(i)
            n1, _s = norm_parts(x1_ref[rows, :])
            h1[rows, :] = (n1 * vec_ref[G1:G1 + 1, :] + vec_ref[B1:B1 + 1, :]).astype(BF)
        for row in range(2):
            slot = lax.broadcasted_iota(jnp.int32, (S, 128), 0)
            lane = lax.broadcasted_iota(jnp.int32, (S, 128), 1)
            packed = jnp.where(slot < HALF, 0, jnp.where(slot < 2 * HALF, 1, 2))
            seg = jnp.where(kind_ref[row] == 1, packed, 0)
            fa[row] = jnp.where((lane < 3) & (seg == lane), -1e30, 0.0).astype(BF)
            fb[row] = jnp.where((lane < 3) & ((seg != lane) | (slot >= SEQ)), 1.0, 0.0).astype(BF)
        act_some(len(waiting))
        transpose_into(h1t_ref, h1)
        for copy in first_out:
            copy.start()
        rl_ref[...] = jnp.zeros_like(rl_ref)
        act((0, 4))
        for copy in (small_c, *small_z, small_x, small_y, *swaps):
            copy.wait_send()

    @pl.when(step < N_ATT)
    def _():
        hq, r = lax.div(step, 2), lax.rem(step, 2)
        tick(2 * step, range(0, 12, 2))

        @pl.when(r == 0)
        def _():
            @pl.loop(0, 2)
            def _(i):
                rows = row_of(i)
                w = watt[:, :, :, :, pl.ds(pl.multiple_of(hq * GW, 128), GW)].reshape(D, GW)
                qkv_ref[rows, :] = (mm(h1[rows, :], w) + bqkv[hq]).astype(BF)

        rows = pl.ds(pl.multiple_of(r * S, 16), S)
        feat_q, feat_k = fa[r], fb[r]
        ones = jnp.ones((S, 128), BF)
        scale = math.log2(math.e) / math.sqrt(HD)
        for j in range(HG // 2):
            if j:
                tick(2 * step + 1, range(1, 12, 2))
            at = j * 384
            qp, kp, vp = (qkv_ref[rows, at + 128 * n: at + 128 * (n + 1)] for n in range(3))
            kcat = jnp.concatenate([kp, feat_k], 1)
            total = None
            for e in range(2):
                keep = head_lanes((S, 128), e)
                qcat = jnp.concatenate([jnp.where(keep, qp, jnp.zeros_like(qp)), feat_q], 1)
                s = mm(qcat, kcat, NT)
                m = jnp.max(s, -1, keepdims=True)
                pb = jnp.exp2((s - m) * scale).astype(BF)
                p_ref[0, 2 * j + e] = pb
                vcat = jnp.concatenate([jnp.where(keep, vp, jnp.zeros_like(vp)), ones], 1)
                o = mm(pb, vcat)
                rl = 1.0 / o[:, 128:]
                part = o[:, :128] * rl
                total = part if total is None else total + part
                spot = lax.broadcasted_iota(jnp.int32, (S, 128), 1) == hq * HG + 2 * j + e
                rl_ref[rows, :] = jnp.where(spot, rl, rl_ref[rows, :])
            out = pl.ds(pl.multiple_of(hq * QW + j * 128, 128), 128)
            attn_ref[rows, out] = total.astype(BF)

    @pl.when(step == N_ATT - 1)
    def _():
        @pl.loop(0, T // MB)
        def _(i):
            rows = rows_of(i)
            wo = watt[:, :, :, :, OUT_AT:UP_AT].reshape(D, D)
            x1 = x1_ref[rows, :] + mm(attn_ref[rows, :], wo) + vec_ref[BO:BO + 1, :]
            x1_ref[rows, :] = x1
            n2, _s = norm_parts(x1)
            h2[rows, :] = (n2 * vec_ref[G2:G2 + 1, :] + vec_ref[B2:B2 + 1, :]).astype(BF)
        transpose_into(h2t_ref, h2)
        for copy in next_out:
            copy.start()

    @pl.when(step >= N_ATT)
    def _():
        part = step - N_ATT

        @pl.loop(0, 2)
        def _(i):
            tick(12 + 4 * part + 2 * i, range(12, len(FORWARD_TICKS), 2))
            tick(12 + 4 * part + 2 * i + 1, range(13, len(FORWARD_TICKS), 2))
            rows = row_of(i)
            w = wup[:, :, :, :, pl.ds(pl.multiple_of(part * D, 128), D)].reshape(D, D)
            g, slope = gelu_both(mm(h2[rows, :], w) + bu[part, 0:1, :])
            g_ref[rows, :] = g.astype(BF)
            slope_ref[rows, :] = slope.astype(BF)

        @pl.loop(0, 2)
        def _(t):
            cols = pl.ds(pl.multiple_of(t * 384, 128), 384)
            gdown_ref[cols, :] = mm(g_ref[:, cols], dmp_ref[...], TN).astype(BF)

    @pl.when(step == N_ATT + N_UP - 1)
    def _():
        for action in late:
            act(action)
        for item in items:
            item.drain()
        for copy in (*keeps, *first_out, *next_out):
            copy.wait()


def forward(kind, x, dm, wqkv, wout, wup, wdown, smalls):
    n = N_WIDE + N_DOWN
    att = lambda s: jnp.minimum(s, N_ATT - 1)
    ff = lambda s: jnp.maximum(s - N_ATT, 0)
    shape = jax.ShapeDtypeStruct
    return pl.pallas_call(
        forward_kernel,
        grid=(N_ATT + N_UP,),
        in_specs=[
            pl.BlockSpec(memory_space=pltpu.SMEM), hbm(), hbm(),
            fixed((24, 3 * D)), fixed((24, D)), fixed((24, FF)), fixed((1, 1, 1, 96, D)),
            *[pl.BlockSpec((w,), lambda s: (0,), pipeline_mode=pl.Buffered(1)) for w in VW],
        ],
        out_specs=[
            hbm(), pl.BlockSpec((T, GW), lambda s: (0, att(s) // 2)),
            pl.BlockSpec((1, HG, S, S), lambda s: (att(s) % 2, att(s) // 2, 0, 0)),
            hbm(), hbm(), hbm(), hbm(), hbm(),
            pl.BlockSpec((T, D), lambda s: (0, ff(s))), pl.BlockSpec((T, D), lambda s: (0, ff(s))),
            pl.BlockSpec((D, D), lambda s: (ff(s), 0)),
            fixed((NV, D)), hbm(), hbm(), hbm(), hbm(),
        ],
        out_shape=[
            shape((D, T), BF), shape((T, 3 * D), BF), shape((2, D // HD, S, S), BF),
            shape((T, D), BF), shape((T, 128), F32), shape((T, D), F32), shape((T, D), BF), shape((D, T), BF),
            shape((T, FF), BF), shape((T, FF), BF), shape((FF, D), BF), shape((NV, D), F32), shape((T, D), BF),
            shape((NZ, 2, 2, CH, UP_AT), BF), shape((NZ, 2, 2, CH, FF), BF), shape((NZ, 2, 2, 4 * CH, D), BF),
        ],
        scratch_shapes=[
            pltpu.VMEM((D, T), BF), pltpu.VMEM((T, D), BF), pltpu.VMEM((T, 128), F32), pltpu.VMEM((T, D), F32),
            pltpu.VMEM((T, D), BF), pltpu.VMEM((D, T), BF), pltpu.VMEM((T, D), BF), *dma_sems(7),
            pltpu.VMEM((SEQ, 2, D), BF), pltpu.VMEM((SEQ, 2, D), BF), *dma_sems(2),
            pltpu.VMEM((2, S, 128), BF), pltpu.VMEM((2, S, 128), BF), pltpu.VMEM((T, D), BF), pltpu.VMEM((T, D), BF),
            pltpu.VMEM((24, AW), F32), pltpu.VMEM((24, AW // 2), F32),
            pltpu.VMEM((NZ, 2, 2, CH, UP_AT), BF), pltpu.VMEM((NZ, 2, 2, CH, FF), BF),
            pltpu.VMEM((3, 1, GW), F32), pltpu.VMEM((N_UP, 8, D), F32), pltpu.VMEM((NZ, 2, 2, 2, SR, 128), F32),
            *dma_sems(n * Gather.COPIES, n * Gather.COPIES, N_WIDE, N_WIDE, 6, 6, n),
        ],
        compiler_params=pltpu.CompilerParams(collective_id=0, has_side_effects=True, vmem_limit_bytes=LIMIT),
        name="forward",
    )(kind, x, dm, wqkv, wout, wup, wdown.reshape(1, 1, 1, 96, D), *smalls)


BACK_LAG = (0.0, 5.0, 15.0, 23.0, 32.0)
FFN_LAG = (0.0, 4.0, 13.0, 20.0, 27.0)
FFN_PACE = 4.0
FFN_TICKS = [4.0 + 9.0 * s + t for s in range(4) for t in (0.0, 0.1, 2.8, 2.9, 5.7, 7.3)]


def ffn_back_kernel(
    x1_in, dm_ref, g_ref, slope_ref, wu_ref, wd_ref, h2t_in, vec_ref, gdown_ref,
    y_ref, dx1_ref, da_ref, gup_ref, sums_ref, odown_ref,
    x1_ref, h2t_ref, in_sem, yacc, dacc, dus, mine, acc, via, last, zs, sems_s, sems_r, own_sem,
):
    step = pl.program_id(0)
    here = where_am_i()
    z, x, y, c = here
    items, own = [], []
    for i in range(N_DOWN):
        rows, cols = down_rows(i, c), down_cols(i)
        own.append(pltpu.make_async_copy(gdown_ref.at[:, :, :, rows, cols], mine.at[i], own_sem.at[i]))
        items.append(Scatter(
            here, (sems_s, sems_r), i * Scatter.COPIES, gdown_ref.at[EVERY, TWO, TWO, down_rows(i, 1 - c), cols],
            lambda a, b, d, i=i: mine[i, a, b, d], acc.at[i], via.at[i], last.at[i], zs.at[i],
        ))
    later = [
        pltpu.make_async_copy(a, b, in_sem.at[n])
        for n, (a, b) in enumerate(((h2t_in, h2t_ref), (x1_in, x1_ref)))
    ]
    entries = [
        (5.0 + FFN_PACE * i + lag, (i, phase)) for i in range(N_DOWN) for phase, lag in enumerate(FFN_LAG) if (i, phase) != (0, 0)
    ]
    table, late = plan(entries, FFN_TICKS)

    def act(action):
        i, phase = action
        if phase == 1:
            own[i].wait()
        if phase == 4:
            odown_ref[pl.ds((i // 2) * CH, CH), down_cols(i)] = items[i].total()
        else:
            items[i].start(phase)

    def tick(slot):
        for n, todo in table.items():
            if todo:
                @pl.when(slot == n)
                def _(todo=todo):
                    for action in todo:
                        act(action)

    @pl.when(step == 0)
    def _():
        say_hello(here)
        for copy in (*later, *own):
            copy.start()

        @pl.loop(0, T // MB)
        def _(i):
            rows = rows_of(i)
            yacc[rows, :] = jnp.broadcast_to(vec_ref[BD:BD + 1, :], (MB, D))
            dacc[rows, :] = jnp.zeros((MB, D), F32)
        sums_ref[...] = jnp.zeros_like(sums_ref)
        sums_ref[2:3, :] = jnp.sum(dm_ref[...].astype(F32), 0, keepdims=True)

    @pl.loop(0, 2)
    def _(i):
        @pl.when((step == 0) & (i == 1))
        def _():
            await_all()
            act((0, 0))

        tick(6 * step + 2 * i)
        tick(6 * step + 2 * i + 1)
        rows = row_of(i)
        g = g_ref[rows, :]
        yacc[rows, :] += mm(g, wd_ref[...])
        du = (mm(dm_ref[rows, :], wd_ref[...], NT) * slope_ref[rows, :].astype(F32)).astype(BF)
        dus[rows, :] = du
        sums_ref[pl.ds(3 + step, 1), :] += jnp.sum(du.astype(F32), 0, keepdims=True)
        dacc[rows, :] += mm(du, wu_ref[...], NT)

    @pl.when(step == 0)
    def _():
        later[0].wait()

    @pl.loop(0, 2)
    def _(t):
        tick(6 * step + 4 + t)
        rows = pl.ds(pl.multiple_of(t * 384, 128), 384)
        gup_ref[rows, :] = mm(h2t_ref[rows, :], dus[...]).astype(BF)

    @pl.when(step == N_UP - 1)
    def _():
        later[1].wait()

        @pl.loop(0, T // MB)
        def _(i):
            rows = rows_of(i)
            x1 = x1_ref[rows, :]
            n2, s2 = norm_parts(x1)
            dh = dacc[rows, :]
            sums_ref[0:1, :] += jnp.sum(dh * n2, 0, keepdims=True)
            sums_ref[1:2, :] += jnp.sum(dh, 0, keepdims=True)
            dx1 = dm_ref[rows, :].astype(F32) + norm_pull(dh, n2, s2, vec_ref[G2:G2 + 1, :])
            dx1_ref[rows, :] = dx1
            da_ref[rows, :] = dx1.astype(BF)
            y_ref[rows, :] = (x1 + yacc[rows, :]).astype(BF)
        for action in late:
            act(action)
        for item in items:
            item.drain()


def ffn_back(x1, dm, g, slope, wup, down, h2t, vec, gdown):
    shape = jax.ShapeDtypeStruct
    col = pl.BlockSpec((T, D), lambda s: (0, s))
    return pl.pallas_call(
        ffn_back_kernel,
        grid=(N_UP,),
        in_specs=[
            hbm(), fixed((T, D)), col, col,
            pl.BlockSpec((D, D), lambda s: (0, s)), pl.BlockSpec((D, D), lambda s: (s, 0)),
            hbm(), fixed((NV, D)), hbm(),
        ],
        out_specs=[
            fixed((T, D)), fixed((T, D)), fixed((T, D)), pl.BlockSpec((D, D), lambda s: (0, s)), fixed((8, D)),
            fixed((96, D)),
        ],
        out_shape=[
            shape((T, D), BF), shape((T, D), F32), shape((T, D), BF), shape((D, FF), BF), shape((8, D), F32),
            shape((96, D), F32),
        ],
        scratch_shapes=[
            pltpu.VMEM((T, D), F32), pltpu.VMEM((D, T), BF), *dma_sems(2),
            pltpu.VMEM((T, D), F32), pltpu.VMEM((T, D), F32), pltpu.VMEM((T, D), BF),
            pltpu.VMEM((N_DOWN, NZ, 2, 2, CH, HW), BF), *scatter_bufs(N_DOWN, HW),
            *dma_sems(N_DOWN * 7, N_DOWN * 7, N_DOWN),
        ],
        compiler_params=pltpu.CompilerParams(collective_id=1, has_side_effects=True, vmem_limit_bytes=LIMIT),
        name="feed_forward_back",
    )(x1, dm, g, slope, wup, down, h2t, vec, gdown.reshape(NZ, 2, 2, 4 * CH, D))


BACK_TICKS = [2.0 + 4.8 * n for n in range(12)]
N_BACK = N_UP + 4
END_LAG = (0.0, 4.0, 9.0, 14.0, 19.0)


def attn_back_kernel(
    xb_in, yb_in, dx1_in, da_ref, h1t_in, qkv_ref, p_ref, attn_ref, rl_ref, wo_ref, wqkv_ref, vec_ref, sums_ref, gup_ref,
    out_hbm, gx_hbm, oqkv_ref, oout_ref, oup_ref, *refs,
):
    small_outs = refs[:NV + 1]
    (
        xb_ref, yb_ref, dx1_ref, h1t_ref, in_sem, out_ref, gx_ref, out_sem, dos, dqkv, dh1, gqkv, gout, mine, acc, via, last, zs, done, landed, small,
        sems_s, sems_r, fin_s, fin_r, small_s, small_r, own_sem,
    ) = refs[NV + 1:]
    step = pl.program_id(0)
    hq, r = lax.div(step, 2), lax.rem(step, 2)
    here = where_am_i()
    z, x, y, c = here
    peers = partners(*here)
    items, own = [], []
    for n in range(N_BACK):
        if n < N_UP:
            theirs = gup_ref.at[EVERY, TWO, TWO, :, half(n, 1 - c)]
            own.append(pltpu.make_async_copy(gup_ref.at[:, :, :, :, half(n, c)], mine.at[n], own_sem.at[n]))
            get = lambda a, b, d, n=n: mine[n, a, b, d]
        elif n == N_UP:
            theirs = gout.at[EVERY, TWO, TWO, :, half(0, 1 - c)]
            get = lambda a, b, d: gout[a, b, d, :, half(0, c)]
        else:
            i = n - N_UP - 1
            theirs = gqkv.at[i, EVERY, TWO, TWO, :, half(0, 1 - c)]
            get = lambda a, b, d, i=i: gqkv[i, a, b, d, :, half(0, c)]
        items.append(Scatter(
            here, (sems_s, sems_r), n * Scatter.COPIES, theirs, get, acc.at[n], via.at[n], last.at[n], zs.at[n]))

    later = [
        pltpu.make_async_copy(a, b, in_sem.at[n])
        for n, (a, b) in enumerate(((h1t_in, h1t_ref), (xb_in, xb_ref), (dx1_in, dx1_ref), (yb_in, yb_ref)))
    ]

    y_out = pltpu.make_async_copy(out_ref, out_hbm, out_sem.at[0])
    gx_out = pltpu.make_async_copy(gx_ref, gx_hbm, out_sem.at[1])

    def final(n):
        theirs = pl.ds(pl.multiple_of((1 - c) * 24, 8), 24)
        return remote(done.at[n, theirs], landed.at[n], (fin_s, fin_r), n, peers[5])

    def put(n, core, value):
        if n > N_UP:
            for b in range(3):
                cols = pl.ds(pl.multiple_of(b * D + (n - N_UP - 1) * QW + core * 128, 128), 128)
                oqkv_ref[:, cols] = value[:, b * 128:(b + 1) * 128]
        elif n == N_UP:
            oout_ref[:, half(0, core)] = value
        else:
            oup_ref[:, half(n, core)] = value

    def finish(n):
        done[n] = items[n].total()
        final(n).start()
        put(n, c, done[n, pl.ds(pl.multiple_of(c * 24, 8), 24)])

    def act(action):
        n, phase = action
        if n < N_UP and phase == 1:
            own[n].wait()
        if phase == 4:
            finish(n)
        else:
            items[n].start(phase)

    entries = []
    begin = 0.0
    for n in range(N_BACK):
        if n > N_UP:
            begin = max(begin, BACK_TICKS[0] + 19.2 * (n - N_UP))
        for phase in range(5):
            if n < N_UP or phase > 0:
                lag = BACK_LAG if n < N_BACK - 2 else END_LAG
                entries.append((begin + lag[phase], (n, phase)))
        begin += PACE
    entries.remove((0.0, (0, 0)))
    table, tail = plan(entries, BACK_TICKS)
    final_steps = [a for a in tail if a[0] == N_BACK - 1]
    earlier = [a for a in tail if a[0] != N_BACK - 1]

    def tick(slot, could_be):
        for n in could_be:
            if table[n]:
                @pl.when(slot == n)
                def _(n=n):
                    for action in table[n]:
                        act(action)

    @pl.when(step == 0)
    def _():
        say_hello(here)
        for copy in (*own, *later):
            copy.start()
        small[0] = jnp.zeros((16, D), F32)
        src = lax.broadcasted_iota(jnp.int32, (128, D), 0)
        dst = lax.broadcasted_iota(jnp.int32, (128, D), 1)
        spread = jnp.where(lax.div(dst, HD) == src, 1.0, 0.0)

        @pl.loop(0, T // MB)
        def _(i):
            rows = rows_of(i)
            d = da_ref[rows, :]
            rl = lax.dot_general(
                rl_ref[rows, :], spread, NN, precision=lax.Precision.HIGHEST, preferred_element_type=F32)
            small[0, 4:5, :] += jnp.sum(d.astype(F32), 0, keepdims=True)
            dos[rows, :] = (mm(d, wo_ref[...], NT) * rl).astype(BF)
            dh1[rows, :] = jnp.zeros((MB, D), F32)
        @pl.loop(0, 2)
        def _(t):
            part = mm(attn_ref[:, pl.ds(pl.multiple_of(t * 384, 128), 384)], da_ref[...], TN)
            gout[pl.ds(2 * t, 2)] = part.astype(BF).reshape(2, 2, 2, CH, D)

        await_all()
        act((0, 0))
        items[N_UP].start(0)

    tick(2 * step, range(0, 12, 2))
    rows = pl.ds(pl.multiple_of(r * S, 16), S)
    scale = 1.0 / math.sqrt(HD)
    for j in range(HG // 2):
        if j:
            tick(2 * step + 1, range(1, 12, 2))
        at = j * 384
        qp, kp, vp = (qkv_ref[rows, at + 128 * n: at + 128 * (n + 1)] for n in range(3))
        lanes = pl.ds(pl.multiple_of(hq * QW + j * 128, 128), 128)
        do = dos[rows, lanes]
        prod = do.astype(F32) * attn_ref[rows, lanes].astype(F32)
        dq = dk = dv = None
        for e in range(2):
            keep = head_lanes((S, 128), e)
            zero = jnp.zeros_like(qp)
            doe = jnp.where(keep, do, zero)
            dot = jnp.sum(jnp.where(keep, prod, 0.0), -1, keepdims=True)
            p = p_ref[0, 2 * j + e]
            ds = (p.astype(F32) * (mm(doe, vp, NT) - dot)).astype(BF)
            a_, b_, c_ = mm(ds, jnp.where(keep, kp, zero)), mm(ds, jnp.where(keep, qp, zero), TN), mm(p, doe, TN)
            dq, dk, dv = (a_, b_, c_) if dq is None else (dq + a_, dk + b_, dv + c_)
        for n, part in enumerate((dq * scale, dk * scale, dv)):
            dqkv[rows, at + 128 * n:at + 128 * (n + 1)] = part.astype(BF)

    @pl.when(step == 1)
    def _():
        later[0].wait()

    @pl.when(r == 1)
    def _():
        sums = jnp.sum(dqkv[...].astype(F32), 0, keepdims=True)
        for j in range(2):
            cols = pl.ds(pl.multiple_of(hq * QW + j * 128, 128), 128)
            small[0, 2:3, cols] = sums[:, j * 384:j * 384 + 128]
            small[0, 3:4, cols] = sums[:, j * 384 + 256:j * 384 + 384]
        @pl.loop(0, 2)
        def _(t):
            part = mm(h1t_ref[pl.ds(pl.multiple_of(t * 384, 16), 384), :], dqkv[...])
            gqkv[hq, pl.ds(2 * t, 2)] = part.astype(BF).reshape(2, 2, 2, CH, GW)

        for i in range(3):
            @pl.when(hq == i)
            def _(i=i):
                items[N_UP + 1 + i].start(0)

        @pl.loop(0, 2)
        def _(i):
            rr = row_of(i)
            dh1[rr, :] += mm(dqkv[rr, :], wqkv_ref[...], NT)

    @pl.when(step == N_ATT - 1)
    def _():
        rest = final_steps[1:]
        for copy in later[1:]:
            copy.wait()

        @pl.loop(0, T // MB)
        def _(i):
            @pl.when(i == 0)
            def _():
                for action in earlier[:-1]:
                    act(action)

            @pl.when(i == 1)
            def _():
                act(final_steps[0])

            @pl.when(i == 3)
            def _():
                for action in earlier[-1:]:
                    act(action)
            rr = rows_of(i)
            dh = dh1[rr, :]
            n1, s1 = norm_parts(xb_ref[rr, :].astype(F32))
            small[0, 0:1, :] += jnp.sum(dh * n1, 0, keepdims=True)
            small[0, 1:2, :] += jnp.sum(dh, 0, keepdims=True)
            xb_ref[rr, :] = (dx1_ref[rr, :] + norm_pull(dh, n1, s1, vec_ref[G1:G1 + 1, :])).astype(BF)
        small[0, 5:12, :] = sums_ref[0:7, :]
        copies = []

        def send_small(n, src, dst, to):
            copy = remote(small.at[src], small.at[dst], (small_s, small_r), n, to)
            copy.start()
            copies.append(copy)

        send_small(0, 0, 1, peers[5])
        act(rest.pop(0))
        copies[0].wait_recv()
        small[2] = small[0] + small[1]
        send_small(1, 2, 3, peers[3])
        for row in range(2):
            rows_out(xb_ref, gx_ref, row)
        gx_out.start()
        copies[1].wait_recv()
        small[4] = small[2] + small[3]
        send_small(2, 4, 5, peers[4])
        act(rest.pop(0))
        for row in range(2):
            rows_out(yb_ref, out_ref, row)
        y_out.start()
        copies[2].wait_recv()
        small[6] = small[4] + small[5]
        for k in range(3):
            send_small(3 + k, 6, 7 + k, peers[k])
        for k in range(3):
            copies[3 + k].wait_recv()
        total = small[6] + small[7] + small[8] + small[9]
        me = lax.axis_index("dp") * lax.axis_size("fsdp") + lax.axis_index("fsdp")
        src = lax.broadcasted_iota(jnp.int32, (D, 128), 0)
        dst = lax.broadcasted_iota(jnp.int32, (D, 128), 1)

        def pick(lines, width, at):
            chosen = jnp.where((src == at + dst) & (dst < width), 1.0, 0.0)
            return lax.dot_general(
                lines, chosen, NN, precision=lax.Precision.HIGHEST, preferred_element_type=F32)

        mine_of = pick(total[:8], 24, me * 24)
        for n in range(NV):
            small_outs[n][...] = mine_of[n, :24]
        row = lax.broadcasted_iota(jnp.int32, (8, D), 0)
        longest = jnp.sum(jnp.where(row == lax.div(me, 8), total[8:16], 0.0), 0, keepdims=True)
        small_outs[NV][...] = pick(jnp.broadcast_to(longest, (8, D)), 96, lax.rem(me, 8) * 96)[0, :96]
        act(rest.pop(0))
        gx_out.wait()
        y_out.wait()
        for n in range(N_BACK):
            copy = final(n)
            copy.wait_recv()
            put(n, 1 - c, landed[n])
            copy.wait_send()
            items[n].drain()
        for copy in copies:
            copy.wait_send()


def attn_back(x, yb, dx1, da, h1t, qkv, p, attn, rl, watt, vec, sums, gup):
    shape = jax.ShapeDtypeStruct
    n_fin = N_BACK
    return pl.pallas_call(
        attn_back_kernel,
        grid=(N_ATT,),
        in_specs=[
            hbm(), hbm(), hbm(), fixed((T, D)), hbm(), pl.BlockSpec((T, GW), lambda s: (0, s // 2)),
            pl.BlockSpec((1, HG, S, S), lambda s: (s % 2, s // 2, 0, 0)), fixed((T, D)), fixed((T, 128)),
            pl.BlockSpec((D, D), lambda s: (0, 3), pipeline_mode=pl.Buffered(1)),
            pl.BlockSpec((D, GW), lambda s: (0, s // 2)), fixed((NV, D)), fixed((8, D)), hbm(),
        ],
        out_specs=[
            hbm(), hbm(), fixed((24, 3 * D)), fixed((24, D)), fixed((24, FF)),
            *[pl.BlockSpec((w,), lambda s: (0,), pipeline_mode=pl.Buffered(1)) for w in VW],
        ],
        out_shape=[
            shape((SEQ, 2, D), BF), shape((SEQ, 2, D), BF), shape((24, 3 * D), F32), shape((24, D), F32),
            shape((24, FF), F32), *[shape((w,), F32) for w in VW],
        ],
        scratch_shapes=[
            pltpu.VMEM((T, D), BF), pltpu.VMEM((T, D), BF), pltpu.VMEM((T, D), F32), pltpu.VMEM((D, T), BF), *dma_sems(4),
            pltpu.VMEM((SEQ, 2, D), BF), pltpu.VMEM((SEQ, 2, D), BF), *dma_sems(2),
            pltpu.VMEM((T, D), BF), pltpu.VMEM((T, GW), BF), pltpu.VMEM((T, D), F32),
            pltpu.VMEM((3, NZ, 2, 2, CH, GW), BF), pltpu.VMEM((NZ, 2, 2, CH, D), BF),
            pltpu.VMEM((N_UP, NZ, 2, 2, CH, HW), BF), *scatter_bufs(N_BACK, HW),
            pltpu.VMEM((N_BACK, CH, HW), F32), pltpu.VMEM((N_BACK, 24, HW), F32), pltpu.VMEM((10, 16, D), F32),
            *dma_sems(N_BACK * 7, N_BACK * 7, n_fin, n_fin, 6, 6, N_UP),
        ],
        compiler_params=pltpu.CompilerParams(collective_id=2, has_side_effects=True, vmem_limit_bytes=LIMIT),
        name="attention_back",
    )(x, yb, dx1, da, h1t, qkv, p, attn, rl, watt, watt, vec, sums, gup.reshape(NZ, 2, 2, CH, FF))


def hand_over_kernel(*refs):
    n = (len(refs) - 2) // 3
    sems_in, sems_out = refs[-2:]
    held = refs[2 * n:3 * n]
    arrive = [pltpu.make_async_copy(refs[i], held[i], sems_in.at[i]) for i in range(n)]
    leave = [pltpu.make_async_copy(held[i], refs[n + i], sems_out.at[i]) for i in range(n)]
    for copy in arrive:
        copy.start()
    for i in range(n):
        arrive[i].wait()
        leave[i].start()
    for copy in leave:
        copy.wait()


def hand_over(values):
    return pl.pallas_call(
        hand_over_kernel,
        in_specs=[hbm()] * len(values),
        out_specs=[hbm()] * len(values),
        out_shape=[jax.ShapeDtypeStruct(v.shape, v.dtype) for v in values],
        scratch_shapes=[*[pltpu.VMEM(v.shape, v.dtype) for v in values], *dma_sems(len(values), len(values))],
        compiler_params=pltpu.CompilerParams(vmem_limit_bytes=LIMIT),
        name="results",
    )(*values)


def by_pair(v):
    return v.reshape(v.shape[0], 3, 6, 128).transpose(0, 2, 1, 3).reshape(v.shape[0], 3 * D)


def by_kind(v):
    return v.reshape(v.shape[0], 6, 3, 128).transpose(0, 2, 1, 3).reshape(v.shape[0], 3 * D)


def with_own_copies(inputs, row_kind, w_qkv, w_out, w_up, w_down, vectors, b_up, out_grad):
    x, dm = inputs.transpose(1, 0, 2), out_grad.transpose(1, 0, 2)
    h1t, qkv, p, attn, rl, x1, dmp, h2t, g, slope, gdown, vec, xb, watt, wup, down = forward(
        row_kind, x, dm, w_qkv, w_out, w_up, w_down, (*vectors, b_up))
    yb, dx1, da, gup, sums, gdown = ffn_back(
        x1, dmp, g, slope, wup.reshape(D, FF), down.reshape(FF, D), h2t, vec, gdown)
    results = attn_back(xb, yb, dx1, da, h1t, qkv, p, attn, rl, watt.reshape(D, UP_AT), vec, sums, gup)
    out, gx, gqkv, gout, gup, gdown, *small = hand_over((*results[:5], gdown, *results[5:]))
    return out.transpose(1, 0, 2), gx.transpose(1, 0, 2), gqkv, gout, gup, gdown, small[:NV], small[NV]


def with_collectives(inputs, row_kind, w_qkv, w_out, w_up, w_down, vectors, b_up, out_grad):
    axes = ("dp", "fsdp")
    get = lambda v: lax.all_gather(v, axes, axis=0, tiled=True)
    wide = jnp.concatenate([by_pair(get(w_qkv)), get(w_out), get(w_up)], 1)
    down = get(w_down)
    full = [get(v).astype(F32) for v in vectors]
    vec = jnp.stack(full)
    bu = get(b_up).astype(F32)[None]
    bqkv = by_pair(jnp.concatenate([full[BQ], jnp.zeros_like(full[BQ]), full[BV]])[None])
    h1, qkv, p, attn, rl, x1 = attn_fwd(row_kind, inputs, wide, bqkv, vec)
    outputs, dx1, gup, gdown, gbu, gg2, gb2, gbd = ffn(x1, out_grad, wide, down, bu, vec)
    input_grad, gqkv, gout, gbqkv, gbo, gg1, gb1 = attn_bwd(inputs, dx1, h1, qkv, p, attn, rl, wide, vec)
    gbqkv = by_kind(gbqkv)
    small = [gg1, gb1, gbqkv[:, :D], gbqkv[:, 2 * D:], gbo, gg2, gb2, gbd]
    give = lambda v: lax.psum_scatter(v.astype(F32), axes, scatter_dimension=0, tiled=True)
    return (
        outputs, input_grad, give(by_kind(gqkv)), give(gout), give(gup), give(gdown),
        [give(v[0]) for v in small], give(gbu[0]),
    )


def on_device(
    copies, inputs, row_kind, ln1_gain, ln1_bias, w_qkv, b_query, b_value, w_out, b_out, ln2_gain, ln2_bias,
    w_up, b_up, w_down, b_down, out_grad,
):
    vectors = (ln1_gain, ln1_bias, b_query, b_value, b_out, ln2_gain, ln2_bias, b_down)
    run = with_own_copies if copies else with_collectives
    outputs, input_grad, gqkv, gout, gup, gdown, small, gbu = run(
        inputs, row_kind, w_qkv, w_out, w_up, w_down, vectors, b_up, out_grad)
    gg1, gb1, gbq, gbv, gbo, gg2, gb2, gbd = small
    return outputs, input_grad, gg1, gb1, gqkv, gbq, gbv, gout, gbo, gg2, gb2, gup, gbu, gdown, gbd


def solution(mesh):
    both = ("dp", "fsdp")
    row = P(both)
    mat = P(both, None)
    act = P(both, None, None)
    in_specs = (act, row, row, row, mat, row, row, mat, row, row, row, mat, row, mat, row, act)
    out_specs = (act, act, row, row, mat, row, row, mat, row, row, row, mat, row, mat, row)
    copies = mesh.shape["dp"] == 2 * NZ and mesh.shape["fsdp"] == 4
    return jax.shard_map(
        functools.partial(on_device, copies), mesh=mesh, in_specs=in_specs, out_specs=out_specs, check_vma=False
    )
```

```python
import functools
import math

import jax
import jax.numpy as jnp
from jax import lax
from jax.experimental import pallas as pl
from jax.experimental.pallas import tpu as pltpu
from jax.sharding import PartitionSpec as P

D = 768
HD = 64
FF = 3072
SEQ = 529
HALF = 264
EPS = 1e-06
S = 544
T = 2 * S
MB = 272
HG = 4
QW = HG * HD
GW = 3 * QW
FC = 512
OUT_AT = 3 * D
UP_AT = 4 * D
AW = 4 * D + FF
F32 = jnp.float32
BF = jnp.bfloat16
LIMIT = 62 * 2**20
MESH = pl.DeviceIdType.MESH
NN = (((1,), (0,)), ((), ()))
NT = (((1,), (1,)), ((), ()))
TN = (((0,), (0,)), ((), ()))


def mm(a, b, dims=NN):
    return lax.dot_general(a, b, dims, preferred_element_type=F32)


def norm_parts(values):
    mean = jnp.mean(values, -1, keepdims=True)
    centred = values - mean
    inverse = lax.rsqrt(jnp.mean(centred * centred, -1, keepdims=True) + EPS)
    return centred * inverse, inverse


def norm_pull(grad, normed, inverse, gain):
    scaled = grad * gain
    return inverse * (
        scaled
        - jnp.mean(scaled, -1, keepdims=True)
        - normed * jnp.mean(scaled * normed, -1, keepdims=True)
    )


def gelu_both(u):
    a = jnp.abs(u)
    t = 1.0 / (1.0 + (0.3275911 / math.sqrt(2.0)) * a)
    e = jnp.exp(-0.5 * u * u)
    poly = t * (
        0.254829592
        + t * (-0.284496736 + t * (1.421413741 + t * (-1.453152027 + t * 1.061405429)))
    )
    tail = 0.5 * poly * e
    phi = jnp.where(u < 0, tail, 1.0 - tail)
    return u * phi, phi + u * e * (1.0 / math.sqrt(2.0 * math.pi))


def head_lanes(shape, e):
    lane = lax.broadcasted_iota(jnp.int32, shape, 1)
    return (lane // HD) == e


def whole(shape):
    return pl.BlockSpec(shape, lambda *_: (0,) * len(shape))


def rows_of(i):
    return pl.ds(pl.multiple_of(i * MB, 16), MB)


def row_of(i):
    return pl.ds(pl.multiple_of(i * S, 16), S)


G1, B1, BQ, BV, BO, G2, B2, BD = range(8)


def attn_fwd_kernel(
    kind_ref, x_ref, wg_ref, bqkv_ref, wo_ref, vec_ref,
    h1_ref, qkv_ref, p_ref, attn_ref, rl_ref, x1_ref, fa, fb,
):
    hq, r = pl.program_id(0), pl.program_id(1)

    @pl.when((hq == 0) & (r == 0))
    def _():
        for row in range(2):
            h1_ref[pl.ds(row * S + S - 16, 16), :] = jnp.zeros((16, D), BF)
            n1, _s = norm_parts(x_ref[row].astype(F32))
            h1_ref[pl.ds(row * S, SEQ), :] = (n1 * vec_ref[G1:G1 + 1, :] + vec_ref[B1:B1 + 1, :]).astype(BF)
            slot = lax.broadcasted_iota(jnp.int32, (S, 128), 0)
            lane = lax.broadcasted_iota(jnp.int32, (S, 128), 1)
            packed = jnp.where(slot < HALF, 0, jnp.where(slot < 2 * HALF, 1, 2))
            seg = jnp.where(kind_ref[row] == 1, packed, 0)
            fa[row] = jnp.where((lane < 3) & (seg == lane), -1e30, 0.0).astype(BF)
            fb[row] = jnp.where((lane < 3) & ((seg != lane) | (slot >= SEQ)), 1.0, 0.0).astype(BF)

    @pl.when(r == 0)
    def _():
        @pl.loop(0, T // MB)
        def _(i):
            rows = rows_of(i)
            qkv_ref[rows, :] = (mm(h1_ref[rows, :], wg_ref[...]) + bqkv_ref[...]).astype(BF)

    rows = pl.ds(pl.multiple_of(r * S, 16), S)
    feat_q, feat_k = fa[r], fb[r]
    ones = jnp.ones((S, 128), BF)
    scale = math.log2(math.e) / math.sqrt(HD)
    for j in range(HG // 2):
        at = j * 384
        qp, kp, vp = (qkv_ref[rows, at + 128 * n: at + 128 * (n + 1)] for n in range(3))
        kcat = jnp.concatenate([kp, feat_k], 1)
        total = None
        inv = None
        for e in range(2):
            keep = head_lanes((S, 128), e)
            qcat = jnp.concatenate([jnp.where(keep, qp, jnp.zeros_like(qp)), feat_q], 1)
            s = mm(qcat, kcat, NT)
            m = jnp.max(s, -1, keepdims=True)
            pb = jnp.exp2((s - m) * scale).astype(BF)
            p_ref[0, 2 * j + e] = pb
            vcat = jnp.concatenate([jnp.where(keep, vp, jnp.zeros_like(vp)), ones], 1)
            o = mm(pb, vcat)
            rl = 1.0 / o[:, 128:]
            part = o[:, :128] * rl
            total = part if total is None else total + part
            inv = rl if inv is None else jnp.where(keep, rl, inv)
        out = pl.ds(pl.multiple_of(hq * QW + j * 128, 128), 128)
        attn_ref[rows, out] = total.astype(BF)
        rl_ref[rows, out] = inv

    @pl.when((hq == D // QW - 1) & (r == 1))
    def _():
        for row in range(2):
            x1_ref[pl.ds(row * S + S - 16, 16), :] = jnp.zeros((16, D), F32)
            x1_ref[pl.ds(row * S, SEQ), :] = x_ref[row].astype(F32)

        @pl.loop(0, T // MB)
        def _(i):
            rr = rows_of(i)
            x1_ref[rr, :] = x1_ref[rr, :] + mm(attn_ref[rr, :], wo_ref[...]) + vec_ref[BO:BO + 1, :]


def attn_fwd(kind, x, wide, bqkv, vec):
    return pl.pallas_call(
        attn_fwd_kernel,
        grid=(D // QW, 2),
        in_specs=[
            pl.BlockSpec(memory_space=pltpu.SMEM), whole((2, SEQ, D)),
            pl.BlockSpec((D, GW), lambda h, r: (0, h)), pl.BlockSpec((1, GW), lambda h, r: (0, h)),
            pl.BlockSpec((D, D), lambda h, r: (0, 3)), whole((8, D)),
        ],
        out_specs=[
            whole((T, D)), pl.BlockSpec((T, GW), lambda h, r: (0, h)),
            pl.BlockSpec((1, HG, S, S), lambda h, r: (r, h, 0, 0)),
            whole((T, D)), whole((T, D)), whole((T, D)),
        ],
        out_shape=[
            jax.ShapeDtypeStruct((T, D), BF), jax.ShapeDtypeStruct((T, 3 * D), BF),
            jax.ShapeDtypeStruct((2, D // HD, S, S), BF),
            jax.ShapeDtypeStruct((T, D), BF), jax.ShapeDtypeStruct((T, D), F32), jax.ShapeDtypeStruct((T, D), F32),
        ],
        scratch_shapes=[pltpu.VMEM((2, S, 128), BF), pltpu.VMEM((2, S, 128), BF)],
        compiler_params=pltpu.CompilerParams(vmem_limit_bytes=LIMIT),
        name="attention_forward",
    )(kind, x, wide, bqkv, wide, vec)


def ffn_kernel(
    x1_ref, dm_ref, wu_ref, wd_ref, bu_ref, vec_ref,
    out_ref, dx1_ref, gwu_ref, gwd_ref, gbu_ref, gg2_ref, gb2_ref, gbd_ref,
    h2, h2t, dm, yacc, dacc, gs, dus,
):
    c = pl.program_id(0)

    @pl.when(c == 0)
    def _():
        for row in range(2):
            dm[pl.ds(row * S + S - 16, 16), :] = jnp.zeros((16, D), BF)
            dm[pl.ds(row * S, SEQ), :] = dm_ref[row]

        @pl.loop(0, T // MB)
        def _(i):
            rows = rows_of(i)
            x1 = x1_ref[rows, :]
            n2, _s = norm_parts(x1)
            h2[rows, :] = (n2 * vec_ref[G2:G2 + 1, :] + vec_ref[B2:B2 + 1, :]).astype(BF)
            yacc[rows, :] = x1 + vec_ref[BD:BD + 1, :]
            dacc[rows, :] = jnp.zeros((MB, D), F32)
        h2t[...] = h2[...].T
        gbd_ref[...] = jnp.sum(dm[...].astype(F32), 0, keepdims=True)

    gbu_ref[...] = jnp.zeros_like(gbu_ref)

    @pl.loop(0, T // MB)
    def _(i):
        rows = rows_of(i)
        u = mm(h2[rows, :], wu_ref[...]) + bu_ref[...]
        g, slope = gelu_both(u)
        gb = g.astype(BF)
        gs[rows, :] = gb
        yacc[rows, :] += mm(gb, wd_ref[...])
        du = (mm(dm[rows, :], wd_ref[...], NT) * slope).astype(BF)
        dus[rows, :] = du
        gbu_ref[...] += jnp.sum(du.astype(F32), 0, keepdims=True)
        dacc[rows, :] += mm(du, wu_ref[...], NT)

    for t in range(FC // 256):
        cols = pl.ds(t * 256, 256)
        gwd_ref[cols, :] = mm(gs[:, cols], dm[...], TN).astype(BF)

    @pl.loop(0, D // 256)
    def _(t):
        rows = pl.ds(pl.multiple_of(t * 256, 256), 256)
        gwu_ref[rows, :] = mm(h2t[rows, :], dus[...]).astype(BF)

    @pl.when(c == FF // FC - 1)
    def _():
        gg2_ref[...] = jnp.zeros_like(gg2_ref)
        gb2_ref[...] = jnp.zeros_like(gb2_ref)
        for row in range(2):
            out_ref[row] = yacc[pl.ds(row * S, SEQ), :].astype(BF)

        @pl.loop(0, T // MB)
        def _(i):
            rows = rows_of(i)
            n2, s2 = norm_parts(x1_ref[rows, :])
            dh = dacc[rows, :]
            gg2_ref[...] += jnp.sum(dh * n2, 0, keepdims=True)
            gb2_ref[...] += jnp.sum(dh, 0, keepdims=True)
            dx1_ref[rows, :] = dm[rows, :].astype(F32) + norm_pull(dh, n2, s2, vec_ref[G2:G2 + 1, :])


def ffn(x1, dm, wide, down, bu, vec):
    one = jax.ShapeDtypeStruct((1, D), F32)
    return pl.pallas_call(
        ffn_kernel,
        grid=(FF // FC,),
        in_specs=[
            whole((T, D)), whole((2, SEQ, D)),
            pl.BlockSpec((D, FC), lambda c: (0, c + UP_AT // FC)), pl.BlockSpec((FC, D), lambda c: (c, 0)),
            pl.BlockSpec((1, FC), lambda c: (0, c)), whole((8, D)),
        ],
        out_specs=[
            whole((2, SEQ, D)), whole((T, D)),
            pl.BlockSpec((D, FC), lambda c: (0, c)), pl.BlockSpec((FC, D), lambda c: (c, 0)),
            pl.BlockSpec((1, FC), lambda c: (0, c)), whole((1, D)), whole((1, D)), whole((1, D)),
        ],
        out_shape=[
            jax.ShapeDtypeStruct((2, SEQ, D), BF), jax.ShapeDtypeStruct((T, D), F32),
            jax.ShapeDtypeStruct((D, FF), BF), jax.ShapeDtypeStruct((FF, D), BF),
            jax.ShapeDtypeStruct((1, FF), F32), one, one, one,
        ],
        scratch_shapes=[
            pltpu.VMEM((T, D), BF), pltpu.VMEM((D, T), BF), pltpu.VMEM((T, D), BF),
            pltpu.VMEM((T, D), F32), pltpu.VMEM((T, D), F32),
            pltpu.VMEM((T, FC), BF), pltpu.VMEM((T, FC), BF),
        ],
        compiler_params=pltpu.CompilerParams(vmem_limit_bytes=LIMIT),
        name="feed_forward",
    )(x1, dm, wide, down, bu, vec)


def attn_bwd_kernel(
    x_ref, dx1_ref, h1_ref, qkv_ref, p_ref, attn_ref, rl_ref, wo_ref, wqkv_ref, vec_ref,
    gx_ref, gwqkv_ref, gwo_ref, gbqkv_ref, gbo_ref, gg1_ref, gb1_ref,
    da, dos, h1t, dqkv,
):
    hq, r = pl.program_id(0), pl.program_id(1)

    @pl.when((hq == 0) & (r == 0))
    def _():
        gbo_ref[...] = jnp.zeros_like(gbo_ref)

        @pl.loop(0, T // MB)
        def _(i):
            rows = rows_of(i)
            d = dx1_ref[rows, :].astype(BF)
            da[rows, :] = d
            gbo_ref[...] += jnp.sum(d.astype(F32), 0, keepdims=True)
            dos[rows, :] = (mm(d, wo_ref[...], NT) * rl_ref[rows, :]).astype(BF)
        h1t[...] = h1_ref[...].T

    rows = pl.ds(pl.multiple_of(r * S, 16), S)
    scale = 1.0 / math.sqrt(HD)
    for j in range(HG // 2):
        at = j * 384
        qp, kp, vp = (qkv_ref[rows, at + 128 * n: at + 128 * (n + 1)] for n in range(3))
        do = dos[rows, pl.ds(pl.multiple_of(hq * QW + j * 128, 128), 128)]
        prod = do.astype(F32) * attn_ref[rows, j * 128:(j + 1) * 128].astype(F32)
        dq = dk = dv = None
        for e in range(2):
            keep = head_lanes((S, 128), e)
            zero = jnp.zeros_like(qp)
            doe = jnp.where(keep, do, zero)
            dot = jnp.sum(jnp.where(keep, prod, 0.0), -1, keepdims=True)
            p = p_ref[0, 2 * j + e]
            ds = (p.astype(F32) * (mm(doe, vp, NT) - dot)).astype(BF)
            a = mm(ds, jnp.where(keep, kp, zero))
            b = mm(ds, jnp.where(keep, qp, zero), TN)
            c = mm(p, doe, TN)
            dq, dk, dv = (a, b, c) if dq is None else (dq + a, dk + b, dv + c)
        for n, part in enumerate((dq * scale, dk * scale, dv)):
            col = hq * GW + j * 384 + n * 128
            dqkv[rows, pl.ds(pl.multiple_of(col, 128), 128)] = part.astype(BF)

    @pl.when(r == 1)
    def _():
        part = dqkv[:, pl.ds(pl.multiple_of(hq * GW, 128), GW)]
        gbqkv_ref[...] = jnp.sum(part.astype(F32), 0, keepdims=True)

        @pl.loop(0, D // 256)
        def _(t):
            rr = pl.ds(pl.multiple_of(t * 256, 256), 256)
            gwqkv_ref[rr, :] = mm(h1t[rr, :], part).astype(BF)
        gwo_ref[...] = mm(attn_ref[...], da[...], TN).astype(BF)

    @pl.when((hq == D // QW - 1) & (r == 1))
    def _():
        gg1_ref[...] = jnp.zeros_like(gg1_ref)
        gb1_ref[...] = jnp.zeros_like(gb1_ref)
        for row in range(2):
            rr = pl.ds(row * S, SEQ)
            dh = mm(dqkv[pl.ds(row * S, S), :], wqkv_ref[...], NT)[:SEQ]
            n1, s1 = norm_parts(x_ref[row].astype(F32))
            gg1_ref[...] += jnp.sum(dh * n1, 0, keepdims=True)
            gb1_ref[...] += jnp.sum(dh, 0, keepdims=True)
            gx_ref[row] = (dx1_ref[rr, :] + norm_pull(dh, n1, s1, vec_ref[G1:G1 + 1, :])).astype(BF)


def attn_bwd(x, dx1, h1, qkv, p, attn, rl, wide, vec):
    act = pl.BlockSpec((T, QW), lambda h, r: (0, h))
    one = jax.ShapeDtypeStruct((1, D), F32)
    return pl.pallas_call(
        attn_bwd_kernel,
        grid=(D // QW, 2),
        in_specs=[
            whole((2, SEQ, D)), whole((T, D)), whole((T, D)), pl.BlockSpec((T, GW), lambda h, r: (0, h)),
            pl.BlockSpec((1, HG, S, S), lambda h, r: (r, h, 0, 0)), act, whole((T, D)),
            pl.BlockSpec((D, D), lambda h, r: (0, 3)), whole((D, 3 * D)), whole((8, D)),
        ],
        out_specs=[
            whole((2, SEQ, D)), pl.BlockSpec((D, GW), lambda h, r: (0, h)),
            pl.BlockSpec((QW, D), lambda h, r: (h, 0)),
            pl.BlockSpec((1, GW), lambda h, r: (0, h)), whole((1, D)), whole((1, D)), whole((1, D)),
        ],
        out_shape=[
            jax.ShapeDtypeStruct((2, SEQ, D), BF), jax.ShapeDtypeStruct((D, 3 * D), BF), jax.ShapeDtypeStruct((D, D), BF),
            jax.ShapeDtypeStruct((1, 3 * D), F32), one, one, one,
        ],
        scratch_shapes=[
            pltpu.VMEM((T, D), BF), pltpu.VMEM((T, D), BF), pltpu.VMEM((D, T), BF), pltpu.VMEM((T, 3 * D), BF),
        ],
        compiler_params=pltpu.CompilerParams(vmem_limit_bytes=LIMIT),
        name="attention_backward",
    )(x, dx1, h1, qkv, p, attn, rl, wide, wide, vec)


NZ = 4
CH = 48
HW = 384
SR = 16
N_WIDE = AW // (2 * HW)
N_DOWN = 4
N_UP = FF // D
DH = 2 * CH
NV = 8
VW = (24,) * NV + (96,)


def one(i):
    return pl.ds(i, 1)


EVERY = pl.ds(0, NZ)
TWO = pl.ds(0, 2)


def where_am_i():
    dp, fs = lax.axis_index("dp"), lax.axis_index("fsdp")
    return lax.div(dp, 2), lax.rem(dp, 2), lax.div(fs, 2), lax.rem(fs, 2)


def device(z, x, y, c):
    return (z * 2 + x, y * 2 + c)


def partners(z, x, y, c):
    found = [device(lax.rem(z + k, NZ), x, y, c) for k in (1, 2, 3)]
    return found + [device(z, 1 - x, y, c), device(z, x, 1 - y, c), device(z, x, y, 1 - c)]


def say_hello(here):
    barrier = pltpu.get_barrier_semaphore()
    for other in partners(*here):
        pl.semaphore_signal(barrier, inc=1, device_id=other, device_id_type=MESH)


def await_all():
    pl.semaphore_wait(pltpu.get_barrier_semaphore(), 6)


def remote(src, dst, sems, n, target):
    return pltpu.make_async_remote_copy(
        src_ref=src, dst_ref=dst, send_sem=sems[0].at[n], recv_sem=sems[1].at[n],
        device_id=target, device_id_type=MESH,
    )


def half(i, core):
    return pl.ds(pl.multiple_of(i * 2 * HW + core * HW, 128), HW)


def down_rows(i, core):
    return pl.ds(pl.multiple_of(core * DH + (i // 2) * CH, 16), CH)


def down_cols(i):
    return pl.ds((i % 2) * HW, HW)


TOK = 48


def rows_in(src, row, *targets):
    for ref in targets:
        ref[pl.ds(row * S + S - 16, 16), :] = jnp.zeros((16, D), ref.dtype)

    @pl.loop(0, SEQ // TOK)
    def _(i):
        part = src[pl.ds(i * TOK, TOK), row, :]
        for ref in targets:
            ref[pl.ds(pl.multiple_of(row * S + i * TOK, 16), TOK), :] = part.astype(ref.dtype)
    last = src[SEQ - 1:SEQ, row, :]
    for ref in targets:
        ref[pl.ds(row * S + SEQ - 1, 1), :] = last.astype(ref.dtype)


def rows_out(src, target, row):
    @pl.loop(0, SEQ // TOK)
    def _(i):
        target[pl.ds(i * TOK, TOK), row, :] = src[pl.ds(pl.multiple_of(row * S + i * TOK, 16), TOK), :]
    target[SEQ - 1:SEQ, row, :] = src[pl.ds(row * S + SEQ - 1, 1), :]


def transpose_into(target, src):
    @pl.loop(0, D // 128)
    def _(i):
        cols = pl.ds(pl.multiple_of(i * 128, 128), 128)
        target[cols, :] = src[:, cols].T


def add(a, b):
    return (a.astype(F32) + b.astype(F32)).astype(BF)


def plan(entries, ticks):
    table = {n: [] for n in range(len(ticks))}
    rest = []
    for due, action in sorted(entries, key=lambda e: e[0]):
        slot = min((n for n, t in enumerate(ticks) if t >= due), default=None)
        (rest if slot is None else table[slot]).append(action)
    return table, rest


class Gather:
    COPIES = 7

    def __init__(self, here, sems, base, view, first):
        z, x, y, c = here
        peers = partners(*here)
        mine = view(one(z), one(x), one(y))
        column = view(EVERY, one(x), one(y))
        fx, fy = jnp.where(c == 0, 1 - x, x), jnp.where(c == 0, y, 1 - y)
        tx, ty = jnp.where(c == 0, x, 1 - x), jnp.where(c == 0, 1 - y, y)
        passed = view(EVERY, one(fx), one(fy))
        all_of = view(EVERY, TWO, TWO)
        make = lambda n, src, dst, to: remote(src, dst, sems, base + n, to)
        self.along_z = [make(k, mine if first is None else first, mine, peers[k]) for k in range(3)]
        self.along_x = make(3, column, column, peers[3])
        self.along_y = make(4, column, column, peers[4])
        self.diagonal = make(5, passed, passed, device(z, tx, ty, c))
        self.sibling = make(6, all_of, all_of, peers[5])

    def start(self, phase):
        if phase == 0:
            for copy in self.along_z:
                copy.start()
        elif phase == 1:
            for copy in self.along_z:
                copy.wait_recv()
            self.along_x.start()
            self.along_y.start()
        elif phase == 2:
            self.along_x.wait_recv()
            self.along_y.wait_recv()
            self.diagonal.start()
        elif phase == 3:
            self.diagonal.wait_recv()
            self.sibling.start()
        else:
            self.sibling.wait_recv()

    def drain(self):
        for copy in (*self.along_z, self.along_x, self.along_y, self.diagonal, self.sibling):
            copy.wait_send()


class Scatter:
    COPIES = 7

    def __init__(self, here, sems, base, theirs, mine, acc, via, last, zs):
        self.mine, self.acc, self.via, self.last, self.zs = mine, acc, via, last, zs
        z, x, y, c = self.here = here
        peers = partners(*here)
        ix, iy = jnp.where(c == 0, x, 1 - x), jnp.where(c == 0, 1 - y, y)
        self.px, self.py = jnp.where(c == 0, 1 - x, x), jnp.where(c == 0, y, 1 - y)
        first, second = device(z, ix, iy, c), device(z, self.px, self.py, c)
        make = lambda n, src, dst, to: remote(src, dst, sems, base + n, to)
        at = lambda xs, ys: acc.at[EVERY, one(xs), one(ys)]
        self.swap = make(0, theirs, acc, peers[5])
        self.far = make(1, at(1 - x, 1 - y), via.at[0], first)
        self.near = make(2, at(ix, iy), via.at[1], first)
        self.next = make(3, at(self.px, self.py), last, second)
        self.along_z = [
            make(4 + k, acc.at[one(lax.rem(z + k + 1, NZ)), one(x), one(y)], zs.at[k], peers[k]) for k in range(3)
        ]

    def start(self, phase):
        z, x, y, c = self.here
        acc = self.acc
        if phase == 0:
            self.swap.start()
        elif phase == 1:
            self.swap.wait_recv()

            @pl.loop(0, NZ)
            def _(i):
                for xi in range(2):
                    for yi in range(2):
                        acc[i, xi, yi] = add(acc[i, xi, yi], self.mine(i, xi, yi))
            self.far.start()
            self.near.start()
        elif phase == 2:
            self.far.wait_recv()
            px, py = self.px, self.py

            @pl.loop(0, NZ)
            def _(i):
                acc[i, px, py] = add(acc[i, px, py], self.via[0, i, 0, 0])
            self.next.start()
            self.near.wait_recv()

            @pl.loop(0, NZ)
            def _(i):
                acc[i, x, y] = add(acc[i, x, y], self.via[1, i, 0, 0])
        elif phase == 3:
            self.next.wait_recv()

            @pl.loop(0, NZ)
            def _(i):
                acc[i, x, y] = add(acc[i, x, y], self.last[i, 0, 0])
            for copy in self.along_z:
                copy.start()

    def total(self):
        z, x, y, c = self.here
        for copy in self.along_z:
            copy.wait_recv()
        parts = [self.acc[z, x, y]] + [self.zs[k, 0, 0, 0] for k in range(3)]
        return sum(part.astype(F32) for part in parts)

    def drain(self):
        for copy in (self.swap, self.far, self.near, self.next, *self.along_z):
            copy.wait_send()


def scatter_bufs(n, width):
    return [
        pltpu.VMEM((n, NZ, 2, 2, CH, width), BF), pltpu.VMEM((n, 2, NZ, 1, 1, CH, width), BF),
        pltpu.VMEM((n, NZ, 1, 1, CH, width), BF), pltpu.VMEM((n, 3, 1, 1, 1, CH, width), BF),
    ]


def dma_sems(*counts):
    return [pltpu.SemaphoreType.DMA((k,)) for k in counts]


def fixed(shape):
    return pl.BlockSpec(shape, lambda s: (0,) * len(shape), pipeline_mode=pl.Buffered(1))


def vmem():
    return pl.BlockSpec(memory_space=pltpu.VMEM)


def hbm():
    return pl.BlockSpec(memory_space=pl.ANY)


N_ATT = 2 * (D // QW)
PACE = 5.4
FORWARD_LAG = (0.0, 10.0, 24.0, 33.0, 40.0)
FORWARD_FROM = 28.0
FIRST_PACE = 3.2
FORWARD_PACE = 5.4
FORWARD_TICKS = [FORWARD_FROM + 2.9 * n for n in range(12)] + [FORWARD_FROM + 35.0 + 2.1 * n for n in range(16)]


def forward_kernel(
    kind_ref, x_in, dm_in, wqkv_ref, wout_ref, wup_ref, wdown_ref, *refs,
):
    small_refs = refs[:NV + 1]
    (
        h1t_out, qkv_ref, p_ref, attn_out, rl_out, x1_out, dmp_out, h2t_out, g_ref, slope_ref, gdown_ref,
        vec_ref, xb_out, watt_out, wup_out, down_out,
        h1t_ref, attn_ref, rl_ref, x1_ref, dmp_ref, h2t_ref, xb_ref, out_sem, x_ref, dm_ref, in_sem,
        fa, fb, h1, h2, staged, swap, watt, wup, bqkv, bu, smalls,
        sems_s, sems_r, swap_s, swap_r, small_s, small_r, copy_sem,
    ) = refs[NV + 1:]
    step = pl.program_id(0)
    here = where_am_i()
    z, x, y, c = here
    peers = partners(*here)
    sems = (sems_s, sems_r)

    swaps = [
        remote(staged.at[:, half(i, 1 - c)], swap.at[:, i * HW:(i + 1) * HW], (swap_s, swap_r), i, peers[5])
        for i in range(N_WIDE)
    ]
    items, own = [], []
    for i in range(N_WIDE):
        buf, at = (watt, i) if i < 4 else (wup, i - 4)
        view = lambda zs, xs, ys, buf=buf, at=at: buf.at[zs, xs, ys, :, half(at, c)]
        items.append(Gather(here, sems, i * Gather.COPIES, view, None))
    for i in range(N_DOWN):
        rows, cols = down_rows(i, c), down_cols(i)
        view = lambda zs, xs, ys, rows=rows, cols=cols: down_out.at[zs, xs, ys, rows, cols]
        first = wdown_ref.at[:, :, :, pl.ds((i // 2) * CH, CH), cols]
        items.append(Gather(here, sems, (N_WIDE + i) * Gather.COPIES, view, first))
        own.append(pltpu.make_async_copy(first, view(one(z), one(x), one(y)), copy_sem.at[N_WIDE + i]))
    keeps = []
    for i in range(N_WIDE):
        src, dst, at = (watt, watt_out, i) if i < 4 else (wup, wup_out, i - 4)
        cols = pl.ds(at * D, D)
        keeps.append(pltpu.make_async_copy(
            src.at[:, :, :, :, cols], dst.at[:, :, :, :, cols], copy_sem.at[i]))

    x_load = pltpu.make_async_copy(x_in, x_ref, in_sem.at[0])
    dm_load = pltpu.make_async_copy(dm_in, dm_ref, in_sem.at[1])
    first_out = [
        pltpu.make_async_copy(a, b, out_sem.at[n])
        for n, (a, b) in enumerate(((h1t_ref, h1t_out), (dmp_ref, dmp_out), (xb_ref, xb_out)))
    ]
    next_out = [
        pltpu.make_async_copy(a, b, out_sem.at[3 + n])
        for n, (a, b) in enumerate(((attn_ref, attn_out), (rl_ref, rl_out), (x1_ref, x1_out), (h2t_ref, h2t_out)))
    ]

    def act(action):
        i, phase = action
        if i >= N_WIDE and phase == 0:
            own[i - N_WIDE].start()
        if i >= N_WIDE and phase == 1:
            own[i - N_WIDE].wait()
        items[i].start(phase)
        if phase == 4 and i < N_WIDE:
            keeps[i].start()

    needed = {1: 4, 2: 8, 3: 11, 4: 12, 5: 16, 6: 20, 7: 24}
    entries = []
    for i in range(1, N_WIDE + N_DOWN):
        for phase in range(5):
            due = FORWARD_PACE * i + FORWARD_LAG[phase] if phase else FIRST_PACE * i
            if i in needed:
                due = min(due, FORWARD_TICKS[needed[i]])
            entries.append((due, (i, phase)))
    early = [a for t, a in sorted(entries, key=lambda e: e[0]) if t < FORWARD_FROM]
    table, late = plan([e for e in entries if e[0] >= FORWARD_FROM], FORWARD_TICKS)

    def tick(slot, could_be):
        for n in could_be:
            if table[n]:
                @pl.when(slot == n)
                def _(n=n):
                    for action in table[n]:
                        act(action)

    @pl.when(step == 0)
    def _():
        say_hello(here)
        x_load.start()
        dm_load.start()
        for pair in range(6):
            for n in range(3):
                at = pair * 384 + n * 128
                staged[:, at:at + 128] = wqkv_ref[:, n * D + pair * 128:n * D + (pair + 1) * 128].astype(F32)
        staged[:, OUT_AT:UP_AT] = wout_ref[...].astype(F32)
        staged[:, UP_AT:] = wup_ref[...].astype(F32)
        line = smalls.at[z, x, y, c]
        line[...] = jnp.zeros((SR, 128), F32)
        for n, (ref, width) in enumerate(zip(small_refs, VW)):
            line[n:n + 1, 0:width] = ref[...].astype(F32).reshape(1, width)
        await_all()
        swaps[0].start()

        def small_copy(n, src, to):
            return remote(src, src, (small_s, small_r), n, to)

        small_c = small_copy(0, smalls.at[one(z), one(x), one(y), one(c)], peers[5])
        both = smalls.at[one(z), one(x), one(y), TWO]
        small_z = [small_copy(1 + k, both, peers[k]) for k in range(3)]
        small_x = small_copy(4, smalls.at[EVERY, one(x), one(y), TWO], peers[3])
        small_y = small_copy(5, smalls.at[EVERY, TWO, one(y), TWO], peers[4])
        small_c.start()
        for i in range(1, N_WIDE):
            swaps[i].start()

        def take_block(i):
            swaps[i].wait_recv()
            mine_part = staged[:, half(i, c)]
            their_part = swap[:, i * HW:(i + 1) * HW]
            buf, at = (watt, i) if i < 4 else (wup, i - 4)
            lower = jnp.where(c == 0, mine_part, their_part)
            upper = jnp.where(c == 0, their_part, mine_part)
            buf[z, x, y, :, half(at, c)] = jnp.concatenate([lower, upper], 0).astype(BF)

        waiting = list(early)

        def act_some(count):
            for _n in range(min(count, len(waiting))):
                act(waiting.pop(0))

        take_block(0)
        items[0].start(0)
        small_c.wait_recv()
        for copy in small_z:
            copy.start()
        for i in range(1, N_WIDE):
            take_block(i)
        x_load.wait()
        rows_in(x_ref, 0, x1_ref, xb_ref)
        for copy in small_z:
            copy.wait_recv()
        small_x.start()
        act_some(1)
        items[0].start(1)
        rows_in(x_ref, 1, x1_ref, xb_ref)
        small_x.wait_recv()
        small_y.start()
        act_some(1)
        items[0].start(2)
        act_some(1)
        dm_load.wait()
        for row in range(2):
            rows_in(dm_ref, row, dmp_ref)
        items[0].start(3)
        small_y.wait_recv()
        src = lax.broadcasted_iota(jnp.int32, (128, D), 0)
        dst = lax.broadcasted_iota(jnp.int32, (128, D), 1)
        spread_short = jnp.where(lax.rem(dst, 24) == src, 1.0, 0.0).astype(BF)
        spread_long = jnp.where(lax.rem(dst, 96) == src, 1.0, 0.0).astype(BF)
        col = lax.broadcasted_iota(jnp.int32, (8, D), 1)
        vec_ref[...] = jnp.zeros_like(vec_ref)

        @pl.loop(0, NZ)
        def _(zi):
            pieces = smalls[zi].reshape(8 * SR, 128).astype(BF)
            short, long = mm(pieces, spread_short), mm(pieces, spread_long)
            for k in range(8):
                at = SR * k
                part = jnp.where(lax.div(col, 24) == zi * 8 + k, short[at:at + NV], 0.0)
                more = jnp.where(lax.div(col, 96) == k, long[at + NV:at + SR], 0.0)
                vectors, hidden_bias = (part, more) if k == 0 else (vectors + part, hidden_bias + more)
            vec_ref[...] += vectors
            bu[zi] = hidden_bias
        for pair in range(6):
            n, at = pair // 2, (pair % 2) * 384
            bqkv[n, :, at:at + 128] = vec_ref[BQ:BQ + 1, pair * 128:(pair + 1) * 128]
            bqkv[n, :, at + 128:at + 256] = jnp.zeros((1, 128), F32)
            bqkv[n, :, at + 256:at + 384] = vec_ref[BV:BV + 1, pair * 128:(pair + 1) * 128]
        act_some(2)

        @pl.loop(0, T // MB)
        def _(i):
            rows = rows_of(i)
            n1, _s = norm_parts(x1_ref[rows, :])
            h1[rows, :] = (n1 * vec_ref[G1:G1 + 1, :] + vec_ref[B1:B1 + 1, :]).astype(BF)
        for row in range(2):
            slot = lax.broadcasted_iota(jnp.int32, (S, 128), 0)
            lane = lax.broadcasted_iota(jnp.int32, (S, 128), 1)
            packed = jnp.where(slot < HALF, 0, jnp.where(slot < 2 * HALF, 1, 2))
            seg = jnp.where(kind_ref[row] == 1, packed, 0)
            fa[row] = jnp.where((lane < 3) & (seg == lane), -1e30, 0.0).astype(BF)
            fb[row] = jnp.where((lane < 3) & ((seg != lane) | (slot >= SEQ)), 1.0, 0.0).astype(BF)
        act_some(len(waiting))
        transpose_into(h1t_ref, h1)
        for copy in first_out:
            copy.start()
        rl_ref[...] = jnp.zeros_like(rl_ref)
        act((0, 4))
        for copy in (small_c, *small_z, small_x, small_y, *swaps):
            copy.wait_send()

    @pl.when(step < N_ATT)
    def _():
        hq, r = lax.div(step, 2), lax.rem(step, 2)
        tick(2 * step, range(0, 12, 2))

        @pl.when(r == 0)
        def _():
            @pl.loop(0, 2)
            def _(i):
                rows = row_of(i)
                w = watt[:, :, :, :, pl.ds(pl.multiple_of(hq * GW, 128), GW)].reshape(D, GW)
                qkv_ref[rows, :] = (mm(h1[rows, :], w) + bqkv[hq]).astype(BF)

        rows = pl.ds(pl.multiple_of(r * S, 16), S)
        feat_q, feat_k = fa[r], fb[r]
        ones = jnp.ones((S, 128), BF)
        scale = math.log2(math.e) / math.sqrt(HD)
        for j in range(HG // 2):
            if j:
                tick(2 * step + 1, range(1, 12, 2))
            at = j * 384
            qp, kp, vp = (qkv_ref[rows, at + 128 * n: at + 128 * (n + 1)] for n in range(3))
            kcat = jnp.concatenate([kp, feat_k], 1)
            total = None
            for e in range(2):
                keep = head_lanes((S, 128), e)
                qcat = jnp.concatenate([jnp.where(keep, qp, jnp.zeros_like(qp)), feat_q], 1)
                s = mm(qcat, kcat, NT)
                m = jnp.max(s, -1, keepdims=True)
                pb = jnp.exp2((s - m) * scale).astype(BF)
                p_ref[0, 2 * j + e] = pb
                vcat = jnp.concatenate([jnp.where(keep, vp, jnp.zeros_like(vp)), ones], 1)
                o = mm(pb, vcat)
                rl = 1.0 / o[:, 128:]
                part = o[:, :128] * rl
                total = part if total is None else total + part
                spot = lax.broadcasted_iota(jnp.int32, (S, 128), 1) == hq * HG + 2 * j + e
                rl_ref[rows, :] = jnp.where(spot, rl, rl_ref[rows, :])
            out = pl.ds(pl.multiple_of(hq * QW + j * 128, 128), 128)
            attn_ref[rows, out] = total.astype(BF)

    @pl.when(step == N_ATT - 1)
    def _():
        @pl.loop(0, T // MB)
        def _(i):
            rows = rows_of(i)
            wo = watt[:, :, :, :, OUT_AT:UP_AT].reshape(D, D)
            x1 = x1_ref[rows, :] + mm(attn_ref[rows, :], wo) + vec_ref[BO:BO + 1, :]
            x1_ref[rows, :] = x1
            n2, _s = norm_parts(x1)
            h2[rows, :] = (n2 * vec_ref[G2:G2 + 1, :] + vec_ref[B2:B2 + 1, :]).astype(BF)
        transpose_into(h2t_ref, h2)
        for copy in next_out:
            copy.start()

    @pl.when(step >= N_ATT)
    def _():
        part = step - N_ATT

        @pl.loop(0, 2)
        def _(i):
            tick(12 + 4 * part + 2 * i, range(12, len(FORWARD_TICKS), 2))
            tick(12 + 4 * part + 2 * i + 1, range(13, len(FORWARD_TICKS), 2))
            rows = row_of(i)
            w = wup[:, :, :, :, pl.ds(pl.multiple_of(part * D, 128), D)].reshape(D, D)
            g, slope = gelu_both(mm(h2[rows, :], w) + bu[part, 0:1, :])
            g_ref[rows, :] = g.astype(BF)
            slope_ref[rows, :] = slope.astype(BF)

        @pl.loop(0, 2)
        def _(t):
            cols = pl.ds(pl.multiple_of(t * 384, 128), 384)
            gdown_ref[cols, :] = mm(g_ref[:, cols], dmp_ref[...], TN).astype(BF)

    @pl.when(step == N_ATT + N_UP - 1)
    def _():
        for action in late:
            act(action)
        for item in items:
            item.drain()
        for copy in (*keeps, *first_out, *next_out):
            copy.wait()


def forward(kind, x, dm, wqkv, wout, wup, wdown, smalls):
    n = N_WIDE + N_DOWN
    att = lambda s: jnp.minimum(s, N_ATT - 1)
    ff = lambda s: jnp.maximum(s - N_ATT, 0)
    shape = jax.ShapeDtypeStruct
    return pl.pallas_call(
        forward_kernel,
        grid=(N_ATT + N_UP,),
        in_specs=[
            pl.BlockSpec(memory_space=pltpu.SMEM), hbm(), hbm(),
            fixed((24, 3 * D)), fixed((24, D)), fixed((24, FF)), fixed((1, 1, 1, 96, D)),
            *[pl.BlockSpec((w,), lambda s: (0,), pipeline_mode=pl.Buffered(1)) for w in VW],
        ],
        out_specs=[
            hbm(), pl.BlockSpec((T, GW), lambda s: (0, att(s) // 2)),
            pl.BlockSpec((1, HG, S, S), lambda s: (att(s) % 2, att(s) // 2, 0, 0)),
            hbm(), hbm(), hbm(), hbm(), hbm(),
            pl.BlockSpec((T, D), lambda s: (0, ff(s))), pl.BlockSpec((T, D), lambda s: (0, ff(s))),
            pl.BlockSpec((D, D), lambda s: (ff(s), 0)),
            fixed((NV, D)), hbm(), hbm(), hbm(), hbm(),
        ],
        out_shape=[
            shape((D, T), BF), shape((T, 3 * D), BF), shape((2, D // HD, S, S), BF),
            shape((T, D), BF), shape((T, 128), F32), shape((T, D), F32), shape((T, D), BF), shape((D, T), BF),
            shape((T, FF), BF), shape((T, FF), BF), shape((FF, D), BF), shape((NV, D), F32), shape((T, D), BF),
            shape((NZ, 2, 2, CH, UP_AT), BF), shape((NZ, 2, 2, CH, FF), BF), shape((NZ, 2, 2, 4 * CH, D), BF),
        ],
        scratch_shapes=[
            pltpu.VMEM((D, T), BF), pltpu.VMEM((T, D), BF), pltpu.VMEM((T, 128), F32), pltpu.VMEM((T, D), F32),
            pltpu.VMEM((T, D), BF), pltpu.VMEM((D, T), BF), pltpu.VMEM((T, D), BF), *dma_sems(7),
            pltpu.VMEM((SEQ, 2, D), BF), pltpu.VMEM((SEQ, 2, D), BF), *dma_sems(2),
            pltpu.VMEM((2, S, 128), BF), pltpu.VMEM((2, S, 128), BF), pltpu.VMEM((T, D), BF), pltpu.VMEM((T, D), BF),
            pltpu.VMEM((24, AW), F32), pltpu.VMEM((24, AW // 2), F32),
            pltpu.VMEM((NZ, 2, 2, CH, UP_AT), BF), pltpu.VMEM((NZ, 2, 2, CH, FF), BF),
            pltpu.VMEM((3, 1, GW), F32), pltpu.VMEM((N_UP, 8, D), F32), pltpu.VMEM((NZ, 2, 2, 2, SR, 128), F32),
            *dma_sems(n * Gather.COPIES, n * Gather.COPIES, N_WIDE, N_WIDE, 6, 6, n),
        ],
        compiler_params=pltpu.CompilerParams(collective_id=0, has_side_effects=True, vmem_limit_bytes=LIMIT),
        name="forward",
    )(kind, x, dm, wqkv, wout, wup, wdown.reshape(1, 1, 1, 96, D), *smalls)


BACK_LAG = (0.0, 5.0, 15.0, 23.0, 32.0)
FFN_LAG = (0.0, 4.0, 13.0, 20.0, 27.0)
FFN_PACE = 4.0
FFN_TICKS = [4.0 + 9.0 * s + t for s in range(4) for t in (0.0, 0.1, 2.8, 2.9, 5.7, 7.3)]


def ffn_back_kernel(
    x1_in, dm_ref, g_ref, slope_ref, wu_ref, wd_ref, h2t_in, vec_ref, gdown_ref,
    y_ref, dx1_ref, da_ref, gup_ref, sums_ref, odown_ref,
    x1_ref, h2t_ref, in_sem, yacc, dacc, dus, mine, acc, via, last, zs, sems_s, sems_r, own_sem,
):
    step = pl.program_id(0)
    here = where_am_i()
    z, x, y, c = here
    items, own = [], []
    for i in range(N_DOWN):
        rows, cols = down_rows(i, c), down_cols(i)
        own.append(pltpu.make_async_copy(gdown_ref.at[:, :, :, rows, cols], mine.at[i], own_sem.at[i]))
        items.append(Scatter(
            here, (sems_s, sems_r), i * Scatter.COPIES, gdown_ref.at[EVERY, TWO, TWO, down_rows(i, 1 - c), cols],
            lambda a, b, d, i=i: mine[i, a, b, d], acc.at[i], via.at[i], last.at[i], zs.at[i],
        ))
    later = [
        pltpu.make_async_copy(a, b, in_sem.at[n])
        for n, (a, b) in enumerate(((h2t_in, h2t_ref), (x1_in, x1_ref)))
    ]
    entries = [
        (5.0 + FFN_PACE * i + lag, (i, phase)) for i in range(N_DOWN) for phase, lag in enumerate(FFN_LAG) if (i, phase) != (0, 0)
    ]
    table, late = plan(entries, FFN_TICKS)

    def act(action):
        i, phase = action
        if phase == 1:
            own[i].wait()
        if phase == 4:
            odown_ref[pl.ds((i // 2) * CH, CH), down_cols(i)] = items[i].total()
        else:
            items[i].start(phase)

    def tick(slot):
        for n, todo in table.items():
            if todo:
                @pl.when(slot == n)
                def _(todo=todo):
                    for action in todo:
                        act(action)

    @pl.when(step == 0)
    def _():
        say_hello(here)
        for copy in (*later, *own):
            copy.start()

        @pl.loop(0, T // MB)
        def _(i):
            rows = rows_of(i)
            yacc[rows, :] = jnp.broadcast_to(vec_ref[BD:BD + 1, :], (MB, D))
            dacc[rows, :] = jnp.zeros((MB, D), F32)
        sums_ref[...] = jnp.zeros_like(sums_ref)
        sums_ref[2:3, :] = jnp.sum(dm_ref[...].astype(F32), 0, keepdims=True)

    @pl.loop(0, 2)
    def _(i):
        @pl.when((step == 0) & (i == 1))
        def _():
            await_all()
            act((0, 0))

        tick(6 * step + 2 * i)
        tick(6 * step + 2 * i + 1)
        rows = row_of(i)
        g = g_ref[rows, :]
        yacc[rows, :] += mm(g, wd_ref[...])
        du = (mm(dm_ref[rows, :], wd_ref[...], NT) * slope_ref[rows, :].astype(F32)).astype(BF)
        dus[rows, :] = du
        sums_ref[pl.ds(3 + step, 1), :] += jnp.sum(du.astype(F32), 0, keepdims=True)
        dacc[rows, :] += mm(du, wu_ref[...], NT)

    @pl.when(step == 0)
    def _():
        later[0].wait()

    @pl.loop(0, 2)
    def _(t):
        tick(6 * step + 4 + t)
        rows = pl.ds(pl.multiple_of(t * 384, 128), 384)
        gup_ref[rows, :] = mm(h2t_ref[rows, :], dus[...]).astype(BF)

    @pl.when(step == N_UP - 1)
    def _():
        later[1].wait()

        @pl.loop(0, T // MB)
        def _(i):
            rows = rows_of(i)
            x1 = x1_ref[rows, :]
            n2, s2 = norm_parts(x1)
            dh = dacc[rows, :]
            sums_ref[0:1, :] += jnp.sum(dh * n2, 0, keepdims=True)
            sums_ref[1:2, :] += jnp.sum(dh, 0, keepdims=True)
            dx1 = dm_ref[rows, :].astype(F32) + norm_pull(dh, n2, s2, vec_ref[G2:G2 + 1, :])
            dx1_ref[rows, :] = dx1
            da_ref[rows, :] = dx1.astype(BF)
            y_ref[rows, :] = (x1 + yacc[rows, :]).astype(BF)
        for action in late:
            act(action)
        for item in items:
            item.drain()


def ffn_back(x1, dm, g, slope, wup, down, h2t, vec, gdown):
    shape = jax.ShapeDtypeStruct
    col = pl.BlockSpec((T, D), lambda s: (0, s))
    return pl.pallas_call(
        ffn_back_kernel,
        grid=(N_UP,),
        in_specs=[
            hbm(), fixed((T, D)), col, col,
            pl.BlockSpec((D, D), lambda s: (0, s)), pl.BlockSpec((D, D), lambda s: (s, 0)),
            hbm(), fixed((NV, D)), hbm(),
        ],
        out_specs=[
            fixed((T, D)), fixed((T, D)), fixed((T, D)), pl.BlockSpec((D, D), lambda s: (0, s)), fixed((8, D)),
            fixed((96, D)),
        ],
        out_shape=[
            shape((T, D), BF), shape((T, D), F32), shape((T, D), BF), shape((D, FF), BF), shape((8, D), F32),
            shape((96, D), F32),
        ],
        scratch_shapes=[
            pltpu.VMEM((T, D), F32), pltpu.VMEM((D, T), BF), *dma_sems(2),
            pltpu.VMEM((T, D), F32), pltpu.VMEM((T, D), F32), pltpu.VMEM((T, D), BF),
            pltpu.VMEM((N_DOWN, NZ, 2, 2, CH, HW), BF), *scatter_bufs(N_DOWN, HW),
            *dma_sems(N_DOWN * 7, N_DOWN * 7, N_DOWN),
        ],
        compiler_params=pltpu.CompilerParams(collective_id=1, has_side_effects=True, vmem_limit_bytes=LIMIT),
        name="feed_forward_back",
    )(x1, dm, g, slope, wup, down, h2t, vec, gdown.reshape(NZ, 2, 2, 4 * CH, D))


BACK_TICKS = [2.0 + 4.8 * n for n in range(12)]
N_BACK = N_UP + 4
END_LAG = (0.0, 4.0, 9.0, 14.0, 19.0)


def attn_back_kernel(
    xb_in, yb_in, dx1_in, da_ref, h1t_in, qkv_ref, p_ref, attn_ref, rl_ref, wo_ref, wqkv_ref, vec_ref, sums_ref, gup_ref,
    out_hbm, gx_hbm, oqkv_ref, oout_ref, oup_ref, *refs,
):
    small_outs = refs[:NV + 1]
    (
        xb_ref, yb_ref, dx1_ref, h1t_ref, in_sem, out_ref, gx_ref, out_sem, dos, dqkv, dh1, gqkv, gout, mine, acc, via, last, zs, done, landed, small,
        sems_s, sems_r, fin_s, fin_r, small_s, small_r, own_sem,
    ) = refs[NV + 1:]
    step = pl.program_id(0)
    hq, r = lax.div(step, 2), lax.rem(step, 2)
    here = where_am_i()
    z, x, y, c = here
    peers = partners(*here)
    items, own = [], []
    for n in range(N_BACK):
        if n < N_UP:
            theirs = gup_ref.at[EVERY, TWO, TWO, :, half(n, 1 - c)]
            own.append(pltpu.make_async_copy(gup_ref.at[:, :, :, :, half(n, c)], mine.at[n], own_sem.at[n]))
            get = lambda a, b, d, n=n: mine[n, a, b, d]
        elif n == N_UP:
            theirs = gout.at[EVERY, TWO, TWO, :, half(0, 1 - c)]
            get = lambda a, b, d: gout[a, b, d, :, half(0, c)]
        else:
            i = n - N_UP - 1
            theirs = gqkv.at[i, EVERY, TWO, TWO, :, half(0, 1 - c)]
            get = lambda a, b, d, i=i: gqkv[i, a, b, d, :, half(0, c)]
        items.append(Scatter(
            here, (sems_s, sems_r), n * Scatter.COPIES, theirs, get, acc.at[n], via.at[n], last.at[n], zs.at[n]))

    later = [
        pltpu.make_async_copy(a, b, in_sem.at[n])
        for n, (a, b) in enumerate(((h1t_in, h1t_ref), (xb_in, xb_ref), (dx1_in, dx1_ref), (yb_in, yb_ref)))
    ]

    y_out = pltpu.make_async_copy(out_ref, out_hbm, out_sem.at[0])
    gx_out = pltpu.make_async_copy(gx_ref, gx_hbm, out_sem.at[1])

    def final(n):
        theirs = pl.ds(pl.multiple_of((1 - c) * 24, 8), 24)
        return remote(done.at[n, theirs], landed.at[n], (fin_s, fin_r), n, peers[5])

    def put(n, core, value):
        if n > N_UP:
            for b in range(3):
                cols = pl.ds(pl.multiple_of(b * D + (n - N_UP - 1) * QW + core * 128, 128), 128)
                oqkv_ref[:, cols] = value[:, b * 128:(b + 1) * 128]
        elif n == N_UP:
            oout_ref[:, half(0, core)] = value
        else:
            oup_ref[:, half(n, core)] = value

    def finish(n):
        done[n] = items[n].total()
        final(n).start()
        put(n, c, done[n, pl.ds(pl.multiple_of(c * 24, 8), 24)])

    def act(action):
        n, phase = action
        if n < N_UP and phase == 1:
            own[n].wait()
        if phase == 4:
            finish(n)
        else:
            items[n].start(phase)

    entries = []
    begin = 0.0
    for n in range(N_BACK):
        if n > N_UP:
            begin = max(begin, BACK_TICKS[0] + 19.2 * (n - N_UP))
        for phase in range(5):
            if n < N_UP or phase > 0:
                lag = BACK_LAG if n < N_BACK - 2 else END_LAG
                entries.append((begin + lag[phase], (n, phase)))
        begin += PACE
    entries.remove((0.0, (0, 0)))
    table, tail = plan(entries, BACK_TICKS)
    final_steps = [a for a in tail if a[0] == N_BACK - 1]
    earlier = [a for a in tail if a[0] != N_BACK - 1]

    def tick(slot, could_be):
        for n in could_be:
            if table[n]:
                @pl.when(slot == n)
                def _(n=n):
                    for action in table[n]:
                        act(action)

    @pl.when(step == 0)
    def _():
        say_hello(here)
        for copy in (*own, *later):
            copy.start()
        small[0] = jnp.zeros((16, D), F32)
        src = lax.broadcasted_iota(jnp.int32, (128, D), 0)
        dst = lax.broadcasted_iota(jnp.int32, (128, D), 1)
        spread = jnp.where(lax.div(dst, HD) == src, 1.0, 0.0)

        @pl.loop(0, T // MB)
        def _(i):
            rows = rows_of(i)
            d = da_ref[rows, :]
            rl = lax.dot_general(
                rl_ref[rows, :], spread, NN, precision=lax.Precision.HIGHEST, preferred_element_type=F32)
            small[0, 4:5, :] += jnp.sum(d.astype(F32), 0, keepdims=True)
            dos[rows, :] = (mm(d, wo_ref[...], NT) * rl).astype(BF)
            dh1[rows, :] = jnp.zeros((MB, D), F32)
        @pl.loop(0, 2)
        def _(t):
            part = mm(attn_ref[:, pl.ds(pl.multiple_of(t * 384, 128), 384)], da_ref[...], TN)
            gout[pl.ds(2 * t, 2)] = part.astype(BF).reshape(2, 2, 2, CH, D)

        await_all()
        act((0, 0))
        items[N_UP].start(0)

    tick(2 * step, range(0, 12, 2))
    rows = pl.ds(pl.multiple_of(r * S, 16), S)
    scale = 1.0 / math.sqrt(HD)
    for j in range(HG // 2):
        if j:
            tick(2 * step + 1, range(1, 12, 2))
        at = j * 384
        qp, kp, vp = (qkv_ref[rows, at + 128 * n: at + 128 * (n + 1)] for n in range(3))
        lanes = pl.ds(pl.multiple_of(hq * QW + j * 128, 128), 128)
        do = dos[rows, lanes]
        prod = do.astype(F32) * attn_ref[rows, lanes].astype(F32)
        dq = dk = dv = None
        for e in range(2):
            keep = head_lanes((S, 128), e)
            zero = jnp.zeros_like(qp)
            doe = jnp.where(keep, do, zero)
            dot = jnp.sum(jnp.where(keep, prod, 0.0), -1, keepdims=True)
            p = p_ref[0, 2 * j + e]
            ds = (p.astype(F32) * (mm(doe, vp, NT) - dot)).astype(BF)
            a_, b_, c_ = mm(ds, jnp.where(keep, kp, zero)), mm(ds, jnp.where(keep, qp, zero), TN), mm(p, doe, TN)
            dq, dk, dv = (a_, b_, c_) if dq is None else (dq + a_, dk + b_, dv + c_)
        for n, part in enumerate((dq * scale, dk * scale, dv)):
            dqkv[rows, at + 128 * n:at + 128 * (n + 1)] = part.astype(BF)

    @pl.when(step == 1)
    def _():
        later[0].wait()

    @pl.when(r == 1)
    def _():
        sums = jnp.sum(dqkv[...].astype(F32), 0, keepdims=True)
        for j in range(2):
            cols = pl.ds(pl.multiple_of(hq * QW + j * 128, 128), 128)
            small[0, 2:3, cols] = sums[:, j * 384:j * 384 + 128]
            small[0, 3:4, cols] = sums[:, j * 384 + 256:j * 384 + 384]
        @pl.loop(0, 2)
        def _(t):
            part = mm(h1t_ref[pl.ds(pl.multiple_of(t * 384, 16), 384), :], dqkv[...])
            gqkv[hq, pl.ds(2 * t, 2)] = part.astype(BF).reshape(2, 2, 2, CH, GW)

        for i in range(3):
            @pl.when(hq == i)
            def _(i=i):
                items[N_UP + 1 + i].start(0)

        @pl.loop(0, 2)
        def _(i):
            rr = row_of(i)
            dh1[rr, :] += mm(dqkv[rr, :], wqkv_ref[...], NT)

    @pl.when(step == N_ATT - 1)
    def _():
        rest = final_steps[1:]
        for copy in later[1:]:
            copy.wait()

        @pl.loop(0, T // MB)
        def _(i):
            @pl.when(i == 0)
            def _():
                for action in earlier[:-1]:
                    act(action)

            @pl.when(i == 0)
            def _():
                act(final_steps[0])

            @pl.when(i == 3)
            def _():
                for action in earlier[-1:]:
                    act(action)
            rr = rows_of(i)
            dh = dh1[rr, :]
            n1, s1 = norm_parts(xb_ref[rr, :].astype(F32))
            small[0, 0:1, :] += jnp.sum(dh * n1, 0, keepdims=True)
            small[0, 1:2, :] += jnp.sum(dh, 0, keepdims=True)
            xb_ref[rr, :] = (dx1_ref[rr, :] + norm_pull(dh, n1, s1, vec_ref[G1:G1 + 1, :])).astype(BF)
        small[0, 5:12, :] = sums_ref[0:7, :]
        copies = []

        def send_small(n, src, dst, to):
            copy = remote(small.at[src], small.at[dst], (small_s, small_r), n, to)
            copy.start()
            copies.append(copy)

        send_small(0, 0, 1, peers[5])
        act(rest.pop(0))
        copies[0].wait_recv()
        small[2] = small[0] + small[1]
        send_small(1, 2, 3, peers[3])
        for row in range(2):
            rows_out(xb_ref, gx_ref, row)
        gx_out.start()
        copies[1].wait_recv()
        small[4] = small[2] + small[3]
        send_small(2, 4, 5, peers[4])
        act(rest.pop(0))
        for row in range(2):
            rows_out(yb_ref, out_ref, row)
        y_out.start()
        copies[2].wait_recv()
        small[6] = small[4] + small[5]
        for k in range(3):
            send_small(3 + k, 6, 7 + k, peers[k])
        for k in range(3):
            copies[3 + k].wait_recv()
        total = small[6] + small[7] + small[8] + small[9]
        me = lax.axis_index("dp") * lax.axis_size("fsdp") + lax.axis_index("fsdp")
        src = lax.broadcasted_iota(jnp.int32, (D, 128), 0)
        dst = lax.broadcasted_iota(jnp.int32, (D, 128), 1)

        def pick(lines, width, at):
            chosen = jnp.where((src == at + dst) & (dst < width), 1.0, 0.0)
            return lax.dot_general(
                lines, chosen, NN, precision=lax.Precision.HIGHEST, preferred_element_type=F32)

        mine_of = pick(total[:8], 24, me * 24)
        for n in range(NV):
            small_outs[n][...] = mine_of[n, :24]
        row = lax.broadcasted_iota(jnp.int32, (8, D), 0)
        longest = jnp.sum(jnp.where(row == lax.div(me, 8), total[8:16], 0.0), 0, keepdims=True)
        small_outs[NV][...] = pick(jnp.broadcast_to(longest, (8, D)), 96, lax.rem(me, 8) * 96)[0, :96]
        act(rest.pop(0))
        gx_out.wait()
        y_out.wait()
        for n in range(N_BACK):
            copy = final(n)
            copy.wait_recv()
            put(n, 1 - c, landed[n])
            copy.wait_send()
            items[n].drain()
        for copy in copies:
            copy.wait_send()


def attn_back(x, yb, dx1, da, h1t, qkv, p, attn, rl, watt, vec, sums, gup):
    shape = jax.ShapeDtypeStruct
    n_fin = N_BACK
    return pl.pallas_call(
        attn_back_kernel,
        grid=(N_ATT,),
        in_specs=[
            hbm(), hbm(), hbm(), fixed((T, D)), hbm(), pl.BlockSpec((T, GW), lambda s: (0, s // 2)),
            pl.BlockSpec((1, HG, S, S), lambda s: (s % 2, s // 2, 0, 0)), fixed((T, D)), fixed((T, 128)),
            pl.BlockSpec((D, D), lambda s: (0, 3), pipeline_mode=pl.Buffered(1)),
            pl.BlockSpec((D, GW), lambda s: (0, s // 2)), fixed((NV, D)), fixed((8, D)), hbm(),
        ],
        out_specs=[
            hbm(), hbm(), fixed((24, 3 * D)), fixed((24, D)), fixed((24, FF)),
            *[pl.BlockSpec((w,), lambda s: (0,), pipeline_mode=pl.Buffered(1)) for w in VW],
        ],
        out_shape=[
            shape((SEQ, 2, D), BF), shape((SEQ, 2, D), BF), shape((24, 3 * D), F32), shape((24, D), F32),
            shape((24, FF), F32), *[shape((w,), F32) for w in VW],
        ],
        scratch_shapes=[
            pltpu.VMEM((T, D), BF), pltpu.VMEM((T, D), BF), pltpu.VMEM((T, D), F32), pltpu.VMEM((D, T), BF), *dma_sems(4),
            pltpu.VMEM((SEQ, 2, D), BF), pltpu.VMEM((SEQ, 2, D), BF), *dma_sems(2),
            pltpu.VMEM((T, D), BF), pltpu.VMEM((T, GW), BF), pltpu.VMEM((T, D), F32),
            pltpu.VMEM((3, NZ, 2, 2, CH, GW), BF), pltpu.VMEM((NZ, 2, 2, CH, D), BF),
            pltpu.VMEM((N_UP, NZ, 2, 2, CH, HW), BF), *scatter_bufs(N_BACK, HW),
            pltpu.VMEM((N_BACK, CH, HW), F32), pltpu.VMEM((N_BACK, 24, HW), F32), pltpu.VMEM((10, 16, D), F32),
            *dma_sems(N_BACK * 7, N_BACK * 7, n_fin, n_fin, 6, 6, N_UP),
        ],
        compiler_params=pltpu.CompilerParams(collective_id=2, has_side_effects=True, vmem_limit_bytes=LIMIT),
        name="attention_back",
    )(x, yb, dx1, da, h1t, qkv, p, attn, rl, watt, watt, vec, sums, gup.reshape(NZ, 2, 2, CH, FF))


def hand_over_kernel(*refs):
    n = (len(refs) - 2) // 3
    sems_in, sems_out = refs[-2:]
    held = refs[2 * n:3 * n]
    arrive = [pltpu.make_async_copy(refs[i], held[i], sems_in.at[i]) for i in range(n)]
    leave = [pltpu.make_async_copy(held[i], refs[n + i], sems_out.at[i]) for i in range(n)]
    for copy in arrive:
        copy.start()
    for i in range(n):
        arrive[i].wait()
        leave[i].start()
    for copy in leave:
        copy.wait()


def hand_over(values):
    return pl.pallas_call(
        hand_over_kernel,
        in_specs=[hbm()] * len(values),
        out_specs=[hbm()] * len(values),
        out_shape=[jax.ShapeDtypeStruct(v.shape, v.dtype) for v in values],
        scratch_shapes=[*[pltpu.VMEM(v.shape, v.dtype) for v in values], *dma_sems(len(values), len(values))],
        compiler_params=pltpu.CompilerParams(vmem_limit_bytes=LIMIT),
        name="results",
    )(*values)


def by_pair(v):
    return v.reshape(v.shape[0], 3, 6, 128).transpose(0, 2, 1, 3).reshape(v.shape[0], 3 * D)


def by_kind(v):
    return v.reshape(v.shape[0], 6, 3, 128).transpose(0, 2, 1, 3).reshape(v.shape[0], 3 * D)


def with_own_copies(inputs, row_kind, w_qkv, w_out, w_up, w_down, vectors, b_up, out_grad):
    x, dm = inputs.transpose(1, 0, 2), out_grad.transpose(1, 0, 2)
    h1t, qkv, p, attn, rl, x1, dmp, h2t, g, slope, gdown, vec, xb, watt, wup, down = forward(
        row_kind, x, dm, w_qkv, w_out, w_up, w_down, (*vectors, b_up))
    yb, dx1, da, gup, sums, gdown = ffn_back(
        x1, dmp, g, slope, wup.reshape(D, FF), down.reshape(FF, D), h2t, vec, gdown)
    results = attn_back(xb, yb, dx1, da, h1t, qkv, p, attn, rl, watt.reshape(D, UP_AT), vec, sums, gup)
    out, gx, gqkv, gout, gup, gdown, *small = hand_over((*results[:5], gdown, *results[5:]))
    return out.transpose(1, 0, 2), gx.transpose(1, 0, 2), gqkv, gout, gup, gdown, small[:NV], small[NV]


def with_collectives(inputs, row_kind, w_qkv, w_out, w_up, w_down, vectors, b_up, out_grad):
    axes = ("dp", "fsdp")
    get = lambda v: lax.all_gather(v, axes, axis=0, tiled=True)
    wide = jnp.concatenate([by_pair(get(w_qkv)), get(w_out), get(w_up)], 1)
    down = get(w_down)
    full = [get(v).astype(F32) for v in vectors]
    vec = jnp.stack(full)
    bu = get(b_up).astype(F32)[None]
    bqkv = by_pair(jnp.concatenate([full[BQ], jnp.zeros_like(full[BQ]), full[BV]])[None])
    h1, qkv, p, attn, rl, x1 = attn_fwd(row_kind, inputs, wide, bqkv, vec)
    outputs, dx1, gup, gdown, gbu, gg2, gb2, gbd = ffn(x1, out_grad, wide, down, bu, vec)
    input_grad, gqkv, gout, gbqkv, gbo, gg1, gb1 = attn_bwd(inputs, dx1, h1, qkv, p, attn, rl, wide, vec)
    gbqkv = by_kind(gbqkv)
    small = [gg1, gb1, gbqkv[:, :D], gbqkv[:, 2 * D:], gbo, gg2, gb2, gbd]
    give = lambda v: lax.psum_scatter(v.astype(F32), axes, scatter_dimension=0, tiled=True)
    return (
        outputs, input_grad, give(by_kind(gqkv)), give(gout), give(gup), give(gdown),
        [give(v[0]) for v in small], give(gbu[0]),
    )


def on_device(
    copies, inputs, row_kind, ln1_gain, ln1_bias, w_qkv, b_query, b_value, w_out, b_out, ln2_gain, ln2_bias,
    w_up, b_up, w_down, b_down, out_grad,
):
    vectors = (ln1_gain, ln1_bias, b_query, b_value, b_out, ln2_gain, ln2_bias, b_down)
    run = with_own_copies if copies else with_collectives
    outputs, input_grad, gqkv, gout, gup, gdown, small, gbu = run(
        inputs, row_kind, w_qkv, w_out, w_up, w_down, vectors, b_up, out_grad)
    gg1, gb1, gbq, gbv, gbo, gg2, gb2, gbd = small
    return outputs, input_grad, gg1, gb1, gqkv, gbq, gbv, gout, gbo, gg2, gb2, gup, gbu, gdown, gbd


def solution(mesh):
    both = ("dp", "fsdp")
    row = P(both)
    mat = P(both, None)
    act = P(both, None, None)
    in_specs = (act, row, row, row, mat, row, row, mat, row, row, row, mat, row, mat, row, act)
    out_specs = (act, act, row, row, mat, row, row, mat, row, row, row, mat, row, mat, row)
    copies = mesh.shape["dp"] == 2 * NZ and mesh.shape["fsdp"] == 4
    return jax.shard_map(
        functools.partial(on_device, copies), mesh=mesh, in_specs=in_specs, out_specs=out_specs, check_vma=False
    )
```
